32 devices in a mesh: groups: 2 (over y), cls: 4 (over z), img: 4 (over x, core).
Axes of the slice: x: 2, y: 2, z: 4, core: 2. Of those that a mesh axis runs over, the one named last changes fastest.
Arguments:
- particles: bfloat16 [512, 2, 4608], P(('groups', 'img', 'cls')), parts along dimension 0, may hold values from -30 to 30
- classes: bfloat16 [256, 2, 4608], P(('groups', 'cls')), parts along dimension 0, may hold values from -4 to 4
- ctf: float32 [128, 4608], P('groups'), parts along dimension 0, may hold values from 0.1 to 1
- noise_weight: float32 [9216], P('groups'), parts along dimension 0, may hold values from 0.01 to 0.1
- group_ids: int32 [512], P(('groups', 'img', 'cls')), parts along dimension 0, may hold values from 0 to 63
- shifts: int32 [48, 2], P('groups'), parts along dimension 0, may hold values from -6 to 6
Outputs:
- log_resp: float32 [512, 128], P(('groups', 'img'), 'cls'), parts along dimension 0
- averages: float32 [256, 2, 4608], P(('groups', 'cls'), None, 'img'), parts along dimension 0
The draws below stay inside these ranges and needn't reach their ends.
There are 2 independent parts, one for each index of `groups`. The reference program is written for one: setup_inputs(seed, part) draws one part's arguments, and reference() takes and returns one part's arrays. A program takes and returns all parts, laid end to end along the dimension named above; each array names one. Nothing has to cross between parts.
All inputs are finite; a program needn't handle non-finite values.
Results may differ from the reference program's by a relative error of at most 0.012.
The reference program's roundings to bfloat16 on the way (of `templates`, `weighted` and `rho_low`) count: a program that leaves them out, or rounds other values in their place, can miss the bound.
Values may be sent and summed in bfloat16 or wider, within the bound.
No kernel may reach another device: no remote copies, remote signals or barrier semaphores. Data moves between devices by JAX's collectives and lax.ppermute only.
A program may use at most 128 MiB of HBM per device.

```python
import math
import jax
import jax.numpy as jnp
from jax import lax

FREQ = 4608
BOX = 128
POSES = 24
GROUPS = 64
CLASSES = 128
PARTICLES = 256


def class_values(key):
    inner = jax.random.fold_in(key, 11)
    values = jnp.clip(jax.random.normal(inner, (CLASSES, 2, FREQ), jnp.float32), -4.0, 4.0)
    return values


def draw_classes(key, part):
    return class_values(key).astype(jnp.bfloat16)


def draw_shifts(key, part):
    return jax.random.randint(jax.random.fold_in(key, 12), (POSES, 2), -6, 7).astype(jnp.int32)


def rotate_rows(values, cos_rows, sin_rows):
    real_part = values[:, 0, :]
    imag_part = values[:, 1, :]
    return jnp.stack([real_part * cos_rows - imag_part * sin_rows, real_part * sin_rows + imag_part * cos_rows], axis=1)


def draw_particles(key, part):
    key_noise = jax.random.fold_in(key, 21)
    key_class = jax.random.fold_in(key, 23)
    key_pose = jax.random.fold_in(key, 24)
    noise = jnp.clip(jax.random.normal(key_noise, (PARTICLES, 2, FREQ), jnp.float32), -4.0, 4.0)
    values = class_values(key).astype(jnp.bfloat16).astype(jnp.float32)
    shifts = draw_shifts(key, part)
    first = jax.random.randint(key_class, (PARTICLES,), 0, CLASSES)
    second = (first + 1) % CLASSES
    pose = jax.random.randint(key_pose, (PARTICLES,), 0, POSES)
    index = jnp.arange(FREQ)
    along_y = (index // BOX).astype(jnp.float32)
    along_x = (index % BOX - BOX // 2).astype(jnp.float32)
    chosen = shifts[pose]
    angle = 2.0 * jnp.pi / BOX * (chosen[:, 0:1].astype(jnp.float32) * along_x[None, :] + chosen[:, 1:2].astype(jnp.float32) * along_y[None, :])
    cos_rows = jnp.cos(angle)
    sin_rows = jnp.sin(angle)
    planted = rotate_rows(values[first], cos_rows, sin_rows) + 0.992 * rotate_rows(values[second], cos_rows, sin_rows)
    rows = jnp.arange(PARTICLES)
    boost = 4608.0 / FREQ
    strength = boost * jnp.where(rows % 3 == 0, 0.9, jnp.where(rows % 3 == 1, 1.3, 1.8))
    chosen_rows = rows % 61 == 7
    result = jnp.where(chosen_rows[:, None, None], strength[:, None, None] * planted, noise)
    return result.astype(jnp.bfloat16)


def with_ends(values, own_key, smallest, top_value):
    extent = values.shape
    index_at = [jax.random.randint(jax.random.fold_in(own_key, axis), (), 0, extent[axis]) for axis in range(len(extent))]
    values = values.at[tuple(index_at)].set(smallest)
    longest = extent.index(max(extent))
    index_at[longest] = (index_at[longest] + 1) % extent[longest]
    return values.at[tuple(index_at)].set(top_value)


def setup_inputs(seed: int = 0, part: int = 0) -> dict:
    splits = jax.random.split(jax.random.key(seed), 7)
    part_splits = jax.random.split(jax.random.fold_in(splits[6], part), 7)
    particles = draw_particles(jax.random.fold_in(jax.random.fold_in(splits[6], part), 71), part)
    classes = draw_classes(jax.random.fold_in(jax.random.fold_in(splits[6], part), 71), part)
    ctf = jnp.clip(jax.random.uniform(part_splits[2], (GROUPS, FREQ), jnp.float32, 0.1, 1.0), 0.1, 1.0)
    noise_weight = jnp.clip(jnp.exp(jax.random.uniform(part_splits[3], (FREQ,), jnp.float32, math.log(0.01), math.log(0.1))), 0.01, 0.1)
    group_ids = with_ends(jax.random.randint(part_splits[4], (PARTICLES,), 0, GROUPS), jax.random.fold_in(part_splits[4], 1), 0, GROUPS - 1).astype(jnp.int32)
    shifts = draw_shifts(jax.random.fold_in(jax.random.fold_in(splits[6], part), 71), part)
    return dict(particles=particles, classes=classes, ctf=ctf, noise_weight=noise_weight, group_ids=group_ids, shifts=shifts)


prior_precision = 0.02


def phase_tables(shifts):
    index = jnp.arange(FREQ)
    along_y = (index // BOX).astype(jnp.float32)
    along_x = (index % BOX - BOX // 2).astype(jnp.float32)
    angle = (2.0 * jnp.pi / BOX) * (shifts[:, 0:1].astype(jnp.float32) * along_x[None, :] + shifts[:, 1:2].astype(jnp.float32) * along_y[None, :])
    return jnp.cos(angle), jnp.sin(angle)


def reference(particles, classes, ctf, noise_weight, group_ids, shifts):
    cos_t, sin_t = phase_tables(shifts)
    real_part = classes[:, 0, :].astype(jnp.float32)
    imag_part = classes[:, 1, :].astype(jnp.float32)
    temp_re = real_part[None] * cos_t[:, None, :] - imag_part[None] * sin_t[:, None, :]
    temp_im = real_part[None] * sin_t[:, None, :] + imag_part[None] * cos_t[:, None, :]
    templates = jnp.stack([temp_re, temp_im], axis=2).astype(jnp.bfloat16)
    templates = templates.reshape(POSES * CLASSES, 2 * FREQ)
    selected = ctf[group_ids]
    weighted = (particles.astype(jnp.float32) * (selected * noise_weight[None, :])[:, None, :]).astype(jnp.bfloat16)
    weighted = weighted.reshape(PARTICLES, 2 * FREQ)
    ctf_weight = ctf * ctf * noise_weight[None, :]
    power = jnp.dot(ctf_weight, (real_part * real_part + imag_part * imag_part).T, precision=lax.Precision.HIGHEST)
    penalty = power[group_ids]
    cross = jnp.dot(weighted.astype(jnp.float32), templates.astype(jnp.float32).T, precision=lax.Precision.HIGHEST)
    scores = cross.reshape(PARTICLES, POSES, CLASSES) - 0.5 * penalty[:, None, :]
    peak = jnp.max(scores, axis=(1, 2))
    log_norm = peak + jnp.log(jnp.sum(jnp.exp(scores - peak[:, None, None]), axis=(1, 2)))
    pose_peak = jnp.max(scores, axis=1)
    log_resp = pose_peak + jnp.log(jnp.sum(jnp.exp(scores - pose_peak[:, None, :]), axis=1)) - log_norm[:, None]
    rho = jnp.exp(scores - log_norm[:, None, None])
    rho_low = rho.astype(jnp.bfloat16).reshape(PARTICLES, POSES * CLASSES)
    sums = jnp.dot(rho_low.astype(jnp.float32).T, weighted.astype(jnp.float32), precision=lax.Precision.HIGHEST)
    sums = sums.reshape(POSES, CLASSES, 2, FREQ)
    cos_b = cos_t[:, None, :]
    sin_b = sin_t[:, None, :]
    numer_re = jnp.sum(sums[:, :, 0, :] * cos_b + sums[:, :, 1, :] * sin_b, axis=0)
    numer_im = jnp.sum(sums[:, :, 1, :] * cos_b - sums[:, :, 0, :] * sin_b, axis=0)
    numer = jnp.stack([numer_re, numer_im], axis=1)
    onehot = (group_ids[:, None] == jnp.arange(GROUPS)[None, :]).astype(jnp.float32)
    pose_total = jnp.sum(rho, axis=1)
    mass = jnp.dot(pose_total.T, onehot, precision=lax.Precision.HIGHEST)
    denom = jnp.dot(mass, ctf_weight, precision=lax.Precision.HIGHEST)
    averages = numer / (denom[:, None, :] + prior_precision)
    return log_resp, averages
```

```python
import functools

import jax
import jax.numpy as jnp
from jax import lax
from jax.experimental import pallas as pl
from jax.experimental.pallas import tpu as pltpu
from jax.sharding import PartitionSpec as P

BOX = 128
CHUNKS = 2
VMEM_LIMIT = 48 * 1024 * 1024

prior_precision = 0.02

NT = (((1,), (1,)), ((), ()))
NN = (((1,), (0,)), ((), ()))
HIGHEST = lax.Precision.HIGHEST
f32 = jnp.float32
bf16 = jnp.bfloat16


def phase_tables(shifts, freq):
    index = jnp.arange(freq)
    along_y = (index // BOX).astype(f32)
    along_x = (index % BOX - BOX // 2).astype(f32)
    angle = (
        2.0
        * jnp.pi
        / BOX
        * (
            shifts[:, 0:1].astype(f32) * along_x[None, :]
            + shifts[:, 1:2].astype(f32) * along_y[None, :]
        )
    )
    return (jnp.cos(angle), jnp.sin(angle))


def tile_of(extent):
    return max(t for t in range(128, 513, 128) if extent % t == 0)


def params(grid_rank):
    return pltpu.CompilerParams(
        dimension_semantics=("arbitrary",) * grid_rank, vmem_limit_bytes=VMEM_LIMIT
    )


def weigh_kernel(ids_ref, p_ref, ctf_ref, nw_ref, *refs):
    out_refs, scale_ref = refs[:-1], refs[-1]
    rows = p_ref.shape[0] // 2
    freq = p_ref.shape[1]
    for n in range(rows):
        row = ctf_ref[pl.ds(ids_ref[n], 1), :] * nw_ref[...]
        scale_ref[2 * n : 2 * n + 2, :] = jnp.broadcast_to(row, (2, freq))
    chunk = freq // len(out_refs)
    for c, out_ref in enumerate(out_refs):
        cut = slice(c * chunk, (c + 1) * chunk)
        out_ref[...] = (p_ref[:, cut].astype(f32) * scale_ref[:, cut]).astype(bf16)


def weigh(particles, ctf, noise_row, group_ids):
    rows, _, freq = particles.shape
    flat = particles.reshape(2 * rows, freq)
    vmem = pl.BlockSpec(memory_space=pltpu.VMEM)
    return pl.pallas_call(
        weigh_kernel,
        in_specs=[pl.BlockSpec(memory_space=pltpu.SMEM), vmem, vmem, vmem],
        out_specs=[vmem] * CHUNKS,
        out_shape=[jax.ShapeDtypeStruct((2 * rows, freq // CHUNKS), bf16)] * CHUNKS,
        scratch_shapes=[pltpu.VMEM((2 * rows, freq), f32)],
        compiler_params=pltpu.CompilerParams(vmem_limit_bytes=VMEM_LIMIT),
        cost_estimate=pl.CostEstimate(
            flops=4 * rows * freq, bytes_accessed=ctf.size * 4 + 8 * rows * freq, transcendentals=0
        ),
        name="weigh",
    )(group_ids, flat, ctf, noise_row)


def even_lanes(shape, axis):
    return lax.rem(lax.broadcasted_iota(jnp.int32, shape, axis), 2) == 0


def group_marks(lane_ids, groups):
    lanes = lane_ids.shape[1]
    return (lax.broadcasted_iota(jnp.int32, (groups, lanes), 0) == lane_ids).astype(f32)


def score_kernel(
    sources, first, last, poses, cls_ref, cos_ref, sin_ref, ctf_ref, nw_ref, ids_ref, *refs
):
    refs = list(refs)
    w_refs = [refs.pop(0) for _ in range(sources)]
    if not first:
        acc_in, pow_in, _ = [refs.pop(0) for _ in range(3)]
    acc_ref, pow_ref, all_ref = [refs.pop(0) for _ in range(3)]
    stat_ref = refs.pop(0) if last else None
    temp_ref = refs.pop(0)
    step = pl.program_id(0)
    rows, tile = cls_ref.shape[1], cls_ref.shape[2]

    @pl.when(step == 0)
    def _():
        acc_ref[...] = jnp.zeros_like(acc_ref) if first else acc_in[...]
        pow_ref[...] = jnp.zeros_like(pow_ref) if first else pow_in[...]

    re = cls_ref[0].astype(f32)
    im = cls_ref[1].astype(f32)
    for r in range(poses):
        cos_r = cos_ref[r : r + 1, :]
        sin_r = sin_ref[r : r + 1, :]
        temp_ref[r * rows : (r + 1) * rows, :tile] = (re * cos_r - im * sin_r).astype(bf16)
        temp_ref[r * rows : (r + 1) * rows, tile:] = (re * sin_r + im * cos_r).astype(bf16)
    weighted = jnp.concatenate([ref[...] for ref in w_refs], axis=0)
    all_ref[...] = weighted
    wide = weighted.astype(f32)
    even = even_lanes(wide.shape, 0)
    parts = jnp.concatenate(
        [jnp.where(even, wide, 0.0).astype(bf16), jnp.where(even, 0.0, wide).astype(bf16)], axis=1
    )
    acc_ref[...] += lax.dot_general(temp_ref[...], parts, NT, preferred_element_type=f32)
    ctf = ctf_ref[...]
    pow_ref[...] += lax.dot_general(
        re * re + im * im,
        ctf * ctf * nw_ref[...],
        NT,
        precision=HIGHEST,
        preferred_element_type=f32,
    )

    if last:

        @pl.when(step == pl.num_programs(0) - 1)
        def _():
            acc = acc_ref[...]
            lanes = acc.shape[1]
            acc = acc + jnp.where(
                even_lanes(acc.shape, 1),
                pltpu.roll(acc, lanes - 1, 1),
                pltpu.roll(acc, 1, 1),
            )
            penalty = lax.dot_general(
                pow_ref[...],
                group_marks(ids_ref[...], ctf.shape[0]),
                NN,
                precision=HIGHEST,
                preferred_element_type=f32,
            )
            scores = acc.reshape(poses, rows, lanes) - 0.5 * penalty[None]
            peak = jnp.max(jnp.max(scores, axis=0), axis=0, keepdims=True)
            total = jnp.sum(jnp.sum(jnp.exp(scores - peak[None]), axis=0), axis=0, keepdims=True)
            acc_ref[...] = scores.reshape(poses * rows, lanes)
            stat_ref[0:1, :] = peak
            stat_ref[1:2, :] = total
            stat_ref[2:8, :] = jnp.zeros((6, lanes), f32)


def score(chunk, parts, classes, cos_t, sin_t, ctf, noise_row, lane_ids, carried):
    rows, freq = classes.shape[1], classes.shape[2]
    poses, groups = cos_t.shape[0], ctf.shape[0]
    lanes = lane_ids.shape[1]
    span = freq // CHUNKS
    tile = tile_of(span)
    steps = span // tile
    first, last = chunk == 0, chunk == CHUNKS - 1
    base = chunk * steps

    def at(j):
        return (0, base + j)

    def whole(shape):
        return pl.BlockSpec(shape, lambda j: (0, 0))

    in_specs = [
        pl.BlockSpec((2, rows, tile), lambda j: (0, 0, base + j)),
        pl.BlockSpec((poses, tile), at),
        pl.BlockSpec((poses, tile), at),
        pl.BlockSpec((groups, tile), at),
        pl.BlockSpec((1, tile), at),
        whole((1, lanes)),
    ] + [pl.BlockSpec((p.shape[0], tile), lambda j: (0, j)) for p in parts]
    operands = [classes, cos_t, sin_t, ctf, noise_row, lane_ids, *parts]
    aliases = {}
    if not first:
        in_specs += [
            whole((poses * rows, lanes)),
            whole((rows, groups)),
            pl.BlockSpec(memory_space=pl.ANY),
        ]
        operands += list(carried)
        aliases = {len(operands) - 1: 2}
    out_specs = [
        whole((poses * rows, lanes)),
        whole((rows, groups)),
        pl.BlockSpec((lanes, tile), at),
    ]
    out_shape = [
        jax.ShapeDtypeStruct((poses * rows, lanes), f32),
        jax.ShapeDtypeStruct((rows, groups), f32),
        jax.ShapeDtypeStruct((lanes, freq), bf16),
    ]
    if last:
        out_specs.append(whole((8, lanes)))
        out_shape.append(jax.ShapeDtypeStruct((8, lanes), f32))
    return pl.pallas_call(
        functools.partial(score_kernel, len(parts), first, last, poses),
        grid=(steps,),
        in_specs=in_specs,
        out_specs=out_specs,
        out_shape=out_shape,
        scratch_shapes=[pltpu.VMEM((poses * rows, 2 * tile), bf16)],
        input_output_aliases=aliases,
        compiler_params=params(1),
        cost_estimate=pl.CostEstimate(
            flops=4 * 128 * poses * rows * span, bytes_accessed=4 * 300 * span, transcendentals=0
        ),
        name=f"score{chunk}",
    )(*operands)


def xor_blocks(values, block, distance):
    lanes = values.shape[1]
    lane = lax.broadcasted_iota(jnp.int32, values.shape, 1)
    width = block
    while distance:
        if distance % 2:
            low = lax.rem(lane // width, 2) == 0
            values = jnp.where(
                low, pltpu.roll(values, lanes - width, 1), pltpu.roll(values, width, 1)
            )
        distance //= 2
        width *= 2
    return values


def rotate_sum(rho, weighted, cos_ref, sin_ref, poses, rows, write):
    tile = weighted.shape[1]
    sums_re = jnp.dot(rho[0], weighted, preferred_element_type=f32)
    sums_im = jnp.dot(rho[1], weighted, preferred_element_type=f32)
    numer_re = jnp.zeros((rows, tile), f32)
    numer_im = jnp.zeros((rows, tile), f32)
    for r in range(poses):
        cos_r = cos_ref[r : r + 1, :]
        sin_r = sin_ref[r : r + 1, :]
        s_re = sums_re[r * rows : (r + 1) * rows]
        s_im = sums_im[r * rows : (r + 1) * rows]
        numer_re = numer_re + s_re * cos_r + s_im * sin_r
        numer_im = numer_im + s_im * cos_r - s_re * sin_r
    write(numer_re, numer_im)


def write_slices(out_refs, steps):
    def write(numer_re, numer_im):
        for s, ref in enumerate(out_refs):

            @pl.when(pl.program_id(0) // steps == s)
            def _():
                ref[0] = numer_re.astype(ref.dtype)
                ref[1] = numer_im.astype(ref.dtype)

    return write


def resp_kernel(
    poses, block, paired, steps, where_ref, s_ref, ids_ref, dest_ref, cos_ref, sin_ref, w_ref, *refs
):
    refs = list(refs)
    stat_refs, refs = refs[: len(paired)], refs[len(paired) :]
    resp_ref, rho_ref, mass_ref = refs[:3]
    out_refs = refs[3:]
    rows = mass_ref.shape[0]
    groups = mass_ref.shape[1]
    lanes = s_ref.shape[1]

    @pl.when(pl.program_id(0) == 0)
    def _():
        peaks, totals = [], []
        for ref, distance in zip(stat_refs, paired):
            for at in range(0, ref.shape[0], 8):
                stats = xor_blocks(ref[at : at + 8, :], block, distance)
                peaks.append(stats[0:1])
                totals.append(stats[1:2])
        peak = functools.reduce(jnp.maximum, peaks)
        total = sum(t * jnp.exp(p - peak) for t, p in zip(totals, peaks))
        log_norm = peak + jnp.log(total)
        scores = s_ref[...].reshape(poses, rows, lanes)
        pose_peak = jnp.max(scores, axis=0)
        log_resp = (
            pose_peak + jnp.log(jnp.sum(jnp.exp(scores - pose_peak[None]), axis=0)) - log_norm
        )
        particle_rows = lax.broadcasted_iota(jnp.int32, (resp_ref.shape[0], lanes), 0)
        resp_ref[...] = lax.dot_general(
            (particle_rows == dest_ref[...]).astype(f32),
            log_resp,
            NT,
            precision=HIGHEST,
            preferred_element_type=f32,
        )
        rho = jnp.exp(scores - log_norm[None])
        even = even_lanes((rows, lanes), 1)
        mass_ref[...] = lax.dot_general(
            jnp.where(even, jnp.sum(rho, axis=0), 0.0),
            group_marks(ids_ref[...], groups),
            NT,
            precision=HIGHEST,
            preferred_element_type=f32,
        )
        flat = rho.reshape(poses * rows, lanes)
        even = even_lanes(flat.shape, 1)
        rho_ref[0] = jnp.where(even, flat, 0.0).astype(bf16)
        rho_ref[1] = jnp.where(even, 0.0, flat).astype(bf16)

    rotate_sum(
        rho_ref, w_ref[...], cos_ref, sin_ref, poses, rows, write_slices(out_refs, steps)
    )


def rest_kernel(poses, rows, steps, where_ref, rho_ref, cos_ref, sin_ref, w_ref, *out_refs):
    rotate_sum(
        rho_ref, w_ref[...], cos_ref, sin_ref, poses, rows, write_slices(out_refs, steps)
    )


def slice_specs(tile, steps, poses, lanes):
    def at(j, where):
        return (0, where[j // steps] * steps + lax.rem(j, steps))

    return [
        pl.BlockSpec((poses, tile), at),
        pl.BlockSpec((poses, tile), at),
        pl.BlockSpec((lanes, tile), at),
    ]


def numer_specs(count, tile, steps, rows):
    def spec(s):
        return pl.BlockSpec(
            (2, rows, tile), lambda j, where: (0, 0, jnp.clip(j - s * steps, 0, steps - 1))
        )

    return [spec(s) for s in range(count)]


def pinned(shape):
    return pl.BlockSpec(shape, lambda j, where: (0,) * len(shape))


def responsibilities(
    where, scores, lane_ids, dest, cos_t, sin_t, weighted, stats, paired, block, rows, groups, span, n_rows
):
    poses, lanes = cos_t.shape[0], scores.shape[1]
    tile = tile_of(span)
    steps = span // tile
    count = where.shape[0]
    return pl.pallas_call(
        functools.partial(resp_kernel, poses, block, paired, steps),
        grid_spec=pltpu.PrefetchScalarGridSpec(
            num_scalar_prefetch=1,
            grid=(count * steps,),
            in_specs=[pinned(scores.shape), pinned(lane_ids.shape), pinned(dest.shape)]
            + slice_specs(tile, steps, poses, lanes)
            + [pinned(s.shape) for s in stats],
            out_specs=[
                pinned((n_rows, rows)),
                pinned((2, poses * rows, lanes)),
                pinned((rows, groups)),
            ]
            + numer_specs(count, tile, steps, rows),
        ),
        out_shape=[
            jax.ShapeDtypeStruct((n_rows, rows), f32),
            jax.ShapeDtypeStruct((2, poses * rows, lanes), bf16),
            jax.ShapeDtypeStruct((rows, groups), f32),
        ]
        + [jax.ShapeDtypeStruct((2, rows, span), bf16)] * count,
        compiler_params=params(1),
        cost_estimate=pl.CostEstimate(
            flops=4 * 128 * poses * rows * span * count,
            bytes_accessed=4 * 300 * span * count,
            transcendentals=0,
        ),
        name="responsibilities",
    )(where, scores, lane_ids, dest, cos_t, sin_t, weighted, *stats)


def remaining(where, rho, cos_t, sin_t, weighted, rows, span, dtypes):
    poses, lanes = cos_t.shape[0], weighted.shape[0]
    tile = tile_of(span)
    steps = span // tile
    count = where.shape[0]
    return pl.pallas_call(
        functools.partial(rest_kernel, poses, rows, steps),
        grid_spec=pltpu.PrefetchScalarGridSpec(
            num_scalar_prefetch=1,
            grid=(count * steps,),
            in_specs=[pinned(rho.shape)] + slice_specs(tile, steps, poses, lanes),
            out_specs=numer_specs(count, tile, steps, rows),
        ),
        out_shape=[jax.ShapeDtypeStruct((2, rows, span), d) for d in dtypes],
        compiler_params=params(1),
        cost_estimate=pl.CostEstimate(
            flops=4 * 128 * poses * rows * span * count,
            bytes_accessed=4 * 300 * span * count,
            transcendentals=0,
        ),
        name="remaining",
    )(where, rho, cos_t, sin_t, weighted)


def finish_kernel(count, where_ref, ctf_ref, nw_ref, *refs):
    mass_refs, refs = refs[:count], refs[count:]
    numer_refs, out_ref = refs[:count], refs[count]
    ctf = ctf_ref[...]
    mass = functools.reduce(jnp.add, [ref[...] for ref in mass_refs])
    denom = (
        lax.dot_general(
            mass, ctf * ctf * nw_ref[...], NN, precision=HIGHEST, preferred_element_type=f32
        )
        + prior_precision
    )
    for part in range(2):
        numer = functools.reduce(jnp.add, [ref[part].astype(f32) for ref in numer_refs])
        out_ref[:, part, :] = numer / denom


def finish(where, ctf, noise_row, masses, numers):
    groups = ctf.shape[0]
    _, rows, span = numers[0].shape
    tile = span
    count = len(masses)
    steps = span // tile

    def at(j, where):
        return (0, where[0] * steps + j)

    return pl.pallas_call(
        functools.partial(finish_kernel, count),
        grid_spec=pltpu.PrefetchScalarGridSpec(
            num_scalar_prefetch=1,
            grid=(steps,),
            in_specs=[pl.BlockSpec((groups, tile), at), pl.BlockSpec((1, tile), at)]
            + [pinned((rows, groups))] * count
            + [pl.BlockSpec((2, rows, tile), lambda j, where: (0, 0, j))] * count,
            out_specs=pl.BlockSpec((rows, 2, tile), lambda j, where: (0, 0, j)),
        ),
        out_shape=jax.ShapeDtypeStruct((rows, 2, span), f32),
        compiler_params=params(1),
        name="finish",
    )(where, ctf, noise_row, *masses, *numers)


def swap(values, axis, distance):
    size = lax.axis_size(axis)
    return lax.ppermute(values, axis, [(i, i ^ distance) for i in range(size)])


def local(particles, classes, ctf, noise_weight, group_ids, shifts):
    part_rows, _, freq = particles.shape
    cls_rows = classes.shape[0]
    groups = ctf.shape[0]
    n_cls = lax.axis_size("cls")
    n_img = lax.axis_size("img")
    me_cls = lax.axis_index("cls")
    me_img = lax.axis_index("img")
    span = freq // n_img
    pairwise = n_cls <= 4
    noise_row = noise_weight[None, :]

    own = weigh(particles, ctf, noise_row, group_ids)
    if pairwise:
        ids = [group_ids] + [swap(group_ids, "cls", k) for k in range(1, n_cls)]
        lane_ids = jnp.repeat(jnp.concatenate(ids), 2)[None, :]
        owners = me_cls ^ jnp.arange(n_cls)
        gathered = [[w] + [swap(w, "cls", k) for k in range(1, n_cls)] for w in own]
    else:
        lane_ids = jnp.repeat(lax.all_gather(group_ids, "cls", axis=0, tiled=True), 2)[None, :]
        owners = jnp.arange(n_cls)
        gathered = [[lax.all_gather(w, "cls", axis=0, tiled=True)] for w in own]
    dest = owners[:, None] * part_rows + jnp.arange(part_rows)[None, :]
    dest = jnp.stack([dest, jnp.full_like(dest, -1)], axis=-1).reshape(1, -1).astype(jnp.int32)

    cos_t, sin_t = phase_tables(shifts, freq)
    split = jnp.transpose(classes, (1, 0, 2))
    carried = None
    for c in range(CHUNKS):
        carried = score(
            c, gathered[c], split, cos_t, sin_t, ctf, noise_row, lane_ids, carried
        )
    scores, _, weighted, stat = carried
    if pairwise:
        stats = [stat] + [swap(stat, "cls", k) for k in range(1, n_cls)]
        paired = tuple(range(n_cls))
    else:
        stats = [lax.all_gather(stat, "cls", axis=0, tiled=True)]
        paired = (0,)

    far = list(range(n_img - 1, 0, -1))
    early = max(1, n_img // 2)
    early, late = far[:early], far[early:]

    def slices(distances):
        return jnp.stack([me_img ^ d for d in distances]).astype(jnp.int32)

    log_resp, rho, mass, *first = responsibilities(
        slices(early),
        scores,
        lane_ids,
        dest,
        cos_t,
        sin_t,
        weighted,
        stats,
        paired,
        2 * part_rows,
        cls_rows,
        groups,
        span,
        part_rows * n_cls,
    )
    masses = [mass] + [swap(mass, "img", d) for d in far]
    numers = [swap(part, "img", d) for part, d in zip(first, early)]
    *second, mine = remaining(
        slices(late + [0]),
        rho,
        cos_t,
        sin_t,
        weighted,
        cls_rows,
        span,
        [bf16] * len(late) + [f32],
    )
    numers += [swap(part, "img", d) for part, d in zip(second, late)]
    averages = finish(slices([0]), ctf, noise_row, masses, [mine] + numers)
    return (log_resp, averages)


def solution(mesh):
    placed = (
        P(("groups", "img", "cls"), None, None),
        P(("groups", "cls"), None, None),
        P("groups", None),
        P("groups"),
        P(("groups", "img", "cls")),
        P("groups", None),
    )
    return jax.shard_map(
        local,
        mesh=mesh,
        in_specs=placed,
        out_specs=(P(("groups", "img"), "cls"), P(("groups", "cls"), None, "img")),
        check_vma=False,
    )
```

```python
import functools

import jax
import jax.numpy as jnp
from jax import lax
from jax.experimental import pallas as pl
from jax.experimental.pallas import tpu as pltpu
from jax.sharding import PartitionSpec as P

BOX = 128
CHUNKS = 2
LANES = 128
VMEM_LIMIT = 24 * 1024 * 1024

prior_precision = 0.02

NT = (((1,), (1,)), ((), ()))
NN = (((1,), (0,)), ((), ()))
HIGHEST = lax.Precision.HIGHEST
f32 = jnp.float32
bf16 = jnp.bfloat16

SMEM = pl.BlockSpec(memory_space=pltpu.SMEM)
VMEM = pl.BlockSpec(memory_space=pltpu.VMEM)
ANY = pl.BlockSpec(memory_space=pl.ANY)


def phase_tables(shifts, freq):
    index = jnp.arange(freq)
    along_y = (index // BOX).astype(f32)
    along_x = (index % BOX - BOX // 2).astype(f32)
    angle = (
        2.0
        * jnp.pi
        / BOX
        * (
            shifts[:, 0:1].astype(f32) * along_x[None, :]
            + shifts[:, 1:2].astype(f32) * along_y[None, :]
        )
    )
    return (jnp.cos(angle), jnp.sin(angle))


def call(kernel, name, in_specs, out_shape, operands, scratch=(), flops=0, moved=0, out_specs=None):
    return pl.pallas_call(
        kernel,
        in_specs=in_specs,
        out_specs=[VMEM] * len(out_shape) if out_specs is None else out_specs,
        out_shape=out_shape,
        scratch_shapes=list(scratch),
        compiler_params=pltpu.CompilerParams(vmem_limit_bytes=VMEM_LIMIT),
        cost_estimate=pl.CostEstimate(flops=flops, bytes_accessed=moved, transcendentals=0),
        name=name,
    )(*operands)


def even_index(shape, axis):
    return lax.rem(lax.broadcasted_iota(jnp.int32, shape, axis), 2) == 0


def weigh_kernel(ids_ref, p_ref, ctf_ref, nw_ref, *refs):
    out_refs, (rows_ref, scale_ref, sem) = refs[:-3], refs[-3:]
    count, _, freq = p_ref.shape
    copies = [
        pltpu.make_async_copy(
            ctf_ref.at[pl.ds(ids_ref[n], 1), :], rows_ref.at[pl.ds(n, 1), :], sem.at[n]
        )
        for n in range(count)
    ]
    for copy in copies:
        copy.start()
    row = lax.broadcasted_iota(jnp.int32, (2 * count, LANES), 0) // 2
    ids = jnp.zeros((2 * count, LANES), f32)
    for n in range(count):
        ids = jnp.where(row == n, ids_ref[n].astype(f32), ids)
    values = p_ref[...].astype(f32).reshape(2 * count, freq)
    for copy in copies:
        copy.wait()
    scale = rows_ref[...] * nw_ref[...]
    for n in range(count):
        scale_ref[2 * n : 2 * n + 2, :] = jnp.broadcast_to(scale[n : n + 1], (2, freq))
    weighted = (values * scale_ref[...]).astype(bf16)
    chunk = freq // len(out_refs)
    for c, out_ref in enumerate(out_refs):
        out_ref[:, :chunk] = weighted[:, c * chunk : (c + 1) * chunk]
    out_refs[0][:, chunk:] = ids.astype(bf16)


def weigh(particles, ctf, noise_weight, group_ids):
    rows, _, freq = particles.shape
    chunk = freq // CHUNKS
    return call(
        weigh_kernel,
        "weigh",
        [SMEM, VMEM, ANY, VMEM],
        [
            jax.ShapeDtypeStruct((2 * rows, chunk + (LANES if c == 0 else 0)), bf16)
            for c in range(CHUNKS)
        ],
        (group_ids, particles, pltpu.with_memory_space_constraint(ctf, pltpu.HBM), noise_weight),
        [
            pltpu.VMEM((rows, freq), f32),
            pltpu.VMEM((2 * rows, freq), f32),
            pltpu.SemaphoreType.DMA((rows,)),
        ],
        flops=4 * rows * freq,
        moved=16 * rows * freq,
    )


def template_kernel(cls_ref, cos_ref, sin_ref, ctf_ref, nw_ref, temp_ref, pow_ref):
    _, rows, freq = cls_ref.shape
    poses = cos_ref.shape[0]

    @pl.loop(0, freq // LANES)
    def _(t):
        at = pl.ds(pl.multiple_of(t * LANES, LANES), LANES)
        later = pl.ds(pl.multiple_of(freq + t * LANES, LANES), LANES)
        re = cls_ref[0, :, at].astype(f32)
        im = cls_ref[1, :, at].astype(f32)
        for r in range(poses):
            cos_r = cos_ref[r : r + 1, at]
            sin_r = sin_ref[r : r + 1, at]
            temp_ref[r * rows : (r + 1) * rows, at] = (re * cos_r - im * sin_r).astype(bf16)
            temp_ref[r * rows : (r + 1) * rows, later] = (re * sin_r + im * cos_r).astype(bf16)

    cut = freq // 4
    power = jnp.zeros(pow_ref.shape, f32)
    for q in range(4):
        at = slice(q * cut, (q + 1) * cut)
        re = cls_ref[0, :, at].astype(f32)
        im = cls_ref[1, :, at].astype(f32)
        ctf = ctf_ref[:, at]
        power += lax.dot_general(
            re * re + im * im,
            ctf * ctf * nw_ref[:, at],
            NT,
            precision=HIGHEST,
            preferred_element_type=f32,
        )
    pow_ref[...] = power


def build_templates(split, cos_t, sin_t, ctf, noise_weight):
    _, rows, freq = split.shape
    poses, groups = cos_t.shape[0], ctf.shape[0]
    return call(
        template_kernel,
        "templates",
        [VMEM] * 5,
        [
            pltpu.VMEM((poses * rows, 2 * freq), bf16),
            jax.ShapeDtypeStruct((rows, groups), f32),
        ],
        (split, cos_t, sin_t, ctf, noise_weight),
        flops=40 * poses * rows * freq,
        moved=4 * poses * rows * freq,
    )


def add_products(acc_ref, temp_ref, parts, chunk, span):
    freq = temp_ref.shape[1] // 2
    tile = max(t for t in range(LANES, 1153, LANES) if span % t == 0)
    lanes = acc_ref.shape[1]
    even = even_index((lanes, tile), 0)
    for t in range(span // tile):
        at = slice(t * tile, (t + 1) * tile)
        where = chunk * span + t * tile
        wide = jnp.concatenate([p[:, at] for p in parts], axis=0).astype(f32)
        acc_ref[...] += lax.dot_general(
            temp_ref[:, where : where + tile],
            jnp.where(even, wide, 0.0).astype(bf16),
            NT,
            preferred_element_type=f32,
        ) + lax.dot_general(
            temp_ref[:, freq + where : freq + where + tile],
            jnp.where(even, 0.0, wide).astype(bf16),
            NT,
            preferred_element_type=f32,
        )


def score_kernel(chunk, span, temp_ref, *refs):
    *parts, acc_ref = refs if chunk == 0 else refs[1:]
    acc_ref[...] = jnp.zeros_like(acc_ref) if chunk == 0 else refs[0][...]
    add_products(acc_ref, temp_ref, parts, chunk, span)


def last_score_kernel(sources, span, temp_ref, pow_ref, *refs):
    refs = list(refs)
    s_ref, all_ref, marks_ref, stat_ref = refs[-4:]
    chunks = [refs[c * sources : (c + 1) * sources] for c in range(CHUNKS)]
    rows, groups = pow_ref.shape
    lanes = s_ref.shape[1]
    poses = s_ref.shape[0] // rows
    s_ref[...] = refs[-5][...] if CHUNKS > 1 else jnp.zeros_like(s_ref)
    add_products(s_ref, temp_ref, chunks[-1], CHUNKS - 1, span)
    for c, parts in enumerate(chunks):
        at = 0
        for p in parts:
            all_ref[at : at + p.shape[0], c * span : (c + 1) * span] = p[:, :span]
            at += p.shape[0]
    ids = jnp.concatenate([p[:, span:] for p in chunks[0]], axis=0).astype(f32)
    group = lax.broadcasted_iota(jnp.int32, (lanes, groups), 1).astype(f32)
    marks = (ids[:, :groups] == group).astype(f32)
    marks_ref[...] = marks
    penalty = lax.dot_general(
        pow_ref[...], marks, NT, precision=HIGHEST, preferred_element_type=f32
    )
    acc = s_ref[...]
    acc = acc + jnp.where(
        even_index(acc.shape, 1), pltpu.roll(acc, lanes - 1, 1), pltpu.roll(acc, 1, 1)
    )
    scores = acc.reshape(poses, rows, lanes) - 0.5 * penalty[None]
    peak = jnp.max(jnp.max(scores, axis=0), axis=0, keepdims=True)
    total = jnp.sum(jnp.sum(jnp.exp(scores - peak[None]), axis=0), axis=0, keepdims=True)
    s_ref[...] = scores.reshape(poses * rows, lanes)
    stat_ref[0:1, :] = peak
    stat_ref[1:2, :] = total
    stat_ref[2:8, :] = jnp.zeros((6, lanes), f32)


def score(temps, power, gathered, freq):
    span = freq // CHUNKS
    lanes = sum(p.shape[0] for p in gathered[0])
    acc_shape = jax.ShapeDtypeStruct((temps.shape[0], lanes), f32)
    flops = 2 * temps.shape[0] * 256 * 2 * span
    acc = []
    for c in range(CHUNKS - 1):
        operands = [temps, *acc, *gathered[c]]
        acc = call(
            functools.partial(score_kernel, c, span),
            f"score{c}",
            [VMEM] * len(operands),
            [acc_shape],
            operands,
            flops=flops,
        )
    operands = [temps, power, *[p for parts in gathered for p in parts], *acc]
    return call(
        functools.partial(last_score_kernel, len(gathered[0]), span),
        f"score{CHUNKS - 1}",
        [VMEM] * len(operands),
        [
            acc_shape,
            jax.ShapeDtypeStruct((lanes, freq), bf16),
            jax.ShapeDtypeStruct((lanes, power.shape[1]), f32),
            jax.ShapeDtypeStruct((8, lanes), f32),
        ],
        operands,
        flops=flops,
    )


def xor_blocks(values, block, distance):
    lanes = values.shape[1]
    lane = lax.broadcasted_iota(jnp.int32, values.shape, 1)
    width = block
    while distance:
        if distance % 2:
            low = lax.rem(lane // width, 2) == 0
            values = jnp.where(
                low, pltpu.roll(values, lanes - width, 1), pltpu.roll(values, width, 1)
            )
        distance //= 2
        width *= 2
    return values


def rotate_slice(rho_ref, w_ref, cos_ref, sin_ref, base, span, poses, buffers, write):
    rows = rho_ref.shape[1] // poses
    tiles = [(a, min(256, span - a)) for a in range(0, span, 256)]

    def products(i):
        start, width = tiles[i]
        at = pl.ds(pl.multiple_of(base + start, LANES), width)
        weighted = w_ref[:, at]
        buffer = buffers[i % 2]
        buffer[0, :, :width] = jnp.dot(rho_ref[0], weighted, preferred_element_type=f32)
        buffer[1, :, :width] = jnp.dot(rho_ref[1], weighted, preferred_element_type=f32)

    def rotate(i):
        start, width = tiles[i]
        buffer = buffers[i % 2]
        for a in range(0, width, LANES):
            at = pl.ds(pl.multiple_of(base + start + a, LANES), LANES)
            numer_re = jnp.zeros((rows, LANES), f32)
            numer_im = jnp.zeros((rows, LANES), f32)
            for r in range(poses):
                cos_r = cos_ref[r : r + 1, at]
                sin_r = sin_ref[r : r + 1, at]
                s_re = buffer[0, r * rows : (r + 1) * rows, a : a + LANES]
                s_im = buffer[1, r * rows : (r + 1) * rows, a : a + LANES]
                numer_re = numer_re + s_re * cos_r + s_im * sin_r
                numer_im = numer_im + s_im * cos_r - s_re * sin_r
            write(start + a, numer_re, numer_im)

    products(0)
    for i in range(1, len(tiles)):
        products(i)
        rotate(i - 1)
    rotate(len(tiles) - 1)


def write_to(ref, span):
    def write(at, numer_re, numer_im):
        ref[:, at : at + LANES] = numer_re.astype(ref.dtype)
        ref[:, span + at : span + at + LANES] = numer_im.astype(ref.dtype)

    return write


def resp_kernel(
    poses, block, paired, far, span, me_ref, s_ref, marks_ref, cos_ref, sin_ref, w_ref, *refs
):
    stat_refs, refs = refs[: len(paired)], refs[len(paired) :]
    resp_ref, rho_ref, mass_ref = refs[:3]
    out_refs, buffers = refs[3:-2], refs[-2:]
    rows, groups = mass_ref.shape
    lanes = s_ref.shape[1]
    peaks, totals = [], []
    for ref, distance in zip(stat_refs, paired):
        for at in range(0, ref.shape[0], 8):
            stats = xor_blocks(ref[at : at + 8, :], block, distance)
            peaks.append(stats[0:1])
            totals.append(stats[1:2])
    peak = functools.reduce(jnp.maximum, peaks)
    total = sum(t * jnp.exp(p - peak) for t, p in zip(totals, peaks))
    log_norm = peak + jnp.log(total)
    scores = s_ref[...].reshape(poses, rows, lanes)
    rho = jnp.exp(scores - log_norm[None])
    even = even_index((rows, lanes), 1)
    mass = lax.dot_general(
        jnp.where(even, jnp.sum(rho, axis=0), 0.0),
        marks_ref[...],
        NN,
        precision=HIGHEST,
        preferred_element_type=f32,
    )
    mass_ref[...] = mass
    high = mass.astype(bf16)
    low = (mass - high.astype(f32)).astype(bf16)
    for ref in out_refs:
        ref[:, 2 * span : 2 * span + groups] = high
        ref[:, 2 * span + groups :] = low
    flat = rho.reshape(poses * rows, lanes)
    even = even_index(flat.shape, 1)
    rho_ref[0] = jnp.where(even, flat, 0.0).astype(bf16)
    rho_ref[1] = jnp.where(even, 0.0, flat).astype(bf16)
    for ref, distance in zip(out_refs, far):
        base = (me_ref[0] ^ distance) * span
        rotate_slice(
            rho_ref, w_ref, cos_ref, sin_ref, base, span, poses, buffers, write_to(ref, span)
        )
    pose_peak = jnp.max(scores, axis=0)
    log_resp = pose_peak + jnp.log(jnp.sum(jnp.exp(scores - pose_peak[None]), axis=0)) - log_norm
    shape = (resp_ref.shape[1], lanes)
    lane = lax.broadcasted_iota(jnp.int32, shape, 1)
    row = ((lane // block) ^ me_ref[1]) * (block // 2) + lax.rem(lane, block) // 2
    take = (lax.broadcasted_iota(jnp.int32, shape, 0) == row) & (lax.rem(lane, 2) == 0)
    resp_ref[...] = lax.dot_general(
        log_resp, take.astype(f32), NT, precision=HIGHEST, preferred_element_type=f32
    )


def responsibilities(me, scores, marks, cos_t, sin_t, weighted, stats, paired, far, block, span):
    poses, lanes = cos_t.shape[0], scores.shape[1]
    rows, groups = scores.shape[0] // poses, marks.shape[1]
    return call(
        functools.partial(resp_kernel, poses, block, paired, far, span),
        "responsibilities",
        [SMEM] + [VMEM] * (5 + len(stats)),
        [
            jax.ShapeDtypeStruct((rows, lanes // 2), f32),
            jax.ShapeDtypeStruct((2, poses * rows, lanes), bf16),
            jax.ShapeDtypeStruct((rows, groups), f32),
        ]
        + [jax.ShapeDtypeStruct((rows, 2 * span + 2 * groups), bf16)] * len(far),
        (me, scores, marks, cos_t, sin_t, weighted, *stats),
        [pltpu.VMEM((2, poses * rows, 256), f32)] * 2,
        flops=4 * 256 * poses * rows * span * len(far),
    )


def own_kernel(poses, span, me_ref, rho_ref, cos_ref, sin_ref, w_ref, out_ref, *buffers):
    base = me_ref[0] * span
    rotate_slice(
        rho_ref, w_ref, cos_ref, sin_ref, base, span, poses, buffers, write_to(out_ref, span)
    )


def own_slice(me, rho, cos_t, sin_t, weighted, span):
    poses = cos_t.shape[0]
    rows = rho.shape[1] // poses
    return call(
        functools.partial(own_kernel, poses, span),
        "own_slice",
        [SMEM] + [VMEM] * 4,
        [jax.ShapeDtypeStruct((rows, 2 * span), f32)],
        (me, rho, cos_t, sin_t, weighted),
        [pltpu.VMEM((2, poses * rows, 256), f32)] * 2,
        flops=4 * 256 * poses * rows * span,
    )[0]


def finish_kernel(span, me_ref, ctf_ref, nw_ref, mass_ref, own_ref, *refs):
    received, out_ref = refs[:-1], refs[-1]
    groups = mass_ref.shape[1]
    at = pl.ds(pl.multiple_of(me_ref[0] * span, LANES), span)
    ctf = ctf_ref[:, at]
    mass = mass_ref[...]
    for ref in received:
        mass += ref[:, 2 * span : 2 * span + groups].astype(f32)
        mass += ref[:, 2 * span + groups :].astype(f32)
    denom = (
        lax.dot_general(
            mass,
            ctf * ctf * nw_ref[:, at],
            NN,
            precision=HIGHEST,
            preferred_element_type=f32,
        )
        + prior_precision
    )
    for part in range(2):
        cut = slice(part * span, (part + 1) * span)
        numer = own_ref[:, cut]
        for ref in received:
            numer += ref[:, cut].astype(f32)
        out_ref[:, part, :] = numer / denom


def finish(me, ctf, noise_weight, mass, own, received, span):
    rows = own.shape[0]
    return call(
        functools.partial(finish_kernel, span),
        "finish",
        [SMEM] + [VMEM] * (4 + len(received)),
        [jax.ShapeDtypeStruct((rows, 2, span), f32)],
        (me, ctf, noise_weight, mass, own, *received),
    )[0]


def swap(values, axis, distance):
    size = lax.axis_size(axis)
    return lax.ppermute(values, axis, [(i, i ^ distance) for i in range(size)])


def gather_pairs(shard):
    size = lax.axis_size("cls")
    slots = [shard]
    hop = 1
    while hop < size:
        if len(slots) == 1:
            slots.append(swap(shard, "cls", hop))
        else:
            direct = swap(shard, "cls", hop)
            slots += [direct] + [swap(direct, "cls", k) for k in range(1, hop)]
        hop *= 2
    return slots


def local(particles, classes, ctf, noise_weight, group_ids, shifts):
    part_rows, _, freq = particles.shape
    n_cls = lax.axis_size("cls")
    n_img = lax.axis_size("img")
    span = freq // n_img
    noise_weight = noise_weight[None, :]
    pairwise = n_cls <= 4
    me_cls = lax.axis_index("cls") if pairwise else 0
    me = jnp.stack([lax.axis_index("img"), me_cls]).astype(jnp.int32)

    shards = weigh(particles, ctf, noise_weight, group_ids)
    if pairwise:
        gathered = [gather_pairs(w) for w in shards]
    else:
        gathered = [[lax.all_gather(w, "cls", axis=0, tiled=True)] for w in shards]

    cos_t, sin_t = phase_tables(shifts, freq)
    split = jnp.transpose(classes, (1, 0, 2))
    temps, power = build_templates(split, cos_t, sin_t, ctf, noise_weight)
    scores, weighted, marks, stat = score(temps, power, gathered, freq)
    if pairwise:
        stats = [stat] + [swap(stat, "cls", k) for k in range(1, n_cls)]
        paired = tuple(range(n_cls))
    else:
        stats = [lax.all_gather(stat, "cls", axis=0, tiled=True)]
        paired = (0,)

    far = tuple(range(n_img - 1, 0, -1))
    log_resp, rho, mass, *parts = responsibilities(
        me, scores, marks, cos_t, sin_t, weighted, stats, paired, far, 2 * part_rows, span
    )
    received = [swap(part, "img", d) for part, d in zip(parts, far)]
    mine = own_slice(me, rho, cos_t, sin_t, weighted, span)
    averages = finish(me, ctf, noise_weight, mass, mine, received, span)
    return (log_resp.T, averages)


def solution(mesh):
    placed = (
        P(("groups", "img", "cls"), None, None),
        P(("groups", "cls"), None, None),
        P("groups", None),
        P("groups"),
        P(("groups", "img", "cls")),
        P("groups", None),
    )
    return jax.shard_map(
        local,
        mesh=mesh,
        in_specs=placed,
        out_specs=(P(("groups", "img"), "cls"), P(("groups", "cls"), None, "img")),
        check_vma=False,
    )
```

```python
import functools

import jax
import jax.numpy as jnp
from jax import lax
from jax.experimental import pallas as pl
from jax.experimental.pallas import tpu as pltpu
from jax.sharding import PartitionSpec as P

BOX = 128
CHUNKS = 2
LANES = 128
VMEM_LIMIT = 24 * 1024 * 1024

prior_precision = 0.02

NT = (((1,), (1,)), ((), ()))
NN = (((1,), (0,)), ((), ()))
HIGHEST = lax.Precision.HIGHEST
f32 = jnp.float32
bf16 = jnp.bfloat16

SMEM = pl.BlockSpec(memory_space=pltpu.SMEM)
VMEM = pl.BlockSpec(memory_space=pltpu.VMEM)
ANY = pl.BlockSpec(memory_space=pl.ANY)


def phase_tables(shifts, freq):
    along_x = (jnp.arange(BOX) - BOX // 2).astype(f32)
    along_y = jnp.arange(freq // BOX).astype(f32)
    step = 2.0 * jnp.pi / BOX
    angle_x = step * (shifts[:, 0:1].astype(f32) * along_x[None, :])
    angle_y = step * (shifts[:, 1:2].astype(f32) * along_y[None, :])
    return (jnp.cos(angle_x), jnp.sin(angle_x), jnp.cos(angle_y), jnp.sin(angle_y))


def call(kernel, name, in_specs, out_shape, operands, scratch=(), flops=0, moved=0, out_specs=None):
    return pl.pallas_call(
        kernel,
        in_specs=in_specs,
        out_specs=[VMEM] * len(out_shape) if out_specs is None else out_specs,
        out_shape=out_shape,
        scratch_shapes=list(scratch),
        compiler_params=pltpu.CompilerParams(vmem_limit_bytes=VMEM_LIMIT),
        cost_estimate=pl.CostEstimate(flops=flops, bytes_accessed=moved, transcendentals=0),
        name=name,
    )(*operands)


def even_index(shape, axis):
    return lax.rem(lax.broadcasted_iota(jnp.int32, shape, axis), 2) == 0


def weigh_kernel(ids_hbm, p_hbm, ctf_hbm, nw_hbm, *refs):
    out_refs, (ids_ref, p_ref, ctf_ref, nw_ref, scale_ref, sem) = refs[:-6], refs[-6:]
    count, _, freq = p_ref.shape
    copies = [
        pltpu.make_async_copy(source, target, sem.at[i])
        for i, (source, target) in enumerate(
            [(ids_hbm, ids_ref), (ctf_hbm, ctf_ref), (nw_hbm, nw_ref), (p_hbm, p_ref)]
        )
    ]
    for copy in copies:
        copy.start()
    copies[0].wait()
    row = lax.broadcasted_iota(jnp.int32, (2 * count, LANES), 0) // 2
    ids = jnp.zeros((2 * count, LANES), f32)
    for n in range(count):
        ids = jnp.where(row == n, ids_ref[n].astype(f32), ids)
    for copy in copies[1:]:
        copy.wait()
    noise = nw_ref[...].reshape(1, freq)
    for n in range(count):
        scale = ctf_ref[pl.ds(ids_ref[n], 1), :] * noise
        scale_ref[2 * n : 2 * n + 2, :] = jnp.broadcast_to(scale, (2, freq))
    values = p_ref[...].astype(f32).reshape(2 * count, freq)
    weighted = (values * scale_ref[...]).astype(bf16)
    chunk = freq // len(out_refs)
    for c, out_ref in enumerate(out_refs):
        out_ref[:, :chunk] = weighted[:, c * chunk : (c + 1) * chunk]
    out_refs[0][:, chunk:] = ids.astype(bf16)


def weigh(particles, ctf, noise_weight, group_ids):
    rows, _, freq = particles.shape
    chunk = freq // CHUNKS
    operands = (group_ids, particles, ctf, noise_weight)
    return call(
        weigh_kernel,
        "weigh",
        [ANY] * 4,
        [
            jax.ShapeDtypeStruct((2 * rows, chunk + (LANES if c == 0 else 0)), bf16)
            for c in range(CHUNKS)
        ],
        [pltpu.with_memory_space_constraint(x, pltpu.HBM) for x in operands],
        [
            pltpu.SMEM((rows,), jnp.int32),
            pltpu.VMEM(particles.shape, bf16),
            pltpu.VMEM(ctf.shape, f32),
            pltpu.VMEM((freq,), f32),
            pltpu.VMEM((2 * rows, freq), f32),
            pltpu.SemaphoreType.DMA((4,)),
        ],
        flops=4 * rows * freq,
        moved=16 * rows * freq,
    )


def template_kernel(
    cls_ref, xc_ref, xs_ref, yc_ref, ys_ref, ctf_ref, nw_ref, temp_ref, cos_ref, sin_ref, pow_ref
):
    _, rows, freq = cls_ref.shape
    poses = cos_ref.shape[0]
    x_cos, x_sin = xc_ref[...], xs_ref[...]
    for t in range(freq // BOX):
        y_cos = jnp.broadcast_to(yc_ref[:, t : t + 1], x_cos.shape)
        y_sin = jnp.broadcast_to(ys_ref[:, t : t + 1], x_cos.shape)
        cos_ref[:, t * BOX : (t + 1) * BOX] = x_cos * y_cos - x_sin * y_sin
        sin_ref[:, t * BOX : (t + 1) * BOX] = x_sin * y_cos + x_cos * y_sin

    @pl.loop(0, freq // LANES)
    def _(t):
        at = pl.ds(pl.multiple_of(t * LANES, LANES), LANES)
        later = pl.ds(pl.multiple_of(freq + t * LANES, LANES), LANES)
        re = cls_ref[0, :, at].astype(f32)
        im = cls_ref[1, :, at].astype(f32)
        for r in range(poses):
            cos_r = cos_ref[r : r + 1, at]
            sin_r = sin_ref[r : r + 1, at]
            temp_ref[r * rows : (r + 1) * rows, at] = (re * cos_r - im * sin_r).astype(bf16)
            temp_ref[r * rows : (r + 1) * rows, later] = (re * sin_r + im * cos_r).astype(bf16)

    cut = freq // 4
    power = jnp.zeros(pow_ref.shape, f32)
    for q in range(4):
        at = slice(q * cut, (q + 1) * cut)
        re = cls_ref[0, :, at].astype(f32)
        im = cls_ref[1, :, at].astype(f32)
        ctf = ctf_ref[:, at]
        power += lax.dot_general(
            re * re + im * im,
            ctf * ctf * nw_ref[:, at],
            NT,
            precision=HIGHEST,
            preferred_element_type=f32,
        )
    pow_ref[...] = power


def build_templates(split, tables, ctf, noise_weight):
    _, rows, freq = split.shape
    poses, groups = tables[0].shape[0], ctf.shape[0]
    return call(
        template_kernel,
        "templates",
        [VMEM] * 7,
        [
            pltpu.VMEM((poses * rows, 2 * freq), bf16),
            pltpu.VMEM((poses, freq), f32),
            pltpu.VMEM((poses, freq), f32),
            jax.ShapeDtypeStruct((rows, groups), f32),
        ],
        (split, *tables, ctf, noise_weight),
        flops=40 * poses * rows * freq,
        moved=4 * poses * rows * freq,
    )


def add_products(acc_ref, temp_ref, parts, chunk, span):
    freq = temp_ref.shape[1] // 2
    tile = max(t for t in range(LANES, 1153, LANES) if span % t == 0)
    lanes = acc_ref.shape[1]
    even = even_index((lanes, tile), 0)
    for t in range(span // tile):
        at = slice(t * tile, (t + 1) * tile)
        where = chunk * span + t * tile
        wide = jnp.concatenate([p[:, at] for p in parts], axis=0).astype(f32)
        acc_ref[...] += lax.dot_general(
            temp_ref[:, where : where + tile],
            jnp.where(even, wide, 0.0).astype(bf16),
            NT,
            preferred_element_type=f32,
        ) + lax.dot_general(
            temp_ref[:, freq + where : freq + where + tile],
            jnp.where(even, 0.0, wide).astype(bf16),
            NT,
            preferred_element_type=f32,
        )


def score_kernel(chunk, span, temp_ref, *refs):
    *parts, acc_ref = refs if chunk == 0 else refs[1:]
    acc_ref[...] = jnp.zeros_like(acc_ref) if chunk == 0 else refs[0][...]
    add_products(acc_ref, temp_ref, parts, chunk, span)


def last_score_kernel(sources, span, temp_ref, pow_ref, *refs):
    refs = list(refs)
    s_ref, all_ref, marks_ref, stat_ref = refs[-4:]
    chunks = [refs[c * sources : (c + 1) * sources] for c in range(CHUNKS)]
    rows, groups = pow_ref.shape
    lanes = s_ref.shape[1]
    poses = s_ref.shape[0] // rows
    s_ref[...] = refs[-5][...] if CHUNKS > 1 else jnp.zeros_like(s_ref)
    add_products(s_ref, temp_ref, chunks[-1], CHUNKS - 1, span)
    for c, parts in enumerate(chunks):
        at = 0
        for p in parts:
            all_ref[at : at + p.shape[0], c * span : (c + 1) * span] = p[:, :span]
            at += p.shape[0]
    ids = jnp.concatenate([p[:, span:] for p in chunks[0]], axis=0).astype(f32)
    group = lax.broadcasted_iota(jnp.int32, (lanes, groups), 1).astype(f32)
    marks = (ids[:, :groups] == group).astype(f32)
    marks_ref[...] = marks
    penalty = lax.dot_general(
        pow_ref[...], marks, NT, precision=HIGHEST, preferred_element_type=f32
    )
    acc = s_ref[...]
    acc = acc + jnp.where(
        even_index(acc.shape, 1), pltpu.roll(acc, lanes - 1, 1), pltpu.roll(acc, 1, 1)
    )
    scores = acc.reshape(poses, rows, lanes) - 0.5 * penalty[None]
    peak = jnp.max(jnp.max(scores, axis=0), axis=0, keepdims=True)
    total = jnp.sum(jnp.sum(jnp.exp(scores - peak[None]), axis=0), axis=0, keepdims=True)
    s_ref[...] = scores.reshape(poses * rows, lanes)
    stat_ref[0:1, :] = peak
    stat_ref[1:2, :] = total
    stat_ref[2:8, :] = jnp.zeros((6, lanes), f32)


def score(temps, power, gathered, freq):
    span = freq // CHUNKS
    lanes = sum(p.shape[0] for p in gathered[0])
    acc_shape = jax.ShapeDtypeStruct((temps.shape[0], lanes), f32)
    flops = 2 * temps.shape[0] * 256 * 2 * span
    acc = []
    for c in range(CHUNKS - 1):
        operands = [temps, *acc, *gathered[c]]
        acc = call(
            functools.partial(score_kernel, c, span),
            f"score{c}",
            [VMEM] * len(operands),
            [acc_shape],
            operands,
            flops=flops,
        )
    operands = [temps, power, *[p for parts in gathered for p in parts], *acc]
    return call(
        functools.partial(last_score_kernel, len(gathered[0]), span),
        f"score{CHUNKS - 1}",
        [VMEM] * len(operands),
        [
            acc_shape,
            jax.ShapeDtypeStruct((lanes, freq), bf16),
            jax.ShapeDtypeStruct((lanes, power.shape[1]), f32),
            jax.ShapeDtypeStruct((8, lanes), f32),
        ],
        operands,
        flops=flops,
    )


def xor_blocks(values, block, distance):
    lanes = values.shape[1]
    lane = lax.broadcasted_iota(jnp.int32, values.shape, 1)
    width = block
    while distance:
        if distance % 2:
            low = lax.rem(lane // width, 2) == 0
            values = jnp.where(
                low, pltpu.roll(values, lanes - width, 1), pltpu.roll(values, width, 1)
            )
        distance //= 2
        width *= 2
    return values


def rotate_slice(rho_ref, w_ref, cos_ref, sin_ref, base, span, poses, buffers, write):
    rows = rho_ref.shape[1] // poses
    tiles = [(a, min(256, span - a)) for a in range(0, span, 256)]

    def products(i):
        start, width = tiles[i]
        at = pl.ds(pl.multiple_of(base + start, LANES), width)
        weighted = w_ref[:, at]
        buffer = buffers[i % 2]
        buffer[0, :, :width] = jnp.dot(rho_ref[0], weighted, preferred_element_type=f32)
        buffer[1, :, :width] = jnp.dot(rho_ref[1], weighted, preferred_element_type=f32)

    def rotate(i):
        start, width = tiles[i]
        buffer = buffers[i % 2]
        for a in range(0, width, LANES):
            at = pl.ds(pl.multiple_of(base + start + a, LANES), LANES)
            numer_re = jnp.zeros((rows, LANES), f32)
            numer_im = jnp.zeros((rows, LANES), f32)
            for r in range(poses):
                cos_r = cos_ref[r : r + 1, at]
                sin_r = sin_ref[r : r + 1, at]
                s_re = buffer[0, r * rows : (r + 1) * rows, a : a + LANES]
                s_im = buffer[1, r * rows : (r + 1) * rows, a : a + LANES]
                numer_re = numer_re + s_re * cos_r + s_im * sin_r
                numer_im = numer_im + s_im * cos_r - s_re * sin_r
            write(start + a, numer_re, numer_im)

    products(0)
    for i in range(1, len(tiles)):
        products(i)
        rotate(i - 1)
    rotate(len(tiles) - 1)


def write_to(ref, span):
    def write(at, numer_re, numer_im):
        ref[:, at : at + LANES] = numer_re.astype(ref.dtype)
        ref[:, span + at : span + at + LANES] = numer_im.astype(ref.dtype)

    return write


def resp_kernel(
    poses, block, paired, far, span, me_ref, s_ref, marks_ref, cos_ref, sin_ref, w_ref, *refs
):
    stat_refs, refs = refs[: len(paired)], refs[len(paired) :]
    resp_ref, rho_ref, mass_ref = refs[:3]
    out_refs, buffers = refs[3:-2], refs[-2:]
    rows, groups = mass_ref.shape
    lanes = s_ref.shape[1]
    peaks, totals = [], []
    for ref, distance in zip(stat_refs, paired):
        for at in range(0, ref.shape[0], 8):
            stats = xor_blocks(ref[at : at + 8, :], block, distance)
            peaks.append(stats[0:1])
            totals.append(stats[1:2])
    peak = functools.reduce(jnp.maximum, peaks)
    total = sum(t * jnp.exp(p - peak) for t, p in zip(totals, peaks))
    log_norm = peak + jnp.log(total)
    scores = s_ref[...].reshape(poses, rows, lanes)
    rho = jnp.exp(scores - log_norm[None])
    even = even_index((rows, lanes), 1)
    mass = lax.dot_general(
        jnp.where(even, jnp.sum(rho, axis=0), 0.0),
        marks_ref[...],
        NN,
        precision=HIGHEST,
        preferred_element_type=f32,
    )
    mass_ref[...] = mass
    high = mass.astype(bf16)
    low = (mass - high.astype(f32)).astype(bf16)
    for ref in out_refs:
        ref[:, 2 * span : 2 * span + groups] = high
        ref[:, 2 * span + groups :] = low
    flat = rho.reshape(poses * rows, lanes)
    even = even_index(flat.shape, 1)
    rho_ref[0] = jnp.where(even, flat, 0.0).astype(bf16)
    rho_ref[1] = jnp.where(even, 0.0, flat).astype(bf16)
    for ref, distance in zip(out_refs, far):
        base = (me_ref[0] ^ distance) * span
        rotate_slice(
            rho_ref, w_ref, cos_ref, sin_ref, base, span, poses, buffers, write_to(ref, span)
        )
    pose_peak = jnp.max(scores, axis=0)
    log_resp = pose_peak + jnp.log(jnp.sum(jnp.exp(scores - pose_peak[None]), axis=0)) - log_norm
    shape = (resp_ref.shape[1], lanes)
    lane = lax.broadcasted_iota(jnp.int32, shape, 1)
    row = ((lane // block) ^ me_ref[1]) * (block // 2) + lax.rem(lane, block) // 2
    take = (lax.broadcasted_iota(jnp.int32, shape, 0) == row) & (lax.rem(lane, 2) == 0)
    resp_ref[...] = lax.dot_general(
        log_resp, take.astype(f32), NT, precision=HIGHEST, preferred_element_type=f32
    )


def responsibilities(me, scores, marks, cos_t, sin_t, weighted, stats, paired, far, block, span):
    poses, lanes = cos_t.shape[0], scores.shape[1]
    rows, groups = scores.shape[0] // poses, marks.shape[1]
    return call(
        functools.partial(resp_kernel, poses, block, paired, far, span),
        "responsibilities",
        [SMEM] + [VMEM] * (5 + len(stats)),
        [
            jax.ShapeDtypeStruct((rows, lanes // 2), f32),
            jax.ShapeDtypeStruct((2, poses * rows, lanes), bf16),
            jax.ShapeDtypeStruct((rows, groups), f32),
        ]
        + [jax.ShapeDtypeStruct((rows, 2 * span + 2 * groups), bf16)] * len(far),
        (me, scores, marks, cos_t, sin_t, weighted, *stats),
        [pltpu.VMEM((2, poses * rows, 256), f32)] * 2,
        flops=4 * 256 * poses * rows * span * len(far),
    )


def own_kernel(
    poses, span, me_ref, rho_ref, cos_ref, sin_ref, w_ref, ctf_ref, nw_ref, out_ref, cw_ref, *buffers
):
    base = me_ref[0] * span
    at = pl.ds(pl.multiple_of(base, LANES), span)
    ctf = ctf_ref[:, at]
    cw_ref[...] = ctf * ctf * nw_ref[:, at]
    rotate_slice(
        rho_ref, w_ref, cos_ref, sin_ref, base, span, poses, buffers, write_to(out_ref, span)
    )


def own_slice(me, rho, cos_t, sin_t, weighted, ctf, noise_weight, span):
    poses = cos_t.shape[0]
    rows = rho.shape[1] // poses
    return call(
        functools.partial(own_kernel, poses, span),
        "own_slice",
        [SMEM] + [VMEM] * 6,
        [
            jax.ShapeDtypeStruct((rows, 2 * span), f32),
            jax.ShapeDtypeStruct((ctf.shape[0], span), f32),
        ],
        (me, rho, cos_t, sin_t, weighted, ctf, noise_weight),
        [pltpu.VMEM((2, poses * rows, 256), f32)] * 2,
        flops=4 * 256 * poses * rows * span,
    )


def finish_kernel(span, cw_ref, mass_ref, own_ref, *refs):
    received, out_ref = refs[:-1], refs[-1]
    groups = mass_ref.shape[1]
    mass = mass_ref[...]
    for ref in received:
        mass += ref[:, 2 * span : 2 * span + groups].astype(f32)
        mass += ref[:, 2 * span + groups :].astype(f32)
    denom = (
        lax.dot_general(
            mass,
            cw_ref[...],
            NN,
            precision=HIGHEST,
            preferred_element_type=f32,
        )
        + prior_precision
    )
    for part in range(2):
        cut = slice(part * span, (part + 1) * span)
        numer = own_ref[:, cut]
        for ref in received:
            numer += ref[:, cut].astype(f32)
        out_ref[:, part, :] = numer / denom


def finish(weight, mass, own, received, span):
    rows = own.shape[0]
    return call(
        functools.partial(finish_kernel, span),
        "finish",
        [VMEM] * (3 + len(received)),
        [jax.ShapeDtypeStruct((rows, 2, span), f32)],
        (weight, mass, own, *received),
    )[0]


def swap(values, axis, distance):
    size = lax.axis_size(axis)
    return lax.ppermute(values, axis, [(i, i ^ distance) for i in range(size)])


def direct_shards(shard):
    distances = [1 << b for b in range(lax.axis_size("cls").bit_length() - 1)]
    return [swap(shard, "cls", d) for d in distances]


def gather_pairs(shard, direct):
    slots = [shard]
    for i, arrived in enumerate(direct):
        slots += [arrived] + [swap(arrived, "cls", k) for k in range(1, 1 << i)]
    return slots


def local(particles, classes, ctf, noise_weight, group_ids, shifts):
    part_rows, _, freq = particles.shape
    n_cls = lax.axis_size("cls")
    n_img = lax.axis_size("img")
    span = freq // n_img
    pairwise = n_cls <= 4
    me_cls = lax.axis_index("cls") if pairwise else 0
    me = jnp.stack([lax.axis_index("img"), me_cls]).astype(jnp.int32)

    shards = weigh(particles, ctf, noise_weight, group_ids)
    noise_weight = noise_weight[None, :]
    if pairwise:
        direct = [direct_shards(w) for w in shards]
    else:
        gathered = [[lax.all_gather(w, "cls", axis=0, tiled=True)] for w in shards]

    split = jnp.transpose(classes, (1, 0, 2))
    temps, cos_t, sin_t, power = build_templates(
        split, phase_tables(shifts, freq), ctf, noise_weight
    )
    if pairwise:
        for shard in direct:
            shard[-1], power = lax.optimization_barrier((shard[-1], power))
        gathered = [gather_pairs(w, d) for w, d in zip(shards, direct)]
    scores, weighted, marks, stat = score(temps, power, gathered, freq)
    if pairwise:
        stats = [stat] + [swap(stat, "cls", k) for k in range(1, n_cls)]
        paired = tuple(range(n_cls))
    else:
        stats = [lax.all_gather(stat, "cls", axis=0, tiled=True)]
        paired = (0,)

    far = tuple(range(n_img - 1, 0, -1))
    log_resp, rho, mass, *parts = responsibilities(
        me, scores, marks, cos_t, sin_t, weighted, stats, paired, far, 2 * part_rows, span
    )
    received = [swap(part, "img", d) for part, d in zip(parts, far)]
    mine, weight = own_slice(me, rho, cos_t, sin_t, weighted, ctf, noise_weight, span)
    averages = finish(weight, mass, mine, received, span)
    return (log_resp.T, averages)


def solution(mesh):
    placed = (
        P(("groups", "img", "cls"), None, None),
        P(("groups", "cls"), None, None),
        P("groups", None),
        P("groups"),
        P(("groups", "img", "cls")),
        P("groups", None),
    )
    return jax.shard_map(
        local,
        mesh=mesh,
        in_specs=placed,
        out_specs=(P(("groups", "img"), "cls"), P(("groups", "cls"), None, "img")),
        check_vma=False,
    )
```

```python
import functools

import jax
import jax.numpy as jnp
from jax import lax
from jax.experimental import pallas as pl
from jax.experimental.pallas import tpu as pltpu
from jax.sharding import PartitionSpec as P

BOX = 128
CHUNKS = 2
LANES = 128
VMEM_LIMIT = 24 * 1024 * 1024

prior_precision = 0.02

NT = (((1,), (1,)), ((), ()))
NN = (((1,), (0,)), ((), ()))
HIGHEST = lax.Precision.HIGHEST
f32 = jnp.float32
bf16 = jnp.bfloat16

SMEM = pl.BlockSpec(memory_space=pltpu.SMEM)
VMEM = pl.BlockSpec(memory_space=pltpu.VMEM)
ANY = pl.BlockSpec(memory_space=pl.ANY)


def phase_tables(shifts, freq):
    along_x = (jnp.arange(BOX) - BOX // 2).astype(f32)
    along_y = jnp.arange(freq // BOX).astype(f32)
    step = 2.0 * jnp.pi / BOX
    angle_x = step * (shifts[:, 0:1].astype(f32) * along_x[None, :])
    angle_y = step * (shifts[:, 1:2].astype(f32) * along_y[None, :])
    return (jnp.cos(angle_x), jnp.sin(angle_x), jnp.cos(angle_y), jnp.sin(angle_y))


def call(kernel, name, in_specs, out_shape, operands, scratch=(), flops=0, moved=0, out_specs=None):
    return pl.pallas_call(
        kernel,
        in_specs=in_specs,
        out_specs=[VMEM] * len(out_shape) if out_specs is None else out_specs,
        out_shape=out_shape,
        scratch_shapes=list(scratch),
        compiler_params=pltpu.CompilerParams(vmem_limit_bytes=VMEM_LIMIT),
        cost_estimate=pl.CostEstimate(flops=flops, bytes_accessed=moved, transcendentals=0),
        name=name,
    )(*operands)


def even_index(shape, axis):
    return lax.rem(lax.broadcasted_iota(jnp.int32, shape, axis), 2) == 0


def weigh_kernel(ids_hbm, p_hbm, ctf_hbm, nw_hbm, *refs):
    out_refs, (ids_ref, p_ref, ctf_ref, nw_ref, scale_ref, sem) = refs[:-6], refs[-6:]
    count, _, freq = p_ref.shape
    copies = [
        pltpu.make_async_copy(source, target, sem.at[i])
        for i, (source, target) in enumerate(
            [(ids_hbm, ids_ref), (ctf_hbm, ctf_ref), (nw_hbm, nw_ref), (p_hbm, p_ref)]
        )
    ]
    for copy in copies:
        copy.start()
    copies[0].wait()
    row = lax.broadcasted_iota(jnp.int32, (2 * count, LANES), 0) // 2
    ids = jnp.zeros((2 * count, LANES), f32)
    for n in range(count):
        ids = jnp.where(row == n, ids_ref[n].astype(f32), ids)
    for copy in copies[1:]:
        copy.wait()
    noise = nw_ref[...].reshape(1, freq)
    for n in range(count):
        scale = ctf_ref[pl.ds(ids_ref[n], 1), :] * noise
        scale_ref[2 * n : 2 * n + 2, :] = jnp.broadcast_to(scale, (2, freq))
    values = p_ref[...].astype(f32).reshape(2 * count, freq)
    weighted = (values * scale_ref[...]).astype(bf16)
    chunk = freq // len(out_refs)
    for c, out_ref in enumerate(out_refs):
        out_ref[:, :chunk] = weighted[:, c * chunk : (c + 1) * chunk]
    out_refs[0][:, chunk:] = ids.astype(bf16)


def weigh(particles, ctf, noise_weight, group_ids):
    rows, _, freq = particles.shape
    chunk = freq // CHUNKS
    operands = (group_ids, particles, ctf, noise_weight)
    return call(
        weigh_kernel,
        "weigh",
        [ANY] * 4,
        [
            jax.ShapeDtypeStruct((2 * rows, chunk + (LANES if c == 0 else 0)), bf16)
            for c in range(CHUNKS)
        ],
        [pltpu.with_memory_space_constraint(x, pltpu.HBM) for x in operands],
        [
            pltpu.SMEM((rows,), jnp.int32),
            pltpu.VMEM(particles.shape, bf16),
            pltpu.VMEM(ctf.shape, f32),
            pltpu.VMEM((freq,), f32),
            pltpu.VMEM((2 * rows, freq), f32),
            pltpu.SemaphoreType.DMA((4,)),
        ],
        flops=4 * rows * freq,
        moved=16 * rows * freq,
    )


def template_kernel(
    cls_ref, xc_ref, xs_ref, yc_ref, ys_ref, ctf_ref, nw_ref, temp_ref, cos_ref, sin_ref, pow_ref
):
    _, rows, freq = cls_ref.shape
    poses = cos_ref.shape[0]
    x_cos, x_sin = xc_ref[...], xs_ref[...]
    for t in range(freq // BOX):
        y_cos = jnp.broadcast_to(yc_ref[:, t : t + 1], x_cos.shape)
        y_sin = jnp.broadcast_to(ys_ref[:, t : t + 1], x_cos.shape)
        cos_ref[:, t * BOX : (t + 1) * BOX] = x_cos * y_cos - x_sin * y_sin
        sin_ref[:, t * BOX : (t + 1) * BOX] = x_sin * y_cos + x_cos * y_sin

    @pl.loop(0, freq // LANES)
    def _(t):
        at = pl.ds(pl.multiple_of(t * LANES, LANES), LANES)
        later = pl.ds(pl.multiple_of(freq + t * LANES, LANES), LANES)
        re = cls_ref[0, :, at].astype(f32)
        im = cls_ref[1, :, at].astype(f32)
        for r in range(poses):
            cos_r = cos_ref[r : r + 1, at]
            sin_r = sin_ref[r : r + 1, at]
            temp_ref[r * rows : (r + 1) * rows, at] = (re * cos_r - im * sin_r).astype(bf16)
            temp_ref[r * rows : (r + 1) * rows, later] = (re * sin_r + im * cos_r).astype(bf16)

    cut = freq // 4
    power = jnp.zeros(pow_ref.shape, f32)
    for q in range(4):
        at = slice(q * cut, (q + 1) * cut)
        re = cls_ref[0, :, at].astype(f32)
        im = cls_ref[1, :, at].astype(f32)
        ctf = ctf_ref[:, at]
        power += lax.dot_general(
            re * re + im * im,
            ctf * ctf * nw_ref[:, at],
            NT,
            precision=HIGHEST,
            preferred_element_type=f32,
        )
    pow_ref[...] = power


def build_templates(split, tables, ctf, noise_weight):
    _, rows, freq = split.shape
    poses, groups = tables[0].shape[0], ctf.shape[0]
    return call(
        template_kernel,
        "templates",
        [VMEM] * 7,
        [
            pltpu.VMEM((poses * rows, 2 * freq), bf16),
            pltpu.VMEM((poses, freq), f32),
            pltpu.VMEM((poses, freq), f32),
            jax.ShapeDtypeStruct((rows, groups), f32),
        ],
        (split, *tables, ctf, noise_weight),
        flops=40 * poses * rows * freq,
        moved=4 * poses * rows * freq,
    )


def add_products(acc_ref, temp_ref, parts, chunk, span):
    freq = temp_ref.shape[1] // 2
    tile = max(t for t in range(LANES, 1153, LANES) if span % t == 0)
    lanes = acc_ref.shape[1]
    even = even_index((lanes, tile), 0)
    for t in range(span // tile):
        at = slice(t * tile, (t + 1) * tile)
        where = chunk * span + t * tile
        wide = jnp.concatenate([p[:, at] for p in parts], axis=0).astype(f32)
        acc_ref[...] += lax.dot_general(
            temp_ref[:, where : where + tile],
            jnp.where(even, wide, 0.0).astype(bf16),
            NT,
            preferred_element_type=f32,
        ) + lax.dot_general(
            temp_ref[:, freq + where : freq + where + tile],
            jnp.where(even, 0.0, wide).astype(bf16),
            NT,
            preferred_element_type=f32,
        )


def score_kernel(chunk, span, temp_ref, *refs):
    *parts, acc_ref = refs if chunk == 0 else refs[1:]
    acc_ref[...] = jnp.zeros_like(acc_ref) if chunk == 0 else refs[0][...]
    add_products(acc_ref, temp_ref, parts, chunk, span)


def last_score_kernel(sources, span, temp_ref, pow_ref, *refs):
    refs = list(refs)
    s_ref, all_ref, marks_ref, stat_ref = refs[-4:]
    chunks = [refs[c * sources : (c + 1) * sources] for c in range(CHUNKS)]
    rows, groups = pow_ref.shape
    lanes = s_ref.shape[1]
    poses = s_ref.shape[0] // rows
    s_ref[...] = refs[-5][...] if CHUNKS > 1 else jnp.zeros_like(s_ref)
    add_products(s_ref, temp_ref, chunks[-1], CHUNKS - 1, span)
    for c, parts in enumerate(chunks):
        at = 0
        for p in parts:
            all_ref[at : at + p.shape[0], c * span : (c + 1) * span] = p[:, :span]
            at += p.shape[0]
    ids = jnp.concatenate([p[:, span:] for p in chunks[0]], axis=0).astype(f32)
    group = lax.broadcasted_iota(jnp.int32, (lanes, groups), 1).astype(f32)
    marks = (ids[:, :groups] == group).astype(f32)
    marks_ref[...] = marks
    penalty = lax.dot_general(
        pow_ref[...], marks, NT, precision=HIGHEST, preferred_element_type=f32
    )
    acc = s_ref[...]
    acc = acc + jnp.where(
        even_index(acc.shape, 1), pltpu.roll(acc, lanes - 1, 1), pltpu.roll(acc, 1, 1)
    )
    scores = acc.reshape(poses, rows, lanes) - 0.5 * penalty[None]
    peak = jnp.max(jnp.max(scores, axis=0), axis=0, keepdims=True)
    total = jnp.sum(jnp.sum(jnp.exp(scores - peak[None]), axis=0), axis=0, keepdims=True)
    s_ref[...] = scores.reshape(poses * rows, lanes)
    stat_ref[0:1, :] = peak
    stat_ref[1:2, :] = total
    stat_ref[2:8, :] = jnp.zeros((6, lanes), f32)


def score(temps, power, gathered, freq):
    span = freq // CHUNKS
    temps = pltpu.with_memory_space_constraint(temps, pltpu.VMEM)
    lanes = sum(p.shape[0] for p in gathered[0])
    acc_shape = jax.ShapeDtypeStruct((temps.shape[0], lanes), f32)
    flops = 2 * temps.shape[0] * 256 * 2 * span
    acc = []
    for c in range(CHUNKS - 1):
        operands = [temps, *acc, *gathered[c]]
        acc = call(
            functools.partial(score_kernel, c, span),
            f"score{c}",
            [VMEM] * len(operands),
            [acc_shape],
            operands,
            flops=flops,
        )
    operands = [temps, power, *[p for parts in gathered for p in parts], *acc]
    return call(
        functools.partial(last_score_kernel, len(gathered[0]), span),
        f"score{CHUNKS - 1}",
        [VMEM] * len(operands),
        [
            acc_shape,
            jax.ShapeDtypeStruct((lanes, freq), bf16),
            jax.ShapeDtypeStruct((lanes, power.shape[1]), f32),
            jax.ShapeDtypeStruct((8, lanes), f32),
        ],
        operands,
        flops=flops,
    )


def xor_blocks(values, block, distance):
    lanes = values.shape[1]
    lane = lax.broadcasted_iota(jnp.int32, values.shape, 1)
    width = block
    while distance:
        if distance % 2:
            low = lax.rem(lane // width, 2) == 0
            values = jnp.where(
                low, pltpu.roll(values, lanes - width, 1), pltpu.roll(values, width, 1)
            )
        distance //= 2
        width *= 2
    return values


def rotate_slice(rho_ref, w_ref, cos_ref, sin_ref, base, span, poses, buffers, write):
    rows = rho_ref.shape[1] // poses
    tiles = [(a, min(256, span - a)) for a in range(0, span, 256)]

    def products(i):
        start, width = tiles[i]
        at = pl.ds(pl.multiple_of(base + start, LANES), width)
        weighted = w_ref[:, at]
        buffer = buffers[i % 2]
        buffer[0, :, :width] = jnp.dot(rho_ref[0], weighted, preferred_element_type=f32)
        buffer[1, :, :width] = jnp.dot(rho_ref[1], weighted, preferred_element_type=f32)

    def rotate(i):
        start, width = tiles[i]
        buffer = buffers[i % 2]
        for a in range(0, width, LANES):
            at = pl.ds(pl.multiple_of(base + start + a, LANES), LANES)
            numer_re = jnp.zeros((rows, LANES), f32)
            numer_im = jnp.zeros((rows, LANES), f32)
            for r in range(poses):
                cos_r = cos_ref[r : r + 1, at]
                sin_r = sin_ref[r : r + 1, at]
                s_re = buffer[0, r * rows : (r + 1) * rows, a : a + LANES]
                s_im = buffer[1, r * rows : (r + 1) * rows, a : a + LANES]
                numer_re = numer_re + s_re * cos_r + s_im * sin_r
                numer_im = numer_im + s_im * cos_r - s_re * sin_r
            write(start + a, numer_re, numer_im)

    products(0)
    for i in range(1, len(tiles)):
        products(i)
        rotate(i - 1)
    rotate(len(tiles) - 1)


def write_to(ref, span):
    def write(at, numer_re, numer_im):
        ref[:, at : at + LANES] = numer_re.astype(ref.dtype)
        ref[:, span + at : span + at + LANES] = numer_im.astype(ref.dtype)

    return write


def resp_kernel(
    poses, block, paired, far, span, me_ref, s_ref, marks_ref, cos_ref, sin_ref, w_ref, *refs
):
    stat_refs, refs = refs[: len(paired)], refs[len(paired) :]
    resp_ref, rho_ref, mass_ref = refs[:3]
    out_refs, buffers = refs[3:-2], refs[-2:]
    rows, groups = mass_ref.shape
    lanes = s_ref.shape[1]
    peaks, totals = [], []
    for ref, distance in zip(stat_refs, paired):
        for at in range(0, ref.shape[0], 8):
            stats = xor_blocks(ref[at : at + 8, :], block, distance)
            peaks.append(stats[0:1])
            totals.append(stats[1:2])
    peak = functools.reduce(jnp.maximum, peaks)
    total = sum(t * jnp.exp(p - peak) for t, p in zip(totals, peaks))
    log_norm = peak + jnp.log(total)
    scores = s_ref[...].reshape(poses, rows, lanes)
    rho = jnp.exp(scores - log_norm[None])
    even = even_index((rows, lanes), 1)
    mass = lax.dot_general(
        jnp.where(even, jnp.sum(rho, axis=0), 0.0),
        marks_ref[...],
        NN,
        precision=HIGHEST,
        preferred_element_type=f32,
    )
    mass_ref[...] = mass
    high = mass.astype(bf16)
    low = (mass - high.astype(f32)).astype(bf16)
    for ref in out_refs:
        ref[:, 2 * span : 2 * span + groups] = high
        ref[:, 2 * span + groups :] = low
    flat = rho.reshape(poses * rows, lanes)
    even = even_index(flat.shape, 1)
    rho_ref[0] = jnp.where(even, flat, 0.0).astype(bf16)
    rho_ref[1] = jnp.where(even, 0.0, flat).astype(bf16)
    for ref, distance in zip(out_refs, far):
        base = (me_ref[0] ^ distance) * span
        rotate_slice(
            rho_ref, w_ref, cos_ref, sin_ref, base, span, poses, buffers, write_to(ref, span)
        )
    pose_peak = jnp.max(scores, axis=0)
    log_resp = pose_peak + jnp.log(jnp.sum(jnp.exp(scores - pose_peak[None]), axis=0)) - log_norm
    shape = (resp_ref.shape[1], lanes)
    lane = lax.broadcasted_iota(jnp.int32, shape, 1)
    row = ((lane // block) ^ me_ref[1]) * (block // 2) + lax.rem(lane, block) // 2
    take = (lax.broadcasted_iota(jnp.int32, shape, 0) == row) & (lax.rem(lane, 2) == 0)
    resp_ref[...] = lax.dot_general(
        log_resp, take.astype(f32), NT, precision=HIGHEST, preferred_element_type=f32
    )


def responsibilities(me, scores, marks, cos_t, sin_t, weighted, stats, paired, far, block, span):
    poses, lanes = cos_t.shape[0], scores.shape[1]
    rows, groups = scores.shape[0] // poses, marks.shape[1]
    return call(
        functools.partial(resp_kernel, poses, block, paired, far, span),
        "responsibilities",
        [SMEM] + [VMEM] * (5 + len(stats)),
        [
            jax.ShapeDtypeStruct((rows, lanes // 2), f32),
            jax.ShapeDtypeStruct((2, poses * rows, lanes), bf16),
            jax.ShapeDtypeStruct((rows, groups), f32),
        ]
        + [jax.ShapeDtypeStruct((rows, 2 * span + 2 * groups), bf16)] * len(far),
        (me, scores, marks, cos_t, sin_t, weighted, *stats),
        [pltpu.VMEM((2, poses * rows, 256), f32)] * 2,
        flops=4 * 256 * poses * rows * span * len(far),
    )


def own_kernel(
    poses, span, me_ref, rho_ref, cos_ref, sin_ref, w_ref, ctf_ref, nw_ref, out_ref, cw_ref, *buffers
):
    base = me_ref[0] * span
    at = pl.ds(pl.multiple_of(base, LANES), span)
    ctf = ctf_ref[:, at]
    cw_ref[...] = ctf * ctf * nw_ref[:, at]
    rotate_slice(
        rho_ref, w_ref, cos_ref, sin_ref, base, span, poses, buffers, write_to(out_ref, span)
    )


def own_slice(me, rho, cos_t, sin_t, weighted, ctf, noise_weight, span):
    poses = cos_t.shape[0]
    rows = rho.shape[1] // poses
    return call(
        functools.partial(own_kernel, poses, span),
        "own_slice",
        [SMEM] + [VMEM] * 6,
        [
            jax.ShapeDtypeStruct((rows, 2 * span), f32),
            jax.ShapeDtypeStruct((ctf.shape[0], span), f32),
        ],
        (me, rho, cos_t, sin_t, weighted, ctf, noise_weight),
        [pltpu.VMEM((2, poses * rows, 256), f32)] * 2,
        flops=4 * 256 * poses * rows * span,
    )


def finish_kernel(span, cw_ref, mass_ref, own_ref, *refs):
    received, out_ref = refs[:-1], refs[-1]
    groups = mass_ref.shape[1]
    mass = mass_ref[...]
    for ref in received:
        mass += ref[:, 2 * span : 2 * span + groups].astype(f32)
        mass += ref[:, 2 * span + groups :].astype(f32)
    denom = (
        lax.dot_general(
            mass,
            cw_ref[...],
            NN,
            precision=HIGHEST,
            preferred_element_type=f32,
        )
        + prior_precision
    )
    for part in range(2):
        cut = slice(part * span, (part + 1) * span)
        numer = own_ref[:, cut]
        for ref in received:
            numer += ref[:, cut].astype(f32)
        out_ref[:, part, :] = numer / denom


def finish(weight, mass, own, received, span):
    rows = own.shape[0]
    return call(
        functools.partial(finish_kernel, span),
        "finish",
        [VMEM] * (3 + len(received)),
        [jax.ShapeDtypeStruct((rows, 2, span), f32)],
        (weight, mass, own, *received),
    )[0]


def swap(values, axis, distance):
    size = lax.axis_size(axis)
    return lax.ppermute(values, axis, [(i, i ^ distance) for i in range(size)])


def direct_shards(shard):
    distances = [1 << b for b in range(lax.axis_size("cls").bit_length() - 1)]
    return [swap(shard, "cls", d) for d in distances]


def gather_pairs(shard, direct):
    slots = [shard]
    for i, arrived in enumerate(direct):
        slots += [arrived] + [swap(arrived, "cls", k) for k in range(1, 1 << i)]
    return slots


def local(particles, classes, ctf, noise_weight, group_ids, shifts):
    part_rows, _, freq = particles.shape
    n_cls = lax.axis_size("cls")
    n_img = lax.axis_size("img")
    span = freq // n_img
    pairwise = n_cls <= 4
    me_cls = lax.axis_index("cls") if pairwise else 0
    me = jnp.stack([lax.axis_index("img"), me_cls]).astype(jnp.int32)

    shards = weigh(particles, ctf, noise_weight, group_ids)
    noise_weight = noise_weight[None, :]
    if pairwise:
        direct = [direct_shards(w) for w in shards]
    else:
        gathered = [[lax.all_gather(w, "cls", axis=0, tiled=True)] for w in shards]

    split = jnp.transpose(classes, (1, 0, 2))
    temps, cos_t, sin_t, power = build_templates(
        split, phase_tables(shifts, freq), ctf, noise_weight
    )
    if pairwise:
        direct, power = lax.optimization_barrier((direct, power))
        gathered = [gather_pairs(w, d) for w, d in zip(shards, direct)]
    scores, weighted, marks, stat = score(temps, power, gathered, freq)
    if pairwise:
        stats = [stat] + [swap(stat, "cls", k) for k in range(1, n_cls)]
        paired = tuple(range(n_cls))
    else:
        stats = [lax.all_gather(stat, "cls", axis=0, tiled=True)]
        paired = (0,)

    far = tuple(range(n_img - 1, 0, -1))
    log_resp, rho, mass, *parts = responsibilities(
        me, scores, marks, cos_t, sin_t, weighted, stats, paired, far, 2 * part_rows, span
    )
    received = [swap(part, "img", d) for part, d in zip(parts, far)]
    mine, weight = own_slice(me, rho, cos_t, sin_t, weighted, ctf, noise_weight, span)
    averages = finish(weight, mass, mine, received, span)
    return (log_resp.T, averages)


def solution(mesh):
    placed = (
        P(("groups", "img", "cls"), None, None),
        P(("groups", "cls"), None, None),
        P("groups", None),
        P("groups"),
        P(("groups", "img", "cls")),
        P("groups", None),
    )
    return jax.shard_map(
        local,
        mesh=mesh,
        in_specs=placed,
        out_specs=(P(("groups", "img"), "cls"), P(("groups", "cls"), None, "img")),
        check_vma=False,
    )
```

```python
import functools

import jax
import jax.numpy as jnp
from jax import lax
from jax.experimental import pallas as pl
from jax.experimental.pallas import tpu as pltpu
from jax.sharding import PartitionSpec as P

BOX = 128
CHUNKS = 2
LANES = 128
VMEM_LIMIT = 24 * 1024 * 1024

prior_precision = 0.02

NT = (((1,), (1,)), ((), ()))
NN = (((1,), (0,)), ((), ()))
HIGHEST = lax.Precision.HIGHEST
f32 = jnp.float32
bf16 = jnp.bfloat16

SMEM = pl.BlockSpec(memory_space=pltpu.SMEM)
VMEM = pl.BlockSpec(memory_space=pltpu.VMEM)
ANY = pl.BlockSpec(memory_space=pl.ANY)


def phase_tables(shifts, freq):
    along_x = (jnp.arange(BOX) - BOX // 2).astype(f32)
    along_y = jnp.arange(freq // BOX).astype(f32)
    step = 2.0 * jnp.pi / BOX
    angle_x = step * (shifts[:, 0:1].astype(f32) * along_x[None, :])
    angle_y = step * (shifts[:, 1:2].astype(f32) * along_y[None, :])
    return (jnp.cos(angle_x), jnp.sin(angle_x), jnp.cos(angle_y), jnp.sin(angle_y))


def call(kernel, name, in_specs, out_shape, operands, scratch=(), flops=0, moved=0, out_specs=None):
    return pl.pallas_call(
        kernel,
        in_specs=in_specs,
        out_specs=[VMEM] * len(out_shape) if out_specs is None else out_specs,
        out_shape=out_shape,
        scratch_shapes=list(scratch),
        compiler_params=pltpu.CompilerParams(vmem_limit_bytes=VMEM_LIMIT),
        cost_estimate=pl.CostEstimate(flops=flops, bytes_accessed=moved, transcendentals=0),
        name=name,
    )(*operands)


def even_index(shape, axis):
    return lax.rem(lax.broadcasted_iota(jnp.int32, shape, axis), 2) == 0


def weigh_kernel(ids_hbm, p_hbm, ctf_hbm, nw_hbm, *refs):
    out_refs, (ids_ref, p_ref, ctf_ref, nw_ref, scale_ref, sem) = refs[:-6], refs[-6:]
    count, _, freq = p_ref.shape
    copies = [
        pltpu.make_async_copy(source, target, sem.at[i])
        for i, (source, target) in enumerate(
            [(ids_hbm, ids_ref), (ctf_hbm, ctf_ref), (nw_hbm, nw_ref), (p_hbm, p_ref)]
        )
    ]
    for copy in copies:
        copy.start()
    copies[0].wait()
    row = lax.broadcasted_iota(jnp.int32, (2 * count, LANES), 0) // 2
    ids = jnp.zeros((2 * count, LANES), f32)
    for n in range(count):
        ids = jnp.where(row == n, ids_ref[n].astype(f32), ids)
    for copy in copies[1:]:
        copy.wait()
    noise = nw_ref[...].reshape(1, freq)
    for n in range(count):
        scale = ctf_ref[pl.ds(ids_ref[n], 1), :] * noise
        scale_ref[2 * n : 2 * n + 2, :] = jnp.broadcast_to(scale, (2, freq))
    values = p_ref[...].astype(f32).reshape(2 * count, freq)
    weighted = (values * scale_ref[...]).astype(bf16)
    chunk = freq // len(out_refs)
    for c, out_ref in enumerate(out_refs):
        out_ref[:, :chunk] = weighted[:, c * chunk : (c + 1) * chunk]
    out_refs[0][:, chunk:] = ids.astype(bf16)


def weigh(particles, ctf, noise_weight, group_ids):
    rows, _, freq = particles.shape
    chunk = freq // CHUNKS
    operands = (group_ids, particles, ctf, noise_weight)
    return call(
        weigh_kernel,
        "weigh",
        [ANY] * 4,
        [
            jax.ShapeDtypeStruct((2 * rows, chunk + (LANES if c == 0 else 0)), bf16)
            for c in range(CHUNKS)
        ],
        [pltpu.with_memory_space_constraint(x, pltpu.HBM) for x in operands],
        [
            pltpu.SMEM((rows,), jnp.int32),
            pltpu.VMEM(particles.shape, bf16),
            pltpu.VMEM(ctf.shape, f32),
            pltpu.VMEM((freq,), f32),
            pltpu.VMEM((2 * rows, freq), f32),
            pltpu.SemaphoreType.DMA((4,)),
        ],
        flops=4 * rows * freq,
        moved=16 * rows * freq,
    )


def prepare_kernel(
    cls_ref, xc_ref, xs_ref, yc_ref, ys_ref, ctf_ref, nw_ref, cos_ref, sin_ref, pow_ref
):
    freq = cls_ref.shape[2]
    x_cos, x_sin = xc_ref[...], xs_ref[...]
    for t in range(freq // BOX):
        y_cos = jnp.broadcast_to(yc_ref[:, t : t + 1], x_cos.shape)
        y_sin = jnp.broadcast_to(ys_ref[:, t : t + 1], x_cos.shape)
        cos_ref[:, t * BOX : (t + 1) * BOX] = x_cos * y_cos - x_sin * y_sin
        sin_ref[:, t * BOX : (t + 1) * BOX] = x_sin * y_cos + x_cos * y_sin
    cut = freq // 4
    power = jnp.zeros(pow_ref.shape, f32)
    for q in range(4):
        at = slice(q * cut, (q + 1) * cut)
        re = cls_ref[0, :, at].astype(f32)
        im = cls_ref[1, :, at].astype(f32)
        ctf = ctf_ref[:, at]
        power += lax.dot_general(
            re * re + im * im,
            ctf * ctf * nw_ref[:, at],
            NT,
            precision=HIGHEST,
            preferred_element_type=f32,
        )
    pow_ref[...] = power


def prepare(split, tables, ctf, noise_weight):
    _, rows, freq = split.shape
    poses, groups = tables[0].shape[0], ctf.shape[0]
    return call(
        prepare_kernel,
        "prepare",
        [VMEM] * 7,
        [
            jax.ShapeDtypeStruct((poses, freq), f32),
            jax.ShapeDtypeStruct((poses, freq), f32),
            jax.ShapeDtypeStruct((rows, groups), f32),
        ],
        (split, *tables, ctf, noise_weight),
        flops=24 * rows * groups * freq,
    )


def template_kernel(cls_ref, cos_ref, sin_ref, temp_ref):
    _, rows, freq = cls_ref.shape
    poses = cos_ref.shape[0]

    @pl.loop(0, freq // LANES)
    def _(t):
        at = pl.ds(pl.multiple_of(t * LANES, LANES), LANES)
        later = pl.ds(pl.multiple_of(freq + t * LANES, LANES), LANES)
        re = cls_ref[0, :, at].astype(f32)
        im = cls_ref[1, :, at].astype(f32)
        for r in range(poses):
            cos_r = cos_ref[r : r + 1, at]
            sin_r = sin_ref[r : r + 1, at]
            temp_ref[r * rows : (r + 1) * rows, at] = (re * cos_r - im * sin_r).astype(bf16)
            temp_ref[r * rows : (r + 1) * rows, later] = (re * sin_r + im * cos_r).astype(bf16)


def build_templates(split, cos_t, sin_t):
    _, rows, freq = split.shape
    poses = cos_t.shape[0]
    return call(
        template_kernel,
        "templates",
        [VMEM] * 3,
        [pltpu.VMEM((poses * rows, 2 * freq), bf16)],
        (split, cos_t, sin_t),
        flops=40 * poses * rows * freq,
        moved=4 * poses * rows * freq,
    )[0]


def add_products(acc_ref, temp_ref, parts, chunk, span):
    freq = temp_ref.shape[1] // 2
    tile = max(t for t in range(LANES, 1153, LANES) if span % t == 0)
    lanes = acc_ref.shape[1]
    even = even_index((lanes, tile), 0)
    for t in range(span // tile):
        at = slice(t * tile, (t + 1) * tile)
        where = chunk * span + t * tile
        wide = jnp.concatenate([p[:, at] for p in parts], axis=0).astype(f32)
        acc_ref[...] += lax.dot_general(
            temp_ref[:, where : where + tile],
            jnp.where(even, wide, 0.0).astype(bf16),
            NT,
            preferred_element_type=f32,
        ) + lax.dot_general(
            temp_ref[:, freq + where : freq + where + tile],
            jnp.where(even, 0.0, wide).astype(bf16),
            NT,
            preferred_element_type=f32,
        )


def score_kernel(chunk, span, temp_ref, *refs):
    *parts, acc_ref = refs if chunk == 0 else refs[1:]
    acc_ref[...] = jnp.zeros_like(acc_ref) if chunk == 0 else refs[0][...]
    add_products(acc_ref, temp_ref, parts, chunk, span)


def last_score_kernel(sources, span, temp_ref, pow_ref, *refs):
    refs = list(refs)
    s_ref, all_ref, marks_ref, stat_ref = refs[-4:]
    chunks = [refs[c * sources : (c + 1) * sources] for c in range(CHUNKS)]
    rows, groups = pow_ref.shape
    lanes = s_ref.shape[1]
    poses = s_ref.shape[0] // rows
    s_ref[...] = refs[-5][...] if CHUNKS > 1 else jnp.zeros_like(s_ref)
    add_products(s_ref, temp_ref, chunks[-1], CHUNKS - 1, span)
    for c, parts in enumerate(chunks):
        at = 0
        for p in parts:
            all_ref[at : at + p.shape[0], c * span : (c + 1) * span] = p[:, :span]
            at += p.shape[0]
    ids = jnp.concatenate([p[:, span:] for p in chunks[0]], axis=0).astype(f32)
    group = lax.broadcasted_iota(jnp.int32, (lanes, groups), 1).astype(f32)
    marks = (ids[:, :groups] == group).astype(f32)
    marks_ref[...] = marks
    penalty = lax.dot_general(
        pow_ref[...], marks, NT, precision=HIGHEST, preferred_element_type=f32
    )
    acc = s_ref[...]
    acc = acc + jnp.where(
        even_index(acc.shape, 1), pltpu.roll(acc, lanes - 1, 1), pltpu.roll(acc, 1, 1)
    )
    scores = acc.reshape(poses, rows, lanes) - 0.5 * penalty[None]
    peak = jnp.max(jnp.max(scores, axis=0), axis=0, keepdims=True)
    total = jnp.sum(jnp.sum(jnp.exp(scores - peak[None]), axis=0), axis=0, keepdims=True)
    s_ref[...] = scores.reshape(poses * rows, lanes)
    stat_ref[0:1, :] = peak
    stat_ref[1:2, :] = total
    stat_ref[2:8, :] = jnp.zeros((6, lanes), f32)


def score(temps, power, gathered, freq):
    span = freq // CHUNKS
    lanes = sum(p.shape[0] for p in gathered[0])
    acc_shape = jax.ShapeDtypeStruct((temps.shape[0], lanes), f32)
    flops = 2 * temps.shape[0] * 256 * 2 * span
    acc = []
    for c in range(CHUNKS - 1):
        operands = [temps, *acc, *gathered[c]]
        acc = call(
            functools.partial(score_kernel, c, span),
            f"score{c}",
            [VMEM] * len(operands),
            [acc_shape],
            operands,
            flops=flops,
        )
    operands = [temps, power, *[p for parts in gathered for p in parts], *acc]
    return call(
        functools.partial(last_score_kernel, len(gathered[0]), span),
        f"score{CHUNKS - 1}",
        [VMEM] * len(operands),
        [
            acc_shape,
            jax.ShapeDtypeStruct((lanes, freq), bf16),
            jax.ShapeDtypeStruct((lanes, power.shape[1]), f32),
            jax.ShapeDtypeStruct((8, lanes), f32),
        ],
        operands,
        flops=flops,
    )


def xor_blocks(values, block, distance):
    lanes = values.shape[1]
    lane = lax.broadcasted_iota(jnp.int32, values.shape, 1)
    width = block
    while distance:
        if distance % 2:
            low = lax.rem(lane // width, 2) == 0
            values = jnp.where(
                low, pltpu.roll(values, lanes - width, 1), pltpu.roll(values, width, 1)
            )
        distance //= 2
        width *= 2
    return values


def rotate_slice(rho_ref, w_ref, cos_ref, sin_ref, base, span, poses, buffers, write):
    rows = rho_ref.shape[1] // poses
    tiles = [(a, min(256, span - a)) for a in range(0, span, 256)]

    def products(i):
        start, width = tiles[i]
        at = pl.ds(pl.multiple_of(base + start, LANES), width)
        weighted = w_ref[:, at]
        buffer = buffers[i % 2]
        buffer[0, :, :width] = jnp.dot(rho_ref[0], weighted, preferred_element_type=f32)
        buffer[1, :, :width] = jnp.dot(rho_ref[1], weighted, preferred_element_type=f32)

    def rotate(i):
        start, width = tiles[i]
        buffer = buffers[i % 2]
        for a in range(0, width, LANES):
            at = pl.ds(pl.multiple_of(base + start + a, LANES), LANES)
            numer_re = jnp.zeros((rows, LANES), f32)
            numer_im = jnp.zeros((rows, LANES), f32)
            for r in range(poses):
                cos_r = cos_ref[r : r + 1, at]
                sin_r = sin_ref[r : r + 1, at]
                s_re = buffer[0, r * rows : (r + 1) * rows, a : a + LANES]
                s_im = buffer[1, r * rows : (r + 1) * rows, a : a + LANES]
                numer_re = numer_re + s_re * cos_r + s_im * sin_r
                numer_im = numer_im + s_im * cos_r - s_re * sin_r
            write(start + a, numer_re, numer_im)

    products(0)
    for i in range(1, len(tiles)):
        products(i)
        rotate(i - 1)
    rotate(len(tiles) - 1)


def write_to(ref, span):
    def write(at, numer_re, numer_im):
        ref[:, at : at + LANES] = numer_re.astype(ref.dtype)
        ref[:, span + at : span + at + LANES] = numer_im.astype(ref.dtype)

    return write


def rho_kernel(poses, block, paired, far, span, me_ref, s_ref, marks_ref, cos_ref, sin_ref, w_ref, *refs):
    stat_refs, refs = refs[: len(paired)], refs[len(paired) :]
    norm_ref, rho_ref, mass_ref = refs[:3]
    out_refs, buffers = refs[3:-2], refs[-2:]
    rows, groups = mass_ref.shape
    lanes = s_ref.shape[1]
    peaks, totals = [], []
    for ref, distance in zip(stat_refs, paired):
        for at in range(0, ref.shape[0], 8):
            stats = xor_blocks(ref[at : at + 8, :], block, distance)
            peaks.append(stats[0:1])
            totals.append(stats[1:2])
    peak = functools.reduce(jnp.maximum, peaks)
    total = sum(t * jnp.exp(p - peak) for t, p in zip(totals, peaks))
    log_norm = peak + jnp.log(total)
    norm_ref[...] = log_norm
    rho = jnp.exp(s_ref[...].reshape(poses, rows, lanes) - log_norm[None])
    even = even_index((rows, lanes), 1)
    mass = lax.dot_general(
        jnp.where(even, jnp.sum(rho, axis=0), 0.0),
        marks_ref[...],
        NN,
        precision=HIGHEST,
        preferred_element_type=f32,
    )
    mass_ref[...] = mass
    high = mass.astype(bf16)
    low = (mass - high.astype(f32)).astype(bf16)
    for ref in out_refs:
        ref[:, 2 * span : 2 * span + groups] = high
        ref[:, 2 * span + groups :] = low
    flat = rho.reshape(poses * rows, lanes)
    even = even_index(flat.shape, 1)
    rho_ref[0] = jnp.where(even, flat, 0.0).astype(bf16)
    rho_ref[1] = jnp.where(even, 0.0, flat).astype(bf16)
    for ref, distance in zip(out_refs, far):
        base = (me_ref[0] ^ distance) * span
        rotate_slice(
            rho_ref, w_ref, cos_ref, sin_ref, base, span, poses, buffers, write_to(ref, span)
        )


def outgoing_slices(me, scores, marks, cos_t, sin_t, weighted, stats, paired, far, block, span):
    poses, lanes = cos_t.shape[0], scores.shape[1]
    rows, groups = scores.shape[0] // poses, marks.shape[1]
    return call(
        functools.partial(rho_kernel, poses, block, paired, far, span),
        "outgoing",
        [SMEM] + [VMEM] * (5 + len(stats)),
        [
            jax.ShapeDtypeStruct((1, lanes), f32),
            jax.ShapeDtypeStruct((2, poses * rows, lanes), bf16),
            jax.ShapeDtypeStruct((rows, groups), f32),
        ]
        + [jax.ShapeDtypeStruct((rows, 2 * span + 2 * groups), bf16)] * len(far),
        (me, scores, marks, cos_t, sin_t, weighted, *stats),
        [pltpu.VMEM((2, poses * rows, 256), f32)] * 2,
        flops=4 * 256 * poses * rows * span * len(far),
    )


def own_kernel(
    poses,
    block,
    span,
    me_ref,
    s_ref,
    norm_ref,
    rho_ref,
    cos_ref,
    sin_ref,
    w_ref,
    ctf_ref,
    nw_ref,
    out_ref,
    cw_ref,
    resp_ref,
    *buffers,
):
    base = me_ref[0] * span
    at = pl.ds(pl.multiple_of(base, LANES), span)
    ctf = ctf_ref[:, at]
    cw_ref[...] = ctf * ctf * nw_ref[:, at]
    rotate_slice(
        rho_ref, w_ref, cos_ref, sin_ref, base, span, poses, buffers, write_to(out_ref, span)
    )
    rows = resp_ref.shape[0]
    lanes = s_ref.shape[1]
    scores = s_ref[...].reshape(poses, rows, lanes)
    pose_peak = jnp.max(scores, axis=0)
    total = jnp.sum(jnp.exp(scores - pose_peak[None]), axis=0)
    log_resp = pose_peak + jnp.log(total) - norm_ref[...]
    shape = (resp_ref.shape[1], lanes)
    lane = lax.broadcasted_iota(jnp.int32, shape, 1)
    row = ((lane // block) ^ me_ref[1]) * (block // 2) + lax.rem(lane, block) // 2
    take = (lax.broadcasted_iota(jnp.int32, shape, 0) == row) & (lax.rem(lane, 2) == 0)
    resp_ref[...] = lax.dot_general(
        log_resp, take.astype(f32), NT, precision=HIGHEST, preferred_element_type=f32
    )


def own_slice(me, scores, norm, rho, cos_t, sin_t, weighted, ctf, noise_weight, block, span):
    poses, lanes = cos_t.shape[0], scores.shape[1]
    rows = scores.shape[0] // poses
    return call(
        functools.partial(own_kernel, poses, block, span),
        "own_slice",
        [SMEM] + [VMEM] * 8,
        [
            jax.ShapeDtypeStruct((rows, 2 * span), f32),
            jax.ShapeDtypeStruct((ctf.shape[0], span), f32),
            jax.ShapeDtypeStruct((rows, lanes // 2), f32),
        ],
        (me, scores, norm, rho, cos_t, sin_t, weighted, ctf, noise_weight),
        [pltpu.VMEM((2, poses * rows, 256), f32)] * 2,
        flops=4 * 256 * poses * rows * span,
    )


def finish_kernel(span, cw_ref, mass_ref, own_ref, *refs):
    received, out_ref = refs[:-1], refs[-1]
    groups = mass_ref.shape[1]
    mass = mass_ref[...]
    for ref in received:
        mass += ref[:, 2 * span : 2 * span + groups].astype(f32)
        mass += ref[:, 2 * span + groups :].astype(f32)
    denom = (
        lax.dot_general(
            mass,
            cw_ref[...],
            NN,
            precision=HIGHEST,
            preferred_element_type=f32,
        )
        + prior_precision
    )
    for part in range(2):
        cut = slice(part * span, (part + 1) * span)
        numer = own_ref[:, cut]
        for ref in received:
            numer += ref[:, cut].astype(f32)
        out_ref[:, part, :] = numer / denom


def finish(weight, mass, own, received, span):
    rows = own.shape[0]
    return call(
        functools.partial(finish_kernel, span),
        "finish",
        [VMEM] * (3 + len(received)),
        [jax.ShapeDtypeStruct((rows, 2, span), f32)],
        (weight, mass, own, *received),
    )[0]


def swap(values, axis, distance):
    size = lax.axis_size(axis)
    return lax.ppermute(values, axis, [(i, i ^ distance) for i in range(size)])


def direct_shards(shard):
    distances = [1 << b for b in range(lax.axis_size("cls").bit_length() - 1)]
    return [swap(shard, "cls", d) for d in distances]


def gather_pairs(shard, direct):
    slots = [shard]
    for i, arrived in enumerate(direct):
        slots += [arrived] + [swap(arrived, "cls", k) for k in range(1, 1 << i)]
    return slots


def local(particles, classes, ctf, noise_weight, group_ids, shifts):
    part_rows, _, freq = particles.shape
    n_cls = lax.axis_size("cls")
    n_img = lax.axis_size("img")
    span = freq // n_img
    pairwise = n_cls <= 4
    me_cls = lax.axis_index("cls") if pairwise else 0
    me = jnp.stack([lax.axis_index("img"), me_cls]).astype(jnp.int32)

    shards = weigh(particles, ctf, noise_weight, group_ids)
    noise_weight = noise_weight[None, :]
    if pairwise:
        direct = [direct_shards(w) for w in shards]
    else:
        gathered = [[lax.all_gather(w, "cls", axis=0, tiled=True)] for w in shards]

    split = jnp.transpose(classes, (1, 0, 2))
    cos_t, sin_t, power = prepare(split, phase_tables(shifts, freq), ctf, noise_weight)
    if pairwise:
        direct, split, cos_t = lax.optimization_barrier((direct, split, cos_t))
        gathered = [gather_pairs(w, d) for w, d in zip(shards, direct)]
    temps = build_templates(split, cos_t, sin_t)
    scores, weighted, marks, stat = score(temps, power, gathered, freq)
    if pairwise:
        stats = [stat] + [swap(stat, "cls", k) for k in range(1, n_cls)]
        paired = tuple(range(n_cls))
    else:
        stats = [lax.all_gather(stat, "cls", axis=0, tiled=True)]
        paired = (0,)

    far = tuple(range(n_img - 1, 0, -1))
    block = 2 * part_rows
    norm, rho, mass, *parts = outgoing_slices(
        me, scores, marks, cos_t, sin_t, weighted, stats, paired, far, block, span
    )
    received = [swap(part, "img", d) for part, d in zip(parts, far)]
    mine, weight, log_resp = own_slice(
        me, scores, norm, rho, cos_t, sin_t, weighted, ctf, noise_weight, block, span
    )
    averages = finish(weight, mass, mine, received, span)
    return (log_resp.T, averages)


def solution(mesh):
    placed = (
        P(("groups", "img", "cls"), None, None),
        P(("groups", "cls"), None, None),
        P("groups", None),
        P("groups"),
        P(("groups", "img", "cls")),
        P("groups", None),
    )
    return jax.shard_map(
        local,
        mesh=mesh,
        in_specs=placed,
        out_specs=(P(("groups", "img"), "cls"), P(("groups", "cls"), None, "img")),
        check_vma=False,
    )
```

```python
import functools

import jax
import jax.numpy as jnp
from jax import lax
from jax.experimental import pallas as pl
from jax.experimental.pallas import tpu as pltpu
from jax.sharding import PartitionSpec as P

BOX = 128
CHUNKS = 2
LANES = 128
VMEM_LIMIT = 24 * 1024 * 1024

prior_precision = 0.02

NT = (((1,), (1,)), ((), ()))
NN = (((1,), (0,)), ((), ()))
HIGHEST = lax.Precision.HIGHEST
f32 = jnp.float32
bf16 = jnp.bfloat16

SMEM = pl.BlockSpec(memory_space=pltpu.SMEM)
VMEM = pl.BlockSpec(memory_space=pltpu.VMEM)
ANY = pl.BlockSpec(memory_space=pl.ANY)


def phase_tables(shifts, freq):
    along_x = (jnp.arange(BOX) - BOX // 2).astype(f32)
    along_y = jnp.arange(freq // BOX).astype(f32)
    step = 2.0 * jnp.pi / BOX
    angle_x = step * (shifts[:, 0:1].astype(f32) * along_x[None, :])
    angle_y = step * (shifts[:, 1:2].astype(f32) * along_y[None, :])
    return (jnp.cos(angle_x), jnp.sin(angle_x), jnp.cos(angle_y), jnp.sin(angle_y))


def call(kernel, name, in_specs, out_shape, operands, scratch=(), flops=0, moved=0, out_specs=None):
    return pl.pallas_call(
        kernel,
        in_specs=in_specs,
        out_specs=[VMEM] * len(out_shape) if out_specs is None else out_specs,
        out_shape=out_shape,
        scratch_shapes=list(scratch),
        compiler_params=pltpu.CompilerParams(vmem_limit_bytes=VMEM_LIMIT),
        cost_estimate=pl.CostEstimate(flops=flops, bytes_accessed=moved, transcendentals=0),
        name=name,
    )(*operands)


def even_index(shape, axis):
    return lax.rem(lax.broadcasted_iota(jnp.int32, shape, axis), 2) == 0


def weigh_kernel(ids_hbm, p_hbm, ctf_hbm, nw_hbm, *refs):
    out_refs, (ids_ref, p_ref, ctf_ref, nw_ref, scale_ref, sem) = refs[:-6], refs[-6:]
    count, _, freq = p_ref.shape
    copies = [
        pltpu.make_async_copy(source, target, sem.at[i])
        for i, (source, target) in enumerate(
            [(ids_hbm, ids_ref), (ctf_hbm, ctf_ref), (nw_hbm, nw_ref), (p_hbm, p_ref)]
        )
    ]
    for copy in copies:
        copy.start()
    copies[0].wait()
    row = lax.broadcasted_iota(jnp.int32, (2 * count, LANES), 0) // 2
    ids = jnp.zeros((2 * count, LANES), f32)
    for n in range(count):
        ids = jnp.where(row == n, ids_ref[n].astype(f32), ids)
    for copy in copies[1:]:
        copy.wait()
    noise = nw_ref[...].reshape(1, freq)
    for n in range(count):
        scale = ctf_ref[pl.ds(ids_ref[n], 1), :] * noise
        scale_ref[2 * n : 2 * n + 2, :] = jnp.broadcast_to(scale, (2, freq))
    values = p_ref[...].astype(f32).reshape(2 * count, freq)
    weighted = (values * scale_ref[...]).astype(bf16)
    chunk = freq // len(out_refs)
    for c, out_ref in enumerate(out_refs):
        out_ref[:, :chunk] = weighted[:, c * chunk : (c + 1) * chunk]
    out_refs[0][:, chunk:] = ids.astype(bf16)


def weigh(particles, ctf, noise_weight, group_ids):
    rows, _, freq = particles.shape
    chunk = freq // CHUNKS
    operands = (group_ids, particles, ctf, noise_weight)
    return call(
        weigh_kernel,
        "weigh",
        [ANY] * 4,
        [
            jax.ShapeDtypeStruct((2 * rows, chunk + (LANES if c == 0 else 0)), bf16)
            for c in range(CHUNKS)
        ],
        [pltpu.with_memory_space_constraint(x, pltpu.HBM) for x in operands],
        [
            pltpu.SMEM((rows,), jnp.int32),
            pltpu.VMEM(particles.shape, bf16),
            pltpu.VMEM(ctf.shape, f32),
            pltpu.VMEM((freq,), f32),
            pltpu.VMEM((2 * rows, freq), f32),
            pltpu.SemaphoreType.DMA((4,)),
        ],
        flops=4 * rows * freq,
        moved=16 * rows * freq,
    )


def prepare_kernel(
    cls_ref, xc_ref, xs_ref, yc_ref, ys_ref, ctf_ref, nw_ref, cos_ref, sin_ref, pow_ref
):
    freq = cls_ref.shape[2]
    x_cos, x_sin = xc_ref[...], xs_ref[...]
    for t in range(freq // BOX):
        y_cos = jnp.broadcast_to(yc_ref[:, t : t + 1], x_cos.shape)
        y_sin = jnp.broadcast_to(ys_ref[:, t : t + 1], x_cos.shape)
        cos_ref[:, t * BOX : (t + 1) * BOX] = x_cos * y_cos - x_sin * y_sin
        sin_ref[:, t * BOX : (t + 1) * BOX] = x_sin * y_cos + x_cos * y_sin
    cut = freq // 4
    power = jnp.zeros(pow_ref.shape, f32)
    for q in range(4):
        at = slice(q * cut, (q + 1) * cut)
        re = cls_ref[0, :, at].astype(f32)
        im = cls_ref[1, :, at].astype(f32)
        ctf = ctf_ref[:, at]
        power += lax.dot_general(
            re * re + im * im,
            ctf * ctf * nw_ref[:, at],
            NT,
            precision=HIGHEST,
            preferred_element_type=f32,
        )
    pow_ref[...] = power


def prepare(split, tables, ctf, noise_weight):
    _, rows, freq = split.shape
    poses, groups = tables[0].shape[0], ctf.shape[0]
    return call(
        prepare_kernel,
        "prepare",
        [VMEM] * 7,
        [
            jax.ShapeDtypeStruct((poses, freq), f32),
            jax.ShapeDtypeStruct((poses, freq), f32),
            jax.ShapeDtypeStruct((rows, groups), f32),
        ],
        (split, *tables, ctf, noise_weight),
        flops=24 * rows * groups * freq,
    )


def template_kernel(cls_ref, cos_ref, sin_ref, temp_ref):
    _, rows, tile = cls_ref.shape
    poses = cos_ref.shape[0]
    for a in range(0, tile, LANES):
        at = slice(a, a + LANES)
        later = slice(tile + a, tile + a + LANES)
        re = cls_ref[0, :, at].astype(f32)
        im = cls_ref[1, :, at].astype(f32)
        for r in range(poses):
            cos_r = cos_ref[r : r + 1, at]
            sin_r = sin_ref[r : r + 1, at]
            temp_ref[r * rows : (r + 1) * rows, at] = (re * cos_r - im * sin_r).astype(bf16)
            temp_ref[r * rows : (r + 1) * rows, later] = (re * sin_r + im * cos_r).astype(bf16)


def build_templates(split, cos_t, sin_t):
    _, rows, freq = split.shape
    poses = cos_t.shape[0]
    tile = max(t for t in range(LANES, 385, LANES) if freq // CHUNKS % t == 0)
    return pl.pallas_call(
        template_kernel,
        grid=(freq // tile,),
        in_specs=[
            pl.BlockSpec((2, rows, tile), lambda j: (0, 0, j)),
            pl.BlockSpec((poses, tile), lambda j: (0, j)),
            pl.BlockSpec((poses, tile), lambda j: (0, j)),
        ],
        out_specs=pl.BlockSpec((None, poses * rows, 2 * tile), lambda j: (j, 0, 0)),
        out_shape=pltpu.HBM((freq // tile, poses * rows, 2 * tile), bf16),
        compiler_params=pltpu.CompilerParams(vmem_limit_bytes=VMEM_LIMIT),
        cost_estimate=pl.CostEstimate(
            flops=40 * poses * rows * freq, bytes_accessed=4 * poses * rows * freq, transcendentals=0
        ),
        name="templates",
    )(split, cos_t, sin_t)


def template_copies(temp_hbm, temp_ref, sem, chunk):
    count = temp_ref.shape[0]
    copies = [
        pltpu.make_async_copy(temp_hbm.at[chunk * count + t], temp_ref.at[t], sem.at[t])
        for t in range(count)
    ]
    for copy in copies:
        copy.start()
    return copies


def add_products(acc_ref, temp_ref, copies, parts):
    tile = temp_ref.shape[2] // 2
    even = even_index((acc_ref.shape[0], tile), 0)
    for t, copy in enumerate(copies):
        at = slice(t * tile, (t + 1) * tile)
        wide = jnp.concatenate([p[:, at] for p in parts], axis=0).astype(f32)
        split = jnp.concatenate(
            [jnp.where(even, wide, 0.0).astype(bf16), jnp.where(even, 0.0, wide).astype(bf16)],
            axis=1,
        )
        copy.wait()
        acc_ref[...] += lax.dot_general(split, temp_ref[t], NT, preferred_element_type=f32)


def score_kernel(chunk, temp_hbm, *refs):
    refs, (acc_ref, temp_ref, sem) = refs[:-3], refs[-3:]
    copies = template_copies(temp_hbm, temp_ref, sem, chunk)
    parts = refs if chunk == 0 else refs[1:]
    acc_ref[...] = jnp.zeros_like(acc_ref) if chunk == 0 else refs[0][...]
    add_products(acc_ref, temp_ref, copies, parts)


def last_score_kernel(sources, span, temp_hbm, pow_ref, *refs):
    refs = list(refs)
    s_ref, all_ref, marks_ref, stat_ref, temp_ref, acc_ref, sem = refs[-7:]
    copies = template_copies(temp_hbm, temp_ref, sem, CHUNKS - 1)
    chunks = [refs[c * sources : (c + 1) * sources] for c in range(CHUNKS)]
    rows, groups = pow_ref.shape
    lanes = s_ref.shape[1]
    poses = s_ref.shape[0] // rows
    for c, parts in enumerate(chunks):
        at = 0
        for p in parts:
            all_ref[at : at + p.shape[0], c * span : (c + 1) * span] = p[:, :span]
            at += p.shape[0]
    ids = jnp.concatenate([p[:, span:] for p in chunks[0]], axis=0).astype(f32)
    group = lax.broadcasted_iota(jnp.int32, (lanes, groups), 1).astype(f32)
    marks = (ids[:, :groups] == group).astype(f32)
    marks_ref[...] = marks
    penalty = lax.dot_general(
        pow_ref[...], marks, NT, precision=HIGHEST, preferred_element_type=f32
    )
    acc_ref[...] = refs[CHUNKS * sources][...] if CHUNKS > 1 else jnp.zeros_like(acc_ref)
    add_products(acc_ref, temp_ref, copies, chunks[-1])
    acc = acc_ref[...].T
    acc = acc + jnp.where(
        even_index(acc.shape, 1), pltpu.roll(acc, lanes - 1, 1), pltpu.roll(acc, 1, 1)
    )
    scores = acc.reshape(poses, rows, lanes) - 0.5 * penalty[None]
    peak = jnp.max(jnp.max(scores, axis=0), axis=0, keepdims=True)
    total = jnp.sum(jnp.sum(jnp.exp(scores - peak[None]), axis=0), axis=0, keepdims=True)
    s_ref[...] = scores.reshape(poses * rows, lanes)
    stat_ref[0:1, :] = peak
    stat_ref[1:2, :] = total
    stat_ref[2:8, :] = jnp.zeros((6, lanes), f32)


def score(temps, power, gathered, freq):
    temps = pltpu.with_memory_space_constraint(temps, pltpu.HBM)
    tiles, columns, width = temps.shape
    span = freq // CHUNKS
    lanes = sum(p.shape[0] for p in gathered[0])
    acc_shape = (lanes, columns)
    scratch = [pltpu.VMEM((tiles // CHUNKS, columns, width), bf16)]
    sems = [pltpu.SemaphoreType.DMA((tiles // CHUNKS,))]
    flops = 2 * columns * 256 * 2 * span
    acc = []
    for c in range(CHUNKS - 1):
        operands = [temps, *acc, *gathered[c]]
        acc = call(
            functools.partial(score_kernel, c),
            f"score{c}",
            [ANY] + [VMEM] * (len(operands) - 1),
            [jax.ShapeDtypeStruct(acc_shape, f32)],
            operands,
            scratch + sems,
            flops=flops,
        )
    operands = [temps, power, *[p for parts in gathered for p in parts], *acc]
    return call(
        functools.partial(last_score_kernel, len(gathered[0]), span),
        f"score{CHUNKS - 1}",
        [ANY] + [VMEM] * (len(operands) - 1),
        [
            jax.ShapeDtypeStruct((columns, lanes), f32),
            jax.ShapeDtypeStruct((lanes, freq), bf16),
            jax.ShapeDtypeStruct((lanes, power.shape[1]), f32),
            jax.ShapeDtypeStruct((8, lanes), f32),
        ],
        operands,
        scratch + [pltpu.VMEM(acc_shape, f32)] + sems,
        flops=flops,
    )


def xor_blocks(values, block, distance):
    lanes = values.shape[1]
    lane = lax.broadcasted_iota(jnp.int32, values.shape, 1)
    width = block
    while distance:
        if distance % 2:
            low = lax.rem(lane // width, 2) == 0
            values = jnp.where(
                low, pltpu.roll(values, lanes - width, 1), pltpu.roll(values, width, 1)
            )
        distance //= 2
        width *= 2
    return values


def rotate_slice(rho_ref, w_ref, cos_ref, sin_ref, base, span, poses, buffers, write):
    rows = rho_ref.shape[1] // poses
    tiles = [(a, min(256, span - a)) for a in range(0, span, 256)]

    def products(i):
        start, width = tiles[i]
        at = pl.ds(pl.multiple_of(base + start, LANES), width)
        weighted = w_ref[:, at]
        buffer = buffers[i % 2]
        buffer[0, :, :width] = jnp.dot(rho_ref[0], weighted, preferred_element_type=f32)
        buffer[1, :, :width] = jnp.dot(rho_ref[1], weighted, preferred_element_type=f32)

    def rotate(i):
        start, width = tiles[i]
        buffer = buffers[i % 2]
        for a in range(0, width, LANES):
            at = pl.ds(pl.multiple_of(base + start + a, LANES), LANES)
            numer_re = jnp.zeros((rows, LANES), f32)
            numer_im = jnp.zeros((rows, LANES), f32)
            for r in range(poses):
                cos_r = cos_ref[r : r + 1, at]
                sin_r = sin_ref[r : r + 1, at]
                s_re = buffer[0, r * rows : (r + 1) * rows, a : a + LANES]
                s_im = buffer[1, r * rows : (r + 1) * rows, a : a + LANES]
                numer_re = numer_re + s_re * cos_r + s_im * sin_r
                numer_im = numer_im + s_im * cos_r - s_re * sin_r
            write(start + a, numer_re, numer_im)

    products(0)
    for i in range(1, len(tiles)):
        products(i)
        rotate(i - 1)
    rotate(len(tiles) - 1)


def write_to(ref, span):
    def write(at, numer_re, numer_im):
        ref[:, at : at + LANES] = numer_re.astype(ref.dtype)
        ref[:, span + at : span + at + LANES] = numer_im.astype(ref.dtype)

    return write


def rho_kernel(poses, block, paired, far, span, me_ref, s_ref, marks_ref, cos_ref, sin_ref, w_ref, *refs):
    stat_refs, refs = refs[: len(paired)], refs[len(paired) :]
    norm_ref, rho_ref, mass_ref = refs[:3]
    out_refs, buffers = refs[3:-2], refs[-2:]
    rows, groups = mass_ref.shape
    lanes = s_ref.shape[1]
    peaks, totals = [], []
    for ref, distance in zip(stat_refs, paired):
        for at in range(0, ref.shape[0], 8):
            stats = xor_blocks(ref[at : at + 8, :], block, distance)
            peaks.append(stats[0:1])
            totals.append(stats[1:2])
    peak = functools.reduce(jnp.maximum, peaks)
    total = sum(t * jnp.exp(p - peak) for t, p in zip(totals, peaks))
    log_norm = peak + jnp.log(total)
    norm_ref[...] = log_norm
    rho = jnp.exp(s_ref[...].reshape(poses, rows, lanes) - log_norm[None])
    even = even_index((rows, lanes), 1)
    mass = lax.dot_general(
        jnp.where(even, jnp.sum(rho, axis=0), 0.0),
        marks_ref[...],
        NN,
        precision=HIGHEST,
        preferred_element_type=f32,
    )
    mass_ref[...] = mass
    high = mass.astype(bf16)
    low = (mass - high.astype(f32)).astype(bf16)
    for ref in out_refs:
        ref[:, 2 * span : 2 * span + groups] = high
        ref[:, 2 * span + groups :] = low
    flat = rho.reshape(poses * rows, lanes)
    even = even_index(flat.shape, 1)
    rho_ref[0] = jnp.where(even, flat, 0.0).astype(bf16)
    rho_ref[1] = jnp.where(even, 0.0, flat).astype(bf16)
    for ref, distance in zip(out_refs, far):
        base = (me_ref[0] ^ distance) * span
        rotate_slice(
            rho_ref, w_ref, cos_ref, sin_ref, base, span, poses, buffers, write_to(ref, span)
        )


def outgoing_slices(me, scores, marks, cos_t, sin_t, weighted, stats, paired, far, block, span):
    poses, lanes = cos_t.shape[0], scores.shape[1]
    rows, groups = scores.shape[0] // poses, marks.shape[1]
    return call(
        functools.partial(rho_kernel, poses, block, paired, far, span),
        "outgoing",
        [SMEM] + [VMEM] * (5 + len(stats)),
        [
            jax.ShapeDtypeStruct((1, lanes), f32),
            jax.ShapeDtypeStruct((2, poses * rows, lanes), bf16),
            jax.ShapeDtypeStruct((rows, groups), f32),
        ]
        + [jax.ShapeDtypeStruct((rows, 2 * span + 2 * groups), bf16)] * len(far),
        (me, scores, marks, cos_t, sin_t, weighted, *stats),
        [pltpu.VMEM((2, poses * rows, 256), f32)] * 2,
        flops=4 * 256 * poses * rows * span * len(far),
    )


def own_kernel(
    poses,
    block,
    span,
    me_ref,
    s_ref,
    norm_ref,
    rho_ref,
    cos_ref,
    sin_ref,
    w_ref,
    ctf_ref,
    nw_ref,
    out_ref,
    cw_ref,
    resp_ref,
    *buffers,
):
    base = me_ref[0] * span
    at = pl.ds(pl.multiple_of(base, LANES), span)
    ctf = ctf_ref[:, at]
    cw_ref[...] = ctf * ctf * nw_ref[:, at]
    rotate_slice(
        rho_ref, w_ref, cos_ref, sin_ref, base, span, poses, buffers, write_to(out_ref, span)
    )
    rows = resp_ref.shape[0]
    lanes = s_ref.shape[1]
    scores = s_ref[...].reshape(poses, rows, lanes)
    pose_peak = jnp.max(scores, axis=0)
    total = jnp.sum(jnp.exp(scores - pose_peak[None]), axis=0)
    log_resp = pose_peak + jnp.log(total) - norm_ref[...]
    shape = (resp_ref.shape[1], lanes)
    lane = lax.broadcasted_iota(jnp.int32, shape, 1)
    row = ((lane // block) ^ me_ref[1]) * (block // 2) + lax.rem(lane, block) // 2
    take = (lax.broadcasted_iota(jnp.int32, shape, 0) == row) & (lax.rem(lane, 2) == 0)
    resp_ref[...] = lax.dot_general(
        log_resp, take.astype(f32), NT, precision=HIGHEST, preferred_element_type=f32
    )


def own_slice(me, scores, norm, rho, cos_t, sin_t, weighted, ctf, noise_weight, block, span):
    poses, lanes = cos_t.shape[0], scores.shape[1]
    rows = scores.shape[0] // poses
    return call(
        functools.partial(own_kernel, poses, block, span),
        "own_slice",
        [SMEM] + [VMEM] * 8,
        [
            jax.ShapeDtypeStruct((rows, 2 * span), f32),
            jax.ShapeDtypeStruct((ctf.shape[0], span), f32),
            jax.ShapeDtypeStruct((rows, lanes // 2), f32),
        ],
        (me, scores, norm, rho, cos_t, sin_t, weighted, ctf, noise_weight),
        [pltpu.VMEM((2, poses * rows, 256), f32)] * 2,
        flops=4 * 256 * poses * rows * span,
    )


def finish_kernel(span, cw_ref, mass_ref, own_ref, *refs):
    received, out_ref = refs[:-1], refs[-1]
    groups = mass_ref.shape[1]
    mass = mass_ref[...]
    for ref in received:
        mass += ref[:, 2 * span : 2 * span + groups].astype(f32)
        mass += ref[:, 2 * span + groups :].astype(f32)
    denom = (
        lax.dot_general(
            mass,
            cw_ref[...],
            NN,
            precision=HIGHEST,
            preferred_element_type=f32,
        )
        + prior_precision
    )
    for part in range(2):
        cut = slice(part * span, (part + 1) * span)
        numer = own_ref[:, cut]
        for ref in received:
            numer += ref[:, cut].astype(f32)
        out_ref[:, part, :] = numer / denom


def finish(weight, mass, own, received, span):
    rows = own.shape[0]
    return call(
        functools.partial(finish_kernel, span),
        "finish",
        [VMEM] * (3 + len(received)),
        [jax.ShapeDtypeStruct((rows, 2, span), f32)],
        (weight, mass, own, *received),
    )[0]


def swap(values, axis, distance):
    size = lax.axis_size(axis)
    return lax.ppermute(values, axis, [(i, i ^ distance) for i in range(size)])


def direct_shards(shard):
    distances = [1 << b for b in range(lax.axis_size("cls").bit_length() - 1)]
    return [swap(shard, "cls", d) for d in distances]


def gather_pairs(shard, direct):
    slots = [shard]
    for i, arrived in enumerate(direct):
        slots += [arrived] + [swap(arrived, "cls", k) for k in range(1, 1 << i)]
    return slots


def local(particles, classes, ctf, noise_weight, group_ids, shifts):
    part_rows, _, freq = particles.shape
    n_cls = lax.axis_size("cls")
    n_img = lax.axis_size("img")
    span = freq // n_img
    pairwise = n_cls <= 4
    me_cls = lax.axis_index("cls") if pairwise else 0
    me = jnp.stack([lax.axis_index("img"), me_cls]).astype(jnp.int32)

    shards = weigh(particles, ctf, noise_weight, group_ids)
    noise_weight = noise_weight[None, :]
    if pairwise:
        direct = [direct_shards(w) for w in shards]
    else:
        gathered = [[lax.all_gather(w, "cls", axis=0, tiled=True)] for w in shards]

    split = jnp.transpose(classes, (1, 0, 2))
    cos_t, sin_t, power = prepare(split, phase_tables(shifts, freq), ctf, noise_weight)
    temps = build_templates(split, cos_t, sin_t)
    if pairwise:
        direct, power, temps = lax.optimization_barrier((direct, power, temps))
        gathered = [gather_pairs(w, d) for w, d in zip(shards, direct)]
    scores, weighted, marks, stat = score(temps, power, gathered, freq)
    if pairwise:
        stats = [stat] + [swap(stat, "cls", k) for k in range(1, n_cls)]
        paired = tuple(range(n_cls))
    else:
        stats = [lax.all_gather(stat, "cls", axis=0, tiled=True)]
        paired = (0,)

    far = tuple(range(n_img - 1, 0, -1))
    block = 2 * part_rows
    norm, rho, mass, *parts = outgoing_slices(
        me, scores, marks, cos_t, sin_t, weighted, stats, paired, far, block, span
    )
    received = [swap(part, "img", d) for part, d in zip(parts, far)]
    mine, weight, log_resp = own_slice(
        me, scores, norm, rho, cos_t, sin_t, weighted, ctf, noise_weight, block, span
    )
    averages = finish(weight, mass, mine, received, span)
    return (log_resp.T, averages)


def solution(mesh):
    placed = (
        P(("groups", "img", "cls"), None, None),
        P(("groups", "cls"), None, None),
        P("groups", None),
        P("groups"),
        P(("groups", "img", "cls")),
        P("groups", None),
    )
    return jax.shard_map(
        local,
        mesh=mesh,
        in_specs=placed,
        out_specs=(P(("groups", "img"), "cls"), P(("groups", "cls"), None, "img")),
        check_vma=False,
    )
```

```python
import functools

import jax
import jax.numpy as jnp
from jax import lax
from jax.experimental import pallas as pl
from jax.experimental.pallas import tpu as pltpu
from jax.sharding import PartitionSpec as P

BOX = 128
CHUNKS = 2
LANES = 128
VMEM_LIMIT = 24 * 1024 * 1024

prior_precision = 0.02

NT = (((1,), (1,)), ((), ()))
NN = (((1,), (0,)), ((), ()))
HIGHEST = lax.Precision.HIGHEST
f32 = jnp.float32
bf16 = jnp.bfloat16

SMEM = pl.BlockSpec(memory_space=pltpu.SMEM)
VMEM = pl.BlockSpec(memory_space=pltpu.VMEM)
ANY = pl.BlockSpec(memory_space=pl.ANY)


def phase_tables(shifts, freq):
    along_x = (jnp.arange(BOX) - BOX // 2).astype(f32)
    along_y = jnp.arange(freq // BOX).astype(f32)
    step = 2.0 * jnp.pi / BOX
    angle_x = step * (shifts[:, 0:1].astype(f32) * along_x[None, :])
    angle_y = step * (shifts[:, 1:2].astype(f32) * along_y[None, :])
    return (jnp.cos(angle_x), jnp.sin(angle_x), jnp.cos(angle_y), jnp.sin(angle_y))


def call(kernel, name, in_specs, out_shape, operands, scratch=(), flops=0, moved=0, out_specs=None):
    return pl.pallas_call(
        kernel,
        in_specs=in_specs,
        out_specs=[VMEM] * len(out_shape) if out_specs is None else out_specs,
        out_shape=out_shape,
        scratch_shapes=list(scratch),
        compiler_params=pltpu.CompilerParams(vmem_limit_bytes=VMEM_LIMIT),
        cost_estimate=pl.CostEstimate(flops=flops, bytes_accessed=moved, transcendentals=0),
        name=name,
    )(*operands)


def even_index(shape, axis):
    return lax.rem(lax.broadcasted_iota(jnp.int32, shape, axis), 2) == 0


def weigh_kernel(ids_hbm, p_hbm, ctf_hbm, nw_hbm, *refs):
    out_refs, (ids_ref, p_ref, ctf_ref, nw_ref, scale_ref, sem) = refs[:-6], refs[-6:]
    count, _, freq = p_ref.shape
    copies = [
        pltpu.make_async_copy(source, target, sem.at[i])
        for i, (source, target) in enumerate(
            [(ids_hbm, ids_ref), (ctf_hbm, ctf_ref), (nw_hbm, nw_ref), (p_hbm, p_ref)]
        )
    ]
    for copy in copies:
        copy.start()
    copies[0].wait()
    row = lax.broadcasted_iota(jnp.int32, (2 * count, LANES), 0) // 2
    ids = jnp.zeros((2 * count, LANES), f32)
    for n in range(count):
        ids = jnp.where(row == n, ids_ref[n].astype(f32), ids)
    for copy in copies[1:]:
        copy.wait()
    noise = nw_ref[...].reshape(1, freq)
    for n in range(count):
        scale = ctf_ref[pl.ds(ids_ref[n], 1), :] * noise
        scale_ref[2 * n : 2 * n + 2, :] = jnp.broadcast_to(scale, (2, freq))
    values = p_ref[...].astype(f32).reshape(2 * count, freq)
    weighted = (values * scale_ref[...]).astype(bf16)
    chunk = freq // (len(out_refs) - 1)
    for c, out_ref in enumerate(out_refs[1:]):
        out_ref[:, :chunk] = weighted[:, c * chunk : (c + 1) * chunk]
    out_refs[0][:, :freq] = weighted
    for out_ref in out_refs[:2]:
        out_ref[:, out_ref.shape[1] - LANES :] = ids.astype(bf16)


def weigh(particles, ctf, noise_weight, group_ids):
    rows, _, freq = particles.shape
    chunk = freq // CHUNKS
    operands = (group_ids, particles, ctf, noise_weight)
    return call(
        weigh_kernel,
        "weigh",
        [ANY] * 4,
        [jax.ShapeDtypeStruct((2 * rows, freq + LANES), bf16)]
        + [
            jax.ShapeDtypeStruct((2 * rows, chunk + (LANES if c == 0 else 0)), bf16)
            for c in range(CHUNKS)
        ],
        [pltpu.with_memory_space_constraint(x, pltpu.HBM) for x in operands],
        [
            pltpu.SMEM((rows,), jnp.int32),
            pltpu.VMEM(particles.shape, bf16),
            pltpu.VMEM(ctf.shape, f32),
            pltpu.VMEM((freq,), f32),
            pltpu.VMEM((2 * rows, freq), f32),
            pltpu.SemaphoreType.DMA((4,)),
        ],
        flops=4 * rows * freq,
        moved=16 * rows * freq,
    )


def prepare_kernel(
    cls_ref, xc_ref, xs_ref, yc_ref, ys_ref, ctf_ref, nw_ref, cos_ref, sin_ref, pow_ref
):
    freq = cls_ref.shape[2]
    x_cos, x_sin = xc_ref[...], xs_ref[...]
    for t in range(freq // BOX):
        y_cos = jnp.broadcast_to(yc_ref[:, t : t + 1], x_cos.shape)
        y_sin = jnp.broadcast_to(ys_ref[:, t : t + 1], x_cos.shape)
        cos_ref[:, t * BOX : (t + 1) * BOX] = x_cos * y_cos - x_sin * y_sin
        sin_ref[:, t * BOX : (t + 1) * BOX] = x_sin * y_cos + x_cos * y_sin
    cut = freq // 4
    power = jnp.zeros(pow_ref.shape, f32)
    for q in range(4):
        at = slice(q * cut, (q + 1) * cut)
        re = cls_ref[0, :, at].astype(f32)
        im = cls_ref[1, :, at].astype(f32)
        ctf = ctf_ref[:, at]
        power += lax.dot_general(
            re * re + im * im,
            ctf * ctf * nw_ref[:, at],
            NT,
            precision=HIGHEST,
            preferred_element_type=f32,
        )
    pow_ref[...] = power


def prepare(split, tables, ctf, noise_weight):
    _, rows, freq = split.shape
    poses, groups = tables[0].shape[0], ctf.shape[0]
    return call(
        prepare_kernel,
        "prepare",
        [VMEM] * 7,
        [
            jax.ShapeDtypeStruct((poses, freq), f32),
            jax.ShapeDtypeStruct((poses, freq), f32),
            jax.ShapeDtypeStruct((rows, groups), f32),
        ],
        (split, *tables, ctf, noise_weight),
        flops=24 * rows * groups * freq,
    )


def template_kernel(cls_ref, cos_ref, sin_ref, temp_ref):
    _, rows, tile = cls_ref.shape
    poses = cos_ref.shape[0]
    for a in range(0, tile, LANES):
        at = slice(a, a + LANES)
        later = slice(tile + a, tile + a + LANES)
        re = cls_ref[0, :, at].astype(f32)
        im = cls_ref[1, :, at].astype(f32)
        for r in range(poses):
            cos_r = cos_ref[r : r + 1, at]
            sin_r = sin_ref[r : r + 1, at]
            temp_ref[r * rows : (r + 1) * rows, at] = (re * cos_r - im * sin_r).astype(bf16)
            temp_ref[r * rows : (r + 1) * rows, later] = (re * sin_r + im * cos_r).astype(bf16)


def build_templates(split, cos_t, sin_t):
    _, rows, freq = split.shape
    poses = cos_t.shape[0]
    tile = max(t for t in range(LANES, 385, LANES) if freq // CHUNKS % t == 0)
    return pl.pallas_call(
        template_kernel,
        grid=(freq // tile,),
        in_specs=[
            pl.BlockSpec((2, rows, tile), lambda j: (0, 0, j)),
            pl.BlockSpec((poses, tile), lambda j: (0, j)),
            pl.BlockSpec((poses, tile), lambda j: (0, j)),
        ],
        out_specs=pl.BlockSpec((None, poses * rows, 2 * tile), lambda j: (j, 0, 0)),
        out_shape=pltpu.HBM((freq // tile, poses * rows, 2 * tile), bf16),
        compiler_params=pltpu.CompilerParams(vmem_limit_bytes=VMEM_LIMIT),
        cost_estimate=pl.CostEstimate(
            flops=40 * poses * rows * freq, bytes_accessed=4 * poses * rows * freq, transcendentals=0
        ),
        name="templates",
    )(split, cos_t, sin_t)


def template_copies(temp_hbm, temp_ref, sem, chunk):
    count = temp_ref.shape[0]
    copies = [
        pltpu.make_async_copy(temp_hbm.at[chunk * count + t], temp_ref.at[t], sem.at[t])
        for t in range(count)
    ]
    for copy in copies:
        copy.start()
    return copies


def add_products(acc_ref, temp_ref, copies, parts):
    tile = temp_ref.shape[2] // 2
    even = even_index((acc_ref.shape[1], tile), 0)
    for t, copy in enumerate(copies):
        wide = jnp.concatenate(
            [ref[:, start + t * tile : start + (t + 1) * tile] for ref, start in parts], axis=0
        ).astype(f32)
        split = jnp.concatenate(
            [jnp.where(even, wide, 0.0).astype(bf16), jnp.where(even, 0.0, wide).astype(bf16)],
            axis=1,
        )
        copy.wait()
        acc_ref[...] += lax.dot_general(temp_ref[t], split, NT, preferred_element_type=f32)


def chunk_parts(refs, chunked, chunk, span):
    whole = [(ref, chunk * span) for ref in refs[: len(refs) - chunked]]
    return whole + [(ref, 0) for ref in refs[len(refs) - chunked :]]


def score_kernel(chunk, span, chunked, temp_hbm, *refs):
    refs, (acc_ref, temp_ref, sem) = refs[:-3], refs[-3:]
    copies = template_copies(temp_hbm, temp_ref, sem, chunk)
    parts = refs if chunk == 0 else refs[1:]
    acc_ref[...] = jnp.zeros_like(acc_ref) if chunk == 0 else refs[0][...]
    add_products(acc_ref, temp_ref, copies, chunk_parts(parts, chunked, chunk, span))


def last_score_kernel(wholes, chunked, span, temp_hbm, pow_ref, *refs):
    refs = list(refs)
    s_ref, all_ref, marks_ref, stat_ref, temp_ref, sem = refs[-6:]
    copies = template_copies(temp_hbm, temp_ref, sem, CHUNKS - 1)
    whole = refs[:wholes]
    chunks = [refs[wholes + c * chunked : wholes + (c + 1) * chunked] for c in range(CHUNKS)]
    rows, groups = pow_ref.shape
    lanes = s_ref.shape[1]
    poses = s_ref.shape[0] // rows
    freq = span * CHUNKS
    at = 0
    for ref in whole:
        all_ref[at : at + ref.shape[0], :] = ref[:, :freq]
        at += ref.shape[0]
    for k in range(chunked):
        height = chunks[0][k].shape[0]
        for c in range(CHUNKS):
            all_ref[at : at + height, c * span : (c + 1) * span] = chunks[c][k][:, :span]
        at += height
    ids = jnp.concatenate([ref[:, freq:] for ref in whole] + [ref[:, span:] for ref in chunks[0]], axis=0)
    group = lax.broadcasted_iota(jnp.int32, (lanes, groups), 1).astype(f32)
    marks = (ids.astype(f32)[:, :groups] == group).astype(f32)
    marks_ref[...] = marks
    penalty = lax.dot_general(
        pow_ref[...], marks, NT, precision=HIGHEST, preferred_element_type=f32
    )
    s_ref[...] = refs[wholes + CHUNKS * chunked][...] if CHUNKS > 1 else jnp.zeros_like(s_ref)
    parts = chunk_parts(whole + chunks[-1], chunked, CHUNKS - 1, span)
    add_products(s_ref, temp_ref, copies, parts)
    acc = s_ref[...]
    acc = acc + jnp.where(
        even_index(acc.shape, 1), pltpu.roll(acc, lanes - 1, 1), pltpu.roll(acc, 1, 1)
    )
    scores = acc.reshape(poses, rows, lanes) - 0.5 * penalty[None]
    peak = jnp.max(jnp.max(scores, axis=0), axis=0, keepdims=True)
    total = jnp.sum(jnp.sum(jnp.exp(scores - peak[None]), axis=0), axis=0, keepdims=True)
    s_ref[...] = scores.reshape(poses * rows, lanes)
    stat_ref[0:1, :] = peak
    stat_ref[1:2, :] = total
    stat_ref[2:8, :] = jnp.zeros((6, lanes), f32)


def score(temps, power, whole, chunks, freq):
    temps = pltpu.with_memory_space_constraint(temps, pltpu.HBM)
    tiles, columns, width = temps.shape
    span = freq // CHUNKS
    chunked = len(chunks[0])
    lanes = sum(p.shape[0] for p in whole + chunks[0])
    acc_shape = jax.ShapeDtypeStruct((columns, lanes), f32)
    scratch = [
        pltpu.VMEM((tiles // CHUNKS, columns, width), bf16),
        pltpu.SemaphoreType.DMA((tiles // CHUNKS,)),
    ]
    flops = 2 * columns * 256 * 2 * span
    acc = []
    for c in range(CHUNKS - 1):
        operands = [temps, *acc, *whole, *chunks[c]]
        acc = call(
            functools.partial(score_kernel, c, span, chunked),
            f"score{c}",
            [ANY] + [VMEM] * (len(operands) - 1),
            [acc_shape],
            operands,
            scratch,
            flops=flops,
        )
    operands = [temps, power, *whole, *[p for parts in chunks for p in parts], *acc]
    return call(
        functools.partial(last_score_kernel, len(whole), chunked, span),
        f"score{CHUNKS - 1}",
        [ANY] + [VMEM] * (len(operands) - 1),
        [
            acc_shape,
            jax.ShapeDtypeStruct((lanes, freq), bf16),
            jax.ShapeDtypeStruct((lanes, power.shape[1]), f32),
            jax.ShapeDtypeStruct((8, lanes), f32),
        ],
        operands,
        scratch,
        flops=flops,
    )


def xor_blocks(values, block, distance):
    lanes = values.shape[1]
    lane = lax.broadcasted_iota(jnp.int32, values.shape, 1)
    width = block
    while distance:
        if distance % 2:
            low = lax.rem(lane // width, 2) == 0
            values = jnp.where(
                low, pltpu.roll(values, lanes - width, 1), pltpu.roll(values, width, 1)
            )
        distance //= 2
        width *= 2
    return values


def rotate_slice(rho_ref, w_ref, cos_ref, sin_ref, base, span, poses, buffers, write):
    rows = rho_ref.shape[1] // poses
    tiles = [(a, min(256, span - a)) for a in range(0, span, 256)]

    def products(i):
        start, width = tiles[i]
        at = pl.ds(pl.multiple_of(base + start, LANES), width)
        weighted = w_ref[:, at]
        buffer = buffers[i % 2]
        buffer[0, :, :width] = jnp.dot(rho_ref[0], weighted, preferred_element_type=f32)
        buffer[1, :, :width] = jnp.dot(rho_ref[1], weighted, preferred_element_type=f32)

    def rotate(i):
        start, width = tiles[i]
        buffer = buffers[i % 2]
        for a in range(0, width, LANES):
            at = pl.ds(pl.multiple_of(base + start + a, LANES), LANES)
            numer_re = jnp.zeros((rows, LANES), f32)
            numer_im = jnp.zeros((rows, LANES), f32)
            for r in range(poses):
                cos_r = cos_ref[r : r + 1, at]
                sin_r = sin_ref[r : r + 1, at]
                s_re = buffer[0, r * rows : (r + 1) * rows, a : a + LANES]
                s_im = buffer[1, r * rows : (r + 1) * rows, a : a + LANES]
                numer_re = numer_re + s_re * cos_r + s_im * sin_r
                numer_im = numer_im + s_im * cos_r - s_re * sin_r
            write(start + a, numer_re, numer_im)

    products(0)
    for i in range(1, len(tiles)):
        products(i)
        rotate(i - 1)
    rotate(len(tiles) - 1)


def write_to(ref, span):
    def write(at, numer_re, numer_im):
        ref[:, at : at + LANES] = numer_re.astype(ref.dtype)
        ref[:, span + at : span + at + LANES] = numer_im.astype(ref.dtype)

    return write


def rho_kernel(poses, block, paired, far, span, me_ref, s_ref, marks_ref, cos_ref, sin_ref, w_ref, *refs):
    stat_refs, refs = refs[: len(paired)], refs[len(paired) :]
    norm_ref, rho_ref, mass_ref = refs[:3]
    out_refs, buffers = refs[3:-2], refs[-2:]
    rows, groups = mass_ref.shape
    lanes = s_ref.shape[1]
    peaks, totals = [], []
    for ref, distance in zip(stat_refs, paired):
        for at in range(0, ref.shape[0], 8):
            stats = xor_blocks(ref[at : at + 8, :], block, distance)
            peaks.append(stats[0:1])
            totals.append(stats[1:2])
    peak = functools.reduce(jnp.maximum, peaks)
    total = sum(t * jnp.exp(p - peak) for t, p in zip(totals, peaks))
    log_norm = peak + jnp.log(total)
    norm_ref[...] = log_norm
    rho = jnp.exp(s_ref[...].reshape(poses, rows, lanes) - log_norm[None])
    even = even_index((rows, lanes), 1)
    mass = lax.dot_general(
        jnp.where(even, jnp.sum(rho, axis=0), 0.0),
        marks_ref[...],
        NN,
        precision=HIGHEST,
        preferred_element_type=f32,
    )
    mass_ref[...] = mass
    high = mass.astype(bf16)
    low = (mass - high.astype(f32)).astype(bf16)
    for ref in out_refs:
        ref[:, 2 * span : 2 * span + groups] = high
        ref[:, 2 * span + groups :] = low
    flat = rho.reshape(poses * rows, lanes)
    even = even_index(flat.shape, 1)
    rho_ref[0] = jnp.where(even, flat, 0.0).astype(bf16)
    rho_ref[1] = jnp.where(even, 0.0, flat).astype(bf16)
    for ref, distance in zip(out_refs, far):
        base = (me_ref[0] ^ distance) * span
        rotate_slice(
            rho_ref, w_ref, cos_ref, sin_ref, base, span, poses, buffers, write_to(ref, span)
        )


def outgoing_slices(me, scores, marks, cos_t, sin_t, weighted, stats, paired, far, block, span):
    poses, lanes = cos_t.shape[0], scores.shape[1]
    rows, groups = scores.shape[0] // poses, marks.shape[1]
    return call(
        functools.partial(rho_kernel, poses, block, paired, far, span),
        "outgoing",
        [SMEM] + [VMEM] * (5 + len(stats)),
        [
            jax.ShapeDtypeStruct((1, lanes), f32),
            jax.ShapeDtypeStruct((2, poses * rows, lanes), bf16),
            jax.ShapeDtypeStruct((rows, groups), f32),
        ]
        + [jax.ShapeDtypeStruct((rows, 2 * span + 2 * groups), bf16)] * len(far),
        (me, scores, marks, cos_t, sin_t, weighted, *stats),
        [pltpu.VMEM((2, poses * rows, 256), f32)] * 2,
        flops=4 * 256 * poses * rows * span * len(far),
    )


def own_kernel(
    poses,
    block,
    span,
    me_ref,
    s_ref,
    norm_ref,
    rho_ref,
    cos_ref,
    sin_ref,
    w_ref,
    ctf_ref,
    nw_ref,
    out_ref,
    cw_ref,
    resp_ref,
    *buffers,
):
    base = me_ref[0] * span
    at = pl.ds(pl.multiple_of(base, LANES), span)
    ctf = ctf_ref[:, at]
    cw_ref[...] = ctf * ctf * nw_ref[:, at]
    rotate_slice(
        rho_ref, w_ref, cos_ref, sin_ref, base, span, poses, buffers, write_to(out_ref, span)
    )
    rows = resp_ref.shape[0]
    lanes = s_ref.shape[1]
    scores = s_ref[...].reshape(poses, rows, lanes)
    pose_peak = jnp.max(scores, axis=0)
    total = jnp.sum(jnp.exp(scores - pose_peak[None]), axis=0)
    log_resp = pose_peak + jnp.log(total) - norm_ref[...]
    shape = (resp_ref.shape[1], lanes)
    lane = lax.broadcasted_iota(jnp.int32, shape, 1)
    row = ((lane // block) ^ me_ref[1]) * (block // 2) + lax.rem(lane, block) // 2
    take = (lax.broadcasted_iota(jnp.int32, shape, 0) == row) & (lax.rem(lane, 2) == 0)
    resp_ref[...] = lax.dot_general(
        log_resp, take.astype(f32), NT, precision=HIGHEST, preferred_element_type=f32
    )


def own_slice(me, scores, norm, rho, cos_t, sin_t, weighted, ctf, noise_weight, block, span):
    poses, lanes = cos_t.shape[0], scores.shape[1]
    rows = scores.shape[0] // poses
    return call(
        functools.partial(own_kernel, poses, block, span),
        "own_slice",
        [SMEM] + [VMEM] * 8,
        [
            jax.ShapeDtypeStruct((rows, 2 * span), f32),
            jax.ShapeDtypeStruct((ctf.shape[0], span), f32),
            jax.ShapeDtypeStruct((rows, lanes // 2), f32),
        ],
        (me, scores, norm, rho, cos_t, sin_t, weighted, ctf, noise_weight),
        [pltpu.VMEM((2, poses * rows, 256), f32)] * 2,
        flops=4 * 256 * poses * rows * span,
    )


def finish_kernel(span, cw_ref, mass_ref, own_ref, *refs):
    received, out_ref = refs[:-1], refs[-1]
    groups = mass_ref.shape[1]
    mass = mass_ref[...]
    for ref in received:
        mass += ref[:, 2 * span : 2 * span + groups].astype(f32)
        mass += ref[:, 2 * span + groups :].astype(f32)
    denom = (
        lax.dot_general(
            mass,
            cw_ref[...],
            NN,
            precision=HIGHEST,
            preferred_element_type=f32,
        )
        + prior_precision
    )
    for part in range(2):
        cut = slice(part * span, (part + 1) * span)
        numer = own_ref[:, cut]
        for ref in received:
            numer += ref[:, cut].astype(f32)
        out_ref[:, part, :] = numer / denom


def finish(weight, mass, own, received, span):
    rows = own.shape[0]
    return call(
        functools.partial(finish_kernel, span),
        "finish",
        [VMEM] * (3 + len(received)),
        [jax.ShapeDtypeStruct((rows, 2, span), f32)],
        (weight, mass, own, *received),
    )[0]


def swap(values, axis, distance):
    size = lax.axis_size(axis)
    return lax.ppermute(values, axis, [(i, i ^ distance) for i in range(size)])


def local(particles, classes, ctf, noise_weight, group_ids, shifts):
    part_rows, _, freq = particles.shape
    n_cls = lax.axis_size("cls")
    n_img = lax.axis_size("img")
    span = freq // n_img
    pairwise = n_cls == 4
    me_cls = lax.axis_index("cls") if pairwise else 0
    me = jnp.stack([lax.axis_index("img"), me_cls]).astype(jnp.int32)

    own, *shards = weigh(particles, ctf, noise_weight, group_ids)
    noise_weight = noise_weight[None, :]
    if pairwise:
        far = [swap(w, "cls", 2) for w in shards]
        near = swap(own, "cls", 1)
    else:
        whole, chunks = [lax.all_gather(own, "cls", axis=0, tiled=True)], [[]] * CHUNKS

    split = jnp.transpose(classes, (1, 0, 2))
    cos_t, sin_t, power = prepare(split, phase_tables(shifts, freq), ctf, noise_weight)
    temps = build_templates(split, cos_t, sin_t)
    if pairwise:
        far, power, temps = lax.optimization_barrier((far, power, temps))
        whole, chunks = [own, near], [[w, swap(w, "cls", 1)] for w in far]
    scores, weighted, marks, stat = score(temps, power, whole, chunks, freq)
    if pairwise:
        stats = [stat] + [swap(stat, "cls", k) for k in range(1, n_cls)]
        paired = tuple(range(n_cls))
    else:
        stats = [lax.all_gather(stat, "cls", axis=0, tiled=True)]
        paired = (0,)

    others = tuple(range(n_img - 1, 0, -1))
    block = 2 * part_rows
    norm, rho, mass, *parts = outgoing_slices(
        me, scores, marks, cos_t, sin_t, weighted, stats, paired, others, block, span
    )
    received = [swap(part, "img", d) for part, d in zip(parts, others)]
    mine, weight, log_resp = own_slice(
        me, scores, norm, rho, cos_t, sin_t, weighted, ctf, noise_weight, block, span
    )
    averages = finish(weight, mass, mine, received, span)
    return (log_resp.T, averages)


def solution(mesh):
    placed = (
        P(("groups", "img", "cls"), None, None),
        P(("groups", "cls"), None, None),
        P("groups", None),
        P("groups"),
        P(("groups", "img", "cls")),
        P("groups", None),
    )
    return jax.shard_map(
        local,
        mesh=mesh,
        in_specs=placed,
        out_specs=(P(("groups", "img"), "cls"), P(("groups", "cls"), None, "img")),
        check_vma=False,
    )
```

```python
import functools

import jax
import jax.numpy as jnp
from jax import lax
from jax.experimental import pallas as pl
from jax.experimental.pallas import tpu as pltpu
from jax.sharding import PartitionSpec as P

BOX = 128
CHUNKS = 2
LANES = 128
VMEM_LIMIT = 24 * 1024 * 1024

prior_precision = 0.02

NT = (((1,), (1,)), ((), ()))
NN = (((1,), (0,)), ((), ()))
HIGHEST = lax.Precision.HIGHEST
f32 = jnp.float32
bf16 = jnp.bfloat16

SMEM = pl.BlockSpec(memory_space=pltpu.SMEM)
VMEM = pl.BlockSpec(memory_space=pltpu.VMEM)
ANY = pl.BlockSpec(memory_space=pl.ANY)


def phase_tables(shifts, freq):
    along_x = (jnp.arange(BOX) - BOX // 2).astype(f32)
    along_y = jnp.arange(freq // BOX).astype(f32)
    step = 2.0 * jnp.pi / BOX
    angle_x = step * (shifts[:, 0:1].astype(f32) * along_x[None, :])
    angle_y = step * (shifts[:, 1:2].astype(f32) * along_y[None, :])
    return (jnp.cos(angle_x), jnp.sin(angle_x), jnp.cos(angle_y), jnp.sin(angle_y))


def call(kernel, name, in_specs, out_shape, operands, scratch=(), flops=0, moved=0, out_specs=None):
    return pl.pallas_call(
        kernel,
        in_specs=in_specs,
        out_specs=[VMEM] * len(out_shape) if out_specs is None else out_specs,
        out_shape=out_shape,
        scratch_shapes=list(scratch),
        compiler_params=pltpu.CompilerParams(vmem_limit_bytes=VMEM_LIMIT),
        cost_estimate=pl.CostEstimate(flops=flops, bytes_accessed=moved, transcendentals=0),
        name=name,
    )(*operands)


def even_index(shape, axis):
    return lax.rem(lax.broadcasted_iota(jnp.int32, shape, axis), 2) == 0


def weigh_kernel(ids_hbm, p_hbm, ctf_hbm, nw_hbm, *refs):
    out_refs, (ids_ref, p_ref, ctf_ref, nw_ref, scale_ref, sem) = refs[:-6], refs[-6:]
    count, _, freq = p_ref.shape
    copies = [
        pltpu.make_async_copy(source, target, sem.at[i])
        for i, (source, target) in enumerate(
            [(ids_hbm, ids_ref), (ctf_hbm, ctf_ref), (nw_hbm, nw_ref), (p_hbm, p_ref)]
        )
    ]
    for copy in copies:
        copy.start()
    copies[0].wait()
    row = lax.broadcasted_iota(jnp.int32, (2 * count, LANES), 0) // 2
    ids = jnp.zeros((2 * count, LANES), f32)
    for n in range(count):
        ids = jnp.where(row == n, ids_ref[n].astype(f32), ids)
    for copy in copies[1:]:
        copy.wait()
    noise = nw_ref[...].reshape(1, freq)
    for n in range(count):
        scale = ctf_ref[pl.ds(ids_ref[n], 1), :] * noise
        scale_ref[2 * n : 2 * n + 2, :] = jnp.broadcast_to(scale, (2, freq))
    values = p_ref[...].astype(f32).reshape(2 * count, freq)
    weighted = (values * scale_ref[...]).astype(bf16)
    chunk = freq // (len(out_refs) - 1)
    for c, out_ref in enumerate(out_refs[1:]):
        out_ref[:, :chunk] = weighted[:, c * chunk : (c + 1) * chunk]
    out_refs[0][:, :freq] = weighted
    for out_ref in out_refs[:2]:
        out_ref[:, out_ref.shape[1] - LANES :] = ids.astype(bf16)


def weigh(particles, ctf, noise_weight, group_ids):
    rows, _, freq = particles.shape
    chunk = freq // CHUNKS
    operands = (group_ids, particles, ctf, noise_weight)
    return call(
        weigh_kernel,
        "weigh",
        [ANY] * 4,
        [jax.ShapeDtypeStruct((2 * rows, freq + LANES), bf16)]
        + [
            jax.ShapeDtypeStruct((2 * rows, chunk + (LANES if c == 0 else 0)), bf16)
            for c in range(CHUNKS)
        ],
        [pltpu.with_memory_space_constraint(x, pltpu.HBM) for x in operands],
        [
            pltpu.SMEM((rows,), jnp.int32),
            pltpu.VMEM(particles.shape, bf16),
            pltpu.VMEM(ctf.shape, f32),
            pltpu.VMEM((freq,), f32),
            pltpu.VMEM((2 * rows, freq), f32),
            pltpu.SemaphoreType.DMA((4,)),
        ],
        flops=4 * rows * freq,
        moved=16 * rows * freq,
    )


def prepare_kernel(
    cls_ref, xc_ref, xs_ref, yc_ref, ys_ref, ctf_ref, nw_ref, cos_ref, sin_ref, pow_ref
):
    freq = cls_ref.shape[2]
    x_cos, x_sin = xc_ref[...], xs_ref[...]
    for t in range(freq // BOX):
        y_cos = jnp.broadcast_to(yc_ref[:, t : t + 1], x_cos.shape)
        y_sin = jnp.broadcast_to(ys_ref[:, t : t + 1], x_cos.shape)
        cos_ref[:, t * BOX : (t + 1) * BOX] = x_cos * y_cos - x_sin * y_sin
        sin_ref[:, t * BOX : (t + 1) * BOX] = x_sin * y_cos + x_cos * y_sin
    cut = freq // 4
    power = jnp.zeros(pow_ref.shape, f32)
    for q in range(4):
        at = slice(q * cut, (q + 1) * cut)
        re = cls_ref[0, :, at].astype(f32)
        im = cls_ref[1, :, at].astype(f32)
        ctf = ctf_ref[:, at]
        power += lax.dot_general(
            re * re + im * im,
            ctf * ctf * nw_ref[:, at],
            NT,
            precision=HIGHEST,
            preferred_element_type=f32,
        )
    pow_ref[...] = power


def prepare(split, tables, ctf, noise_weight):
    _, rows, freq = split.shape
    poses, groups = tables[0].shape[0], ctf.shape[0]
    return call(
        prepare_kernel,
        "prepare",
        [VMEM] * 7,
        [
            jax.ShapeDtypeStruct((poses, freq), f32),
            jax.ShapeDtypeStruct((poses, freq), f32),
            jax.ShapeDtypeStruct((rows, groups), f32),
        ],
        (split, *tables, ctf, noise_weight),
        flops=24 * rows * groups * freq,
    )


def write_templates(cls_ref, cos_ref, sin_ref, temp_ref, start, tile):
    rows = cls_ref.shape[1]
    for a in range(0, tile, LANES):
        at = pl.ds(pl.multiple_of(start + a, LANES), LANES)
        re = cls_ref[0, :, at].astype(f32)
        im = cls_ref[1, :, at].astype(f32)
        for r in range(cos_ref.shape[0]):
            cos_r = cos_ref[r : r + 1, at]
            sin_r = sin_ref[r : r + 1, at]
            here = slice(r * rows, (r + 1) * rows)
            temp_ref[here, a : a + LANES] = (re * cos_r - im * sin_r).astype(bf16)
            temp_ref[here, tile + a : tile + a + LANES] = (re * sin_r + im * cos_r).astype(bf16)


def template_tile(freq):
    return max(t for t in range(LANES, 385, LANES) if freq // CHUNKS % t == 0)


def early_kernel(cls_ref, cos_ref, sin_ref, temp_ref):
    write_templates(cls_ref, cos_ref, sin_ref, temp_ref, 0, cls_ref.shape[2])


def early_templates(split, cos_t, sin_t):
    _, rows, freq = split.shape
    poses = cos_t.shape[0]
    tile = template_tile(freq)
    count = freq // tile // 2
    skip = freq // tile - count
    return pl.pallas_call(
        early_kernel,
        grid=(count,),
        in_specs=[
            pl.BlockSpec((2, rows, tile), lambda j: (0, 0, skip + j)),
            pl.BlockSpec((poses, tile), lambda j: (0, skip + j)),
            pl.BlockSpec((poses, tile), lambda j: (0, skip + j)),
        ],
        out_specs=pl.BlockSpec((None, poses * rows, 2 * tile), lambda j: (j, 0, 0)),
        out_shape=pltpu.HBM((count, poses * rows, 2 * tile), bf16),
        compiler_params=pltpu.CompilerParams(vmem_limit_bytes=VMEM_LIMIT),
        cost_estimate=pl.CostEstimate(
            flops=20 * poses * rows * freq, bytes_accessed=2 * poses * rows * freq, transcendentals=0
        ),
        name="early_templates",
    )(split, cos_t, sin_t)


def template_kernel(early_hbm, cls_ref, cos_ref, sin_ref, temp_ref, sem):
    count = early_hbm.shape[0]
    built = temp_ref.shape[0] - count
    tile = temp_ref.shape[2] // 2
    copies = [
        pltpu.make_async_copy(early_hbm.at[t], temp_ref.at[built + t], sem.at[t])
        for t in range(count)
    ]
    for copy in copies:
        copy.start()

    @pl.loop(0, built)
    def _(t):
        write_templates(cls_ref, cos_ref, sin_ref, temp_ref.at[t], t * tile, tile)

    for copy in copies:
        copy.wait()


def all_templates(early, split, cos_t, sin_t):
    _, rows, freq = split.shape
    poses = cos_t.shape[0]
    count, columns, width = early.shape
    return call(
        template_kernel,
        "templates",
        [ANY] + [VMEM] * 3,
        [pltpu.VMEM((freq // (width // 2), columns, width), bf16)],
        (pltpu.with_memory_space_constraint(early, pltpu.HBM), split, cos_t, sin_t),
        [pltpu.SemaphoreType.DMA((count,))],
        flops=20 * poses * rows * freq,
        moved=2 * poses * rows * freq,
    )[0]


def add_products(acc_ref, temp_ref, chunk, parts):
    count = temp_ref.shape[0] // CHUNKS
    tile = temp_ref.shape[2] // 2
    even = even_index((acc_ref.shape[0], tile), 0)
    for t in range(count):
        wide = jnp.concatenate(
            [ref[:, start + t * tile : start + (t + 1) * tile] for ref, start in parts], axis=0
        ).astype(f32)
        split = jnp.concatenate(
            [jnp.where(even, wide, 0.0).astype(bf16), jnp.where(even, 0.0, wide).astype(bf16)],
            axis=1,
        )
        acc_ref[...] += lax.dot_general(
            split, temp_ref[chunk * count + t], NT, preferred_element_type=f32
        )


def chunk_parts(refs, chunked, chunk, span):
    whole = [(ref, chunk * span) for ref in refs[: len(refs) - chunked]]
    return whole + [(ref, 0) for ref in refs[len(refs) - chunked :]]


def score_kernel(chunk, span, chunked, temp_ref, *refs):
    refs, acc_ref = refs[:-1], refs[-1]
    parts = refs if chunk == 0 else refs[1:]
    acc_ref[...] = jnp.zeros_like(acc_ref) if chunk == 0 else refs[0][...]
    add_products(acc_ref, temp_ref, chunk, chunk_parts(parts, chunked, chunk, span))


def last_score_kernel(wholes, chunked, span, temp_ref, pow_ref, *refs):
    refs = list(refs)
    s_ref, all_ref, marks_ref, stat_ref, acc_ref = refs[-5:]
    whole = refs[:wholes]
    chunks = [refs[wholes + c * chunked : wholes + (c + 1) * chunked] for c in range(CHUNKS)]
    rows, groups = pow_ref.shape
    lanes = s_ref.shape[1]
    poses = s_ref.shape[0] // rows
    freq = span * CHUNKS
    at = 0
    for ref in whole:
        all_ref[at : at + ref.shape[0], :] = ref[:, :freq]
        at += ref.shape[0]
    for k in range(chunked):
        height = chunks[0][k].shape[0]
        for c in range(CHUNKS):
            all_ref[at : at + height, c * span : (c + 1) * span] = chunks[c][k][:, :span]
        at += height
    ids = jnp.concatenate([ref[:, freq:] for ref in whole] + [ref[:, span:] for ref in chunks[0]], axis=0)
    group = lax.broadcasted_iota(jnp.int32, (lanes, groups), 1).astype(f32)
    marks = (ids.astype(f32)[:, :groups] == group).astype(f32)
    marks_ref[...] = marks
    penalty = lax.dot_general(
        pow_ref[...], marks, NT, precision=HIGHEST, preferred_element_type=f32
    )
    acc_ref[...] = refs[wholes + CHUNKS * chunked][...] if CHUNKS > 1 else jnp.zeros_like(acc_ref)
    parts = chunk_parts(whole + chunks[-1], chunked, CHUNKS - 1, span)
    add_products(acc_ref, temp_ref, CHUNKS - 1, parts)
    acc = acc_ref[...].T
    acc = acc + jnp.where(
        even_index(acc.shape, 1), pltpu.roll(acc, lanes - 1, 1), pltpu.roll(acc, 1, 1)
    )
    scores = acc.reshape(poses, rows, lanes) - 0.5 * penalty[None]
    peak = jnp.max(jnp.max(scores, axis=0), axis=0, keepdims=True)
    total = jnp.sum(jnp.sum(jnp.exp(scores - peak[None]), axis=0), axis=0, keepdims=True)
    s_ref[...] = scores.reshape(poses * rows, lanes)
    stat_ref[0:1, :] = peak
    stat_ref[1:2, :] = total
    stat_ref[2:8, :] = jnp.zeros((6, lanes), f32)


def score(temps, power, whole, chunks, freq):
    columns = temps.shape[1]
    span = freq // CHUNKS
    chunked = len(chunks[0])
    lanes = sum(p.shape[0] for p in whole + chunks[0])
    flops = 2 * columns * 256 * 2 * span
    acc = []
    for c in range(CHUNKS - 1):
        operands = [temps, *acc, *whole, *chunks[c]]
        acc = call(
            functools.partial(score_kernel, c, span, chunked),
            f"score{c}",
            [VMEM] * len(operands),
            [jax.ShapeDtypeStruct((lanes, columns), f32)],
            operands,
            flops=flops,
        )
    operands = [temps, power, *whole, *[p for parts in chunks for p in parts], *acc]
    return call(
        functools.partial(last_score_kernel, len(whole), chunked, span),
        f"score{CHUNKS - 1}",
        [VMEM] * len(operands),
        [
            jax.ShapeDtypeStruct((columns, lanes), f32),
            jax.ShapeDtypeStruct((lanes, freq), bf16),
            jax.ShapeDtypeStruct((lanes, power.shape[1]), f32),
            jax.ShapeDtypeStruct((8, lanes), f32),
        ],
        operands,
        [pltpu.VMEM((lanes, columns), f32)],
        flops=flops,
    )


def xor_blocks(values, block, distance):
    lanes = values.shape[1]
    lane = lax.broadcasted_iota(jnp.int32, values.shape, 1)
    width = block
    while distance:
        if distance % 2:
            low = lax.rem(lane // width, 2) == 0
            values = jnp.where(
                low, pltpu.roll(values, lanes - width, 1), pltpu.roll(values, width, 1)
            )
        distance //= 2
        width *= 2
    return values


def rotate_slice(rho_ref, w_ref, cos_ref, sin_ref, base, span, poses, buffers, write):
    rows = rho_ref.shape[1] // poses
    tiles = [(a, min(256, span - a)) for a in range(0, span, 256)]

    def products(i):
        start, width = tiles[i]
        at = pl.ds(pl.multiple_of(base + start, LANES), width)
        weighted = w_ref[:, at]
        buffer = buffers[i % 2]
        buffer[0, :, :width] = jnp.dot(rho_ref[0], weighted, preferred_element_type=f32)
        buffer[1, :, :width] = jnp.dot(rho_ref[1], weighted, preferred_element_type=f32)

    def rotate(i):
        start, width = tiles[i]
        buffer = buffers[i % 2]
        for a in range(0, width, LANES):
            at = pl.ds(pl.multiple_of(base + start + a, LANES), LANES)
            numer_re = jnp.zeros((rows, LANES), f32)
            numer_im = jnp.zeros((rows, LANES), f32)
            for r in range(poses):
                cos_r = cos_ref[r : r + 1, at]
                sin_r = sin_ref[r : r + 1, at]
                s_re = buffer[0, r * rows : (r + 1) * rows, a : a + LANES]
                s_im = buffer[1, r * rows : (r + 1) * rows, a : a + LANES]
                numer_re = numer_re + s_re * cos_r + s_im * sin_r
                numer_im = numer_im + s_im * cos_r - s_re * sin_r
            write(start + a, numer_re, numer_im)

    products(0)
    for i in range(1, len(tiles)):
        products(i)
        rotate(i - 1)
    rotate(len(tiles) - 1)


def write_to(ref, span):
    def write(at, numer_re, numer_im):
        ref[:, at : at + LANES] = numer_re.astype(ref.dtype)
        ref[:, span + at : span + at + LANES] = numer_im.astype(ref.dtype)

    return write


def rho_kernel(poses, block, paired, far, span, me_ref, s_ref, marks_ref, cos_ref, sin_ref, w_ref, *refs):
    stat_refs, refs = refs[: len(paired)], refs[len(paired) :]
    norm_ref, rho_ref, mass_ref = refs[:3]
    out_refs, buffers = refs[3:-2], refs[-2:]
    rows, groups = mass_ref.shape
    lanes = s_ref.shape[1]
    peaks, totals = [], []
    for ref, distance in zip(stat_refs, paired):
        for at in range(0, ref.shape[0], 8):
            stats = xor_blocks(ref[at : at + 8, :], block, distance)
            peaks.append(stats[0:1])
            totals.append(stats[1:2])
    peak = functools.reduce(jnp.maximum, peaks)
    total = sum(t * jnp.exp(p - peak) for t, p in zip(totals, peaks))
    log_norm = peak + jnp.log(total)
    norm_ref[...] = log_norm
    rho = jnp.exp(s_ref[...].reshape(poses, rows, lanes) - log_norm[None])
    even = even_index((rows, lanes), 1)
    mass = lax.dot_general(
        jnp.where(even, jnp.sum(rho, axis=0), 0.0),
        marks_ref[...],
        NN,
        precision=HIGHEST,
        preferred_element_type=f32,
    )
    mass_ref[...] = mass
    high = mass.astype(bf16)
    low = (mass - high.astype(f32)).astype(bf16)
    for ref in out_refs:
        ref[:, 2 * span : 2 * span + groups] = high
        ref[:, 2 * span + groups :] = low
    flat = rho.reshape(poses * rows, lanes)
    even = even_index(flat.shape, 1)
    rho_ref[0] = jnp.where(even, flat, 0.0).astype(bf16)
    rho_ref[1] = jnp.where(even, 0.0, flat).astype(bf16)
    for ref, distance in zip(out_refs, far):
        base = (me_ref[0] ^ distance) * span
        rotate_slice(
            rho_ref, w_ref, cos_ref, sin_ref, base, span, poses, buffers, write_to(ref, span)
        )


def outgoing_slices(me, scores, marks, cos_t, sin_t, weighted, stats, paired, far, block, span):
    poses, lanes = cos_t.shape[0], scores.shape[1]
    rows, groups = scores.shape[0] // poses, marks.shape[1]
    return call(
        functools.partial(rho_kernel, poses, block, paired, far, span),
        "outgoing",
        [SMEM] + [VMEM] * (5 + len(stats)),
        [
            jax.ShapeDtypeStruct((1, lanes), f32),
            jax.ShapeDtypeStruct((2, poses * rows, lanes), bf16),
            jax.ShapeDtypeStruct((rows, groups), f32),
        ]
        + [jax.ShapeDtypeStruct((rows, 2 * span + 2 * groups), bf16)] * len(far),
        (me, scores, marks, cos_t, sin_t, weighted, *stats),
        [pltpu.VMEM((2, poses * rows, 256), f32)] * 2,
        flops=4 * 256 * poses * rows * span * len(far),
    )


def own_kernel(
    poses,
    block,
    span,
    me_ref,
    s_ref,
    norm_ref,
    rho_ref,
    cos_ref,
    sin_ref,
    w_ref,
    ctf_ref,
    nw_ref,
    out_ref,
    cw_ref,
    resp_ref,
    *buffers,
):
    base = me_ref[0] * span
    at = pl.ds(pl.multiple_of(base, LANES), span)
    ctf = ctf_ref[:, at]
    cw_ref[...] = ctf * ctf * nw_ref[:, at]
    rotate_slice(
        rho_ref, w_ref, cos_ref, sin_ref, base, span, poses, buffers, write_to(out_ref, span)
    )
    rows = resp_ref.shape[0]
    lanes = s_ref.shape[1]
    scores = s_ref[...].reshape(poses, rows, lanes)
    pose_peak = jnp.max(scores, axis=0)
    total = jnp.sum(jnp.exp(scores - pose_peak[None]), axis=0)
    log_resp = pose_peak + jnp.log(total) - norm_ref[...]
    shape = (resp_ref.shape[1], lanes)
    lane = lax.broadcasted_iota(jnp.int32, shape, 1)
    row = ((lane // block) ^ me_ref[1]) * (block // 2) + lax.rem(lane, block) // 2
    take = (lax.broadcasted_iota(jnp.int32, shape, 0) == row) & (lax.rem(lane, 2) == 0)
    resp_ref[...] = lax.dot_general(
        log_resp, take.astype(f32), NT, precision=HIGHEST, preferred_element_type=f32
    )


def own_slice(me, scores, norm, rho, cos_t, sin_t, weighted, ctf, noise_weight, block, span):
    poses, lanes = cos_t.shape[0], scores.shape[1]
    rows = scores.shape[0] // poses
    return call(
        functools.partial(own_kernel, poses, block, span),
        "own_slice",
        [SMEM] + [VMEM] * 8,
        [
            jax.ShapeDtypeStruct((rows, 2 * span), f32),
            jax.ShapeDtypeStruct((ctf.shape[0], span), f32),
            jax.ShapeDtypeStruct((rows, lanes // 2), f32),
        ],
        (me, scores, norm, rho, cos_t, sin_t, weighted, ctf, noise_weight),
        [pltpu.VMEM((2, poses * rows, 256), f32)] * 2,
        flops=4 * 256 * poses * rows * span,
    )


def finish_kernel(span, cw_ref, mass_ref, own_ref, *refs):
    received, out_ref = refs[:-1], refs[-1]
    groups = mass_ref.shape[1]
    mass = mass_ref[...]
    for ref in received:
        mass += ref[:, 2 * span : 2 * span + groups].astype(f32)
        mass += ref[:, 2 * span + groups :].astype(f32)
    denom = (
        lax.dot_general(
            mass,
            cw_ref[...],
            NN,
            precision=HIGHEST,
            preferred_element_type=f32,
        )
        + prior_precision
    )
    for part in range(2):
        cut = slice(part * span, (part + 1) * span)
        numer = own_ref[:, cut]
        for ref in received:
            numer += ref[:, cut].astype(f32)
        out_ref[:, part, :] = numer / denom


def finish(weight, mass, own, received, span):
    rows = own.shape[0]
    return call(
        functools.partial(finish_kernel, span),
        "finish",
        [VMEM] * (3 + len(received)),
        [jax.ShapeDtypeStruct((rows, 2, span), f32)],
        (weight, mass, own, *received),
    )[0]


def swap(values, axis, distance):
    size = lax.axis_size(axis)
    return lax.ppermute(values, axis, [(i, i ^ distance) for i in range(size)])


def local(particles, classes, ctf, noise_weight, group_ids, shifts):
    part_rows, _, freq = particles.shape
    n_cls = lax.axis_size("cls")
    n_img = lax.axis_size("img")
    span = freq // n_img
    pairwise = n_cls == 4
    me_cls = lax.axis_index("cls") if pairwise else 0
    me = jnp.stack([lax.axis_index("img"), me_cls]).astype(jnp.int32)

    own, *shards = weigh(particles, ctf, noise_weight, group_ids)
    noise_weight = noise_weight[None, :]
    if pairwise:
        far = [swap(w, "cls", 2) for w in shards]
        near = swap(own, "cls", 1)
    else:
        whole, chunks = [lax.all_gather(own, "cls", axis=0, tiled=True)], [[]] * CHUNKS

    split = jnp.transpose(classes, (1, 0, 2))
    cos_t, sin_t, power = prepare(split, phase_tables(shifts, freq), ctf, noise_weight)
    early = early_templates(split, cos_t, sin_t)
    if pairwise:
        far, split, early = lax.optimization_barrier((far, split, early))
        whole, chunks = [own, near], [[w, swap(w, "cls", 1)] for w in far]
    temps = all_templates(early, split, cos_t, sin_t)
    scores, weighted, marks, stat = score(temps, power, whole, chunks, freq)
    if pairwise:
        stats = [stat] + [swap(stat, "cls", k) for k in range(1, n_cls)]
        paired = tuple(range(n_cls))
    else:
        stats = [lax.all_gather(stat, "cls", axis=0, tiled=True)]
        paired = (0,)

    others = tuple(range(n_img - 1, 0, -1))
    block = 2 * part_rows
    norm, rho, mass, *parts = outgoing_slices(
        me, scores, marks, cos_t, sin_t, weighted, stats, paired, others, block, span
    )
    received = [swap(part, "img", d) for part, d in zip(parts, others)]
    mine, weight, log_resp = own_slice(
        me, scores, norm, rho, cos_t, sin_t, weighted, ctf, noise_weight, block, span
    )
    averages = finish(weight, mass, mine, received, span)
    return (log_resp.T, averages)


def solution(mesh):
    placed = (
        P(("groups", "img", "cls"), None, None),
        P(("groups", "cls"), None, None),
        P("groups", None),
        P("groups"),
        P(("groups", "img", "cls")),
        P("groups", None),
    )
    return jax.shard_map(
        local,
        mesh=mesh,
        in_specs=placed,
        out_specs=(P(("groups", "img"), "cls"), P(("groups", "cls"), None, "img")),
        check_vma=False,
    )
```

```python
import functools

import jax
import jax.numpy as jnp
from jax import lax
from jax.experimental import pallas as pl
from jax.experimental.pallas import tpu as pltpu
from jax.sharding import PartitionSpec as P

BOX = 128
CHUNKS = 2
LANES = 128
VMEM_LIMIT = 24 * 1024 * 1024

prior_precision = 0.02

NT = (((1,), (1,)), ((), ()))
NN = (((1,), (0,)), ((), ()))
HIGHEST = lax.Precision.HIGHEST
f32 = jnp.float32
bf16 = jnp.bfloat16

SMEM = pl.BlockSpec(memory_space=pltpu.SMEM)
VMEM = pl.BlockSpec(memory_space=pltpu.VMEM)
ANY = pl.BlockSpec(memory_space=pl.ANY)


def phase_tables(shifts, freq):
    along_x = (jnp.arange(BOX) - BOX // 2).astype(f32)
    along_y = jnp.arange(freq // BOX).astype(f32)
    step = 2.0 * jnp.pi / BOX
    angle_x = step * (shifts[:, 0:1].astype(f32) * along_x[None, :])
    angle_y = step * (shifts[:, 1:2].astype(f32) * along_y[None, :])
    return (jnp.cos(angle_x), jnp.sin(angle_x), jnp.cos(angle_y), jnp.sin(angle_y))


def call(kernel, name, in_specs, out_shape, operands, scratch=(), flops=0, moved=0, out_specs=None):
    return pl.pallas_call(
        kernel,
        in_specs=in_specs,
        out_specs=[VMEM] * len(out_shape) if out_specs is None else out_specs,
        out_shape=out_shape,
        scratch_shapes=list(scratch),
        compiler_params=pltpu.CompilerParams(vmem_limit_bytes=VMEM_LIMIT),
        cost_estimate=pl.CostEstimate(flops=flops, bytes_accessed=moved, transcendentals=0),
        name=name,
    )(*operands)


def even_index(shape, axis):
    return lax.rem(lax.broadcasted_iota(jnp.int32, shape, axis), 2) == 0


def weigh_kernel(ids_hbm, p_hbm, ctf_hbm, nw_hbm, *refs):
    out_refs, (ids_ref, p_ref, ctf_ref, nw_ref, scale_ref, sem) = refs[:-6], refs[-6:]
    count, _, freq = p_ref.shape
    copies = [
        pltpu.make_async_copy(source, target, sem.at[i])
        for i, (source, target) in enumerate(
            [(ids_hbm, ids_ref), (ctf_hbm, ctf_ref), (nw_hbm, nw_ref), (p_hbm, p_ref)]
        )
    ]
    for copy in copies:
        copy.start()
    copies[0].wait()
    row = lax.broadcasted_iota(jnp.int32, (2 * count, LANES), 0) // 2
    ids = jnp.zeros((2 * count, LANES), f32)
    for n in range(count):
        ids = jnp.where(row == n, ids_ref[n].astype(f32), ids)
    for copy in copies[1:]:
        copy.wait()
    noise = nw_ref[...].reshape(1, freq)
    for n in range(count):
        scale = ctf_ref[pl.ds(ids_ref[n], 1), :] * noise
        scale_ref[2 * n : 2 * n + 2, :] = jnp.broadcast_to(scale, (2, freq))
    values = p_ref[...].astype(f32).reshape(2 * count, freq)
    weighted = (values * scale_ref[...]).astype(bf16)
    chunk = freq // (len(out_refs) - 1)
    for c, out_ref in enumerate(out_refs[1:]):
        out_ref[:, :chunk] = weighted[:, c * chunk : (c + 1) * chunk]
    out_refs[0][:, :freq] = weighted
    for out_ref in out_refs[:2]:
        out_ref[:, out_ref.shape[1] - LANES :] = ids.astype(bf16)


def weigh(particles, ctf, noise_weight, group_ids):
    rows, _, freq = particles.shape
    chunk = freq // CHUNKS
    operands = (group_ids, particles, ctf, noise_weight)
    return call(
        weigh_kernel,
        "weigh",
        [ANY] * 4,
        [jax.ShapeDtypeStruct((2 * rows, freq + LANES), bf16)]
        + [
            jax.ShapeDtypeStruct((2 * rows, chunk + (LANES if c == 0 else 0)), bf16)
            for c in range(CHUNKS)
        ],
        [pltpu.with_memory_space_constraint(x, pltpu.HBM) for x in operands],
        [
            pltpu.SMEM((rows,), jnp.int32),
            pltpu.VMEM(particles.shape, bf16),
            pltpu.VMEM(ctf.shape, f32),
            pltpu.VMEM((freq,), f32),
            pltpu.VMEM((2 * rows, freq), f32),
            pltpu.SemaphoreType.DMA((4,)),
        ],
        flops=4 * rows * freq,
        moved=16 * rows * freq,
    )


def prepare_kernel(
    cls_ref, xc_ref, xs_ref, yc_ref, ys_ref, ctf_ref, nw_ref, cos_ref, sin_ref, pow_ref
):
    freq = cls_ref.shape[2]
    x_cos, x_sin = xc_ref[...], xs_ref[...]
    for t in range(freq // BOX):
        y_cos = jnp.broadcast_to(yc_ref[:, t : t + 1], x_cos.shape)
        y_sin = jnp.broadcast_to(ys_ref[:, t : t + 1], x_cos.shape)
        cos_ref[:, t * BOX : (t + 1) * BOX] = x_cos * y_cos - x_sin * y_sin
        sin_ref[:, t * BOX : (t + 1) * BOX] = x_sin * y_cos + x_cos * y_sin
    cut = freq // 4
    power = jnp.zeros(pow_ref.shape, f32)
    for q in range(4):
        at = slice(q * cut, (q + 1) * cut)
        re = cls_ref[0, :, at].astype(f32)
        im = cls_ref[1, :, at].astype(f32)
        ctf = ctf_ref[:, at]
        power += lax.dot_general(
            re * re + im * im,
            ctf * ctf * nw_ref[:, at],
            NT,
            precision=HIGHEST,
            preferred_element_type=f32,
        )
    pow_ref[...] = power


def prepare(split, tables, ctf, noise_weight):
    _, rows, freq = split.shape
    poses, groups = tables[0].shape[0], ctf.shape[0]
    return call(
        prepare_kernel,
        "prepare",
        [VMEM] * 7,
        [
            jax.ShapeDtypeStruct((poses, freq), f32),
            jax.ShapeDtypeStruct((poses, freq), f32),
            jax.ShapeDtypeStruct((rows, groups), f32),
        ],
        (split, *tables, ctf, noise_weight),
        flops=24 * rows * groups * freq,
    )


def write_templates(cls_ref, cos_ref, sin_ref, temp_ref, start, tile):
    rows = cls_ref.shape[1]
    for a in range(0, tile, LANES):
        at = pl.ds(pl.multiple_of(start + a, LANES), LANES)
        re = cls_ref[0, :, at].astype(f32)
        im = cls_ref[1, :, at].astype(f32)
        for r in range(cos_ref.shape[0]):
            cos_r = cos_ref[r : r + 1, at]
            sin_r = sin_ref[r : r + 1, at]
            here = slice(r * rows, (r + 1) * rows)
            temp_ref[here, a : a + LANES] = (re * cos_r - im * sin_r).astype(bf16)
            temp_ref[here, tile + a : tile + a + LANES] = (re * sin_r + im * cos_r).astype(bf16)


def template_tile(freq):
    return max(t for t in range(LANES, 385, LANES) if freq // CHUNKS % t == 0)


def early_kernel(cls_ref, cos_ref, sin_ref, temp_ref):
    write_templates(cls_ref, cos_ref, sin_ref, temp_ref, 0, cls_ref.shape[2])


def early_templates(split, cos_t, sin_t):
    _, rows, freq = split.shape
    poses = cos_t.shape[0]
    tile = template_tile(freq)
    count = freq // tile // 2
    skip = freq // tile - count
    return pl.pallas_call(
        early_kernel,
        grid=(count,),
        in_specs=[
            pl.BlockSpec((2, rows, tile), lambda j: (0, 0, skip + j)),
            pl.BlockSpec((poses, tile), lambda j: (0, skip + j)),
            pl.BlockSpec((poses, tile), lambda j: (0, skip + j)),
        ],
        out_specs=pl.BlockSpec((None, poses * rows, 2 * tile), lambda j: (j, 0, 0)),
        out_shape=pltpu.HBM((count, poses * rows, 2 * tile), bf16),
        compiler_params=pltpu.CompilerParams(vmem_limit_bytes=VMEM_LIMIT),
        cost_estimate=pl.CostEstimate(
            flops=20 * poses * rows * freq, bytes_accessed=2 * poses * rows * freq, transcendentals=0
        ),
        name="early_templates",
    )(split, cos_t, sin_t)


def template_kernel(early_hbm, cls_ref, cos_ref, sin_ref, temp_ref, sem):
    count = early_hbm.shape[0]
    built = temp_ref.shape[0] - count
    tile = temp_ref.shape[2] // 2
    copies = [
        pltpu.make_async_copy(early_hbm.at[t], temp_ref.at[built + t], sem.at[t])
        for t in range(count)
    ]
    for copy in copies:
        copy.start()

    @pl.loop(0, built)
    def _(t):
        write_templates(cls_ref, cos_ref, sin_ref, temp_ref.at[t], t * tile, tile)

    for copy in copies:
        copy.wait()


def all_templates(early, split, cos_t, sin_t):
    _, rows, freq = split.shape
    poses = cos_t.shape[0]
    count, columns, width = early.shape
    return call(
        template_kernel,
        "templates",
        [ANY] + [VMEM] * 3,
        [pltpu.VMEM((freq // (width // 2), columns, width), bf16)],
        (pltpu.with_memory_space_constraint(early, pltpu.HBM), split, cos_t, sin_t),
        [pltpu.SemaphoreType.DMA((count,))],
        flops=20 * poses * rows * freq,
        moved=2 * poses * rows * freq,
    )[0]


def add_products(acc_ref, temp_ref, chunk, parts):
    count = temp_ref.shape[0] // CHUNKS
    tile = temp_ref.shape[2] // 2
    even = even_index((acc_ref.shape[1], tile), 0)
    for t in range(count):
        wide = jnp.concatenate(
            [ref[:, start + t * tile : start + (t + 1) * tile] for ref, start in parts], axis=0
        ).astype(f32)
        split = jnp.concatenate(
            [jnp.where(even, wide, 0.0).astype(bf16), jnp.where(even, 0.0, wide).astype(bf16)],
            axis=1,
        )
        acc_ref[...] += lax.dot_general(
            temp_ref[chunk * count + t], split, NT, preferred_element_type=f32
        )


def chunk_parts(refs, chunked, chunk, span):
    whole = [(ref, chunk * span) for ref in refs[: len(refs) - chunked]]
    return whole + [(ref, 0) for ref in refs[len(refs) - chunked :]]


def score_kernel(chunk, span, chunked, temp_ref, *refs):
    refs, acc_ref = refs[:-1], refs[-1]
    parts = refs if chunk == 0 else refs[1:]
    acc_ref[...] = jnp.zeros_like(acc_ref) if chunk == 0 else refs[0][...]
    add_products(acc_ref, temp_ref, chunk, chunk_parts(parts, chunked, chunk, span))


def last_score_kernel(wholes, chunked, span, temp_ref, pow_ref, *refs):
    refs = list(refs)
    s_ref, all_ref, marks_ref, stat_ref = refs[-4:]
    whole = refs[:wholes]
    chunks = [refs[wholes + c * chunked : wholes + (c + 1) * chunked] for c in range(CHUNKS)]
    rows, groups = pow_ref.shape
    lanes = s_ref.shape[1]
    poses = s_ref.shape[0] // rows
    freq = span * CHUNKS
    at = 0
    for ref in whole:
        all_ref[at : at + ref.shape[0], :] = ref[:, :freq]
        at += ref.shape[0]
    for k in range(chunked):
        height = chunks[0][k].shape[0]
        for c in range(CHUNKS):
            all_ref[at : at + height, c * span : (c + 1) * span] = chunks[c][k][:, :span]
        at += height
    ids = jnp.concatenate([ref[:, freq:] for ref in whole] + [ref[:, span:] for ref in chunks[0]], axis=0)
    group = lax.broadcasted_iota(jnp.int32, (lanes, groups), 1).astype(f32)
    marks = (ids.astype(f32)[:, :groups] == group).astype(f32)
    marks_ref[...] = marks
    penalty = lax.dot_general(
        pow_ref[...], marks, NT, precision=HIGHEST, preferred_element_type=f32
    )
    s_ref[...] = refs[wholes + CHUNKS * chunked][...] if CHUNKS > 1 else jnp.zeros_like(s_ref)
    parts = chunk_parts(whole + chunks[-1], chunked, CHUNKS - 1, span)
    add_products(s_ref, temp_ref, CHUNKS - 1, parts)
    acc = s_ref[...]
    acc = acc + jnp.where(
        even_index(acc.shape, 1), pltpu.roll(acc, lanes - 1, 1), pltpu.roll(acc, 1, 1)
    )
    scores = acc.reshape(poses, rows, lanes) - 0.5 * penalty[None]
    peak = jnp.max(jnp.max(scores, axis=0), axis=0, keepdims=True)
    total = jnp.sum(jnp.sum(jnp.exp(scores - peak[None]), axis=0), axis=0, keepdims=True)
    s_ref[...] = scores.reshape(poses * rows, lanes)
    stat_ref[0:1, :] = peak
    stat_ref[1:2, :] = total
    stat_ref[2:8, :] = jnp.zeros((6, lanes), f32)


def score(temps, power, whole, chunks, freq):
    columns = temps.shape[1]
    span = freq // CHUNKS
    chunked = len(chunks[0])
    lanes = sum(p.shape[0] for p in whole + chunks[0])
    flops = 2 * columns * 256 * 2 * span
    acc = []
    for c in range(CHUNKS - 1):
        operands = [temps, *acc, *whole, *chunks[c]]
        acc = call(
            functools.partial(score_kernel, c, span, chunked),
            f"score{c}",
            [VMEM] * len(operands),
            [jax.ShapeDtypeStruct((columns, lanes), f32)],
            operands,
            flops=flops,
        )
    operands = [temps, power, *whole, *[p for parts in chunks for p in parts], *acc]
    return call(
        functools.partial(last_score_kernel, len(whole), chunked, span),
        f"score{CHUNKS - 1}",
        [VMEM] * len(operands),
        [
            jax.ShapeDtypeStruct((columns, lanes), f32),
            jax.ShapeDtypeStruct((lanes, freq), bf16),
            jax.ShapeDtypeStruct((lanes, power.shape[1]), f32),
            jax.ShapeDtypeStruct((8, lanes), f32),
        ],
        operands,
        flops=flops,
    )


def xor_blocks(values, block, distance):
    lanes = values.shape[1]
    lane = lax.broadcasted_iota(jnp.int32, values.shape, 1)
    width = block
    while distance:
        if distance % 2:
            low = lax.rem(lane // width, 2) == 0
            values = jnp.where(
                low, pltpu.roll(values, lanes - width, 1), pltpu.roll(values, width, 1)
            )
        distance //= 2
        width *= 2
    return values


def rotate_slice(rho_ref, w_ref, cos_ref, sin_ref, base, span, poses, buffers, write):
    rows = rho_ref.shape[1] // poses
    tiles = [(a, min(256, span - a)) for a in range(0, span, 256)]

    def products(i):
        start, width = tiles[i]
        at = pl.ds(pl.multiple_of(base + start, LANES), width)
        weighted = w_ref[:, at]
        buffer = buffers[i % 2]
        buffer[0, :, :width] = jnp.dot(rho_ref[0], weighted, preferred_element_type=f32)
        buffer[1, :, :width] = jnp.dot(rho_ref[1], weighted, preferred_element_type=f32)

    def rotate(i):
        start, width = tiles[i]
        buffer = buffers[i % 2]
        for a in range(0, width, LANES):
            at = pl.ds(pl.multiple_of(base + start + a, LANES), LANES)
            numer_re = jnp.zeros((rows, LANES), f32)
            numer_im = jnp.zeros((rows, LANES), f32)
            for r in range(poses):
                cos_r = cos_ref[r : r + 1, at]
                sin_r = sin_ref[r : r + 1, at]
                s_re = buffer[0, r * rows : (r + 1) * rows, a : a + LANES]
                s_im = buffer[1, r * rows : (r + 1) * rows, a : a + LANES]
                numer_re = numer_re + s_re * cos_r + s_im * sin_r
                numer_im = numer_im + s_im * cos_r - s_re * sin_r
            write(start + a, numer_re, numer_im)

    products(0)
    for i in range(1, len(tiles)):
        products(i)
        rotate(i - 1)
    rotate(len(tiles) - 1)


def write_to(ref, span):
    def write(at, numer_re, numer_im):
        ref[:, at : at + LANES] = numer_re.astype(ref.dtype)
        ref[:, span + at : span + at + LANES] = numer_im.astype(ref.dtype)

    return write


def rho_kernel(poses, block, paired, far, span, me_ref, s_ref, marks_ref, cos_ref, sin_ref, w_ref, *refs):
    stat_refs, refs = refs[: len(paired)], refs[len(paired) :]
    norm_ref, rho_ref, mass_ref = refs[:3]
    out_refs, buffers = refs[3:-2], refs[-2:]
    rows, groups = mass_ref.shape
    lanes = s_ref.shape[1]
    peaks, totals = [], []
    for ref, distance in zip(stat_refs, paired):
        for at in range(0, ref.shape[0], 8):
            stats = xor_blocks(ref[at : at + 8, :], block, distance)
            peaks.append(stats[0:1])
            totals.append(stats[1:2])
    peak = functools.reduce(jnp.maximum, peaks)
    total = sum(t * jnp.exp(p - peak) for t, p in zip(totals, peaks))
    log_norm = peak + jnp.log(total)
    norm_ref[...] = log_norm
    rho = jnp.exp(s_ref[...].reshape(poses, rows, lanes) - log_norm[None])
    even = even_index((rows, lanes), 1)
    mass = lax.dot_general(
        jnp.where(even, jnp.sum(rho, axis=0), 0.0),
        marks_ref[...],
        NN,
        precision=HIGHEST,
        preferred_element_type=f32,
    )
    mass_ref[...] = mass
    high = mass.astype(bf16)
    low = (mass - high.astype(f32)).astype(bf16)
    for ref in out_refs:
        ref[:, 2 * span : 2 * span + groups] = high
        ref[:, 2 * span + groups :] = low
    flat = rho.reshape(poses * rows, lanes)
    even = even_index(flat.shape, 1)
    rho_ref[0] = jnp.where(even, flat, 0.0).astype(bf16)
    rho_ref[1] = jnp.where(even, 0.0, flat).astype(bf16)
    for ref, distance in zip(out_refs, far):
        base = (me_ref[0] ^ distance) * span
        rotate_slice(
            rho_ref, w_ref, cos_ref, sin_ref, base, span, poses, buffers, write_to(ref, span)
        )


def outgoing_slices(me, scores, marks, cos_t, sin_t, weighted, stats, paired, far, block, span):
    poses, lanes = cos_t.shape[0], scores.shape[1]
    rows, groups = scores.shape[0] // poses, marks.shape[1]
    return call(
        functools.partial(rho_kernel, poses, block, paired, far, span),
        "outgoing",
        [SMEM] + [VMEM] * (5 + len(stats)),
        [
            jax.ShapeDtypeStruct((1, lanes), f32),
            jax.ShapeDtypeStruct((2, poses * rows, lanes), bf16),
            jax.ShapeDtypeStruct((rows, groups), f32),
        ]
        + [jax.ShapeDtypeStruct((rows, 2 * span + 2 * groups), bf16)] * len(far),
        (me, scores, marks, cos_t, sin_t, weighted, *stats),
        [pltpu.VMEM((2, poses * rows, 256), f32)] * 2,
        flops=4 * 256 * poses * rows * span * len(far),
    )


def own_kernel(
    poses,
    block,
    span,
    me_ref,
    s_ref,
    norm_ref,
    rho_ref,
    cos_ref,
    sin_ref,
    w_ref,
    ctf_ref,
    nw_ref,
    out_ref,
    cw_ref,
    resp_ref,
    *buffers,
):
    base = me_ref[0] * span
    at = pl.ds(pl.multiple_of(base, LANES), span)
    ctf = ctf_ref[:, at]
    cw_ref[...] = ctf * ctf * nw_ref[:, at]
    rotate_slice(
        rho_ref, w_ref, cos_ref, sin_ref, base, span, poses, buffers, write_to(out_ref, span)
    )
    rows = resp_ref.shape[0]
    lanes = s_ref.shape[1]
    scores = s_ref[...].reshape(poses, rows, lanes)
    pose_peak = jnp.max(scores, axis=0)
    total = jnp.sum(jnp.exp(scores - pose_peak[None]), axis=0)
    log_resp = pose_peak + jnp.log(total) - norm_ref[...]
    shape = (resp_ref.shape[1], lanes)
    lane = lax.broadcasted_iota(jnp.int32, shape, 1)
    row = ((lane // block) ^ me_ref[1]) * (block // 2) + lax.rem(lane, block) // 2
    take = (lax.broadcasted_iota(jnp.int32, shape, 0) == row) & (lax.rem(lane, 2) == 0)
    resp_ref[...] = lax.dot_general(
        log_resp, take.astype(f32), NT, precision=HIGHEST, preferred_element_type=f32
    )


def own_slice(me, scores, norm, rho, cos_t, sin_t, weighted, ctf, noise_weight, block, span):
    poses, lanes = cos_t.shape[0], scores.shape[1]
    rows = scores.shape[0] // poses
    return call(
        functools.partial(own_kernel, poses, block, span),
        "own_slice",
        [SMEM] + [VMEM] * 8,
        [
            jax.ShapeDtypeStruct((rows, 2 * span), f32),
            jax.ShapeDtypeStruct((ctf.shape[0], span), f32),
            jax.ShapeDtypeStruct((rows, lanes // 2), f32),
        ],
        (me, scores, norm, rho, cos_t, sin_t, weighted, ctf, noise_weight),
        [pltpu.VMEM((2, poses * rows, 256), f32)] * 2,
        flops=4 * 256 * poses * rows * span,
    )


def finish_kernel(span, cw_ref, mass_ref, own_ref, *refs):
    received, out_ref = refs[:-1], refs[-1]
    groups = mass_ref.shape[1]
    mass = mass_ref[...]
    for ref in received:
        mass += ref[:, 2 * span : 2 * span + groups].astype(f32)
        mass += ref[:, 2 * span + groups :].astype(f32)
    denom = (
        lax.dot_general(
            mass,
            cw_ref[...],
            NN,
            precision=HIGHEST,
            preferred_element_type=f32,
        )
        + prior_precision
    )
    for part in range(2):
        cut = slice(part * span, (part + 1) * span)
        numer = own_ref[:, cut]
        for ref in received:
            numer += ref[:, cut].astype(f32)
        out_ref[:, part, :] = numer / denom


def finish(weight, mass, own, received, span):
    rows = own.shape[0]
    return call(
        functools.partial(finish_kernel, span),
        "finish",
        [VMEM] * (3 + len(received)),
        [jax.ShapeDtypeStruct((rows, 2, span), f32)],
        (weight, mass, own, *received),
    )[0]


def swap(values, axis, distance):
    size = lax.axis_size(axis)
    return lax.ppermute(values, axis, [(i, i ^ distance) for i in range(size)])


def local(particles, classes, ctf, noise_weight, group_ids, shifts):
    part_rows, _, freq = particles.shape
    n_cls = lax.axis_size("cls")
    n_img = lax.axis_size("img")
    span = freq // n_img
    pairwise = n_cls == 4
    me_cls = lax.axis_index("cls") if pairwise else 0
    me = jnp.stack([lax.axis_index("img"), me_cls]).astype(jnp.int32)

    own, *shards = weigh(particles, ctf, noise_weight, group_ids)
    noise_weight = noise_weight[None, :]
    if pairwise:
        far = [swap(w, "cls", 2) for w in shards]
        near = swap(own, "cls", 1)
    else:
        whole, chunks = [lax.all_gather(own, "cls", axis=0, tiled=True)], [[]] * CHUNKS

    split = jnp.transpose(classes, (1, 0, 2))
    cos_t, sin_t, power = prepare(split, phase_tables(shifts, freq), ctf, noise_weight)
    early = early_templates(split, cos_t, sin_t)
    if pairwise:
        far, split, early = lax.optimization_barrier((far, split, early))
        whole, chunks = [own, near], [[w, swap(w, "cls", 1)] for w in far]
    temps = all_templates(early, split, cos_t, sin_t)
    scores, weighted, marks, stat = score(temps, power, whole, chunks, freq)
    if pairwise:
        stats = [stat] + [swap(stat, "cls", k) for k in range(1, n_cls)]
        paired = tuple(range(n_cls))
    else:
        stats = [lax.all_gather(stat, "cls", axis=0, tiled=True)]
        paired = (0,)

    others = tuple(range(n_img - 1, 0, -1))
    block = 2 * part_rows
    norm, rho, mass, *parts = outgoing_slices(
        me, scores, marks, cos_t, sin_t, weighted, stats, paired, others, block, span
    )
    received = [swap(part, "img", d) for part, d in zip(parts[:-1], others[:-1])]
    mine, weight, log_resp = own_slice(
        me, scores, norm, rho, cos_t, sin_t, weighted, ctf, noise_weight, block, span
    )
    last, mine = lax.optimization_barrier((parts[-1], mine))
    received.append(swap(last, "img", others[-1]))
    averages = finish(weight, mass, mine, received, span)
    return (log_resp.T, averages)


def solution(mesh):
    placed = (
        P(("groups", "img", "cls"), None, None),
        P(("groups", "cls"), None, None),
        P("groups", None),
        P("groups"),
        P(("groups", "img", "cls")),
        P("groups", None),
    )
    return jax.shard_map(
        local,
        mesh=mesh,
        in_specs=placed,
        out_specs=(P(("groups", "img"), "cls"), P(("groups", "cls"), None, "img")),
        check_vma=False,
    )
```

```python
import functools

import jax
import jax.numpy as jnp
from jax import lax
from jax.experimental import pallas as pl
from jax.experimental.pallas import tpu as pltpu
from jax.sharding import PartitionSpec as P

BOX = 128
LANES = 128
VMEM_LIMIT = 24 * 1024 * 1024

prior_precision = 0.02

NT = (((1,), (1,)), ((), ()))
NN = (((1,), (0,)), ((), ()))
HIGHEST = lax.Precision.HIGHEST
f32 = jnp.float32
bf16 = jnp.bfloat16

SMEM = pl.BlockSpec(memory_space=pltpu.SMEM)
VMEM = pl.BlockSpec(memory_space=pltpu.VMEM)
ANY = pl.BlockSpec(memory_space=pl.ANY)


def phase_tables(shifts, freq):
    along_x = (jnp.arange(BOX) - BOX // 2).astype(f32)
    along_y = jnp.arange(freq // BOX).astype(f32)
    step = 2.0 * jnp.pi / BOX
    angle_x = step * (shifts[:, 0:1].astype(f32) * along_x[None, :])
    angle_y = step * (shifts[:, 1:2].astype(f32) * along_y[None, :])
    return (jnp.cos(angle_x), jnp.sin(angle_x), jnp.cos(angle_y), jnp.sin(angle_y))


def call(kernel, name, in_specs, out_shape, operands, scratch=(), flops=0, moved=0, limit=VMEM_LIMIT):
    return pl.pallas_call(
        kernel,
        in_specs=in_specs,
        out_specs=[VMEM] * len(out_shape),
        out_shape=out_shape,
        scratch_shapes=list(scratch),
        compiler_params=pltpu.CompilerParams(vmem_limit_bytes=limit),
        cost_estimate=pl.CostEstimate(flops=flops, bytes_accessed=moved, transcendentals=0),
        name=name,
    )(*operands)


def real_index(shape, axis, half):
    return lax.rem(lax.broadcasted_iota(jnp.int32, shape, axis) // half, 2) == 0


def weigh_kernel(
    ids_hbm, p_hbm, ctf_hbm, nw_hbm, out_ref, ids_ref, p_ref, ctf_ref, nw_ref, scale_ref, sem
):
    count, _, freq = p_ref.shape
    copies = [
        pltpu.make_async_copy(source, target, sem.at[i])
        for i, (source, target) in enumerate(
            [(ids_hbm, ids_ref), (ctf_hbm, ctf_ref), (nw_hbm, nw_ref), (p_hbm, p_ref)]
        )
    ]
    for copy in copies:
        copy.start()
    copies[0].wait()
    row = lax.rem(lax.broadcasted_iota(jnp.int32, (2 * count, LANES), 0), count)
    ids = jnp.zeros((2 * count, LANES), f32)
    for n in range(count):
        ids = jnp.where(row == n, ids_ref[n].astype(f32), ids)
    for copy in copies[1:]:
        copy.wait()
    noise = nw_ref[...].reshape(1, freq)
    for n in range(count):
        scale_ref[n : n + 1, :] = ctf_ref[pl.ds(ids_ref[n], 1), :] * noise
    scale = scale_ref[...]
    values = p_ref[...].astype(f32)
    out_ref[:count, :freq] = (values[:, 0, :] * scale).astype(bf16)
    out_ref[count:, :freq] = (values[:, 1, :] * scale).astype(bf16)
    out_ref[:, freq:] = ids.astype(bf16)


def weigh(particles, ctf, noise_weight, group_ids):
    rows, _, freq = particles.shape
    operands = (group_ids, particles, ctf, noise_weight)
    return call(
        weigh_kernel,
        "weigh",
        [ANY] * 4,
        [jax.ShapeDtypeStruct((2 * rows, freq + LANES), bf16)],
        [pltpu.with_memory_space_constraint(x, pltpu.HBM) for x in operands],
        [
            pltpu.SMEM((rows,), jnp.int32),
            pltpu.VMEM(particles.shape, bf16),
            pltpu.VMEM(ctf.shape, f32),
            pltpu.VMEM((freq,), f32),
            pltpu.VMEM((rows, freq), f32),
            pltpu.SemaphoreType.DMA((4,)),
        ],
        flops=4 * rows * freq,
        moved=16 * rows * freq,
    )[0]


def prepare_kernel(
    cls_ref, xc_ref, xs_ref, yc_ref, ys_ref, ctf_ref, nw_ref, cos_ref, sin_ref, pow_ref
):
    freq = cls_ref.shape[2]
    x_cos, x_sin = xc_ref[...], xs_ref[...]
    for t in range(freq // BOX):
        y_cos = jnp.broadcast_to(yc_ref[:, t : t + 1], x_cos.shape)
        y_sin = jnp.broadcast_to(ys_ref[:, t : t + 1], x_cos.shape)
        cos_ref[:, t * BOX : (t + 1) * BOX] = x_cos * y_cos - x_sin * y_sin
        sin_ref[:, t * BOX : (t + 1) * BOX] = x_sin * y_cos + x_cos * y_sin
    cut = freq // 4
    power = jnp.zeros(pow_ref.shape, f32)
    for q in range(4):
        at = slice(q * cut, (q + 1) * cut)
        re = cls_ref[0, :, at].astype(f32)
        im = cls_ref[1, :, at].astype(f32)
        ctf = ctf_ref[:, at]
        power += lax.dot_general(
            re * re + im * im,
            ctf * ctf * nw_ref[:, at],
            NT,
            precision=HIGHEST,
            preferred_element_type=f32,
        )
    pow_ref[...] = power


def prepare(split, tables, ctf, noise_weight):
    _, rows, freq = split.shape
    poses, groups = tables[0].shape[0], ctf.shape[0]
    return call(
        prepare_kernel,
        "prepare",
        [VMEM] * 7,
        [
            jax.ShapeDtypeStruct((poses, freq), f32),
            jax.ShapeDtypeStruct((poses, freq), f32),
            jax.ShapeDtypeStruct((rows, groups), f32),
        ],
        (split, *tables, ctf, noise_weight),
        flops=24 * rows * groups * freq,
    )


def write_templates(cls_ref, cos_ref, sin_ref, temp_ref, start, tile):
    rows = cls_ref.shape[1]
    for a in range(0, tile, LANES):
        at = pl.ds(pl.multiple_of(start + a, LANES), LANES)
        re = cls_ref[0, :, at].astype(f32)
        im = cls_ref[1, :, at].astype(f32)
        for r in range(cos_ref.shape[0]):
            cos_r = cos_ref[r : r + 1, at]
            sin_r = sin_ref[r : r + 1, at]
            here = slice(r * rows, (r + 1) * rows)
            temp_ref[here, a : a + LANES] = (re * cos_r - im * sin_r).astype(bf16)
            temp_ref[here, tile + a : tile + a + LANES] = (re * sin_r + im * cos_r).astype(bf16)


def template_tile(freq):
    return max(t for t in range(LANES, 385, LANES) if freq % t == 0)


def early_kernel(cls_ref, cos_ref, sin_ref, temp_ref):
    write_templates(cls_ref, cos_ref, sin_ref, temp_ref, 0, cls_ref.shape[2])


def early_templates(split, cos_t, sin_t):
    _, rows, freq = split.shape
    poses = cos_t.shape[0]
    tile = template_tile(freq)
    count = freq // tile // 2
    skip = freq // tile - count
    return pl.pallas_call(
        early_kernel,
        grid=(count,),
        in_specs=[
            pl.BlockSpec((2, rows, tile), lambda j: (0, 0, skip + j)),
            pl.BlockSpec((poses, tile), lambda j: (0, skip + j)),
            pl.BlockSpec((poses, tile), lambda j: (0, skip + j)),
        ],
        out_specs=pl.BlockSpec((None, poses * rows, 2 * tile), lambda j: (j, 0, 0)),
        out_shape=pltpu.HBM((count, poses * rows, 2 * tile), bf16),
        compiler_params=pltpu.CompilerParams(vmem_limit_bytes=VMEM_LIMIT),
        cost_estimate=pl.CostEstimate(
            flops=20 * poses * rows * freq, bytes_accessed=2 * poses * rows * freq, transcendentals=0
        ),
        name="early_templates",
    )(split, cos_t, sin_t)


def template_kernel(early_hbm, cls_ref, cos_ref, sin_ref, temp_ref, sem):
    count = early_hbm.shape[0]
    built = temp_ref.shape[0] - count
    tile = temp_ref.shape[2] // 2
    copies = [
        pltpu.make_async_copy(early_hbm.at[t], temp_ref.at[built + t], sem.at[t])
        for t in range(count)
    ]
    for copy in copies:
        copy.start()

    @pl.loop(0, built)
    def _(t):
        write_templates(cls_ref, cos_ref, sin_ref, temp_ref.at[t], t * tile, tile)

    for copy in copies:
        copy.wait()


def all_templates(early, split, cos_t, sin_t):
    _, rows, freq = split.shape
    poses = cos_t.shape[0]
    count, columns, width = early.shape
    return call(
        template_kernel,
        "templates",
        [ANY] + [VMEM] * 3,
        [pltpu.VMEM((freq // (width // 2), columns, width), bf16)],
        (pltpu.with_memory_space_constraint(early, pltpu.HBM), split, cos_t, sin_t),
        [pltpu.SemaphoreType.DMA((count,))],
        flops=20 * poses * rows * freq,
        moved=2 * poses * rows * freq,
    )[0]


def score_kernel(half, temp_ref, pow_ref, *refs):
    shards, (s_ref, marks_ref, stat_ref) = refs[:-3], refs[-3:]
    rows, groups = pow_ref.shape
    lanes = s_ref.shape[1]
    poses = s_ref.shape[0] // rows
    count = temp_ref.shape[0]
    tile = temp_ref.shape[2] // 2
    ids = jnp.concatenate([ref[:, count * tile :] for ref in shards], axis=0).astype(f32)
    group = lax.broadcasted_iota(jnp.int32, (lanes, groups), 1).astype(f32)
    marks = (ids[:, :groups] == group).astype(f32)
    marks_ref[...] = marks
    penalty = lax.dot_general(
        pow_ref[...], marks, NT, precision=HIGHEST, preferred_element_type=f32
    )
    s_ref[...] = jnp.zeros_like(s_ref)
    real = real_index((lanes, tile), 0, half)
    for t in range(count):
        at = slice(t * tile, (t + 1) * tile)
        wide = jnp.concatenate([ref[:, at] for ref in shards], axis=0).astype(f32)
        split = jnp.concatenate(
            [jnp.where(real, wide, 0.0).astype(bf16), jnp.where(real, 0.0, wide).astype(bf16)],
            axis=1,
        )
        s_ref[...] += lax.dot_general(temp_ref[t], split, NT, preferred_element_type=f32)
    acc = s_ref[...]
    acc = acc + jnp.where(
        real_index(acc.shape, 1, half), pltpu.roll(acc, lanes - half, 1), pltpu.roll(acc, half, 1)
    )
    scores = acc.reshape(poses, rows, lanes) - 0.5 * penalty[None]
    peak = jnp.max(jnp.max(scores, axis=0), axis=0, keepdims=True)
    total = jnp.sum(jnp.sum(jnp.exp(scores - peak[None]), axis=0), axis=0, keepdims=True)
    s_ref[...] = scores.reshape(poses * rows, lanes)
    stat_ref[0:1, :] = peak
    stat_ref[1:2, :] = total
    stat_ref[2:8, :] = jnp.zeros((6, lanes), f32)


def score(temps, power, shards, half):
    count, columns, width = temps.shape
    lanes = sum(p.shape[0] for p in shards)
    operands = [temps, power, *shards]
    return call(
        functools.partial(score_kernel, half),
        "score",
        [VMEM] * len(operands),
        [
            jax.ShapeDtypeStruct((columns, lanes), f32),
            jax.ShapeDtypeStruct((lanes, power.shape[1]), f32),
            jax.ShapeDtypeStruct((8, lanes), f32),
        ],
        operands,
        flops=2 * columns * 256 * count * width,
    )


def slices_kernel(targets, me_ref, *refs):
    shards, out_refs = refs[: -len(targets)], refs[-len(targets) :]
    span = out_refs[0].shape[1]
    at = 0
    for ref in shards:
        for out_ref, distance in zip(out_refs, targets):
            base = pl.multiple_of((me_ref[0] ^ distance) * span, LANES)
            out_ref[at : at + ref.shape[0], :] = ref[:, pl.ds(base, span)]
        at += ref.shape[0]


def cut_slices(me, shards, targets, span):
    height = sum(ref.shape[0] for ref in shards)
    return call(
        functools.partial(slices_kernel, targets),
        "cut_slices",
        [SMEM] + [VMEM] * len(shards),
        [jax.ShapeDtypeStruct((height, span), bf16)] * len(targets),
        (me, *shards),
        moved=4 * height * span * len(targets),
        limit=VMEM_LIMIT if height <= 128 else 2 * VMEM_LIMIT,
    )


def bundle_kernel(*refs):
    sources, out_ref = refs[:-1], refs[-1]
    rows = sources[0].shape[0] // 2
    for i, ref in enumerate(sources):
        out_ref[i * rows : (i + 1) * rows, :] = ref[rows:, :]


def bundle(slices):
    rows, span = slices[0].shape
    return call(
        bundle_kernel,
        "bundle",
        [VMEM] * len(slices),
        [jax.ShapeDtypeStruct((len(slices) * rows // 2, span), bf16)],
        slices,
        moved=2 * len(slices) * rows * span,
    )[0]


def xor_blocks(values, block, distance):
    lanes = values.shape[1]
    lane = lax.broadcasted_iota(jnp.int32, values.shape, 1)
    width = block
    while distance:
        if distance % 2:
            low = lax.rem(lane // width, 2) == 0
            values = jnp.where(
                low, pltpu.roll(values, lanes - width, 1), pltpu.roll(values, width, 1)
            )
        distance //= 2
        width *= 2
    return values


def rho_kernel(poses, half, paired, s_ref, marks_ref, *refs):
    stat_refs, (norm_ref, out_ref) = refs[: len(paired)], refs[len(paired) :]
    lanes = s_ref.shape[1]
    rows = s_ref.shape[0] // poses
    groups = marks_ref.shape[1]
    block = 2 * half
    peaks, totals = [], []
    for ref, distance in zip(stat_refs, paired):
        for at in range(0, ref.shape[0], 8):
            stats = xor_blocks(ref[at : at + 8, :], block, distance)
            peaks.append(stats[0:1])
            totals.append(stats[1:2])
    peak = functools.reduce(jnp.maximum, peaks)
    total = sum(t * jnp.exp(p - peak) for t, p in zip(totals, peaks))
    log_norm = peak + jnp.log(total)
    norm_ref[...] = log_norm
    rho = jnp.exp(s_ref[...].reshape(poses, rows, lanes) - log_norm[None])
    mass = lax.dot_general(
        jnp.where(real_index((rows, lanes), 1, half), jnp.sum(rho, axis=0), 0.0),
        marks_ref[...],
        NN,
        precision=HIGHEST,
        preferred_element_type=f32,
    )
    high = mass.astype(bf16)
    low = (mass - high.astype(f32)).astype(bf16)
    rho_low = rho.reshape(poses * rows, lanes).astype(bf16)
    cut = poses // 2 * rows
    lane = lax.broadcasted_iota(jnp.int32, (lanes, lanes), 0)
    column = lax.broadcasted_iota(jnp.int32, (lanes, lanes), 1)
    particle = lane // block * half + lax.rem(lane, block)
    real = lax.rem(lane, block) < half
    first = (real & (column == particle)).astype(f32).astype(bf16)
    second = (real & (column == particle + lanes // 2)).astype(f32).astype(bf16)
    packed = jnp.dot(rho_low[:cut], first, preferred_element_type=f32)
    packed += jnp.dot(rho_low[cut:], second, preferred_element_type=f32)
    out_ref[:cut, :] = packed.astype(bf16)
    if lanes > 2 * groups:
        out_ref[cut:, :] = jnp.zeros((rows, lanes), bf16)
    out_ref[cut:, :groups] = high
    out_ref[cut:, groups : 2 * groups] = low


def responsibilities(scores, marks, stats, paired, poses, half):
    columns, lanes = scores.shape
    return call(
        functools.partial(rho_kernel, poses, half, paired),
        "responsibilities",
        [VMEM] * (2 + len(stats)),
        [
            jax.ShapeDtypeStruct((1, lanes), f32),
            jax.ShapeDtypeStruct((columns // 2 + columns // poses, lanes), bf16),
        ],
        (scores, marks, *stats),
        flops=40 * columns * lanes,
    )


def gather_kernel(poses, half, sources, bundled, me_ref, s_ref, norm_ref, ctf_ref, nw_ref, *refs):
    w_refs, (resp_ref, cw_ref, rows_ref) = refs[:-3], refs[-3:]
    last, w_refs = w_refs[: 2 * bundled], w_refs[2 * bundled :]
    span = rows_ref.shape[2]
    block = 2 * half
    here = pl.ds(pl.multiple_of(me_ref[0] * span, LANES), span)
    at = 0

    def put(real, imag):
        rows_ref[0, at : at + half, :] = real
        rows_ref[1, at : at + half, :] = imag
        return at + half

    for i in range(sources):
        for ref in w_refs[i::sources]:
            for start in range(0, ref.shape[0], block):
                at = put(ref[start : start + half, :], ref[start + half : start + block, :])
        if bundled and i == 0:
            at = put(last[0][:half, here], last[0][half:, here])
        elif bundled:
            start = (i - 1) * block
            at = put(last[1][start : start + half, :], last[1][start + half : start + block, :])
    ctf = ctf_ref[:, here]
    cw_ref[...] = ctf * ctf * nw_ref[:, here]
    rows = resp_ref.shape[0]
    lanes = s_ref.shape[1]
    scores = s_ref[...].reshape(poses, rows, lanes)
    pose_peak = jnp.max(scores, axis=0)
    total = jnp.sum(jnp.exp(scores - pose_peak[None]), axis=0)
    log_resp = pose_peak + jnp.log(total) - norm_ref[...]
    shape = (resp_ref.shape[1], lanes)
    lane = lax.broadcasted_iota(jnp.int32, shape, 1)
    row = ((lane // block) ^ me_ref[1]) * half + lax.rem(lane, block)
    take = (lax.broadcasted_iota(jnp.int32, shape, 0) == row) & (lax.rem(lane, block) < half)
    resp_ref[...] = lax.dot_general(
        log_resp, take.astype(f32), NT, precision=HIGHEST, preferred_element_type=f32
    )


def gather_rows(me, scores, norm, ctf, noise_weight, slices, last, sources, poses, half, span):
    columns, lanes = scores.shape
    particles = sources * lanes // 2
    return call(
        functools.partial(gather_kernel, poses, half, sources, len(last) // 2),
        "gather_rows",
        [SMEM] + [VMEM] * (4 + len(last) + len(slices)),
        [
            jax.ShapeDtypeStruct((columns // poses, lanes // 2), f32),
            jax.ShapeDtypeStruct((ctf.shape[0], span), f32),
            jax.ShapeDtypeStruct((2, particles, span), bf16),
        ],
        (me, scores, norm, ctf, noise_weight, *last, *slices),
        flops=40 * columns * lanes,
        moved=8 * particles * span,
        limit=VMEM_LIMIT if particles <= 512 else 2 * VMEM_LIMIT,
    )


def finish_kernel(poses, groups, sources, me_ref, cw_ref, cos_ref, sin_ref, rows_ref, *refs):
    payloads, (out_ref, rho_ref, denom_ref, *buffers) = refs[:sources], refs[sources:]
    rows, _, span = out_ref.shape
    cut = poses // 2 * rows
    count = payloads[0].shape[1] // 2
    mass = jnp.zeros((rows, groups), f32)
    for i, ref in enumerate(payloads):
        rho_ref[:cut, i * count : (i + 1) * count] = ref[:cut, :count]
        rho_ref[cut:, i * count : (i + 1) * count] = ref[:cut, count:]
        mass += ref[cut:, :groups].astype(f32) + ref[cut:, groups : 2 * groups].astype(f32)
    denom_ref[...] = (
        lax.dot_general(mass, cw_ref[...], NN, precision=HIGHEST, preferred_element_type=f32)
        + prior_precision
    )
    tiles = [(a, min(256, span - a)) for a in range(0, span, 256)]

    def products(i):
        start, width = tiles[i]
        for part in range(2):
            buffers[i % 2][part, :, :width] = jnp.dot(
                rho_ref[...],
                rows_ref[part, :, start : start + width],
                preferred_element_type=f32,
            )

    def rotate(i):
        start, width = tiles[i]
        buffer = buffers[i % 2]
        for a in range(0, width, LANES):
            at = pl.ds(pl.multiple_of(me_ref[0] * span + start + a, LANES), LANES)
            numer_re = jnp.zeros((rows, LANES), f32)
            numer_im = jnp.zeros((rows, LANES), f32)
            for r in range(poses):
                cos_r = cos_ref[r : r + 1, at]
                sin_r = sin_ref[r : r + 1, at]
                s_re = buffer[0, r * rows : (r + 1) * rows, a : a + LANES]
                s_im = buffer[1, r * rows : (r + 1) * rows, a : a + LANES]
                numer_re = numer_re + s_re * cos_r + s_im * sin_r
                numer_im = numer_im + s_im * cos_r - s_re * sin_r
            here = slice(start + a, start + a + LANES)
            denom = denom_ref[:, here]
            out_ref[:, 0, here] = numer_re / denom
            out_ref[:, 1, here] = numer_im / denom

    products(0)
    for i in range(1, len(tiles)):
        products(i)
        rotate(i - 1)
    rotate(len(tiles) - 1)


def finish(me, weight, cos_t, sin_t, rows, payloads, cls_rows):
    poses = cos_t.shape[0]
    _, particles, span = rows.shape
    return call(
        functools.partial(finish_kernel, poses, weight.shape[0], len(payloads)),
        "finish",
        [SMEM] + [VMEM] * (4 + len(payloads)),
        [jax.ShapeDtypeStruct((cls_rows, 2, span), f32)],
        (me, weight, cos_t, sin_t, rows, *payloads),
        [
            pltpu.VMEM((poses * cls_rows, particles), bf16),
            pltpu.VMEM((cls_rows, span), f32),
            pltpu.VMEM((2, poses * cls_rows, 256), f32),
            pltpu.VMEM((2, poses * cls_rows, 256), f32),
        ],
        flops=4 * poses * cls_rows * particles * span,
        limit=VMEM_LIMIT if particles <= 512 else 2 * VMEM_LIMIT,
    )[0]


def swap(values, axis, distance):
    size = lax.axis_size(axis)
    return lax.ppermute(values, axis, [(i, i ^ distance) for i in range(size)])


def local(particles, classes, ctf, noise_weight, group_ids, shifts):
    half, _, freq = particles.shape
    cls_rows = classes.shape[0]
    poses = shifts.shape[0]
    n_cls = lax.axis_size("cls")
    n_img = lax.axis_size("img")
    span = freq // n_img
    pairwise = n_cls == 4
    me_cls = lax.axis_index("cls") if pairwise else 0
    me = jnp.stack([lax.axis_index("img"), me_cls]).astype(jnp.int32)
    others = tuple(range(n_img - 1, 0, -1))
    targets = (0,) + others

    def share(*shards):
        mine, *outgoing = cut_slices(me, shards, targets, span)
        return [mine] + [swap(w, "img", d) for w, d in zip(outgoing, others)]

    own = weigh(particles, ctf, noise_weight, group_ids)
    noise_weight = noise_weight[None, :]
    if pairwise:
        far, near = swap(own, "cls", 2), swap(own, "cls", 1)
        slices = share(own)
    else:
        shards = [lax.all_gather(own, "cls", axis=0, tiled=True)]
        slices = share(*shards)

    split = jnp.transpose(classes, (1, 0, 2))
    cos_t, sin_t, power = prepare(split, phase_tables(shifts, freq), ctf, noise_weight)
    early = early_templates(split, cos_t, sin_t)
    if pairwise:
        far, split, early, slices = lax.optimization_barrier((far, split, early, slices))
        third = swap(far, "cls", 1)
        slices += share(near, far)
        shards = [own, near, far, third]
    temps = all_templates(early, split, cos_t, sin_t)
    scores, marks, stat = score(temps, power, shards, half)
    if pairwise:
        stat, slices = lax.optimization_barrier((stat, slices))
        stats = [stat] + [swap(stat, "cls", k) for k in range(1, n_cls)]
        paired = tuple(range(n_cls))
        last = [third, swap(bundle(slices[-len(others) :]), "cls", 1)]
    else:
        stats = [lax.all_gather(stat, "cls", axis=0, tiled=True)]
        paired = (0,)
        last = []
    norm, payload = responsibilities(scores, marks, stats, paired, poses, half)
    payloads = [payload] + [swap(payload, "img", d) for d in others]
    log_resp, weight, rows = gather_rows(
        me, scores, norm, ctf, noise_weight, slices, last, n_img, poses, half, span
    )
    averages = finish(me, weight, cos_t, sin_t, rows, payloads, cls_rows)
    return (log_resp.T, averages)


def solution(mesh):
    placed = (
        P(("groups", "img", "cls"), None, None),
        P(("groups", "cls"), None, None),
        P("groups", None),
        P("groups"),
        P(("groups", "img", "cls")),
        P("groups", None),
    )
    return jax.shard_map(
        local,
        mesh=mesh,
        in_specs=placed,
        out_specs=(P(("groups", "img"), "cls"), P(("groups", "cls"), None, "img")),
        check_vma=False,
    )
```

```python
import functools

import jax
import jax.numpy as jnp
from jax import lax
from jax.experimental import pallas as pl
from jax.experimental.pallas import tpu as pltpu
from jax.sharding import PartitionSpec as P

BOX = 128
CHUNKS = 2
LANES = 128
VMEM_LIMIT = 24 * 1024 * 1024

prior_precision = 0.02

NT = (((1,), (1,)), ((), ()))
NN = (((1,), (0,)), ((), ()))
HIGHEST = lax.Precision.HIGHEST
f32 = jnp.float32
bf16 = jnp.bfloat16

SMEM = pl.BlockSpec(memory_space=pltpu.SMEM)
VMEM = pl.BlockSpec(memory_space=pltpu.VMEM)
ANY = pl.BlockSpec(memory_space=pl.ANY)


def call(kernel, name, in_specs, out_shape, operands, scratch=(), flops=0, moved=0, limit=VMEM_LIMIT):
    return pl.pallas_call(
        kernel,
        in_specs=in_specs,
        out_specs=[VMEM] * len(out_shape),
        out_shape=out_shape,
        scratch_shapes=list(scratch),
        compiler_params=pltpu.CompilerParams(vmem_limit_bytes=limit),
        cost_estimate=pl.CostEstimate(flops=flops, bytes_accessed=moved, transcendentals=0),
        name=name,
    )(*operands)


def real_index(shape, axis, half):
    return lax.rem(lax.broadcasted_iota(jnp.int32, shape, axis) // half, 2) == 0


def weigh_kernel(ids_hbm, p_hbm, ctf_hbm, nw_hbm, *refs):
    out_refs, (ids_ref, p_ref, ctf_ref, nw_ref, scale_ref, sem) = refs[:-6], refs[-6:]
    count, _, freq = p_ref.shape
    copies = [
        pltpu.make_async_copy(source, target, sem.at[i])
        for i, (source, target) in enumerate(
            [(ids_hbm, ids_ref), (ctf_hbm, ctf_ref), (nw_hbm, nw_ref), (p_hbm, p_ref)]
        )
    ]
    for copy in copies:
        copy.start()
    copies[0].wait()
    row = lax.rem(lax.broadcasted_iota(jnp.int32, (2 * count, LANES), 0), count)
    ids = jnp.zeros((2 * count, LANES), f32)
    for n in range(count):
        ids = jnp.where(row == n, ids_ref[n].astype(f32), ids)
    for copy in copies[1:]:
        copy.wait()
    noise = nw_ref[...].reshape(1, freq)
    for n in range(count):
        scale_ref[n : n + 1, :] = ctf_ref[pl.ds(ids_ref[n], 1), :] * noise
    scale = scale_ref[...]
    values = p_ref[...].astype(f32)
    chunk = freq // CHUNKS
    for part in range(2):
        weighted = (values[:, part, :] * scale).astype(bf16)
        here = slice(part * count, (part + 1) * count)
        out_refs[0][here, :freq] = weighted
        for c, out_ref in enumerate(out_refs[1:]):
            out_ref[here, :chunk] = weighted[:, c * chunk : (c + 1) * chunk]
    for out_ref in out_refs[:2]:
        out_ref[:, out_ref.shape[1] - LANES :] = ids.astype(bf16)


def weigh(particles, ctf, noise_weight, group_ids):
    rows, _, freq = particles.shape
    operands = (group_ids, particles, ctf, noise_weight)
    return call(
        weigh_kernel,
        "weigh",
        [ANY] * 4,
        [
            jax.ShapeDtypeStruct((2 * rows, width), bf16)
            for width in [freq + LANES, freq // CHUNKS + LANES] + [freq // CHUNKS] * (CHUNKS - 1)
        ],
        [pltpu.with_memory_space_constraint(x, pltpu.HBM) for x in operands],
        [
            pltpu.SMEM((rows,), jnp.int32),
            pltpu.VMEM(particles.shape, bf16),
            pltpu.VMEM(ctf.shape, f32),
            pltpu.VMEM((freq,), f32),
            pltpu.VMEM((rows, freq), f32),
            pltpu.SemaphoreType.DMA((4,)),
        ],
        flops=4 * rows * freq,
        moved=16 * rows * freq,
    )


def prepare_kernel(
    shifts_ref, cls_hbm, ctf_hbm, nw_hbm, cos_ref, sin_ref, pow_ref, split_ref, cw_ref, *scratch
):
    cls_ref, ctf_ref, nw_ref, angle_ref, sem = scratch
    rows, _, freq = cls_ref.shape
    poses = cos_ref.shape[0]
    copies = [
        pltpu.make_async_copy(source, target, sem.at[i])
        for i, (source, target) in enumerate(
            [(cls_hbm, cls_ref), (ctf_hbm, ctf_ref), (nw_hbm, nw_ref)]
        )
    ]
    for copy in copies:
        copy.start()
    lane = lax.broadcasted_iota(jnp.int32, (1, BOX), 1).astype(f32)
    step = 2.0 * jnp.pi / BOX
    for r in range(poses):
        angle_ref[0, r : r + 1, :] = step * (shifts_ref[0, r].astype(f32) * (lane - BOX // 2))
        angle_ref[1, r : r + 1, :] = step * (shifts_ref[1, r].astype(f32) * lane)
    x_cos, x_sin = jnp.cos(angle_ref[0]), jnp.sin(angle_ref[0])
    y_cos, y_sin = jnp.cos(angle_ref[1]), jnp.sin(angle_ref[1])
    for t in range(freq // BOX):
        c = jnp.broadcast_to(y_cos[:, t : t + 1], x_cos.shape)
        s = jnp.broadcast_to(y_sin[:, t : t + 1], x_cos.shape)
        cos_ref[:, t * BOX : (t + 1) * BOX] = x_cos * c - x_sin * s
        sin_ref[:, t * BOX : (t + 1) * BOX] = x_sin * c + x_cos * s
    for copy in copies:
        copy.wait()
    noise = nw_ref[...].reshape(1, freq)
    cut = freq // 4
    power = jnp.zeros(pow_ref.shape, f32)
    for q in range(4):
        at = slice(q * cut, (q + 1) * cut)
        values = cls_ref[:, :, at].astype(f32)
        re, im = values[:, 0, :], values[:, 1, :]
        split_ref[0, :, at] = re.astype(bf16)
        split_ref[1, :, at] = im.astype(bf16)
        ctf = ctf_ref[:, at]
        weight = ctf * ctf * noise[:, at]
        cw_ref[:, at] = weight
        power += lax.dot_general(
            re * re + im * im, weight, NT, precision=HIGHEST, preferred_element_type=f32
        )
    pow_ref[...] = power


def prepare(shifts, classes, ctf, noise_weight):
    rows, _, freq = classes.shape
    poses, groups = shifts.shape[0], ctf.shape[0]
    return call(
        prepare_kernel,
        "prepare",
        [SMEM, ANY, ANY, ANY],
        [
            jax.ShapeDtypeStruct((poses, freq), f32),
            jax.ShapeDtypeStruct((poses, freq), f32),
            jax.ShapeDtypeStruct((rows, groups), f32),
            jax.ShapeDtypeStruct((2, rows, freq), bf16),
            jax.ShapeDtypeStruct((groups, freq), f32),
        ],
        (
            shifts.T,
            *[pltpu.with_memory_space_constraint(x, pltpu.HBM) for x in (classes, ctf, noise_weight)],
        ),
        [
            pltpu.VMEM(classes.shape, bf16),
            pltpu.VMEM(ctf.shape, f32),
            pltpu.VMEM((freq,), f32),
            pltpu.VMEM((2, poses, BOX), f32),
            pltpu.SemaphoreType.DMA((3,)),
        ],
        flops=24 * rows * groups * freq,
    )


def write_templates(cls_ref, cos_ref, sin_ref, temp_ref, start, tile):
    rows = cls_ref.shape[1]
    for a in range(0, tile, LANES):
        at = pl.ds(pl.multiple_of(start + a, LANES), LANES)
        re = cls_ref[0, :, at].astype(f32)
        im = cls_ref[1, :, at].astype(f32)
        for r in range(cos_ref.shape[0]):
            cos_r = cos_ref[r : r + 1, at]
            sin_r = sin_ref[r : r + 1, at]
            here = slice(r * rows, (r + 1) * rows)
            temp_ref[here, a : a + LANES] = (re * cos_r - im * sin_r).astype(bf16)
            temp_ref[here, tile + a : tile + a + LANES] = (re * sin_r + im * cos_r).astype(bf16)


def template_tile(freq):
    return max(t for t in range(LANES, 385, LANES) if freq // CHUNKS % t == 0)


def early_kernel(cls_ref, cos_ref, sin_ref, temp_ref):
    write_templates(cls_ref, cos_ref, sin_ref, temp_ref, 0, cls_ref.shape[2])


def early_templates(split, cos_t, sin_t):
    _, rows, freq = split.shape
    poses = cos_t.shape[0]
    tile = template_tile(freq)
    count = freq // tile // 2
    skip = freq // tile - count
    return pl.pallas_call(
        early_kernel,
        grid=(count,),
        in_specs=[
            pl.BlockSpec((2, rows, tile), lambda j: (0, 0, skip + j)),
            pl.BlockSpec((poses, tile), lambda j: (0, skip + j)),
            pl.BlockSpec((poses, tile), lambda j: (0, skip + j)),
        ],
        out_specs=pl.BlockSpec((None, poses * rows, 2 * tile), lambda j: (j, 0, 0)),
        out_shape=pltpu.HBM((count, poses * rows, 2 * tile), bf16),
        compiler_params=pltpu.CompilerParams(vmem_limit_bytes=VMEM_LIMIT),
        cost_estimate=pl.CostEstimate(
            flops=20 * poses * rows * freq, bytes_accessed=2 * poses * rows * freq, transcendentals=0
        ),
        name="early_templates",
    )(split, cos_t, sin_t)


def template_kernel(early_hbm, cls_ref, cos_ref, sin_ref, temp_ref, sem):
    count = early_hbm.shape[0]
    built = temp_ref.shape[0] - count
    tile = temp_ref.shape[2] // 2
    copies = [
        pltpu.make_async_copy(early_hbm.at[t], temp_ref.at[built + t], sem.at[t])
        for t in range(count)
    ]
    for copy in copies:
        copy.start()

    @pl.loop(0, built)
    def _(t):
        write_templates(cls_ref, cos_ref, sin_ref, temp_ref.at[t], t * tile, tile)

    for copy in copies:
        copy.wait()


def all_templates(early, split, cos_t, sin_t):
    _, rows, freq = split.shape
    poses = cos_t.shape[0]
    count, columns, width = early.shape
    return call(
        template_kernel,
        "templates",
        [ANY] + [VMEM] * 3,
        [pltpu.VMEM((freq // (width // 2), columns, width), bf16)],
        (pltpu.with_memory_space_constraint(early, pltpu.HBM), split, cos_t, sin_t),
        [pltpu.SemaphoreType.DMA((count,))],
        flops=20 * poses * rows * freq,
        moved=2 * poses * rows * freq,
    )[0]


def add_products(acc_ref, temp_ref, chunk, shards, half):
    count = temp_ref.shape[0] // CHUNKS
    tile = temp_ref.shape[2] // 2
    real = real_index((acc_ref.shape[1], tile), 0, half)
    for t in range(count):
        cuts = []
        for refs in shards:
            ref, at = (refs[0], chunk * count * tile) if len(refs) == 1 else (refs[chunk], 0)
            cuts.append(ref[:, at + t * tile : at + (t + 1) * tile])
        wide = jnp.concatenate(cuts, axis=0).astype(f32)
        split = jnp.concatenate(
            [jnp.where(real, wide, 0.0).astype(bf16), jnp.where(real, 0.0, wide).astype(bf16)],
            axis=1,
        )
        acc_ref[...] += lax.dot_general(
            temp_ref[chunk * count + t], split, NT, preferred_element_type=f32
        )


def regroup(refs, counts):
    refs = list(refs)
    return [[refs.pop(0) for _ in range(count)] for count in counts]


def score_kernel(chunk, counts, half, temp_ref, *refs):
    *refs, acc_ref = refs
    acc_ref[...] = jnp.zeros_like(acc_ref) if chunk == 0 else refs.pop(0)[...]
    add_products(acc_ref, temp_ref, chunk, regroup(refs, counts), half)


def last_score_kernel(counts, half, temp_ref, pow_ref, acc_ref, *refs):
    refs, (s_ref, marks_ref, stat_ref) = refs[:-3], refs[-3:]
    shards = regroup(refs, counts)
    rows, groups = pow_ref.shape
    lanes = s_ref.shape[1]
    poses = s_ref.shape[0] // rows
    tails = [refs[0][:, refs[0].shape[1] - LANES :] for refs in shards]
    ids = jnp.concatenate(tails, axis=0).astype(f32)
    group = lax.broadcasted_iota(jnp.int32, (lanes, groups), 1).astype(f32)
    marks = (ids[:, :groups] == group).astype(f32)
    marks_ref[...] = marks
    penalty = lax.dot_general(
        pow_ref[...], marks, NT, precision=HIGHEST, preferred_element_type=f32
    )
    s_ref[...] = acc_ref[...]
    add_products(s_ref, temp_ref, CHUNKS - 1, shards, half)
    acc = s_ref[...]
    acc = acc + jnp.where(
        real_index(acc.shape, 1, half), pltpu.roll(acc, lanes - half, 1), pltpu.roll(acc, half, 1)
    )
    scores = acc.reshape(poses, rows, lanes) - 0.5 * penalty[None]
    peak = jnp.max(jnp.max(scores, axis=0), axis=0, keepdims=True)
    total = jnp.sum(jnp.sum(jnp.exp(scores - peak[None]), axis=0), axis=0, keepdims=True)
    s_ref[...] = scores.reshape(poses * rows, lanes)
    stat_ref[0:1, :] = peak
    stat_ref[1:2, :] = total
    stat_ref[2:8, :] = jnp.zeros((6, lanes), f32)


def score(temps, power, shards, half):
    count, columns, width = temps.shape
    lanes = sum(refs[0].shape[0] for refs in shards)
    flops = 2 * columns * 256 * count * width // CHUNKS
    acc_shape = jax.ShapeDtypeStruct((columns, lanes), f32)
    acc = []
    for c in range(CHUNKS - 1):
        counts = [1 if len(refs) == 1 else CHUNKS for refs in shards]
        operands = [temps, *acc]
        for refs in shards:
            operands += refs if len(refs) == 1 else [refs[c]] * CHUNKS
        acc = call(
            functools.partial(score_kernel, c, counts, half),
            f"score{c}",
            [VMEM] * len(operands),
            [acc_shape],
            operands,
            flops=flops,
        )
    operands = [temps, power, *acc, *[ref for refs in shards for ref in refs]]
    return call(
        functools.partial(last_score_kernel, [len(refs) for refs in shards], half),
        f"score{CHUNKS - 1}",
        [VMEM] * len(operands),
        [
            acc_shape,
            jax.ShapeDtypeStruct((lanes, power.shape[1]), f32),
            jax.ShapeDtypeStruct((8, lanes), f32),
        ],
        operands,
        flops=flops,
    )


def slices_kernel(counts, targets, me_ref, *refs):
    whole_ref, refs = refs[-1], refs[:-1]
    shards, out_refs = regroup(refs[: -len(targets)], counts), refs[-len(targets) :]
    span = out_refs[0].shape[1]
    at = 0
    for refs in shards:
        source = refs[0]
        height = source.shape[0]
        if len(refs) > 1:
            width = refs[-1].shape[1]
            for c, ref in enumerate(refs):
                whole_ref[:, c * width : (c + 1) * width] = ref[:, :width]
            source = whole_ref
        for out_ref, distance in zip(out_refs, targets):
            base = pl.multiple_of((me_ref[0] ^ distance) * span, LANES)
            out_ref[at : at + height, :] = source[:, pl.ds(base, span)]
        at += height


def cut_slices(me, shards, targets, span, freq):
    height = sum(refs[0].shape[0] for refs in shards)
    operands = [me, *[ref for refs in shards for ref in refs]]
    return call(
        functools.partial(slices_kernel, [len(refs) for refs in shards], targets),
        "cut_slices",
        [SMEM] + [VMEM] * (len(operands) - 1),
        [jax.ShapeDtypeStruct((height, span), bf16)] * len(targets),
        operands,
        [pltpu.VMEM((shards[-1][0].shape[0], freq), bf16)],
        moved=4 * height * span * len(targets),
        limit=VMEM_LIMIT if height <= 128 else 2 * VMEM_LIMIT,
    )


def bundle_kernel(*refs):
    sources, out_ref = refs[:-1], refs[-1]
    rows = out_ref.shape[0] // len(sources)
    for i, ref in enumerate(sources):
        out_ref[i * rows : (i + 1) * rows, :] = ref[ref.shape[0] - rows :, :]


def bundle(slices, rows):
    span = slices[0].shape[1]
    return call(
        bundle_kernel,
        "bundle",
        [VMEM] * len(slices),
        [jax.ShapeDtypeStruct((len(slices) * rows, span), bf16)],
        slices,
        moved=4 * len(slices) * rows * span,
    )[0]


def xor_blocks(values, block, distance):
    lanes = values.shape[1]
    lane = lax.broadcasted_iota(jnp.int32, values.shape, 1)
    width = block
    while distance:
        if distance % 2:
            low = lax.rem(lane // width, 2) == 0
            values = jnp.where(
                low, pltpu.roll(values, lanes - width, 1), pltpu.roll(values, width, 1)
            )
        distance //= 2
        width *= 2
    return values


def rho_kernel(poses, half, paired, s_ref, marks_ref, *refs):
    stat_refs, (norm_ref, out_ref) = refs[: len(paired)], refs[len(paired) :]
    lanes = s_ref.shape[1]
    rows = s_ref.shape[0] // poses
    groups = marks_ref.shape[1]
    block = 2 * half
    peaks, totals = [], []
    for ref, distance in zip(stat_refs, paired):
        for at in range(0, ref.shape[0], 8):
            stats = xor_blocks(ref[at : at + 8, :], block, distance)
            peaks.append(stats[0:1])
            totals.append(stats[1:2])
    peak = functools.reduce(jnp.maximum, peaks)
    total = sum(t * jnp.exp(p - peak) for t, p in zip(totals, peaks))
    log_norm = peak + jnp.log(total)
    norm_ref[...] = log_norm
    rho = jnp.exp(s_ref[...].reshape(poses, rows, lanes) - log_norm[None])
    mass = lax.dot_general(
        jnp.where(real_index((rows, lanes), 1, half), jnp.sum(rho, axis=0), 0.0),
        marks_ref[...],
        NN,
        precision=HIGHEST,
        preferred_element_type=f32,
    )
    high = mass.astype(bf16)
    low = (mass - high.astype(f32)).astype(bf16)
    rho_low = rho.reshape(poses * rows, lanes).astype(bf16)
    cut = poses // 2 * rows
    lane = lax.broadcasted_iota(jnp.int32, (lanes, lanes), 0)
    column = lax.broadcasted_iota(jnp.int32, (lanes, lanes), 1)
    particle = lane // block * half + lax.rem(lane, block)
    real = lax.rem(lane, block) < half
    first = (real & (column == particle)).astype(f32).astype(bf16)
    second = (real & (column == particle + lanes // 2)).astype(f32).astype(bf16)
    packed = jnp.dot(rho_low[:cut], first, preferred_element_type=f32)
    packed += jnp.dot(rho_low[cut:], second, preferred_element_type=f32)
    out_ref[:cut, :] = packed.astype(bf16)
    if lanes > 2 * groups:
        out_ref[cut:, :] = jnp.zeros((rows, lanes), bf16)
    out_ref[cut:, :groups] = high
    out_ref[cut:, groups : 2 * groups] = low


def responsibilities(scores, marks, stats, paired, poses, half):
    columns, lanes = scores.shape
    return call(
        functools.partial(rho_kernel, poses, half, paired),
        "responsibilities",
        [VMEM] * (2 + len(stats)),
        [
            jax.ShapeDtypeStruct((1, lanes), f32),
            jax.ShapeDtypeStruct((columns // 2 + columns // poses, lanes), bf16),
        ],
        (scores, marks, *stats),
        flops=40 * columns * lanes,
    )


def gather_kernel(poses, half, sources, me_ref, s_ref, norm_ref, weight_ref, *refs):
    w_refs, (resp_ref, cw_ref, rows_ref) = refs[:-3], refs[-3:]
    span = rows_ref.shape[2]
    block = 2 * half
    here = pl.ds(pl.multiple_of(me_ref[0] * span, LANES), span)
    at = 0
    for i in range(sources):
        for ref in w_refs[i::sources]:
            for start in range(0, ref.shape[0], block):
                rows_ref[0, at : at + half, :] = ref[start : start + half, :]
                rows_ref[1, at : at + half, :] = ref[start + half : start + block, :]
                at += half
    cw_ref[...] = weight_ref[:, here]
    rows = resp_ref.shape[0]
    lanes = s_ref.shape[1]
    scores = s_ref[...].reshape(poses, rows, lanes)
    pose_peak = jnp.max(scores, axis=0)
    total = jnp.sum(jnp.exp(scores - pose_peak[None]), axis=0)
    log_resp = pose_peak + jnp.log(total) - norm_ref[...]
    shape = (resp_ref.shape[1], lanes)
    lane = lax.broadcasted_iota(jnp.int32, shape, 1)
    row = ((lane // block) ^ me_ref[1]) * half + lax.rem(lane, block)
    take = (lax.broadcasted_iota(jnp.int32, shape, 0) == row) & (lax.rem(lane, block) < half)
    resp_ref[...] = lax.dot_general(
        log_resp, take.astype(f32), NT, precision=HIGHEST, preferred_element_type=f32
    )


def gather_rows(me, scores, norm, weight, slices, sources, poses, half, span):
    columns, lanes = scores.shape
    particles = sum(w.shape[0] for w in slices) // 2
    return call(
        functools.partial(gather_kernel, poses, half, sources),
        "gather_rows",
        [SMEM] + [VMEM] * (3 + len(slices)),
        [
            jax.ShapeDtypeStruct((columns // poses, lanes // 2), f32),
            jax.ShapeDtypeStruct((weight.shape[0], span), f32),
            jax.ShapeDtypeStruct((2, particles, span), bf16),
        ],
        (me, scores, norm, weight, *slices),
        flops=40 * columns * lanes,
        moved=8 * particles * span,
        limit=VMEM_LIMIT if particles <= 512 else 2 * VMEM_LIMIT,
    )


def finish_kernel(poses, groups, sources, half, me_ref, cw_ref, cos_ref, sin_ref, rows_ref, *refs):
    payloads, refs = refs[:sources], refs[sources:]
    last, (out_ref, rho_ref, denom_ref, *buffers) = refs[:-5], refs[-5:]
    rows, _, span = out_ref.shape
    cut = poses // 2 * rows
    count = payloads[0].shape[1] // 2
    mass = jnp.zeros((rows, groups), f32)
    for i, ref in enumerate(payloads):
        rho_ref[:cut, i * count : (i + 1) * count] = ref[:cut, :count]
        rho_ref[cut:, i * count : (i + 1) * count] = ref[:cut, count:]
        mass += ref[cut:, :groups].astype(f32) + ref[cut:, groups : 2 * groups].astype(f32)
    denom_ref[...] = (
        lax.dot_general(mass, cw_ref[...], NN, precision=HIGHEST, preferred_element_type=f32)
        + prior_precision
    )
    tiles = [(a, min(256, span - a)) for a in range(0, span, 256)]
    known = rows_ref.shape[1] // sources

    def rows_of(part, start, width):
        here = slice(start, start + width)
        if not last:
            return rows_ref[part, :, here]
        pieces = []
        for i in range(sources):
            pieces.append(rows_ref[part, i * known : (i + 1) * known, here])
            if i == 0:
                pieces.append(last[0][part * half : (part + 1) * half, here])
            else:
                at = (2 * (i - 1) + part) * half
                pieces.append(last[1][at : at + half, here])
        return jnp.concatenate(pieces, axis=0)

    def products(i):
        start, width = tiles[i]
        for part in range(2):
            buffers[i % 2][part, :, :width] = jnp.dot(
                rho_ref[...], rows_of(part, start, width), preferred_element_type=f32
            )

    def rotate(i):
        start, width = tiles[i]
        buffer = buffers[i % 2]
        for a in range(0, width, LANES):
            at = pl.ds(pl.multiple_of(me_ref[0] * span + start + a, LANES), LANES)
            numer_re = jnp.zeros((rows, LANES), f32)
            numer_im = jnp.zeros((rows, LANES), f32)
            for r in range(poses):
                cos_r = cos_ref[r : r + 1, at]
                sin_r = sin_ref[r : r + 1, at]
                s_re = buffer[0, r * rows : (r + 1) * rows, a : a + LANES]
                s_im = buffer[1, r * rows : (r + 1) * rows, a : a + LANES]
                numer_re = numer_re + s_re * cos_r + s_im * sin_r
                numer_im = numer_im + s_im * cos_r - s_re * sin_r
            here = slice(start + a, start + a + LANES)
            denom = denom_ref[:, here]
            out_ref[:, 0, here] = numer_re / denom
            out_ref[:, 1, here] = numer_im / denom

    products(0)
    for i in range(1, len(tiles)):
        products(i)
        rotate(i - 1)
    rotate(len(tiles) - 1)


def finish(me, weight, cos_t, sin_t, rows, payloads, last, cls_rows, half):
    poses = cos_t.shape[0]
    span = rows.shape[2]
    particles = len(payloads) * payloads[0].shape[1] // 2
    return call(
        functools.partial(finish_kernel, poses, weight.shape[0], len(payloads), half),
        "finish",
        [SMEM] + [VMEM] * (4 + len(payloads) + len(last)),
        [jax.ShapeDtypeStruct((cls_rows, 2, span), f32)],
        (me, weight, cos_t, sin_t, rows, *payloads, *last),
        [
            pltpu.VMEM((poses * cls_rows, particles), bf16),
            pltpu.VMEM((cls_rows, span), f32),
            pltpu.VMEM((2, poses * cls_rows, 256), f32),
            pltpu.VMEM((2, poses * cls_rows, 256), f32),
        ],
        flops=4 * poses * cls_rows * particles * span,
        limit=VMEM_LIMIT if particles <= 512 else 2 * VMEM_LIMIT,
    )[0]


def swap(values, axis, distance):
    size = lax.axis_size(axis)
    return lax.ppermute(values, axis, [(i, i ^ distance) for i in range(size)])


def local(particles, classes, ctf, noise_weight, group_ids, shifts):
    half, _, freq = particles.shape
    cls_rows = classes.shape[0]
    poses = shifts.shape[0]
    n_cls = lax.axis_size("cls")
    n_img = lax.axis_size("img")
    span = freq // n_img
    pairwise = n_cls == 4
    me_cls = lax.axis_index("cls") if pairwise else 0
    me = jnp.stack([lax.axis_index("img"), me_cls]).astype(jnp.int32)
    others = tuple(range(n_img - 1, 0, -1))
    targets = (0,) + others

    def share(*shards):
        mine, *outgoing = cut_slices(me, shards, targets, span, freq)
        return [mine] + [swap(w, "img", d) for w, d in zip(outgoing, others)]

    own, *own_chunks = weigh(particles, ctf, noise_weight, group_ids)
    if pairwise:
        far = [swap(w, "cls", 2) for w in own_chunks]
        near = swap(own, "cls", 1)
    else:
        shards = [[lax.all_gather(own, "cls", axis=0, tiled=True)]]
        slices = share(*shards)

    cos_t, sin_t, power, split, weight = prepare(shifts, classes, ctf, noise_weight)
    early = early_templates(split, cos_t, sin_t)
    if pairwise:
        far, near, split, early = lax.optimization_barrier((far, near, split, early))
        third = [swap(w, "cls", 1) for w in far]
        slices = share([own], [near], far)
        shards = [[own], [near], far, third]
    temps = all_templates(early, split, cos_t, sin_t)
    scores, marks, stat = score(temps, power, shards, half)
    if pairwise:
        stat, slices = lax.optimization_barrier((stat, slices))
        stats = [stat] + [swap(stat, "cls", k) for k in range(1, n_cls)]
        paired = tuple(range(n_cls))
        last = [*cut_slices(me, [third], (0,), span, freq)]
        last.append(swap(bundle(slices[1:], 2 * half), "cls", 1))
    else:
        stats = [lax.all_gather(stat, "cls", axis=0, tiled=True)]
        paired = (0,)
        last = []
    norm, payload = responsibilities(scores, marks, stats, paired, poses, half)
    payloads = [payload] + [swap(payload, "img", d) for d in others]
    log_resp, weight_here, rows = gather_rows(
        me, scores, norm, weight, slices, n_img, poses, half, span
    )
    averages = finish(me, weight_here, cos_t, sin_t, rows, payloads, last, cls_rows, half)
    return (log_resp.T, averages)


def solution(mesh):
    placed = (
        P(("groups", "img", "cls"), None, None),
        P(("groups", "cls"), None, None),
        P("groups", None),
        P("groups"),
        P(("groups", "img", "cls")),
        P("groups", None),
    )
    return jax.shard_map(
        local,
        mesh=mesh,
        in_specs=placed,
        out_specs=(P(("groups", "img"), "cls"), P(("groups", "cls"), None, "img")),
        check_vma=False,
    )
```

```python
import functools

import jax
import jax.numpy as jnp
from jax import lax
from jax.experimental import pallas as pl
from jax.experimental.pallas import tpu as pltpu
from jax.sharding import PartitionSpec as P

BOX = 128
CHUNKS = 2
LANES = 128
VMEM_LIMIT = 24 * 1024 * 1024
GATHER_FLOPS = 20_000_000_000

prior_precision = 0.02

NT = (((1,), (1,)), ((), ()))
NN = (((1,), (0,)), ((), ()))
HIGHEST = lax.Precision.HIGHEST
f32 = jnp.float32
bf16 = jnp.bfloat16

SMEM = pl.BlockSpec(memory_space=pltpu.SMEM)
VMEM = pl.BlockSpec(memory_space=pltpu.VMEM)
ANY = pl.BlockSpec(memory_space=pl.ANY)


def call(kernel, name, in_specs, out_shape, operands, scratch=(), flops=0, moved=0, limit=VMEM_LIMIT):
    return pl.pallas_call(
        kernel,
        in_specs=in_specs,
        out_specs=[VMEM] * len(out_shape),
        out_shape=out_shape,
        scratch_shapes=list(scratch),
        compiler_params=pltpu.CompilerParams(vmem_limit_bytes=limit),
        cost_estimate=pl.CostEstimate(flops=flops, bytes_accessed=moved, transcendentals=0),
        name=name,
    )(*operands)


def real_index(shape, axis, half):
    return lax.rem(lax.broadcasted_iota(jnp.int32, shape, axis) // half, 2) == 0


def weigh_kernel(ids_hbm, p_hbm, ctf_hbm, nw_hbm, *refs):
    out_refs, (ids_ref, p_ref, ctf_ref, nw_ref, scale_ref, sem) = refs[:-6], refs[-6:]
    count, _, freq = p_ref.shape
    copies = [
        pltpu.make_async_copy(source, target, sem.at[i])
        for i, (source, target) in enumerate(
            [(ids_hbm, ids_ref), (ctf_hbm, ctf_ref), (nw_hbm, nw_ref), (p_hbm, p_ref)]
        )
    ]
    for copy in copies:
        copy.start()
    copies[0].wait()
    row = lax.rem(lax.broadcasted_iota(jnp.int32, (2 * count, LANES), 0), count)
    ids = jnp.zeros((2 * count, LANES), f32)
    for n in range(count):
        ids = jnp.where(row == n, ids_ref[n].astype(f32), ids)
    for copy in copies[1:]:
        copy.wait()
    noise = nw_ref[...].reshape(1, freq)
    for n in range(count):
        scale_ref[n : n + 1, :] = ctf_ref[pl.ds(ids_ref[n], 1), :] * noise
    scale = scale_ref[...]
    values = p_ref[...].astype(f32)
    chunk = freq // CHUNKS
    for part in range(2):
        weighted = (values[:, part, :] * scale).astype(bf16)
        here = slice(part * count, (part + 1) * count)
        out_refs[0][here, :freq] = weighted
        for c, out_ref in enumerate(out_refs[1:]):
            out_ref[here, :chunk] = weighted[:, c * chunk : (c + 1) * chunk]
    for out_ref in out_refs[:2]:
        out_ref[:, out_ref.shape[1] - LANES :] = ids.astype(bf16)


def weigh(particles, ctf, noise_weight, group_ids):
    rows, _, freq = particles.shape
    operands = (group_ids, particles, ctf, noise_weight)
    return call(
        weigh_kernel,
        "weigh",
        [ANY] * 4,
        [
            jax.ShapeDtypeStruct((2 * rows, width), bf16)
            for width in [freq + LANES, freq // CHUNKS + LANES] + [freq // CHUNKS] * (CHUNKS - 1)
        ],
        [pltpu.with_memory_space_constraint(x, pltpu.HBM) for x in operands],
        [
            pltpu.SMEM((rows,), jnp.int32),
            pltpu.VMEM(particles.shape, bf16),
            pltpu.VMEM(ctf.shape, f32),
            pltpu.VMEM((freq,), f32),
            pltpu.VMEM((rows, freq), f32),
            pltpu.SemaphoreType.DMA((4,)),
        ],
        flops=4 * rows * freq,
        moved=16 * rows * freq,
    )


def prepare_kernel(
    shifts_ref, cls_hbm, ctf_hbm, nw_hbm, cos_ref, sin_ref, pow_ref, split_ref, cw_ref, *scratch
):
    cls_ref, ctf_ref, nw_ref, angle_ref, sem = scratch
    rows, _, freq = cls_ref.shape
    poses = cos_ref.shape[0]
    copies = [
        pltpu.make_async_copy(source, target, sem.at[i])
        for i, (source, target) in enumerate(
            [(cls_hbm, cls_ref), (ctf_hbm, ctf_ref), (nw_hbm, nw_ref)]
        )
    ]
    for copy in copies:
        copy.start()
    lane = lax.broadcasted_iota(jnp.int32, (1, BOX), 1).astype(f32)
    step = 2.0 * jnp.pi / BOX
    for r in range(poses):
        angle_ref[0, r : r + 1, :] = step * (shifts_ref[0, r].astype(f32) * (lane - BOX // 2))
        angle_ref[1, r : r + 1, :] = step * (shifts_ref[1, r].astype(f32) * lane)
    x_cos, x_sin = jnp.cos(angle_ref[0]), jnp.sin(angle_ref[0])
    y_cos, y_sin = jnp.cos(angle_ref[1]), jnp.sin(angle_ref[1])
    for t in range(freq // BOX):
        c = jnp.broadcast_to(y_cos[:, t : t + 1], x_cos.shape)
        s = jnp.broadcast_to(y_sin[:, t : t + 1], x_cos.shape)
        cos_ref[:, t * BOX : (t + 1) * BOX] = x_cos * c - x_sin * s
        sin_ref[:, t * BOX : (t + 1) * BOX] = x_sin * c + x_cos * s
    for copy in copies:
        copy.wait()
    noise = nw_ref[...].reshape(1, freq)
    cut = freq // 4
    power = jnp.zeros(pow_ref.shape, f32)
    for q in range(4):
        at = slice(q * cut, (q + 1) * cut)
        values = cls_ref[:, :, at].astype(f32)
        re, im = values[:, 0, :], values[:, 1, :]
        split_ref[0, :, at] = re.astype(bf16)
        split_ref[1, :, at] = im.astype(bf16)
        ctf = ctf_ref[:, at]
        weight = ctf * ctf * noise[:, at]
        cw_ref[:, at] = weight
        power += lax.dot_general(
            re * re + im * im, weight, NT, precision=HIGHEST, preferred_element_type=f32
        )
    pow_ref[...] = power


def prepare(shifts, classes, ctf, noise_weight):
    rows, _, freq = classes.shape
    poses, groups = shifts.shape[0], ctf.shape[0]
    return call(
        prepare_kernel,
        "prepare",
        [SMEM, ANY, ANY, ANY],
        [
            jax.ShapeDtypeStruct((poses, freq), f32),
            jax.ShapeDtypeStruct((poses, freq), f32),
            jax.ShapeDtypeStruct((rows, groups), f32),
            jax.ShapeDtypeStruct((2, rows, freq), bf16),
            jax.ShapeDtypeStruct((groups, freq), f32),
        ],
        (
            shifts.T,
            *[pltpu.with_memory_space_constraint(x, pltpu.HBM) for x in (classes, ctf, noise_weight)],
        ),
        [
            pltpu.VMEM(classes.shape, bf16),
            pltpu.VMEM(ctf.shape, f32),
            pltpu.VMEM((freq,), f32),
            pltpu.VMEM((2, poses, BOX), f32),
            pltpu.SemaphoreType.DMA((3,)),
        ],
        flops=24 * rows * groups * freq,
    )


def write_templates(cls_ref, cos_ref, sin_ref, temp_ref, start, tile):
    rows = cls_ref.shape[1]
    for a in range(0, tile, LANES):
        at = pl.ds(pl.multiple_of(start + a, LANES), LANES)
        re = cls_ref[0, :, at].astype(f32)
        im = cls_ref[1, :, at].astype(f32)
        for r in range(cos_ref.shape[0]):
            cos_r = cos_ref[r : r + 1, at]
            sin_r = sin_ref[r : r + 1, at]
            here = slice(r * rows, (r + 1) * rows)
            temp_ref[here, a : a + LANES] = (re * cos_r - im * sin_r).astype(bf16)
            temp_ref[here, tile + a : tile + a + LANES] = (re * sin_r + im * cos_r).astype(bf16)


def template_tile(freq):
    return max(t for t in range(LANES, 385, LANES) if freq // CHUNKS % t == 0)


def early_kernel(cls_ref, cos_ref, sin_ref, temp_ref):
    write_templates(cls_ref, cos_ref, sin_ref, temp_ref, 0, cls_ref.shape[2])


def early_templates(split, cos_t, sin_t):
    _, rows, freq = split.shape
    poses = cos_t.shape[0]
    tile = template_tile(freq)
    count = freq // tile // 2
    skip = freq // tile - count
    return pl.pallas_call(
        early_kernel,
        grid=(count,),
        in_specs=[
            pl.BlockSpec((2, rows, tile), lambda j: (0, 0, skip + j)),
            pl.BlockSpec((poses, tile), lambda j: (0, skip + j)),
            pl.BlockSpec((poses, tile), lambda j: (0, skip + j)),
        ],
        out_specs=pl.BlockSpec((None, poses * rows, 2 * tile), lambda j: (j, 0, 0)),
        out_shape=pltpu.HBM((count, poses * rows, 2 * tile), bf16),
        compiler_params=pltpu.CompilerParams(vmem_limit_bytes=VMEM_LIMIT),
        cost_estimate=pl.CostEstimate(
            flops=20 * poses * rows * freq, bytes_accessed=2 * poses * rows * freq, transcendentals=0
        ),
        name="early_templates",
    )(split, cos_t, sin_t)


def template_kernel(early_hbm, cls_ref, cos_ref, sin_ref, temp_ref, sem):
    count = early_hbm.shape[0]
    built = temp_ref.shape[0] - count
    tile = temp_ref.shape[2] // 2
    copies = [
        pltpu.make_async_copy(early_hbm.at[t], temp_ref.at[built + t], sem.at[t])
        for t in range(count)
    ]
    for copy in copies:
        copy.start()

    @pl.loop(0, built)
    def _(t):
        write_templates(cls_ref, cos_ref, sin_ref, temp_ref.at[t], t * tile, tile)

    for copy in copies:
        copy.wait()


def all_templates(early, split, cos_t, sin_t):
    _, rows, freq = split.shape
    poses = cos_t.shape[0]
    count, columns, width = early.shape
    return call(
        template_kernel,
        "templates",
        [ANY] + [VMEM] * 3,
        [pltpu.VMEM((freq // (width // 2), columns, width), bf16)],
        (pltpu.with_memory_space_constraint(early, pltpu.HBM), split, cos_t, sin_t),
        [pltpu.SemaphoreType.DMA((count,))],
        flops=20 * poses * rows * freq,
        moved=2 * poses * rows * freq,
    )[0]


def add_products(acc_ref, temp_ref, chunk, shards, half):
    count = temp_ref.shape[0] // CHUNKS
    tile = temp_ref.shape[2] // 2
    real = real_index((acc_ref.shape[1], tile), 0, half)
    for t in range(count):
        cuts = []
        for refs in shards:
            ref, at = (refs[0], chunk * count * tile) if len(refs) == 1 else (refs[chunk], 0)
            cuts.append(ref[:, at + t * tile : at + (t + 1) * tile])
        wide = jnp.concatenate(cuts, axis=0).astype(f32)
        split = jnp.concatenate(
            [jnp.where(real, wide, 0.0).astype(bf16), jnp.where(real, 0.0, wide).astype(bf16)],
            axis=1,
        )
        acc_ref[...] += lax.dot_general(
            temp_ref[chunk * count + t], split, NT, preferred_element_type=f32
        )


def regroup(refs, counts):
    refs = list(refs)
    return [[refs.pop(0) for _ in range(count)] for count in counts]


def score_kernel(chunk, counts, half, temp_ref, *refs):
    *refs, acc_ref = refs
    acc_ref[...] = jnp.zeros_like(acc_ref) if chunk == 0 else refs.pop(0)[...]
    add_products(acc_ref, temp_ref, chunk, regroup(refs, counts), half)


def last_score_kernel(counts, half, temp_ref, pow_ref, acc_ref, *refs):
    refs, (s_ref, marks_ref, stat_ref) = refs[:-3], refs[-3:]
    shards = regroup(refs, counts)
    rows, groups = pow_ref.shape
    lanes = s_ref.shape[1]
    poses = s_ref.shape[0] // rows
    tails = [refs[0][:, refs[0].shape[1] - LANES :] for refs in shards]
    ids = jnp.concatenate(tails, axis=0).astype(f32)
    group = lax.broadcasted_iota(jnp.int32, (lanes, groups), 1).astype(f32)
    marks = (ids[:, :groups] == group).astype(f32)
    marks_ref[...] = marks
    penalty = lax.dot_general(
        pow_ref[...], marks, NT, precision=HIGHEST, preferred_element_type=f32
    )
    s_ref[...] = acc_ref[...]
    add_products(s_ref, temp_ref, CHUNKS - 1, shards, half)
    acc = s_ref[...]
    acc = acc + jnp.where(
        real_index(acc.shape, 1, half), pltpu.roll(acc, lanes - half, 1), pltpu.roll(acc, half, 1)
    )
    scores = acc.reshape(poses, rows, lanes) - 0.5 * penalty[None]
    peak = jnp.max(jnp.max(scores, axis=0), axis=0, keepdims=True)
    total = jnp.sum(jnp.sum(jnp.exp(scores - peak[None]), axis=0), axis=0, keepdims=True)
    s_ref[...] = scores.reshape(poses * rows, lanes)
    stat_ref[0:1, :] = peak
    stat_ref[1:2, :] = total
    stat_ref[2:8, :] = jnp.zeros((6, lanes), f32)


def score(temps, power, shards, half):
    count, columns, width = temps.shape
    lanes = sum(refs[0].shape[0] for refs in shards)
    flops = 2 * columns * 256 * count * width // CHUNKS
    acc_shape = jax.ShapeDtypeStruct((columns, lanes), f32)
    acc = []
    for c in range(CHUNKS - 1):
        counts = [1 if len(refs) == 1 else CHUNKS for refs in shards]
        operands = [temps, *acc]
        for refs in shards:
            operands += refs if len(refs) == 1 else [refs[c]] * CHUNKS
        acc = call(
            functools.partial(score_kernel, c, counts, half),
            f"score{c}",
            [VMEM] * len(operands),
            [acc_shape],
            operands,
            flops=flops,
        )
    operands = [temps, power, *acc, *[ref for refs in shards for ref in refs]]
    return call(
        functools.partial(last_score_kernel, [len(refs) for refs in shards], half),
        f"score{CHUNKS - 1}",
        [VMEM] * len(operands),
        [
            acc_shape,
            jax.ShapeDtypeStruct((lanes, power.shape[1]), f32),
            jax.ShapeDtypeStruct((8, lanes), f32),
        ],
        operands,
        flops=flops,
    )


def slices_kernel(counts, targets, me_ref, *refs):
    whole_ref, refs = refs[-1], refs[:-1]
    shards, out_refs = regroup(refs[: -len(targets)], counts), refs[-len(targets) :]
    span = out_refs[0].shape[1]
    filled = [0] * len(targets)
    for k, refs in enumerate(shards):
        source = refs[0]
        height = source.shape[0]
        if len(refs) > 1:
            width = refs[-1].shape[1]
            for c, ref in enumerate(refs):
                whole_ref[:, c * width : (c + 1) * width] = ref[:, :width]
            source = whole_ref
        for i, (distance, skip) in enumerate(targets):
            if k >= skip:
                base = pl.multiple_of((me_ref[0] ^ distance) * span, LANES)
                out_refs[i][filled[i] : filled[i] + height, :] = source[:, pl.ds(base, span)]
                filled[i] += height


def cut_slices(me, shards, targets, span, freq):
    heights = [refs[0].shape[0] for refs in shards]
    operands = [me, *[ref for refs in shards for ref in refs]]
    out_heights = [sum(heights[skip:]) for _, skip in targets]
    return call(
        functools.partial(slices_kernel, [len(refs) for refs in shards], targets),
        "cut_slices",
        [SMEM] + [VMEM] * (len(operands) - 1),
        [jax.ShapeDtypeStruct((height, span), bf16) for height in out_heights],
        operands,
        [pltpu.VMEM((heights[-1], freq), bf16)],
        moved=4 * span * sum(out_heights),
        limit=VMEM_LIMIT if sum(heights) <= 128 else 2 * VMEM_LIMIT,
    )


def bundle_kernel(*refs):
    sources, out_ref = refs[:-1], refs[-1]
    rows = out_ref.shape[0] // len(sources)
    for i, ref in enumerate(sources):
        out_ref[i * rows : (i + 1) * rows, :] = ref[ref.shape[0] - rows :, :]


def bundle(slices, rows):
    span = slices[0].shape[1]
    return call(
        bundle_kernel,
        "bundle",
        [VMEM] * len(slices),
        [jax.ShapeDtypeStruct((len(slices) * rows, span), bf16)],
        slices,
        moved=4 * len(slices) * rows * span,
    )[0]


def xor_blocks(values, block, distance):
    lanes = values.shape[1]
    lane = lax.broadcasted_iota(jnp.int32, values.shape, 1)
    width = block
    while distance:
        if distance % 2:
            low = lax.rem(lane // width, 2) == 0
            values = jnp.where(
                low, pltpu.roll(values, lanes - width, 1), pltpu.roll(values, width, 1)
            )
        distance //= 2
        width *= 2
    return values


def rho_kernel(poses, half, paired, s_ref, marks_ref, *refs):
    stat_refs, (norm_ref, out_ref) = refs[: len(paired)], refs[len(paired) :]
    lanes = s_ref.shape[1]
    rows = s_ref.shape[0] // poses
    groups = marks_ref.shape[1]
    block = 2 * half
    peaks, totals = [], []
    for ref, distance in zip(stat_refs, paired):
        for at in range(0, ref.shape[0], 8):
            stats = xor_blocks(ref[at : at + 8, :], block, distance)
            peaks.append(stats[0:1])
            totals.append(stats[1:2])
    peak = functools.reduce(jnp.maximum, peaks)
    total = sum(t * jnp.exp(p - peak) for t, p in zip(totals, peaks))
    log_norm = peak + jnp.log(total)
    norm_ref[...] = log_norm
    rho = jnp.exp(s_ref[...].reshape(poses, rows, lanes) - log_norm[None])
    mass = lax.dot_general(
        jnp.where(real_index((rows, lanes), 1, half), jnp.sum(rho, axis=0), 0.0),
        marks_ref[...],
        NN,
        precision=HIGHEST,
        preferred_element_type=f32,
    )
    high = mass.astype(bf16)
    low = (mass - high.astype(f32)).astype(bf16)
    rho_low = rho.reshape(poses * rows, lanes).astype(bf16)
    cut = poses // 2 * rows
    lane = lax.broadcasted_iota(jnp.int32, (lanes, lanes), 0)
    column = lax.broadcasted_iota(jnp.int32, (lanes, lanes), 1)
    particle = lane // block * half + lax.rem(lane, block)
    real = lax.rem(lane, block) < half
    first = (real & (column == particle)).astype(f32).astype(bf16)
    second = (real & (column == particle + lanes // 2)).astype(f32).astype(bf16)
    packed = jnp.dot(rho_low[:cut], first, preferred_element_type=f32)
    packed += jnp.dot(rho_low[cut:], second, preferred_element_type=f32)
    out_ref[:cut, :] = packed.astype(bf16)
    if lanes > 2 * groups:
        out_ref[cut:, :] = jnp.zeros((rows, lanes), bf16)
    out_ref[cut:, :groups] = high
    out_ref[cut:, groups : 2 * groups] = low


def responsibilities(scores, marks, stats, paired, poses, half):
    columns, lanes = scores.shape
    return call(
        functools.partial(rho_kernel, poses, half, paired),
        "responsibilities",
        [VMEM] * (2 + len(stats)),
        [
            jax.ShapeDtypeStruct((1, lanes), f32),
            jax.ShapeDtypeStruct((columns // 2 + columns // poses, lanes), bf16),
        ],
        (scores, marks, *stats),
        flops=40 * columns * lanes,
    )


def gather_kernel(poses, half, counts, me_ref, s_ref, norm_ref, weight_ref, *refs):
    w_refs, (resp_ref, cw_ref, rows_ref) = refs[:-3], refs[-3:]
    span = rows_ref.shape[2]
    block = 2 * half
    here = pl.ds(pl.multiple_of(me_ref[0] * span, LANES), span)
    at = 0
    for refs in regroup(w_refs, counts):
        for ref in refs:
            for start in range(0, ref.shape[0], block):
                rows_ref[0, at : at + half, :] = ref[start : start + half, :]
                rows_ref[1, at : at + half, :] = ref[start + half : start + block, :]
                at += half
    cw_ref[...] = weight_ref[:, here]
    rows = resp_ref.shape[0]
    lanes = s_ref.shape[1]
    scores = s_ref[...].reshape(poses, rows, lanes)
    pose_peak = jnp.max(scores, axis=0)
    total = jnp.sum(jnp.exp(scores - pose_peak[None]), axis=0)
    log_resp = pose_peak + jnp.log(total) - norm_ref[...]
    shape = (resp_ref.shape[1], lanes)
    lane = lax.broadcasted_iota(jnp.int32, shape, 1)
    row = ((lane // block) ^ me_ref[1]) * half + lax.rem(lane, block)
    take = (lax.broadcasted_iota(jnp.int32, shape, 0) == row) & (lax.rem(lane, block) < half)
    resp_ref[...] = lax.dot_general(
        log_resp, take.astype(f32), NT, precision=HIGHEST, preferred_element_type=f32
    )


def gather_rows(me, scores, norm, weight, slices, poses, half, span):
    columns, lanes = scores.shape
    counts = [len(refs) for refs in slices]
    slices = [w for refs in slices for w in refs]
    particles = sum(w.shape[0] for w in slices) // 2
    return call(
        functools.partial(gather_kernel, poses, half, counts),
        "gather_rows",
        [SMEM] + [VMEM] * (3 + len(slices)),
        [
            jax.ShapeDtypeStruct((columns // poses, lanes // 2), f32),
            jax.ShapeDtypeStruct((weight.shape[0], span), f32),
            jax.ShapeDtypeStruct((2, particles, span), bf16),
        ],
        (me, scores, norm, weight, *slices),
        flops=GATHER_FLOPS,
        moved=8 * particles * span,
        limit=VMEM_LIMIT if particles <= 512 else 2 * VMEM_LIMIT,
    )


def finish_kernel(poses, groups, sources, half, me_ref, cw_ref, cos_ref, sin_ref, rows_ref, *refs):
    payloads, refs = refs[:sources], refs[sources:]
    last, (out_ref, rho_ref, denom_ref, *buffers) = refs[:-5], refs[-5:]
    rows, _, span = out_ref.shape
    cut = poses // 2 * rows
    count = payloads[0].shape[1] // 2
    mass = jnp.zeros((rows, groups), f32)
    for i, ref in enumerate(payloads):
        rho_ref[:cut, i * count : (i + 1) * count] = ref[:cut, :count]
        rho_ref[cut:, i * count : (i + 1) * count] = ref[:cut, count:]
        mass += ref[cut:, :groups].astype(f32) + ref[cut:, groups : 2 * groups].astype(f32)
    denom_ref[...] = (
        lax.dot_general(mass, cw_ref[...], NN, precision=HIGHEST, preferred_element_type=f32)
        + prior_precision
    )
    tiles = [(a, min(256, span - a)) for a in range(0, span, 256)]
    known = rows_ref.shape[1] // sources

    def rows_of(part, start, width):
        here = slice(start, start + width)
        if not last:
            return rows_ref[part, :, here]
        pieces = []
        for i in range(sources):
            pieces.append(rows_ref[part, i * known : (i + 1) * known, here])
            if i == 0:
                pieces.append(last[0][part * half : (part + 1) * half, here])
            else:
                at = (2 * (i - 1) + part) * half
                pieces.append(last[1][at : at + half, here])
        return jnp.concatenate(pieces, axis=0)

    def products(i):
        start, width = tiles[i]
        for part in range(2):
            buffers[i % 2][part, :, :width] = jnp.dot(
                rho_ref[...], rows_of(part, start, width), preferred_element_type=f32
            )

    def rotate(i):
        start, width = tiles[i]
        buffer = buffers[i % 2]
        for a in range(0, width, LANES):
            at = pl.ds(pl.multiple_of(me_ref[0] * span + start + a, LANES), LANES)
            numer_re = jnp.zeros((rows, LANES), f32)
            numer_im = jnp.zeros((rows, LANES), f32)
            for r in range(poses):
                cos_r = cos_ref[r : r + 1, at]
                sin_r = sin_ref[r : r + 1, at]
                s_re = buffer[0, r * rows : (r + 1) * rows, a : a + LANES]
                s_im = buffer[1, r * rows : (r + 1) * rows, a : a + LANES]
                numer_re = numer_re + s_re * cos_r + s_im * sin_r
                numer_im = numer_im + s_im * cos_r - s_re * sin_r
            here = slice(start + a, start + a + LANES)
            denom = denom_ref[:, here]
            out_ref[:, 0, here] = numer_re / denom
            out_ref[:, 1, here] = numer_im / denom

    products(0)
    for i in range(1, len(tiles)):
        products(i)
        rotate(i - 1)
    rotate(len(tiles) - 1)


def finish(me, weight, cos_t, sin_t, rows, payloads, last, cls_rows, half):
    poses = cos_t.shape[0]
    span = rows.shape[2]
    particles = len(payloads) * payloads[0].shape[1] // 2
    return call(
        functools.partial(finish_kernel, poses, weight.shape[0], len(payloads), half),
        "finish",
        [SMEM] + [VMEM] * (4 + len(payloads) + len(last)),
        [jax.ShapeDtypeStruct((cls_rows, 2, span), f32)],
        (me, weight, cos_t, sin_t, rows, *payloads, *last),
        [
            pltpu.VMEM((poses * cls_rows, particles), bf16),
            pltpu.VMEM((cls_rows, span), f32),
            pltpu.VMEM((2, poses * cls_rows, 256), f32),
            pltpu.VMEM((2, poses * cls_rows, 256), f32),
        ],
        flops=4 * poses * cls_rows * particles * span,
        limit=VMEM_LIMIT if particles <= 512 else 2 * VMEM_LIMIT,
    )[0]


def swap(values, axis, distance):
    size = lax.axis_size(axis)
    return lax.ppermute(values, axis, [(i, i ^ distance) for i in range(size)])


def local(particles, classes, ctf, noise_weight, group_ids, shifts):
    half, _, freq = particles.shape
    cls_rows = classes.shape[0]
    poses = shifts.shape[0]
    n_cls = lax.axis_size("cls")
    n_img = lax.axis_size("img")
    span = freq // n_img
    pairwise = n_cls == 4
    me_cls = lax.axis_index("cls") if pairwise else 0
    me = jnp.stack([lax.axis_index("img"), me_cls]).astype(jnp.int32)
    others = tuple(range(n_img - 1, 0, -1))

    own, *own_chunks = weigh(particles, ctf, noise_weight, group_ids)
    if pairwise:
        far = [swap(w, "cls", 2) for w in own_chunks]
        near = swap(own, "cls", 1)
        mine, *outgoing = cut_slices(me, [[own]], [(d, 0) for d in (0,) + others[:-1]], span, freq)
        slices = [mine] + [swap(w, "img", d) for w, d in zip(outgoing, others)]
    else:
        shards = [[lax.all_gather(own, "cls", axis=0, tiled=True)]]
        mine, *outgoing = cut_slices(me, shards, [(d, 0) for d in (0,) + others], span, freq)
        slices = [[w] for w in [mine] + [swap(w, "img", d) for w, d in zip(outgoing, others)]]

    cos_t, sin_t, power, split, weight = prepare(shifts, classes, ctf, noise_weight)
    early = early_templates(split, cos_t, sin_t)
    if pairwise:
        far, near, slices, split, early = lax.optimization_barrier(
            (far, near, slices, split, early)
        )
        third = [swap(w, "cls", 1) for w in far]
        targets = [(d, 1) for d in (0,) + others[:-1]] + [(others[-1], 0)]
        mine, *outgoing = cut_slices(me, [[own], [near], far], targets, span, freq)
        arrived = [mine] + [swap(w, "img", d) for w, d in zip(outgoing, others)]
        shards = [[own], [near], far, third]
    temps = all_templates(early, split, cos_t, sin_t)
    scores, marks, stat = score(temps, power, shards, half)
    if pairwise:
        stat, arrived[-1] = lax.optimization_barrier((stat, arrived[-1]))
        stats = [stat] + [swap(stat, "cls", k) for k in range(1, n_cls)]
        paired = tuple(range(n_cls))
        last = [*cut_slices(me, [third], [(0, 0)], span, freq)]
        last.append(swap(bundle(arrived[1:], 2 * half), "cls", 1))
        slices = [[a, b] for a, b in zip(slices, arrived)] + [arrived[-1:]]
    else:
        stats = [lax.all_gather(stat, "cls", axis=0, tiled=True)]
        paired = (0,)
        last = []
    norm, payload = responsibilities(scores, marks, stats, paired, poses, half)
    payloads = [payload] + [swap(payload, "img", d) for d in others]
    log_resp, weight_here, rows = gather_rows(
        me, scores, norm, weight, slices, poses, half, span
    )
    averages = finish(me, weight_here, cos_t, sin_t, rows, payloads, last, cls_rows, half)
    return (log_resp.T, averages)


def solution(mesh):
    placed = (
        P(("groups", "img", "cls"), None, None),
        P(("groups", "cls"), None, None),
        P("groups", None),
        P("groups"),
        P(("groups", "img", "cls")),
        P("groups", None),
    )
    return jax.shard_map(
        local,
        mesh=mesh,
        in_specs=placed,
        out_specs=(P(("groups", "img"), "cls"), P(("groups", "cls"), None, "img")),
        check_vma=False,
    )
```

```python
import functools

import jax
import jax.numpy as jnp
from jax import lax
from jax.experimental import pallas as pl
from jax.experimental.pallas import tpu as pltpu
from jax.sharding import PartitionSpec as P

BOX = 128
CHUNKS = 2
LANES = 128
VMEM_LIMIT = 24 * 1024 * 1024
GATHER_FLOPS = 20_000_000_000

prior_precision = 0.02

NT = (((1,), (1,)), ((), ()))
NN = (((1,), (0,)), ((), ()))
HIGHEST = lax.Precision.HIGHEST
f32 = jnp.float32
bf16 = jnp.bfloat16

SMEM = pl.BlockSpec(memory_space=pltpu.SMEM)
VMEM = pl.BlockSpec(memory_space=pltpu.VMEM)
ANY = pl.BlockSpec(memory_space=pl.ANY)


def call(kernel, name, in_specs, out_shape, operands, scratch=(), flops=0, moved=0, limit=VMEM_LIMIT):
    return pl.pallas_call(
        kernel,
        in_specs=in_specs,
        out_specs=[VMEM] * len(out_shape),
        out_shape=out_shape,
        scratch_shapes=list(scratch),
        compiler_params=pltpu.CompilerParams(vmem_limit_bytes=limit),
        cost_estimate=pl.CostEstimate(flops=flops, bytes_accessed=moved, transcendentals=0),
        name=name,
    )(*operands)


def real_index(shape, axis, half):
    return lax.rem(lax.broadcasted_iota(jnp.int32, shape, axis) // half, 2) == 0


def weigh_kernel(ids_hbm, p_hbm, ctf_hbm, nw_hbm, *refs):
    out_refs, (ids_ref, p_ref, ctf_ref, nw_ref, scale_ref, sem) = refs[:-6], refs[-6:]
    count, _, freq = p_ref.shape
    copies = [
        pltpu.make_async_copy(source, target, sem.at[i])
        for i, (source, target) in enumerate(
            [(ids_hbm, ids_ref), (ctf_hbm, ctf_ref), (nw_hbm, nw_ref), (p_hbm, p_ref)]
        )
    ]
    for copy in copies:
        copy.start()
    copies[0].wait()
    row = lax.rem(lax.broadcasted_iota(jnp.int32, (2 * count, LANES), 0), count)
    ids = jnp.zeros((2 * count, LANES), f32)
    for n in range(count):
        ids = jnp.where(row == n, ids_ref[n].astype(f32), ids)
    for copy in copies[1:]:
        copy.wait()
    noise = nw_ref[...].reshape(1, freq)
    for n in range(count):
        scale_ref[n : n + 1, :] = ctf_ref[pl.ds(ids_ref[n], 1), :] * noise
    scale = scale_ref[...]
    values = p_ref[...].astype(f32)
    chunk = freq // CHUNKS
    for part in range(2):
        weighted = (values[:, part, :] * scale).astype(bf16)
        here = slice(part * count, (part + 1) * count)
        out_refs[0][here, :freq] = weighted
        for c, out_ref in enumerate(out_refs[1:]):
            out_ref[here, :chunk] = weighted[:, c * chunk : (c + 1) * chunk]
    for out_ref in out_refs[:2]:
        out_ref[:, out_ref.shape[1] - LANES :] = ids.astype(bf16)


def weigh(particles, ctf, noise_weight, group_ids):
    rows, _, freq = particles.shape
    operands = (group_ids, particles, ctf, noise_weight)
    return call(
        weigh_kernel,
        "weigh",
        [ANY] * 4,
        [
            jax.ShapeDtypeStruct((2 * rows, width), bf16)
            for width in [freq + LANES, freq // CHUNKS + LANES] + [freq // CHUNKS] * (CHUNKS - 1)
        ],
        [pltpu.with_memory_space_constraint(x, pltpu.HBM) for x in operands],
        [
            pltpu.SMEM((rows,), jnp.int32),
            pltpu.VMEM(particles.shape, bf16),
            pltpu.VMEM(ctf.shape, f32),
            pltpu.VMEM((freq,), f32),
            pltpu.VMEM((rows, freq), f32),
            pltpu.SemaphoreType.DMA((4,)),
        ],
        flops=4 * rows * freq,
        moved=16 * rows * freq,
    )


def prepare_kernel(
    shifts_ref, cls_ref, ctf_hbm, nw_hbm, cos_ref, sin_ref, pow_ref, cw_ref, *scratch
):
    ctf_ref, nw_ref, angle_ref, sem = scratch
    freq = cls_ref.shape[2]
    poses = cos_ref.shape[0]
    copies = [
        pltpu.make_async_copy(source, target, sem.at[i])
        for i, (source, target) in enumerate(
            [(ctf_hbm, ctf_ref), (nw_hbm, nw_ref)]
        )
    ]
    for copy in copies:
        copy.start()
    lane = lax.broadcasted_iota(jnp.int32, (1, BOX), 1).astype(f32)
    step = 2.0 * jnp.pi / BOX
    for r in range(poses):
        angle_ref[0, r : r + 1, :] = step * (shifts_ref[0, r].astype(f32) * (lane - BOX // 2))
        angle_ref[1, r : r + 1, :] = step * (shifts_ref[1, r].astype(f32) * lane)
    x_cos, x_sin = jnp.cos(angle_ref[0]), jnp.sin(angle_ref[0])
    y_cos, y_sin = jnp.cos(angle_ref[1]), jnp.sin(angle_ref[1])
    for t in range(freq // BOX):
        c = jnp.broadcast_to(y_cos[:, t : t + 1], x_cos.shape)
        s = jnp.broadcast_to(y_sin[:, t : t + 1], x_cos.shape)
        cos_ref[:, t * BOX : (t + 1) * BOX] = x_cos * c - x_sin * s
        sin_ref[:, t * BOX : (t + 1) * BOX] = x_sin * c + x_cos * s
    for copy in copies:
        copy.wait()
    noise = nw_ref[...].reshape(1, freq)
    cut = freq // 4
    power = jnp.zeros(pow_ref.shape, f32)
    for q in range(4):
        at = slice(q * cut, (q + 1) * cut)
        re = cls_ref[0, :, at].astype(f32)
        im = cls_ref[1, :, at].astype(f32)
        ctf = ctf_ref[:, at]
        weight = ctf * ctf * noise[:, at]
        cw_ref[:, at] = weight
        power += lax.dot_general(
            re * re + im * im, weight, NT, precision=HIGHEST, preferred_element_type=f32
        )
    pow_ref[...] = power


def prepare(shifts, split, ctf, noise_weight):
    _, rows, freq = split.shape
    poses, groups = shifts.shape[0], ctf.shape[0]
    return call(
        prepare_kernel,
        "prepare",
        [SMEM, VMEM, ANY, ANY],
        [
            jax.ShapeDtypeStruct((poses, freq), f32),
            jax.ShapeDtypeStruct((poses, freq), f32),
            jax.ShapeDtypeStruct((rows, groups), f32),
            jax.ShapeDtypeStruct((groups, freq), f32),
        ],
        (
            shifts.T,
            split,
            *[pltpu.with_memory_space_constraint(x, pltpu.HBM) for x in (ctf, noise_weight)],
        ),
        [
            pltpu.VMEM(ctf.shape, f32),
            pltpu.VMEM((freq,), f32),
            pltpu.VMEM((2, poses, BOX), f32),
            pltpu.SemaphoreType.DMA((2,)),
        ],
        flops=24 * rows * groups * freq,
    )


def write_templates(cls_ref, cos_ref, sin_ref, temp_ref, start, tile):
    rows = cls_ref.shape[1]
    for a in range(0, tile, LANES):
        at = pl.ds(pl.multiple_of(start + a, LANES), LANES)
        re = cls_ref[0, :, at].astype(f32)
        im = cls_ref[1, :, at].astype(f32)
        for r in range(cos_ref.shape[0]):
            cos_r = cos_ref[r : r + 1, at]
            sin_r = sin_ref[r : r + 1, at]
            here = slice(r * rows, (r + 1) * rows)
            temp_ref[here, a : a + LANES] = (re * cos_r - im * sin_r).astype(bf16)
            temp_ref[here, tile + a : tile + a + LANES] = (re * sin_r + im * cos_r).astype(bf16)


def template_tile(freq):
    return max(t for t in range(LANES, 385, LANES) if freq // CHUNKS % t == 0)


def early_kernel(cls_ref, cos_ref, sin_ref, temp_ref):
    write_templates(cls_ref, cos_ref, sin_ref, temp_ref, 0, cls_ref.shape[2])


def early_templates(split, cos_t, sin_t):
    _, rows, freq = split.shape
    poses = cos_t.shape[0]
    tile = template_tile(freq)
    count = freq // tile // 2
    skip = freq // tile - count
    return pl.pallas_call(
        early_kernel,
        grid=(count,),
        in_specs=[
            pl.BlockSpec((2, rows, tile), lambda j: (0, 0, skip + j)),
            pl.BlockSpec((poses, tile), lambda j: (0, skip + j)),
            pl.BlockSpec((poses, tile), lambda j: (0, skip + j)),
        ],
        out_specs=pl.BlockSpec((None, poses * rows, 2 * tile), lambda j: (j, 0, 0)),
        out_shape=pltpu.HBM((count, poses * rows, 2 * tile), bf16),
        compiler_params=pltpu.CompilerParams(vmem_limit_bytes=VMEM_LIMIT),
        cost_estimate=pl.CostEstimate(
            flops=20 * poses * rows * freq, bytes_accessed=2 * poses * rows * freq, transcendentals=0
        ),
        name="early_templates",
    )(split, cos_t, sin_t)


def regroup(refs, counts):
    refs = list(refs)
    return [[refs.pop(0) for _ in range(count)] for count in counts]


def tile_of_particles(shards, chunk, span, t, tile, half):
    cuts = []
    for ref, chunked in shards:
        at = t * tile if chunked else chunk * span + t * tile
        cuts.append(ref[:, at : at + tile])
    wide = jnp.concatenate(cuts, axis=0).astype(f32)
    real = real_index(wide.shape, 0, half)
    return jnp.concatenate(
        [jnp.where(real, wide, 0.0).astype(bf16), jnp.where(real, 0.0, wide).astype(bf16)], axis=1
    )


def first_score_kernel(chunked, half, early_hbm, cls_ref, cos_ref, sin_ref, *refs):
    refs, (acc_ref, late_ref, *buffers, sem) = refs[:-5], refs[-5:]
    count, _, width = late_ref.shape
    tile = width // 2
    copies = [
        pltpu.make_async_copy(early_hbm.at[t], late_ref.at[t], sem.at[t]) for t in range(count)
    ]
    for copy in copies:
        copy.start()
    shards = list(zip(refs, chunked))
    built = cls_ref.shape[2] // tile - count
    acc_ref[...] = jnp.zeros_like(acc_ref)
    write_templates(cls_ref, cos_ref, sin_ref, buffers[0], 0, tile)
    for t in range(built):
        if t + 1 < built:
            write_templates(cls_ref, cos_ref, sin_ref, buffers[(t + 1) % 2], (t + 1) * tile, tile)
        acc_ref[...] += lax.dot_general(
            buffers[t % 2][...],
            tile_of_particles(shards, 0, built * tile, t, tile, half),
            NT,
            preferred_element_type=f32,
        )
    for copy in copies:
        copy.wait()


def last_score_kernel(chunked, half, temp_ref, pow_ref, acc_ref, *refs):
    refs, (s_ref, marks_ref, stat_ref) = refs[:-3], refs[-3:]
    tail_refs, shards = refs[: len(chunked)], list(zip(refs[len(chunked) :], chunked))
    count, _, width = temp_ref.shape
    tile = width // 2
    rows, groups = pow_ref.shape
    lanes = s_ref.shape[1]
    poses = s_ref.shape[0] // rows
    tails = [ref[:, ref.shape[1] - LANES :] for ref in tail_refs]
    ids = jnp.concatenate(tails, axis=0).astype(f32)
    group = lax.broadcasted_iota(jnp.int32, (lanes, groups), 1).astype(f32)
    marks = (ids[:, :groups] == group).astype(f32)
    marks_ref[...] = marks
    penalty = lax.dot_general(
        pow_ref[...], marks, NT, precision=HIGHEST, preferred_element_type=f32
    )
    s_ref[...] = acc_ref[...]
    for t in range(count):
        s_ref[...] += lax.dot_general(
            temp_ref[t],
            tile_of_particles(shards, 1, count * tile, t, tile, half),
            NT,
            preferred_element_type=f32,
        )
    acc = s_ref[...]
    acc = acc + jnp.where(
        real_index(acc.shape, 1, half), pltpu.roll(acc, lanes - half, 1), pltpu.roll(acc, half, 1)
    )
    scores = acc.reshape(poses, rows, lanes) - 0.5 * penalty[None]
    peak = jnp.max(jnp.max(scores, axis=0), axis=0, keepdims=True)
    total = jnp.sum(jnp.sum(jnp.exp(scores - peak[None]), axis=0), axis=0, keepdims=True)
    s_ref[...] = scores.reshape(poses * rows, lanes)
    stat_ref[0:1, :] = peak
    stat_ref[1:2, :] = total
    stat_ref[2:8, :] = jnp.zeros((6, lanes), f32)


def score(early, split, cos_t, sin_t, power, shards, half):
    count, columns, width = early.shape
    lanes = sum(refs[0].shape[0] for refs in shards)
    chunked = [len(refs) > 1 for refs in shards]
    flops = 2 * columns * 256 * count * width
    acc_shape = jax.ShapeDtypeStruct((columns, lanes), f32)
    operands = [pltpu.with_memory_space_constraint(early, pltpu.HBM), split, cos_t, sin_t]
    operands += [refs[0] for refs in shards]
    acc, late = call(
        functools.partial(first_score_kernel, chunked, half),
        "score0",
        [ANY] + [VMEM] * (len(operands) - 1),
        [acc_shape, pltpu.VMEM(early.shape, bf16)],
        operands,
        [
            pltpu.VMEM((columns, width), bf16),
            pltpu.VMEM((columns, width), bf16),
            pltpu.SemaphoreType.DMA((count,)),
        ],
        flops=4 * flops,
    )
    operands = [late, power, acc, *[refs[0] for refs in shards], *[refs[-1] for refs in shards]]
    return call(
        functools.partial(last_score_kernel, chunked, half),
        "score1",
        [VMEM] * len(operands),
        [
            acc_shape,
            jax.ShapeDtypeStruct((lanes, power.shape[1]), f32),
            jax.ShapeDtypeStruct((8, lanes), f32),
        ],
        operands,
        flops=flops,
    )


def slices_kernel(counts, targets, me_ref, *refs):
    whole_ref, refs = refs[-1], refs[:-1]
    shards, out_refs = regroup(refs[: -len(targets)], counts), refs[-len(targets) :]
    span = out_refs[0].shape[1]
    filled = [0] * len(targets)
    for k, refs in enumerate(shards):
        source = refs[0]
        height = source.shape[0]
        if len(refs) > 1:
            width = refs[-1].shape[1]
            for c, ref in enumerate(refs):
                whole_ref[:, c * width : (c + 1) * width] = ref[:, :width]
            source = whole_ref
        for i, (distance, skip) in enumerate(targets):
            if k >= skip:
                base = pl.multiple_of((me_ref[0] ^ distance) * span, LANES)
                out_refs[i][filled[i] : filled[i] + height, :] = source[:, pl.ds(base, span)]
                filled[i] += height


def cut_slices(me, shards, targets, span, freq):
    heights = [refs[0].shape[0] for refs in shards]
    operands = [me, *[ref for refs in shards for ref in refs]]
    out_heights = [sum(heights[skip:]) for _, skip in targets]
    return call(
        functools.partial(slices_kernel, [len(refs) for refs in shards], targets),
        "cut_slices",
        [SMEM] + [VMEM] * (len(operands) - 1),
        [jax.ShapeDtypeStruct((height, span), bf16) for height in out_heights],
        operands,
        [pltpu.VMEM((heights[-1], freq), bf16)],
        moved=4 * span * sum(out_heights),
        limit=VMEM_LIMIT if sum(heights) <= 128 else 2 * VMEM_LIMIT,
    )


def bundle_kernel(*refs):
    sources, out_ref = refs[:-1], refs[-1]
    rows = out_ref.shape[0] // len(sources)
    for i, ref in enumerate(sources):
        out_ref[i * rows : (i + 1) * rows, :] = ref[ref.shape[0] - rows :, :]


def bundle(slices, rows):
    span = slices[0].shape[1]
    return call(
        bundle_kernel,
        "bundle",
        [VMEM] * len(slices),
        [jax.ShapeDtypeStruct((len(slices) * rows, span), bf16)],
        slices,
        moved=4 * len(slices) * rows * span,
    )[0]


def xor_blocks(values, block, distance):
    lanes = values.shape[1]
    lane = lax.broadcasted_iota(jnp.int32, values.shape, 1)
    width = block
    while distance:
        if distance % 2:
            low = lax.rem(lane // width, 2) == 0
            values = jnp.where(
                low, pltpu.roll(values, lanes - width, 1), pltpu.roll(values, width, 1)
            )
        distance //= 2
        width *= 2
    return values


def rho_kernel(poses, half, paired, s_ref, marks_ref, *refs):
    stat_refs, (norm_ref, out_ref) = refs[: len(paired)], refs[len(paired) :]
    lanes = s_ref.shape[1]
    rows = s_ref.shape[0] // poses
    groups = marks_ref.shape[1]
    block = 2 * half
    peaks, totals = [], []
    for ref, distance in zip(stat_refs, paired):
        for at in range(0, ref.shape[0], 8):
            stats = xor_blocks(ref[at : at + 8, :], block, distance)
            peaks.append(stats[0:1])
            totals.append(stats[1:2])
    peak = functools.reduce(jnp.maximum, peaks)
    total = sum(t * jnp.exp(p - peak) for t, p in zip(totals, peaks))
    log_norm = peak + jnp.log(total)
    norm_ref[...] = log_norm
    rho = jnp.exp(s_ref[...].reshape(poses, rows, lanes) - log_norm[None])
    mass = lax.dot_general(
        jnp.where(real_index((rows, lanes), 1, half), jnp.sum(rho, axis=0), 0.0),
        marks_ref[...],
        NN,
        precision=HIGHEST,
        preferred_element_type=f32,
    )
    high = mass.astype(bf16)
    low = (mass - high.astype(f32)).astype(bf16)
    rho_low = rho.reshape(poses * rows, lanes).astype(bf16)
    cut = poses // 2 * rows
    lane = lax.broadcasted_iota(jnp.int32, (lanes, lanes), 0)
    column = lax.broadcasted_iota(jnp.int32, (lanes, lanes), 1)
    particle = lane // block * half + lax.rem(lane, block)
    real = lax.rem(lane, block) < half
    first = (real & (column == particle)).astype(f32).astype(bf16)
    second = (real & (column == particle + lanes // 2)).astype(f32).astype(bf16)
    packed = jnp.dot(rho_low[:cut], first, preferred_element_type=f32)
    packed += jnp.dot(rho_low[cut:], second, preferred_element_type=f32)
    out_ref[:cut, :] = packed.astype(bf16)
    if lanes > 2 * groups:
        out_ref[cut:, :] = jnp.zeros((rows, lanes), bf16)
    out_ref[cut:, :groups] = high
    out_ref[cut:, groups : 2 * groups] = low


def responsibilities(scores, marks, stats, paired, poses, half):
    columns, lanes = scores.shape
    return call(
        functools.partial(rho_kernel, poses, half, paired),
        "responsibilities",
        [VMEM] * (2 + len(stats)),
        [
            jax.ShapeDtypeStruct((1, lanes), f32),
            jax.ShapeDtypeStruct((columns // 2 + columns // poses, lanes), bf16),
        ],
        (scores, marks, *stats),
        flops=40 * columns * lanes,
    )


def gather_kernel(poses, half, counts, me_ref, s_ref, norm_ref, weight_ref, *refs):
    w_refs, (resp_ref, cw_ref, rows_ref) = refs[:-3], refs[-3:]
    span = rows_ref.shape[2]
    block = 2 * half
    here = pl.ds(pl.multiple_of(me_ref[0] * span, LANES), span)
    at = 0
    for refs in regroup(w_refs, counts):
        for ref in refs:
            for start in range(0, ref.shape[0], block):
                rows_ref[0, at : at + half, :] = ref[start : start + half, :]
                rows_ref[1, at : at + half, :] = ref[start + half : start + block, :]
                at += half
    weight = weight_ref[:, here]
    high = weight.astype(bf16)
    cw_ref[:, :span] = high
    cw_ref[:, span:] = (weight - high.astype(f32)).astype(bf16)
    rows = resp_ref.shape[0]
    lanes = s_ref.shape[1]
    scores = s_ref[...].reshape(poses, rows, lanes)
    pose_peak = jnp.max(scores, axis=0)
    total = jnp.sum(jnp.exp(scores - pose_peak[None]), axis=0)
    log_resp = pose_peak + jnp.log(total) - norm_ref[...]
    shape = (resp_ref.shape[1], lanes)
    lane = lax.broadcasted_iota(jnp.int32, shape, 1)
    row = ((lane // block) ^ me_ref[1]) * half + lax.rem(lane, block)
    take = (lax.broadcasted_iota(jnp.int32, shape, 0) == row) & (lax.rem(lane, block) < half)
    resp_ref[...] = lax.dot_general(
        log_resp, take.astype(f32), NT, precision=HIGHEST, preferred_element_type=f32
    )


def gather_rows(me, scores, norm, weight, slices, poses, half, span):
    columns, lanes = scores.shape
    counts = [len(refs) for refs in slices]
    slices = [w for refs in slices for w in refs]
    particles = sum(w.shape[0] for w in slices) // 2
    return call(
        functools.partial(gather_kernel, poses, half, counts),
        "gather_rows",
        [SMEM] + [VMEM] * (3 + len(slices)),
        [
            jax.ShapeDtypeStruct((columns // poses, lanes // 2), f32),
            jax.ShapeDtypeStruct((weight.shape[0], 2 * span), bf16),
            jax.ShapeDtypeStruct((2, particles, span), bf16),
        ],
        (me, scores, norm, weight, *slices),
        flops=GATHER_FLOPS,
        moved=8 * particles * span,
        limit=VMEM_LIMIT if particles <= 512 else 2 * VMEM_LIMIT,
    )


def finish_kernel(poses, groups, sources, half, me_ref, cw_ref, cos_ref, sin_ref, rows_ref, *refs):
    payloads, refs = refs[:sources], refs[sources:]
    last, (out_ref, rho_ref, inverse_ref, *buffers) = refs[:-5], refs[-5:]
    rows, _, span = out_ref.shape
    cut = poses // 2 * rows
    count = payloads[0].shape[1] // 2
    mass = jnp.zeros((rows, groups), f32)
    for i, ref in enumerate(payloads):
        rho_ref[:cut, i * count : (i + 1) * count] = ref[:cut, :count]
        rho_ref[cut:, i * count : (i + 1) * count] = ref[:cut, count:]
        mass += ref[cut:, :groups].astype(f32) + ref[cut:, groups : 2 * groups].astype(f32)
    high = mass.astype(bf16)
    mass = jnp.concatenate([high, (mass - high.astype(f32)).astype(bf16)], axis=0)
    terms = jnp.dot(mass, cw_ref[...], preferred_element_type=f32)
    denom = (terms[:rows, :span] + terms[rows:, :span]) + (terms[:rows, span:] + terms[rows:, span:])
    inverse_ref[...] = 1.0 / (denom + prior_precision)
    tiles = [(a, min(256, span - a)) for a in range(0, span, 256)]
    known = rows_ref.shape[1] // sources

    def rows_of(part, start, width):
        here = slice(start, start + width)
        if not last:
            return rows_ref[part, :, here]
        pieces = []
        for i in range(sources):
            pieces.append(rows_ref[part, i * known : (i + 1) * known, here])
            if i == 0:
                pieces.append(last[0][part * half : (part + 1) * half, here])
            else:
                at = (2 * (i - 1) + part) * half
                pieces.append(last[1][at : at + half, here])
        return jnp.concatenate(pieces, axis=0)

    def products(i):
        start, width = tiles[i]
        for part in range(2):
            buffers[i % 2][part, :, :width] = jnp.dot(
                rho_ref[...], rows_of(part, start, width), preferred_element_type=f32
            )

    def rotate(i):
        start, width = tiles[i]
        buffer = buffers[i % 2]
        for a in range(0, width, LANES):
            at = pl.ds(pl.multiple_of(me_ref[0] * span + start + a, LANES), LANES)
            numer_re = jnp.zeros((rows, LANES), f32)
            numer_im = jnp.zeros((rows, LANES), f32)
            for r in range(poses):
                cos_r = cos_ref[r : r + 1, at]
                sin_r = sin_ref[r : r + 1, at]
                s_re = buffer[0, r * rows : (r + 1) * rows, a : a + LANES]
                s_im = buffer[1, r * rows : (r + 1) * rows, a : a + LANES]
                numer_re = numer_re + s_re * cos_r + s_im * sin_r
                numer_im = numer_im + s_im * cos_r - s_re * sin_r
            here = slice(start + a, start + a + LANES)
            inverse = inverse_ref[:, here]
            out_ref[:, 0, here] = numer_re * inverse
            out_ref[:, 1, here] = numer_im * inverse

    products(0)
    for i in range(1, len(tiles)):
        products(i)
        rotate(i - 1)
    rotate(len(tiles) - 1)


def finish(me, weight, cos_t, sin_t, rows, payloads, last, cls_rows, half):
    poses = cos_t.shape[0]
    span = rows.shape[2]
    particles = len(payloads) * payloads[0].shape[1] // 2
    return call(
        functools.partial(finish_kernel, poses, weight.shape[0], len(payloads), half),
        "finish",
        [SMEM] + [VMEM] * (4 + len(payloads) + len(last)),
        [jax.ShapeDtypeStruct((cls_rows, 2, span), f32)],
        (me, weight, cos_t, sin_t, rows, *payloads, *last),
        [
            pltpu.VMEM((poses * cls_rows, particles), bf16),
            pltpu.VMEM((cls_rows, span), f32),
            pltpu.VMEM((2, poses * cls_rows, 256), f32),
            pltpu.VMEM((2, poses * cls_rows, 256), f32),
        ],
        flops=4 * poses * cls_rows * particles * span,
        limit=VMEM_LIMIT if particles <= 512 else 2 * VMEM_LIMIT,
    )[0]


def swap(values, axis, distance):
    size = lax.axis_size(axis)
    return lax.ppermute(values, axis, [(i, i ^ distance) for i in range(size)])


def local(particles, classes, ctf, noise_weight, group_ids, shifts):
    half, _, freq = particles.shape
    cls_rows = classes.shape[0]
    poses = shifts.shape[0]
    n_cls = lax.axis_size("cls")
    n_img = lax.axis_size("img")
    span = freq // n_img
    pairwise = n_cls == 4
    me_cls = lax.axis_index("cls") if pairwise else 0
    me = jnp.stack([lax.axis_index("img"), me_cls]).astype(jnp.int32)
    others = tuple(range(n_img - 1, 0, -1))

    own, *own_chunks = weigh(particles, ctf, noise_weight, group_ids)
    if pairwise:
        far = [swap(w, "cls", 2) for w in own_chunks]
        near = swap(own, "cls", 1)
        mine, *outgoing = cut_slices(me, [[own]], [(d, 0) for d in (0,) + others[:-1]], span, freq)
        slices = [mine] + [swap(w, "img", d) for w, d in zip(outgoing, others)]
    else:
        shards = [[lax.all_gather(own, "cls", axis=0, tiled=True)]]
        mine, *outgoing = cut_slices(me, shards, [(d, 0) for d in (0,) + others], span, freq)
        slices = [[w] for w in [mine] + [swap(w, "img", d) for w, d in zip(outgoing, others)]]

    split = jnp.transpose(classes, (1, 0, 2))
    cos_t, sin_t, power, weight = prepare(shifts, split, ctf, noise_weight)
    early = early_templates(split, cos_t, sin_t)
    if pairwise:
        far, near, slices, split, early = lax.optimization_barrier(
            (far, near, slices, split, early)
        )
        third = [swap(w, "cls", 1) for w in far]
        targets = [(d, 1) for d in (0,) + others[:-1]] + [(others[-1], 0)]
        mine, *outgoing = cut_slices(me, [[own], [near], far], targets, span, freq)
        arrived = [mine] + [swap(w, "img", d) for w, d in zip(outgoing, others)]
        shards = [[own], [near], far, third]
    scores, marks, stat = score(early, split, cos_t, sin_t, power, shards, half)
    if pairwise:
        stat, arrived[-1] = lax.optimization_barrier((stat, arrived[-1]))
        stats = [stat] + [swap(stat, "cls", k) for k in range(1, n_cls)]
        paired = tuple(range(n_cls))
        last = [*cut_slices(me, [third], [(0, 0)], span, freq)]
        last.append(swap(bundle(arrived[1:], 2 * half), "cls", 1))
        slices = [[a, b] for a, b in zip(slices, arrived)] + [arrived[-1:]]
    else:
        stats = [lax.all_gather(stat, "cls", axis=0, tiled=True)]
        paired = (0,)
        last = []
    norm, payload = responsibilities(scores, marks, stats, paired, poses, half)
    payloads = [payload] + [swap(payload, "img", d) for d in others]
    log_resp, weight_here, rows = gather_rows(
        me, scores, norm, weight, slices, poses, half, span
    )
    averages = finish(me, weight_here, cos_t, sin_t, rows, payloads, last, cls_rows, half)
    return (log_resp.T, averages)


def solution(mesh):
    placed = (
        P(("groups", "img", "cls"), None, None),
        P(("groups", "cls"), None, None),
        P("groups", None),
        P("groups"),
        P(("groups", "img", "cls")),
        P("groups", None),
    )
    return jax.shard_map(
        local,
        mesh=mesh,
        in_specs=placed,
        out_specs=(P(("groups", "img"), "cls"), P(("groups", "cls"), None, "img")),
        check_vma=False,
    )
```

```python
import functools

import jax
import jax.numpy as jnp
from jax import lax
from jax.experimental import pallas as pl
from jax.experimental.pallas import tpu as pltpu
from jax.sharding import PartitionSpec as P

BOX = 128
CHUNKS = 2
LANES = 128
VMEM_LIMIT = 24 * 1024 * 1024
GATHER_FLOPS = 20_000_000_000

prior_precision = 0.02

NT = (((1,), (1,)), ((), ()))
NN = (((1,), (0,)), ((), ()))
HIGHEST = lax.Precision.HIGHEST
f32 = jnp.float32
bf16 = jnp.bfloat16

SMEM = pl.BlockSpec(memory_space=pltpu.SMEM)
VMEM = pl.BlockSpec(memory_space=pltpu.VMEM)
ANY = pl.BlockSpec(memory_space=pl.ANY)


def call(kernel, name, in_specs, out_shape, operands, scratch=(), flops=0, moved=0, limit=VMEM_LIMIT):
    return pl.pallas_call(
        kernel,
        in_specs=in_specs,
        out_specs=[VMEM] * len(out_shape),
        out_shape=out_shape,
        scratch_shapes=list(scratch),
        compiler_params=pltpu.CompilerParams(vmem_limit_bytes=limit),
        cost_estimate=pl.CostEstimate(flops=flops, bytes_accessed=moved, transcendentals=0),
        name=name,
    )(*operands)


def real_index(shape, axis, half):
    return lax.rem(lax.broadcasted_iota(jnp.int32, shape, axis) // half, 2) == 0


def weigh_kernel(ids_hbm, p_hbm, ctf_hbm, nw_hbm, *refs):
    out_refs, (ids_ref, p_ref, ctf_ref, nw_ref, scale_ref, sem) = refs[:-6], refs[-6:]
    count, _, freq = p_ref.shape
    copies = [
        pltpu.make_async_copy(source, target, sem.at[i])
        for i, (source, target) in enumerate(
            [(ids_hbm, ids_ref), (ctf_hbm, ctf_ref), (nw_hbm, nw_ref), (p_hbm, p_ref)]
        )
    ]
    for copy in copies:
        copy.start()
    copies[0].wait()
    row = lax.rem(lax.broadcasted_iota(jnp.int32, (2 * count, LANES), 0), count)
    ids = jnp.zeros((2 * count, LANES), f32)
    for n in range(count):
        ids = jnp.where(row == n, ids_ref[n].astype(f32), ids)
    for copy in copies[1:]:
        copy.wait()
    noise = nw_ref[...].reshape(1, freq)
    for n in range(count):
        scale_ref[n : n + 1, :] = ctf_ref[pl.ds(ids_ref[n], 1), :] * noise
    scale = scale_ref[...]
    values = p_ref[...].astype(f32)
    chunk = freq // CHUNKS
    for part in range(2):
        weighted = (values[:, part, :] * scale).astype(bf16)
        here = slice(part * count, (part + 1) * count)
        out_refs[0][here, :freq] = weighted
        for c, out_ref in enumerate(out_refs[1:]):
            out_ref[here, :chunk] = weighted[:, c * chunk : (c + 1) * chunk]
    for out_ref in out_refs[:2]:
        out_ref[:, out_ref.shape[1] - LANES :] = ids.astype(bf16)


def weigh(particles, ctf, noise_weight, group_ids):
    rows, _, freq = particles.shape
    operands = (group_ids, particles, ctf, noise_weight)
    return call(
        weigh_kernel,
        "weigh",
        [ANY] * 4,
        [
            jax.ShapeDtypeStruct((2 * rows, width), bf16)
            for width in [freq + LANES, freq // CHUNKS + LANES] + [freq // CHUNKS] * (CHUNKS - 1)
        ],
        [pltpu.with_memory_space_constraint(x, pltpu.HBM) for x in operands],
        [
            pltpu.SMEM((rows,), jnp.int32),
            pltpu.VMEM(particles.shape, bf16),
            pltpu.VMEM(ctf.shape, f32),
            pltpu.VMEM((freq,), f32),
            pltpu.VMEM((rows, freq), f32),
            pltpu.SemaphoreType.DMA((4,)),
        ],
        flops=4 * rows * freq,
        moved=16 * rows * freq,
    )


def prepare_kernel(
    shifts_ref, cls_ref, ctf_hbm, nw_hbm, cos_ref, sin_ref, pow_ref, cw_ref, *scratch
):
    ctf_ref, nw_ref, angle_ref, sem = scratch
    freq = cls_ref.shape[2]
    poses = cos_ref.shape[0]
    copies = [
        pltpu.make_async_copy(source, target, sem.at[i])
        for i, (source, target) in enumerate(
            [(ctf_hbm, ctf_ref), (nw_hbm, nw_ref)]
        )
    ]
    for copy in copies:
        copy.start()
    lane = lax.broadcasted_iota(jnp.int32, (1, BOX), 1).astype(f32)
    step = 2.0 * jnp.pi / BOX
    for r in range(poses):
        angle_ref[0, r : r + 1, :] = step * (shifts_ref[0, r].astype(f32) * (lane - BOX // 2))
        angle_ref[1, r : r + 1, :] = step * (shifts_ref[1, r].astype(f32) * lane)
    x_cos, x_sin = jnp.cos(angle_ref[0]), jnp.sin(angle_ref[0])
    y_cos, y_sin = jnp.cos(angle_ref[1]), jnp.sin(angle_ref[1])
    for t in range(freq // BOX):
        c = jnp.broadcast_to(y_cos[:, t : t + 1], x_cos.shape)
        s = jnp.broadcast_to(y_sin[:, t : t + 1], x_cos.shape)
        cos_ref[:, t * BOX : (t + 1) * BOX] = x_cos * c - x_sin * s
        sin_ref[:, t * BOX : (t + 1) * BOX] = x_sin * c + x_cos * s
    for copy in copies:
        copy.wait()
    noise = nw_ref[...].reshape(1, freq)
    cut = freq // 4
    power = jnp.zeros(pow_ref.shape, f32)
    for q in range(4):
        at = slice(q * cut, (q + 1) * cut)
        re = cls_ref[0, :, at].astype(f32)
        im = cls_ref[1, :, at].astype(f32)
        ctf = ctf_ref[:, at]
        weight = ctf * ctf * noise[:, at]
        cw_ref[:, at] = weight
        power += lax.dot_general(
            re * re + im * im, weight, NT, precision=HIGHEST, preferred_element_type=f32
        )
    pow_ref[...] = power


def prepare(shifts, split, ctf, noise_weight):
    _, rows, freq = split.shape
    poses, groups = shifts.shape[0], ctf.shape[0]
    return call(
        prepare_kernel,
        "prepare",
        [SMEM, VMEM, ANY, ANY],
        [
            jax.ShapeDtypeStruct((poses, freq), f32),
            jax.ShapeDtypeStruct((poses, freq), f32),
            jax.ShapeDtypeStruct((rows, groups), f32),
            jax.ShapeDtypeStruct((groups, freq), f32),
        ],
        (
            shifts.T,
            split,
            *[pltpu.with_memory_space_constraint(x, pltpu.HBM) for x in (ctf, noise_weight)],
        ),
        [
            pltpu.VMEM(ctf.shape, f32),
            pltpu.VMEM((freq,), f32),
            pltpu.VMEM((2, poses, BOX), f32),
            pltpu.SemaphoreType.DMA((2,)),
        ],
        flops=24 * rows * groups * freq,
    )


def write_templates(cls_ref, cos_ref, sin_ref, temp_ref, start, tile):
    rows = cls_ref.shape[1]
    for a in range(0, tile, LANES):
        at = pl.ds(pl.multiple_of(start + a, LANES), LANES)
        re = cls_ref[0, :, at].astype(f32)
        im = cls_ref[1, :, at].astype(f32)
        for r in range(cos_ref.shape[0]):
            cos_r = cos_ref[r : r + 1, at]
            sin_r = sin_ref[r : r + 1, at]
            here = slice(r * rows, (r + 1) * rows)
            temp_ref[here, a : a + LANES] = (re * cos_r - im * sin_r).astype(bf16)
            temp_ref[here, tile + a : tile + a + LANES] = (re * sin_r + im * cos_r).astype(bf16)


def template_tile(freq):
    return max(t for t in range(LANES, 385, LANES) if freq // CHUNKS % t == 0)


def early_kernel(cls_ref, cos_ref, sin_ref, temp_ref):
    write_templates(cls_ref, cos_ref, sin_ref, temp_ref, 0, cls_ref.shape[2])


def early_templates(split, cos_t, sin_t):
    _, rows, freq = split.shape
    poses = cos_t.shape[0]
    tile = template_tile(freq)
    count = freq // tile // 2 + 1
    skip = freq // tile - count
    return pl.pallas_call(
        early_kernel,
        grid=(count,),
        in_specs=[
            pl.BlockSpec((2, rows, tile), lambda j: (0, 0, skip + j)),
            pl.BlockSpec((poses, tile), lambda j: (0, skip + j)),
            pl.BlockSpec((poses, tile), lambda j: (0, skip + j)),
        ],
        out_specs=pl.BlockSpec((None, poses * rows, 2 * tile), lambda j: (j, 0, 0)),
        out_shape=pltpu.HBM((count, poses * rows, 2 * tile), bf16),
        compiler_params=pltpu.CompilerParams(vmem_limit_bytes=VMEM_LIMIT),
        cost_estimate=pl.CostEstimate(
            flops=20 * poses * rows * freq, bytes_accessed=2 * poses * rows * freq, transcendentals=0
        ),
        name="early_templates",
    )(split, cos_t, sin_t)


def regroup(refs, counts):
    refs = list(refs)
    return [[refs.pop(0) for _ in range(count)] for count in counts]


def tile_of_particles(shards, chunk, span, t, tile, half):
    cuts = []
    for ref, chunked in shards:
        at = t * tile if chunked else chunk * span + t * tile
        cuts.append(ref[:, at : at + tile])
    wide = jnp.concatenate(cuts, axis=0).astype(f32)
    real = real_index(wide.shape, 0, half)
    return jnp.concatenate(
        [jnp.where(real, wide, 0.0).astype(bf16), jnp.where(real, 0.0, wide).astype(bf16)], axis=1
    )


def start_copies(early_hbm, moves, sem):
    copies = [
        pltpu.make_async_copy(early_hbm.at[source], target, sem.at[i])
        for i, (source, target) in enumerate(moves)
    ]
    for copy in copies:
        copy.start()
    return copies


def template_kernel(early_hbm, cls_ref, cos_ref, sin_ref, temp_ref, late_ref, sem):
    built = temp_ref.shape[0] - 1
    tile = temp_ref.shape[2] // 2
    moves = [(0, temp_ref.at[built])]
    moves += [(1 + t, late_ref.at[t]) for t in range(late_ref.shape[0])]
    copies = start_copies(early_hbm, moves, sem)

    @pl.loop(0, built)
    def _(t):
        write_templates(cls_ref, cos_ref, sin_ref, temp_ref.at[t], t * tile, tile)

    for copy in copies:
        copy.wait()


def first_score_kernel(chunked, half, early_hbm, temp_ref, *refs):
    refs, (acc_ref, late_ref, sem) = refs[:-3], refs[-3:]
    count, _, width = temp_ref.shape
    tile = width // 2
    rest = late_ref.shape[0]
    skip = early_hbm.shape[0] - rest
    copies = start_copies(early_hbm, [(skip + t, late_ref.at[t]) for t in range(rest)], sem)
    shards = list(zip(refs, chunked))
    acc_ref[...] = jnp.zeros_like(acc_ref)
    for t in range(count):
        acc_ref[...] += lax.dot_general(
            temp_ref[t],
            tile_of_particles(shards, 0, count * tile, t, tile, half),
            NT,
            preferred_element_type=f32,
        )
    for copy in copies:
        copy.wait()


def last_score_kernel(chunked, half, temp_ref, rest_ref, pow_ref, acc_ref, *refs):
    refs, (s_ref, marks_ref, stat_ref) = refs[:-3], refs[-3:]
    tail_refs, shards = refs[: len(chunked)], list(zip(refs[len(chunked) :], chunked))
    tile = temp_ref.shape[2] // 2
    temps = [ref.at[t] for ref in (temp_ref, rest_ref) for t in range(ref.shape[0])]
    rows, groups = pow_ref.shape
    lanes = s_ref.shape[1]
    poses = s_ref.shape[0] // rows
    tails = [ref[:, ref.shape[1] - LANES :] for ref in tail_refs]
    ids = jnp.concatenate(tails, axis=0).astype(f32)
    group = lax.broadcasted_iota(jnp.int32, (lanes, groups), 1).astype(f32)
    marks = (ids[:, :groups] == group).astype(f32)
    marks_ref[...] = marks
    penalty = lax.dot_general(
        pow_ref[...], marks, NT, precision=HIGHEST, preferred_element_type=f32
    )
    s_ref[...] = acc_ref[...]
    for t, temp in enumerate(temps):
        s_ref[...] += lax.dot_general(
            temp[...],
            tile_of_particles(shards, 1, len(temps) * tile, t, tile, half),
            NT,
            preferred_element_type=f32,
        )
    acc = s_ref[...]
    acc = acc + jnp.where(
        real_index(acc.shape, 1, half), pltpu.roll(acc, lanes - half, 1), pltpu.roll(acc, half, 1)
    )
    scores = acc.reshape(poses, rows, lanes) - 0.5 * penalty[None]
    peak = jnp.max(jnp.max(scores, axis=0), axis=0, keepdims=True)
    total = jnp.sum(jnp.sum(jnp.exp(scores - peak[None]), axis=0), axis=0, keepdims=True)
    s_ref[...] = scores.reshape(poses * rows, lanes)
    stat_ref[0:1, :] = peak
    stat_ref[1:2, :] = total
    stat_ref[2:8, :] = jnp.zeros((6, lanes), f32)


def score(early, split, cos_t, sin_t, power, shards, half):
    count, columns, width = early.shape
    count -= 1
    some = count // 2
    freq = split.shape[2]
    lanes = sum(refs[0].shape[0] for refs in shards)
    chunked = [len(refs) > 1 for refs in shards]
    flops = 2 * columns * 256 * count * width
    acc_shape = jax.ShapeDtypeStruct((columns, lanes), f32)
    early = pltpu.with_memory_space_constraint(early, pltpu.HBM)
    temps, late = call(
        template_kernel,
        "templates",
        [ANY] + [VMEM] * 3,
        [
            pltpu.VMEM((count, columns, width), bf16),
            pltpu.VMEM((some, columns, width), bf16),
        ],
        (early, split, cos_t, sin_t),
        [pltpu.SemaphoreType.DMA((some + 1,))],
        flops=20 * columns * freq,
        moved=2 * columns * freq,
    )
    operands = [early, temps, *[refs[0] for refs in shards]]
    acc, rest = call(
        functools.partial(first_score_kernel, chunked, half),
        "score0",
        [ANY] + [VMEM] * (len(operands) - 1),
        [acc_shape, pltpu.VMEM((count - some, columns, width), bf16)],
        operands,
        [pltpu.SemaphoreType.DMA((count - some,))],
        flops=flops,
    )
    operands = [late, rest, power, acc]
    operands += [refs[0] for refs in shards] + [refs[-1] for refs in shards]
    return call(
        functools.partial(last_score_kernel, chunked, half),
        "score1",
        [VMEM] * len(operands),
        [
            acc_shape,
            jax.ShapeDtypeStruct((lanes, power.shape[1]), f32),
            jax.ShapeDtypeStruct((8, lanes), f32),
        ],
        operands,
        flops=flops,
    )


def slices_kernel(counts, targets, me_ref, *refs):
    whole_ref, refs = refs[-1], refs[:-1]
    shards, out_refs = regroup(refs[: -len(targets)], counts), refs[-len(targets) :]
    span = out_refs[0].shape[1]
    filled = [0] * len(targets)
    for k, refs in enumerate(shards):
        source = refs[0]
        height = source.shape[0]
        if len(refs) > 1:
            width = refs[-1].shape[1]
            for c, ref in enumerate(refs):
                whole_ref[:, c * width : (c + 1) * width] = ref[:, :width]
            source = whole_ref
        for i, (distance, skip) in enumerate(targets):
            if k >= skip:
                base = pl.multiple_of((me_ref[0] ^ distance) * span, LANES)
                out_refs[i][filled[i] : filled[i] + height, :] = source[:, pl.ds(base, span)]
                filled[i] += height


def cut_slices(me, shards, targets, span, freq):
    heights = [refs[0].shape[0] for refs in shards]
    operands = [me, *[ref for refs in shards for ref in refs]]
    out_heights = [sum(heights[skip:]) for _, skip in targets]
    return call(
        functools.partial(slices_kernel, [len(refs) for refs in shards], targets),
        "cut_slices",
        [SMEM] + [VMEM] * (len(operands) - 1),
        [jax.ShapeDtypeStruct((height, span), bf16) for height in out_heights],
        operands,
        [pltpu.VMEM((heights[-1], freq), bf16)],
        moved=4 * span * sum(out_heights),
        limit=VMEM_LIMIT if sum(heights) <= 128 else 2 * VMEM_LIMIT,
    )


def bundle_kernel(*refs):
    sources, out_ref = refs[:-1], refs[-1]
    rows = out_ref.shape[0] // len(sources)
    for i, ref in enumerate(sources):
        out_ref[i * rows : (i + 1) * rows, :] = ref[ref.shape[0] - rows :, :]


def bundle(slices, rows):
    span = slices[0].shape[1]
    return call(
        bundle_kernel,
        "bundle",
        [VMEM] * len(slices),
        [jax.ShapeDtypeStruct((len(slices) * rows, span), bf16)],
        slices,
        moved=4 * len(slices) * rows * span,
    )[0]


def xor_blocks(values, block, distance):
    lanes = values.shape[1]
    lane = lax.broadcasted_iota(jnp.int32, values.shape, 1)
    width = block
    while distance:
        if distance % 2:
            low = lax.rem(lane // width, 2) == 0
            values = jnp.where(
                low, pltpu.roll(values, lanes - width, 1), pltpu.roll(values, width, 1)
            )
        distance //= 2
        width *= 2
    return values


def rho_kernel(poses, half, paired, s_ref, marks_ref, *refs):
    stat_refs, (norm_ref, out_ref) = refs[: len(paired)], refs[len(paired) :]
    lanes = s_ref.shape[1]
    rows = s_ref.shape[0] // poses
    groups = marks_ref.shape[1]
    block = 2 * half
    peaks, totals = [], []
    for ref, distance in zip(stat_refs, paired):
        for at in range(0, ref.shape[0], 8):
            stats = xor_blocks(ref[at : at + 8, :], block, distance)
            peaks.append(stats[0:1])
            totals.append(stats[1:2])
    peak = functools.reduce(jnp.maximum, peaks)
    total = sum(t * jnp.exp(p - peak) for t, p in zip(totals, peaks))
    log_norm = peak + jnp.log(total)
    norm_ref[...] = log_norm
    rho = jnp.exp(s_ref[...].reshape(poses, rows, lanes) - log_norm[None])
    mass = lax.dot_general(
        jnp.where(real_index((rows, lanes), 1, half), jnp.sum(rho, axis=0), 0.0),
        marks_ref[...],
        NN,
        precision=HIGHEST,
        preferred_element_type=f32,
    )
    high = mass.astype(bf16)
    low = (mass - high.astype(f32)).astype(bf16)
    rho_low = rho.reshape(poses * rows, lanes).astype(bf16)
    cut = poses // 2 * rows
    lane = lax.broadcasted_iota(jnp.int32, (lanes, lanes), 0)
    column = lax.broadcasted_iota(jnp.int32, (lanes, lanes), 1)
    particle = lane // block * half + lax.rem(lane, block)
    real = lax.rem(lane, block) < half
    first = (real & (column == particle)).astype(f32).astype(bf16)
    second = (real & (column == particle + lanes // 2)).astype(f32).astype(bf16)
    packed = jnp.dot(rho_low[:cut], first, preferred_element_type=f32)
    packed += jnp.dot(rho_low[cut:], second, preferred_element_type=f32)
    out_ref[:cut, :] = packed.astype(bf16)
    if lanes > 2 * groups:
        out_ref[cut:, :] = jnp.zeros((rows, lanes), bf16)
    out_ref[cut:, :groups] = high
    out_ref[cut:, groups : 2 * groups] = low


def responsibilities(scores, marks, stats, paired, poses, half):
    columns, lanes = scores.shape
    return call(
        functools.partial(rho_kernel, poses, half, paired),
        "responsibilities",
        [VMEM] * (2 + len(stats)),
        [
            jax.ShapeDtypeStruct((1, lanes), f32),
            jax.ShapeDtypeStruct((columns // 2 + columns // poses, lanes), bf16),
        ],
        (scores, marks, *stats),
        flops=40 * columns * lanes,
    )


def gather_kernel(poses, half, counts, me_ref, s_ref, norm_ref, weight_ref, *refs):
    w_refs, (resp_ref, cw_ref, rows_ref) = refs[:-3], refs[-3:]
    span = rows_ref.shape[2]
    block = 2 * half
    here = pl.ds(pl.multiple_of(me_ref[0] * span, LANES), span)
    at = 0
    for refs in regroup(w_refs, counts):
        for ref in refs:
            for start in range(0, ref.shape[0], block):
                rows_ref[0, at : at + half, :] = ref[start : start + half, :]
                rows_ref[1, at : at + half, :] = ref[start + half : start + block, :]
                at += half
    weight = weight_ref[:, here]
    high = weight.astype(bf16)
    cw_ref[:, :span] = high
    cw_ref[:, span:] = (weight - high.astype(f32)).astype(bf16)
    rows = resp_ref.shape[0]
    lanes = s_ref.shape[1]
    scores = s_ref[...].reshape(poses, rows, lanes)
    pose_peak = jnp.max(scores, axis=0)
    total = jnp.sum(jnp.exp(scores - pose_peak[None]), axis=0)
    log_resp = pose_peak + jnp.log(total) - norm_ref[...]
    shape = (resp_ref.shape[1], lanes)
    lane = lax.broadcasted_iota(jnp.int32, shape, 1)
    row = ((lane // block) ^ me_ref[1]) * half + lax.rem(lane, block)
    take = (lax.broadcasted_iota(jnp.int32, shape, 0) == row) & (lax.rem(lane, block) < half)
    resp_ref[...] = lax.dot_general(
        log_resp, take.astype(f32), NT, precision=HIGHEST, preferred_element_type=f32
    )


def gather_rows(me, scores, norm, weight, slices, poses, half, span):
    columns, lanes = scores.shape
    counts = [len(refs) for refs in slices]
    slices = [w for refs in slices for w in refs]
    particles = sum(w.shape[0] for w in slices) // 2
    return call(
        functools.partial(gather_kernel, poses, half, counts),
        "gather_rows",
        [SMEM] + [VMEM] * (3 + len(slices)),
        [
            jax.ShapeDtypeStruct((columns // poses, lanes // 2), f32),
            jax.ShapeDtypeStruct((weight.shape[0], 2 * span), bf16),
            jax.ShapeDtypeStruct((2, particles, span), bf16),
        ],
        (me, scores, norm, weight, *slices),
        flops=GATHER_FLOPS,
        moved=8 * particles * span,
        limit=VMEM_LIMIT if particles <= 512 else 2 * VMEM_LIMIT,
    )


def finish_kernel(poses, groups, sources, half, me_ref, cw_ref, cos_ref, sin_ref, rows_ref, *refs):
    payloads, refs = refs[:sources], refs[sources:]
    last, (out_ref, rho_ref, inverse_ref, *buffers) = refs[:-5], refs[-5:]
    rows, _, span = out_ref.shape
    cut = poses // 2 * rows
    count = payloads[0].shape[1] // 2
    mass = jnp.zeros((rows, groups), f32)
    for i, ref in enumerate(payloads):
        rho_ref[:cut, i * count : (i + 1) * count] = ref[:cut, :count]
        rho_ref[cut:, i * count : (i + 1) * count] = ref[:cut, count:]
        mass += ref[cut:, :groups].astype(f32) + ref[cut:, groups : 2 * groups].astype(f32)
    high = mass.astype(bf16)
    mass = jnp.concatenate([high, (mass - high.astype(f32)).astype(bf16)], axis=0)
    terms = jnp.dot(mass, cw_ref[...], preferred_element_type=f32)
    denom = (terms[:rows, :span] + terms[rows:, :span]) + (terms[:rows, span:] + terms[rows:, span:])
    inverse_ref[...] = 1.0 / (denom + prior_precision)
    tiles = [(a, min(256, span - a)) for a in range(0, span, 256)]
    known = rows_ref.shape[1] // sources

    def rows_of(part, start, width):
        here = slice(start, start + width)
        if not last:
            return rows_ref[part, :, here]
        pieces = []
        for i in range(sources):
            pieces.append(rows_ref[part, i * known : (i + 1) * known, here])
            if i == 0:
                pieces.append(last[0][part * half : (part + 1) * half, here])
            else:
                at = (2 * (i - 1) + part) * half
                pieces.append(last[1][at : at + half, here])
        return jnp.concatenate(pieces, axis=0)

    def products(i):
        start, width = tiles[i]
        for part in range(2):
            buffers[i % 2][part, :, :width] = jnp.dot(
                rho_ref[...], rows_of(part, start, width), preferred_element_type=f32
            )

    def rotate(i):
        start, width = tiles[i]
        buffer = buffers[i % 2]
        for a in range(0, width, LANES):
            at = pl.ds(pl.multiple_of(me_ref[0] * span + start + a, LANES), LANES)
            numer_re = jnp.zeros((rows, LANES), f32)
            numer_im = jnp.zeros((rows, LANES), f32)
            for r in range(poses):
                cos_r = cos_ref[r : r + 1, at]
                sin_r = sin_ref[r : r + 1, at]
                s_re = buffer[0, r * rows : (r + 1) * rows, a : a + LANES]
                s_im = buffer[1, r * rows : (r + 1) * rows, a : a + LANES]
                numer_re = numer_re + s_re * cos_r + s_im * sin_r
                numer_im = numer_im + s_im * cos_r - s_re * sin_r
            here = slice(start + a, start + a + LANES)
            inverse = inverse_ref[:, here]
            out_ref[:, 0, here] = numer_re * inverse
            out_ref[:, 1, here] = numer_im * inverse

    products(0)
    for i in range(1, len(tiles)):
        products(i)
        rotate(i - 1)
    rotate(len(tiles) - 1)


def finish(me, weight, cos_t, sin_t, rows, payloads, last, cls_rows, half):
    poses = cos_t.shape[0]
    span = rows.shape[2]
    particles = len(payloads) * payloads[0].shape[1] // 2
    return call(
        functools.partial(finish_kernel, poses, weight.shape[0], len(payloads), half),
        "finish",
        [SMEM] + [VMEM] * (4 + len(payloads) + len(last)),
        [jax.ShapeDtypeStruct((cls_rows, 2, span), f32)],
        (me, weight, cos_t, sin_t, rows, *payloads, *last),
        [
            pltpu.VMEM((poses * cls_rows, particles), bf16),
            pltpu.VMEM((cls_rows, span), f32),
            pltpu.VMEM((2, poses * cls_rows, 256), f32),
            pltpu.VMEM((2, poses * cls_rows, 256), f32),
        ],
        flops=4 * poses * cls_rows * particles * span,
        limit=VMEM_LIMIT if particles <= 512 else 2 * VMEM_LIMIT,
    )[0]


def swap(values, axis, distance):
    size = lax.axis_size(axis)
    return lax.ppermute(values, axis, [(i, i ^ distance) for i in range(size)])


def local(particles, classes, ctf, noise_weight, group_ids, shifts):
    half, _, freq = particles.shape
    cls_rows = classes.shape[0]
    poses = shifts.shape[0]
    n_cls = lax.axis_size("cls")
    n_img = lax.axis_size("img")
    span = freq // n_img
    pairwise = n_cls == 4
    me_cls = lax.axis_index("cls") if pairwise else 0
    me = jnp.stack([lax.axis_index("img"), me_cls]).astype(jnp.int32)
    others = tuple(range(n_img - 1, 0, -1))

    own, *own_chunks = weigh(particles, ctf, noise_weight, group_ids)
    if pairwise:
        far = [swap(w, "cls", 2) for w in own_chunks]
        near = swap(own, "cls", 1)
        mine, *outgoing = cut_slices(me, [[own]], [(d, 0) for d in (0,) + others[:-1]], span, freq)
        slices = [mine] + [swap(w, "img", d) for w, d in zip(outgoing, others)]
    else:
        shards = [[lax.all_gather(own, "cls", axis=0, tiled=True)]]
        mine, *outgoing = cut_slices(me, shards, [(d, 0) for d in (0,) + others], span, freq)
        slices = [[w] for w in [mine] + [swap(w, "img", d) for w, d in zip(outgoing, others)]]

    split = jnp.transpose(classes, (1, 0, 2))
    cos_t, sin_t, power, weight = prepare(shifts, split, ctf, noise_weight)
    early = early_templates(split, cos_t, sin_t)
    if pairwise:
        far, near, slices, split, early = lax.optimization_barrier(
            (far, near, slices, split, early)
        )
        third = [swap(w, "cls", 1) for w in far]
        targets = [(d, 1) for d in (0,) + others[:-1]] + [(others[-1], 0)]
        mine, *outgoing = cut_slices(me, [[own], [near], far], targets, span, freq)
        arrived = [mine] + [swap(w, "img", d) for w, d in zip(outgoing, others)]
        shards = [[own], [near], far, third]
    scores, marks, stat = score(early, split, cos_t, sin_t, power, shards, half)
    if pairwise:
        stat, arrived[-1] = lax.optimization_barrier((stat, arrived[-1]))
        stats = [stat] + [swap(stat, "cls", k) for k in range(1, n_cls)]
        paired = tuple(range(n_cls))
        last = [*cut_slices(me, [third], [(0, 0)], span, freq)]
        last.append(swap(bundle(arrived[1:], 2 * half), "cls", 1))
        slices = [[a, b] for a, b in zip(slices, arrived)] + [arrived[-1:]]
    else:
        stats = [lax.all_gather(stat, "cls", axis=0, tiled=True)]
        paired = (0,)
        last = []
    norm, payload = responsibilities(scores, marks, stats, paired, poses, half)
    payloads = [payload] + [swap(payload, "img", d) for d in others]
    log_resp, weight_here, rows = gather_rows(
        me, scores, norm, weight, slices, poses, half, span
    )
    averages = finish(me, weight_here, cos_t, sin_t, rows, payloads, last, cls_rows, half)
    return (log_resp.T, averages)


def solution(mesh):
    placed = (
        P(("groups", "img", "cls"), None, None),
        P(("groups", "cls"), None, None),
        P("groups", None),
        P("groups"),
        P(("groups", "img", "cls")),
        P("groups", None),
    )
    return jax.shard_map(
        local,
        mesh=mesh,
        in_specs=placed,
        out_specs=(P(("groups", "img"), "cls"), P(("groups", "cls"), None, "img")),
        check_vma=False,
    )
```

```python
import functools

import jax
import jax.numpy as jnp
from jax import lax
from jax.experimental import pallas as pl
from jax.experimental.pallas import tpu as pltpu
from jax.sharding import PartitionSpec as P

BOX = 128
CHUNKS = 2
LANES = 128
VMEM_LIMIT = 24 * 1024 * 1024
GATHER_FLOPS = 20_000_000_000

prior_precision = 0.02

NT = (((1,), (1,)), ((), ()))
NN = (((1,), (0,)), ((), ()))
HIGHEST = lax.Precision.HIGHEST
f32 = jnp.float32
bf16 = jnp.bfloat16

SMEM = pl.BlockSpec(memory_space=pltpu.SMEM)
VMEM = pl.BlockSpec(memory_space=pltpu.VMEM)
ANY = pl.BlockSpec(memory_space=pl.ANY)


def call(kernel, name, in_specs, out_shape, operands, scratch=(), flops=0, moved=0, limit=VMEM_LIMIT):
    return pl.pallas_call(
        kernel,
        in_specs=in_specs,
        out_specs=[VMEM] * len(out_shape),
        out_shape=out_shape,
        scratch_shapes=list(scratch),
        compiler_params=pltpu.CompilerParams(vmem_limit_bytes=limit),
        cost_estimate=pl.CostEstimate(flops=flops, bytes_accessed=moved, transcendentals=0),
        name=name,
    )(*operands)


def real_index(shape, axis, half):
    return lax.rem(lax.broadcasted_iota(jnp.int32, shape, axis) // half, 2) == 0


def weigh_kernel(ids_hbm, p_hbm, ctf_hbm, nw_hbm, *refs):
    out_refs, (ids_ref, p_ref, ctf_ref, nw_ref, scale_ref, sem) = refs[:-6], refs[-6:]
    count, _, freq = p_ref.shape
    copies = [
        pltpu.make_async_copy(source, target, sem.at[i])
        for i, (source, target) in enumerate(
            [(ids_hbm, ids_ref), (ctf_hbm, ctf_ref), (nw_hbm, nw_ref), (p_hbm, p_ref)]
        )
    ]
    for copy in copies:
        copy.start()
    copies[0].wait()
    row = lax.rem(lax.broadcasted_iota(jnp.int32, (2 * count, LANES), 0), count)
    ids = jnp.zeros((2 * count, LANES), f32)
    for n in range(count):
        ids = jnp.where(row == n, ids_ref[n].astype(f32), ids)
    for copy in copies[1:]:
        copy.wait()
    noise = nw_ref[...].reshape(1, freq)
    for n in range(count):
        scale_ref[n : n + 1, :] = ctf_ref[pl.ds(ids_ref[n], 1), :] * noise
    scale = scale_ref[...]
    values = p_ref[...].astype(f32)
    chunk = freq // CHUNKS
    for part in range(2):
        weighted = (values[:, part, :] * scale).astype(bf16)
        here = slice(part * count, (part + 1) * count)
        out_refs[0][here, :freq] = weighted
        for c, out_ref in enumerate(out_refs[1:]):
            out_ref[here, :chunk] = weighted[:, c * chunk : (c + 1) * chunk]
    for out_ref in out_refs[:2]:
        out_ref[:, out_ref.shape[1] - LANES :] = ids.astype(bf16)


def weigh(particles, ctf, noise_weight, group_ids):
    rows, _, freq = particles.shape
    operands = (group_ids, particles, ctf, noise_weight)
    return call(
        weigh_kernel,
        "weigh",
        [ANY] * 4,
        [
            jax.ShapeDtypeStruct((2 * rows, width), bf16)
            for width in [freq + LANES, freq // CHUNKS + LANES] + [freq // CHUNKS] * (CHUNKS - 1)
        ],
        [pltpu.with_memory_space_constraint(x, pltpu.HBM) for x in operands],
        [
            pltpu.SMEM((rows,), jnp.int32),
            pltpu.VMEM(particles.shape, bf16),
            pltpu.VMEM(ctf.shape, f32),
            pltpu.VMEM((freq,), f32),
            pltpu.VMEM((rows, freq), f32),
            pltpu.SemaphoreType.DMA((4,)),
        ],
        flops=4 * rows * freq,
        moved=16 * rows * freq,
    )


def prepare_kernel(
    shifts_ref, cls_ref, ctf_hbm, nw_hbm, cos_ref, sin_ref, pow_ref, cw_ref, *scratch
):
    ctf_ref, nw_ref, angle_ref, sem = scratch
    freq = cls_ref.shape[2]
    poses = cos_ref.shape[0]
    copies = [
        pltpu.make_async_copy(source, target, sem.at[i])
        for i, (source, target) in enumerate(
            [(ctf_hbm, ctf_ref), (nw_hbm, nw_ref)]
        )
    ]
    for copy in copies:
        copy.start()
    lane = lax.broadcasted_iota(jnp.int32, (1, BOX), 1).astype(f32)
    step = 2.0 * jnp.pi / BOX
    for r in range(poses):
        angle_ref[0, r : r + 1, :] = step * (shifts_ref[0, r].astype(f32) * (lane - BOX // 2))
        angle_ref[1, r : r + 1, :] = step * (shifts_ref[1, r].astype(f32) * lane)
    x_cos, x_sin = jnp.cos(angle_ref[0]), jnp.sin(angle_ref[0])
    y_cos, y_sin = jnp.cos(angle_ref[1]), jnp.sin(angle_ref[1])
    for t in range(freq // BOX):
        c = jnp.broadcast_to(y_cos[:, t : t + 1], x_cos.shape)
        s = jnp.broadcast_to(y_sin[:, t : t + 1], x_cos.shape)
        cos_ref[:, t * BOX : (t + 1) * BOX] = x_cos * c - x_sin * s
        sin_ref[:, t * BOX : (t + 1) * BOX] = x_sin * c + x_cos * s
    for copy in copies:
        copy.wait()
    noise = nw_ref[...].reshape(1, freq)
    cut = freq // 4
    power = jnp.zeros(pow_ref.shape, f32)
    for q in range(4):
        at = slice(q * cut, (q + 1) * cut)
        re = cls_ref[0, :, at].astype(f32)
        im = cls_ref[1, :, at].astype(f32)
        ctf = ctf_ref[:, at]
        weight = ctf * ctf * noise[:, at]
        cw_ref[:, at] = weight
        power += lax.dot_general(
            re * re + im * im, weight, NT, precision=HIGHEST, preferred_element_type=f32
        )
    pow_ref[...] = power


def prepare(shifts, split, ctf, noise_weight):
    _, rows, freq = split.shape
    poses, groups = shifts.shape[0], ctf.shape[0]
    return call(
        prepare_kernel,
        "prepare",
        [SMEM, VMEM, ANY, ANY],
        [
            jax.ShapeDtypeStruct((poses, freq), f32),
            jax.ShapeDtypeStruct((poses, freq), f32),
            jax.ShapeDtypeStruct((rows, groups), f32),
            jax.ShapeDtypeStruct((groups, freq), f32),
        ],
        (
            shifts.T,
            split,
            *[pltpu.with_memory_space_constraint(x, pltpu.HBM) for x in (ctf, noise_weight)],
        ),
        [
            pltpu.VMEM(ctf.shape, f32),
            pltpu.VMEM((freq,), f32),
            pltpu.VMEM((2, poses, BOX), f32),
            pltpu.SemaphoreType.DMA((2,)),
        ],
        flops=24 * rows * groups * freq,
    )


def write_templates(cls_ref, cos_ref, sin_ref, temp_ref, start, tile):
    rows = cls_ref.shape[1]
    for a in range(0, tile, LANES):
        at = pl.ds(pl.multiple_of(start + a, LANES), LANES)
        re = cls_ref[0, :, at].astype(f32)
        im = cls_ref[1, :, at].astype(f32)
        for r in range(cos_ref.shape[0]):
            cos_r = cos_ref[r : r + 1, at]
            sin_r = sin_ref[r : r + 1, at]
            here = slice(r * rows, (r + 1) * rows)
            temp_ref[here, a : a + LANES] = (re * cos_r - im * sin_r).astype(bf16)
            temp_ref[here, tile + a : tile + a + LANES] = (re * sin_r + im * cos_r).astype(bf16)


def template_tile(freq):
    return max(t for t in range(LANES, 385, LANES) if freq // CHUNKS % t == 0)


def early_kernel(cls_ref, cos_ref, sin_ref, temp_ref):
    write_templates(cls_ref, cos_ref, sin_ref, temp_ref, 0, cls_ref.shape[2])


def early_templates(split, cos_t, sin_t):
    _, rows, freq = split.shape
    poses = cos_t.shape[0]
    tile = template_tile(freq)
    count = freq // tile // 2
    skip = freq // tile - count
    return pl.pallas_call(
        early_kernel,
        grid=(count,),
        in_specs=[
            pl.BlockSpec((2, rows, tile), lambda j: (0, 0, skip + j)),
            pl.BlockSpec((poses, tile), lambda j: (0, skip + j)),
            pl.BlockSpec((poses, tile), lambda j: (0, skip + j)),
        ],
        out_specs=pl.BlockSpec((None, poses * rows, 2 * tile), lambda j: (j, 0, 0)),
        out_shape=pltpu.HBM((count, poses * rows, 2 * tile), bf16),
        compiler_params=pltpu.CompilerParams(vmem_limit_bytes=VMEM_LIMIT),
        cost_estimate=pl.CostEstimate(
            flops=20 * poses * rows * freq, bytes_accessed=2 * poses * rows * freq, transcendentals=0
        ),
        name="early_templates",
    )(split, cos_t, sin_t)


def regroup(refs, counts):
    refs = list(refs)
    return [[refs.pop(0) for _ in range(count)] for count in counts]


def tile_of_particles(shards, chunk, span, t, tile, half):
    cuts = []
    for ref, chunked in shards:
        at = t * tile if chunked else chunk * span + t * tile
        cuts.append(ref[:, at : at + tile])
    wide = jnp.concatenate(cuts, axis=0).astype(f32)
    real = real_index(wide.shape, 0, half)
    return jnp.concatenate(
        [jnp.where(real, wide, 0.0).astype(bf16), jnp.where(real, 0.0, wide).astype(bf16)], axis=1
    )


def template_kernel(early_hbm, cls_ref, cos_ref, sin_ref, temp_ref, late_ref, sem):
    count, _, width = temp_ref.shape
    tile = width // 2
    copies = [
        pltpu.make_async_copy(early_hbm.at[t], late_ref.at[t], sem.at[t])
        for t in range(late_ref.shape[0])
    ]
    for copy in copies:
        copy.start()

    @pl.loop(0, count)
    def _(t):
        write_templates(cls_ref, cos_ref, sin_ref, temp_ref.at[t], t * tile, tile)

    for copy in copies:
        copy.wait()


def first_score_kernel(chunked, half, temp_ref, *refs):
    refs, acc_ref = refs[:-1], refs[-1]
    count, _, width = temp_ref.shape
    tile = width // 2
    shards = list(zip(refs, chunked))
    acc_ref[...] = jnp.zeros_like(acc_ref)
    for t in range(count):
        acc_ref[...] += lax.dot_general(
            temp_ref[t],
            tile_of_particles(shards, 0, count * tile, t, tile, half),
            NT,
            preferred_element_type=f32,
        )


def last_score_kernel(chunked, half, temp_ref, pow_ref, acc_ref, *refs):
    refs, (s_ref, marks_ref, stat_ref) = refs[:-3], refs[-3:]
    tail_refs, shards = refs[: len(chunked)], list(zip(refs[len(chunked) :], chunked))
    count, _, width = temp_ref.shape
    tile = width // 2
    rows, groups = pow_ref.shape
    lanes = s_ref.shape[1]
    poses = s_ref.shape[0] // rows
    tails = [ref[:, ref.shape[1] - LANES :] for ref in tail_refs]
    ids = jnp.concatenate(tails, axis=0).astype(f32)
    group = lax.broadcasted_iota(jnp.int32, (lanes, groups), 1).astype(f32)
    marks = (ids[:, :groups] == group).astype(f32)
    marks_ref[...] = marks
    penalty = lax.dot_general(
        pow_ref[...], marks, NT, precision=HIGHEST, preferred_element_type=f32
    )
    s_ref[...] = acc_ref[...]
    for t in range(count):
        s_ref[...] += lax.dot_general(
            temp_ref[t],
            tile_of_particles(shards, 1, count * tile, t, tile, half),
            NT,
            preferred_element_type=f32,
        )
    acc = s_ref[...]
    acc = acc + jnp.where(
        real_index(acc.shape, 1, half), pltpu.roll(acc, lanes - half, 1), pltpu.roll(acc, half, 1)
    )
    scores = acc.reshape(poses, rows, lanes) - 0.5 * penalty[None]
    peak = jnp.max(jnp.max(scores, axis=0), axis=0, keepdims=True)
    total = jnp.sum(jnp.sum(jnp.exp(scores - peak[None]), axis=0), axis=0, keepdims=True)
    s_ref[...] = scores.reshape(poses * rows, lanes)
    stat_ref[0:1, :] = peak
    stat_ref[1:2, :] = total
    stat_ref[2:8, :] = jnp.zeros((6, lanes), f32)


def score(early, split, cos_t, sin_t, power, shards, half):
    count, columns, width = early.shape
    freq = split.shape[2]
    lanes = sum(refs[0].shape[0] for refs in shards)
    chunked = [len(refs) > 1 for refs in shards]
    flops = 2 * columns * 256 * count * width
    acc_shape = jax.ShapeDtypeStruct((columns, lanes), f32)
    temps, late = call(
        template_kernel,
        "templates",
        [ANY] + [VMEM] * 3,
        [pltpu.VMEM(early.shape, bf16)] * 2,
        (pltpu.with_memory_space_constraint(early, pltpu.HBM), split, cos_t, sin_t),
        [pltpu.SemaphoreType.DMA((count,))],
        flops=20 * columns * freq,
        moved=2 * columns * freq,
    )
    operands = [temps, *[refs[0] for refs in shards]]
    acc = call(
        functools.partial(first_score_kernel, chunked, half),
        "score0",
        [VMEM] * len(operands),
        [acc_shape],
        operands,
        flops=flops,
    )[0]
    operands = [late, power, acc]
    operands += [refs[0] for refs in shards] + [refs[-1] for refs in shards]
    return call(
        functools.partial(last_score_kernel, chunked, half),
        "score1",
        [VMEM] * len(operands),
        [
            acc_shape,
            jax.ShapeDtypeStruct((lanes, power.shape[1]), f32),
            jax.ShapeDtypeStruct((8, lanes), f32),
        ],
        operands,
        flops=flops,
    )


def slices_kernel(counts, targets, me_ref, *refs):
    whole_ref, refs = refs[-1], refs[:-1]
    shards, out_refs = regroup(refs[: -len(targets)], counts), refs[-len(targets) :]
    span = out_refs[0].shape[1]
    filled = [0] * len(targets)
    for k, refs in enumerate(shards):
        source = refs[0]
        height = source.shape[0]
        if len(refs) > 1:
            width = refs[-1].shape[1]
            for c, ref in enumerate(refs):
                whole_ref[:, c * width : (c + 1) * width] = ref[:, :width]
            source = whole_ref
        for i, (distance, skip) in enumerate(targets):
            if k >= skip:
                base = pl.multiple_of((me_ref[0] ^ distance) * span, LANES)
                out_refs[i][filled[i] : filled[i] + height, :] = source[:, pl.ds(base, span)]
                filled[i] += height


def cut_slices(me, shards, targets, span, freq):
    heights = [refs[0].shape[0] for refs in shards]
    operands = [me, *[ref for refs in shards for ref in refs]]
    out_heights = [sum(heights[skip:]) for _, skip in targets]
    return call(
        functools.partial(slices_kernel, [len(refs) for refs in shards], targets),
        "cut_slices",
        [SMEM] + [VMEM] * (len(operands) - 1),
        [jax.ShapeDtypeStruct((height, span), bf16) for height in out_heights],
        operands,
        [pltpu.VMEM((heights[-1], freq), bf16)],
        moved=4 * span * sum(out_heights),
        limit=VMEM_LIMIT if sum(heights) <= 128 else 2 * VMEM_LIMIT,
    )


def bundle_kernel(*refs):
    sources, out_ref = refs[:-1], refs[-1]
    rows = out_ref.shape[0] // len(sources)
    for i, ref in enumerate(sources):
        out_ref[i * rows : (i + 1) * rows, :] = ref[ref.shape[0] - rows :, :]


def bundle(slices, rows):
    span = slices[0].shape[1]
    return call(
        bundle_kernel,
        "bundle",
        [VMEM] * len(slices),
        [jax.ShapeDtypeStruct((len(slices) * rows, span), bf16)],
        slices,
        moved=4 * len(slices) * rows * span,
    )[0]


def xor_blocks(values, block, distance):
    lanes = values.shape[1]
    lane = lax.broadcasted_iota(jnp.int32, values.shape, 1)
    width = block
    while distance:
        if distance % 2:
            low = lax.rem(lane // width, 2) == 0
            values = jnp.where(
                low, pltpu.roll(values, lanes - width, 1), pltpu.roll(values, width, 1)
            )
        distance //= 2
        width *= 2
    return values


def rho_kernel(poses, half, paired, s_ref, marks_ref, *refs):
    stat_refs, (norm_ref, out_ref) = refs[: len(paired)], refs[len(paired) :]
    lanes = s_ref.shape[1]
    rows = s_ref.shape[0] // poses
    groups = marks_ref.shape[1]
    block = 2 * half
    peaks, totals = [], []
    for ref, distance in zip(stat_refs, paired):
        for at in range(0, ref.shape[0], 8):
            stats = xor_blocks(ref[at : at + 8, :], block, distance)
            peaks.append(stats[0:1])
            totals.append(stats[1:2])
    peak = functools.reduce(jnp.maximum, peaks)
    total = sum(t * jnp.exp(p - peak) for t, p in zip(totals, peaks))
    log_norm = peak + jnp.log(total)
    norm_ref[...] = log_norm
    rho = jnp.exp(s_ref[...].reshape(poses, rows, lanes) - log_norm[None])
    mass = lax.dot_general(
        jnp.where(real_index((rows, lanes), 1, half), jnp.sum(rho, axis=0), 0.0),
        marks_ref[...],
        NN,
        precision=HIGHEST,
        preferred_element_type=f32,
    )
    high = mass.astype(bf16)
    low = (mass - high.astype(f32)).astype(bf16)
    rho_low = rho.reshape(poses * rows, lanes).astype(bf16)
    cut = poses // 2 * rows
    lane = lax.broadcasted_iota(jnp.int32, (lanes, lanes), 0)
    column = lax.broadcasted_iota(jnp.int32, (lanes, lanes), 1)
    particle = lane // block * half + lax.rem(lane, block)
    real = lax.rem(lane, block) < half
    first = (real & (column == particle)).astype(f32).astype(bf16)
    second = (real & (column == particle + lanes // 2)).astype(f32).astype(bf16)
    packed = jnp.dot(rho_low[:cut], first, preferred_element_type=f32)
    packed += jnp.dot(rho_low[cut:], second, preferred_element_type=f32)
    out_ref[:cut, :] = packed.astype(bf16)
    if lanes > 2 * groups:
        out_ref[cut:, :] = jnp.zeros((rows, lanes), bf16)
    out_ref[cut:, :groups] = high
    out_ref[cut:, groups : 2 * groups] = low


def responsibilities(scores, marks, stats, paired, poses, half):
    columns, lanes = scores.shape
    return call(
        functools.partial(rho_kernel, poses, half, paired),
        "responsibilities",
        [VMEM] * (2 + len(stats)),
        [
            jax.ShapeDtypeStruct((1, lanes), f32),
            jax.ShapeDtypeStruct((columns // 2 + columns // poses, lanes), bf16),
        ],
        (scores, marks, *stats),
        flops=40 * columns * lanes,
    )


def gather_kernel(poses, half, counts, me_ref, s_ref, norm_ref, weight_ref, *refs):
    w_refs, (resp_ref, cw_ref, rows_ref) = refs[:-3], refs[-3:]
    span = rows_ref.shape[2]
    block = 2 * half
    here = pl.ds(pl.multiple_of(me_ref[0] * span, LANES), span)
    at = 0
    for refs in regroup(w_refs, counts):
        for ref in refs:
            for start in range(0, ref.shape[0], block):
                rows_ref[0, at : at + half, :] = ref[start : start + half, :]
                rows_ref[1, at : at + half, :] = ref[start + half : start + block, :]
                at += half
    weight = weight_ref[:, here]
    high = weight.astype(bf16)
    cw_ref[:, :span] = high
    cw_ref[:, span:] = (weight - high.astype(f32)).astype(bf16)
    rows = resp_ref.shape[0]
    lanes = s_ref.shape[1]
    scores = s_ref[...].reshape(poses, rows, lanes)
    pose_peak = jnp.max(scores, axis=0)
    total = jnp.sum(jnp.exp(scores - pose_peak[None]), axis=0)
    log_resp = pose_peak + jnp.log(total) - norm_ref[...]
    shape = (resp_ref.shape[1], lanes)
    lane = lax.broadcasted_iota(jnp.int32, shape, 1)
    row = ((lane // block) ^ me_ref[1]) * half + lax.rem(lane, block)
    take = (lax.broadcasted_iota(jnp.int32, shape, 0) == row) & (lax.rem(lane, block) < half)
    resp_ref[...] = lax.dot_general(
        log_resp, take.astype(f32), NT, precision=HIGHEST, preferred_element_type=f32
    )


def gather_rows(me, scores, norm, weight, slices, poses, half, span):
    columns, lanes = scores.shape
    counts = [len(refs) for refs in slices]
    slices = [w for refs in slices for w in refs]
    particles = sum(w.shape[0] for w in slices) // 2
    return call(
        functools.partial(gather_kernel, poses, half, counts),
        "gather_rows",
        [SMEM] + [VMEM] * (3 + len(slices)),
        [
            jax.ShapeDtypeStruct((columns // poses, lanes // 2), f32),
            jax.ShapeDtypeStruct((weight.shape[0], 2 * span), bf16),
            jax.ShapeDtypeStruct((2, particles, span), bf16),
        ],
        (me, scores, norm, weight, *slices),
        flops=GATHER_FLOPS,
        moved=8 * particles * span,
        limit=VMEM_LIMIT if particles <= 512 else 2 * VMEM_LIMIT,
    )


def finish_kernel(poses, groups, sources, half, me_ref, cw_ref, cos_ref, sin_ref, rows_ref, *refs):
    payloads, refs = refs[:sources], refs[sources:]
    last, (out_ref, rho_ref, inverse_ref, *buffers) = refs[:-5], refs[-5:]
    rows, _, span = out_ref.shape
    cut = poses // 2 * rows
    count = payloads[0].shape[1] // 2
    mass = jnp.zeros((rows, groups), f32)
    for i, ref in enumerate(payloads):
        rho_ref[:cut, i * count : (i + 1) * count] = ref[:cut, :count]
        rho_ref[cut:, i * count : (i + 1) * count] = ref[:cut, count:]
        mass += ref[cut:, :groups].astype(f32) + ref[cut:, groups : 2 * groups].astype(f32)
    high = mass.astype(bf16)
    mass = jnp.concatenate([high, (mass - high.astype(f32)).astype(bf16)], axis=0)
    terms = jnp.dot(mass, cw_ref[...], preferred_element_type=f32)
    denom = (terms[:rows, :span] + terms[rows:, :span]) + (terms[:rows, span:] + terms[rows:, span:])
    inverse_ref[...] = 1.0 / (denom + prior_precision)
    tiles = [(a, min(256, span - a)) for a in range(0, span, 256)]
    known = rows_ref.shape[1] // sources

    def rows_of(part, start, width):
        here = slice(start, start + width)
        if not last:
            return rows_ref[part, :, here]
        pieces = []
        for i in range(sources):
            pieces.append(rows_ref[part, i * known : (i + 1) * known, here])
            if i == 0:
                pieces.append(last[0][part * half : (part + 1) * half, here])
            else:
                at = (2 * (i - 1) + part) * half
                pieces.append(last[1][at : at + half, here])
        return jnp.concatenate(pieces, axis=0)

    def products(i):
        start, width = tiles[i]
        for part in range(2):
            buffers[i % 2][part, :, :width] = jnp.dot(
                rho_ref[...], rows_of(part, start, width), preferred_element_type=f32
            )

    def rotate(i):
        start, width = tiles[i]
        buffer = buffers[i % 2]
        for a in range(0, width, LANES):
            at = pl.ds(pl.multiple_of(me_ref[0] * span + start + a, LANES), LANES)
            numer_re = jnp.zeros((rows, LANES), f32)
            numer_im = jnp.zeros((rows, LANES), f32)
            for r in range(poses):
                cos_r = cos_ref[r : r + 1, at]
                sin_r = sin_ref[r : r + 1, at]
                s_re = buffer[0, r * rows : (r + 1) * rows, a : a + LANES]
                s_im = buffer[1, r * rows : (r + 1) * rows, a : a + LANES]
                numer_re = numer_re + s_re * cos_r + s_im * sin_r
                numer_im = numer_im + s_im * cos_r - s_re * sin_r
            here = slice(start + a, start + a + LANES)
            inverse = inverse_ref[:, here]
            out_ref[:, 0, here] = numer_re * inverse
            out_ref[:, 1, here] = numer_im * inverse

    products(0)
    for i in range(1, len(tiles)):
        products(i)
        rotate(i - 1)
    rotate(len(tiles) - 1)


def finish(me, weight, cos_t, sin_t, rows, payloads, last, cls_rows, half):
    poses = cos_t.shape[0]
    span = rows.shape[2]
    particles = len(payloads) * payloads[0].shape[1] // 2
    return call(
        functools.partial(finish_kernel, poses, weight.shape[0], len(payloads), half),
        "finish",
        [SMEM] + [VMEM] * (4 + len(payloads) + len(last)),
        [jax.ShapeDtypeStruct((cls_rows, 2, span), f32)],
        (me, weight, cos_t, sin_t, rows, *payloads, *last),
        [
            pltpu.VMEM((poses * cls_rows, particles), bf16),
            pltpu.VMEM((cls_rows, span), f32),
            pltpu.VMEM((2, poses * cls_rows, 256), f32),
            pltpu.VMEM((2, poses * cls_rows, 256), f32),
        ],
        flops=4 * poses * cls_rows * particles * span,
        limit=VMEM_LIMIT if particles <= 512 else 2 * VMEM_LIMIT,
    )[0]


def swap(values, axis, distance):
    size = lax.axis_size(axis)
    return lax.ppermute(values, axis, [(i, i ^ distance) for i in range(size)])


def local(particles, classes, ctf, noise_weight, group_ids, shifts):
    half, _, freq = particles.shape
    cls_rows = classes.shape[0]
    poses = shifts.shape[0]
    n_cls = lax.axis_size("cls")
    n_img = lax.axis_size("img")
    span = freq // n_img
    pairwise = n_cls == 4
    me_cls = lax.axis_index("cls") if pairwise else 0
    me = jnp.stack([lax.axis_index("img"), me_cls]).astype(jnp.int32)
    others = tuple(range(n_img - 1, 0, -1))

    own, *own_chunks = weigh(particles, ctf, noise_weight, group_ids)
    if pairwise:
        far = [swap(w, "cls", 2) for w in own_chunks]
        near = swap(own, "cls", 1)
        mine, *outgoing = cut_slices(me, [[own]], [(d, 0) for d in (0,) + others[:-1]], span, freq)
        slices = [mine] + [swap(w, "img", d) for w, d in zip(outgoing, others)]
    else:
        shards = [[lax.all_gather(own, "cls", axis=0, tiled=True)]]
        mine, *outgoing = cut_slices(me, shards, [(d, 0) for d in (0,) + others], span, freq)
        slices = [[w] for w in [mine] + [swap(w, "img", d) for w, d in zip(outgoing, others)]]

    split = jnp.transpose(classes, (1, 0, 2))
    cos_t, sin_t, power, weight = prepare(shifts, split, ctf, noise_weight)
    early = early_templates(split, cos_t, sin_t)
    if pairwise:
        far, near, slices, split, early = lax.optimization_barrier(
            (far, near, slices, split, early)
        )
        third = [swap(w, "cls", 1) for w in far]
        targets = [(d, 1) for d in (0,) + others[:-1]] + [(others[-1], 0)]
        mine, *outgoing = cut_slices(me, [[own], [near], far], targets, span, freq)
        arrived = [mine] + [swap(w, "img", d) for w, d in zip(outgoing, others)]
        shards = [[own], [near], far, third]
    scores, marks, stat = score(early, split, cos_t, sin_t, power, shards, half)
    if pairwise:
        stat, arrived[-1] = lax.optimization_barrier((stat, arrived[-1]))
        stats = [stat] + [swap(stat, "cls", k) for k in range(n_cls - 1, 0, -1)]
        paired = (0,) + tuple(range(n_cls - 1, 0, -1))
        last = [*cut_slices(me, [third], [(0, 0)], span, freq)]
        last.append(swap(bundle(arrived[1:], 2 * half), "cls", 1))
        slices = [[a, b] for a, b in zip(slices, arrived)] + [arrived[-1:]]
    else:
        stats = [lax.all_gather(stat, "cls", axis=0, tiled=True)]
        paired = (0,)
        last = []
    norm, payload = responsibilities(scores, marks, stats, paired, poses, half)
    payloads = [payload] + [swap(payload, "img", d) for d in others]
    log_resp, weight_here, rows = gather_rows(
        me, scores, norm, weight, slices, poses, half, span
    )
    averages = finish(me, weight_here, cos_t, sin_t, rows, payloads, last, cls_rows, half)
    return (log_resp.T, averages)


def solution(mesh):
    placed = (
        P(("groups", "img", "cls"), None, None),
        P(("groups", "cls"), None, None),
        P("groups", None),
        P("groups"),
        P(("groups", "img", "cls")),
        P("groups", None),
    )
    return jax.shard_map(
        local,
        mesh=mesh,
        in_specs=placed,
        out_specs=(P(("groups", "img"), "cls"), P(("groups", "cls"), None, "img")),
        check_vma=False,
    )
```

```python
import functools

import jax
import jax.numpy as jnp
from jax import lax
from jax.experimental import pallas as pl
from jax.experimental.pallas import tpu as pltpu
from jax.sharding import PartitionSpec as P

BOX = 128
CHUNKS = 2
LANES = 128
VMEM_LIMIT = 24 * 1024 * 1024
GATHER_FLOPS = 20_000_000_000

prior_precision = 0.02

NT = (((1,), (1,)), ((), ()))
NN = (((1,), (0,)), ((), ()))
HIGHEST = lax.Precision.HIGHEST
f32 = jnp.float32
bf16 = jnp.bfloat16

SMEM = pl.BlockSpec(memory_space=pltpu.SMEM)
VMEM = pl.BlockSpec(memory_space=pltpu.VMEM)
ANY = pl.BlockSpec(memory_space=pl.ANY)


def call(kernel, name, in_specs, out_shape, operands, scratch=(), flops=0, moved=0, limit=VMEM_LIMIT):
    return pl.pallas_call(
        kernel,
        in_specs=in_specs,
        out_specs=[VMEM] * len(out_shape),
        out_shape=out_shape,
        scratch_shapes=list(scratch),
        compiler_params=pltpu.CompilerParams(vmem_limit_bytes=limit),
        cost_estimate=pl.CostEstimate(flops=flops, bytes_accessed=moved, transcendentals=0),
        name=name,
    )(*operands)


def real_index(shape, axis, half):
    return lax.rem(lax.broadcasted_iota(jnp.int32, shape, axis) // half, 2) == 0


def weigh_kernel(ids_hbm, p_hbm, ctf_hbm, nw_hbm, *refs):
    out_refs, (ids_ref, p_ref, ctf_ref, nw_ref, scale_ref, sem) = refs[:-6], refs[-6:]
    count, _, freq = p_ref.shape
    copies = [
        pltpu.make_async_copy(source, target, sem.at[i])
        for i, (source, target) in enumerate(
            [(ids_hbm, ids_ref), (ctf_hbm, ctf_ref), (nw_hbm, nw_ref), (p_hbm, p_ref)]
        )
    ]
    for copy in copies:
        copy.start()
    copies[0].wait()
    row = lax.rem(lax.broadcasted_iota(jnp.int32, (2 * count, LANES), 0), count)
    ids = jnp.zeros((2 * count, LANES), f32)
    for n in range(count):
        ids = jnp.where(row == n, ids_ref[n].astype(f32), ids)
    for copy in copies[1:]:
        copy.wait()
    noise = nw_ref[...].reshape(1, freq)
    for n in range(count):
        scale_ref[n : n + 1, :] = ctf_ref[pl.ds(ids_ref[n], 1), :] * noise
    scale = scale_ref[...]
    values = p_ref[...].astype(f32)
    chunk = freq // CHUNKS
    for part in range(2):
        weighted = (values[:, part, :] * scale).astype(bf16)
        here = slice(part * count, (part + 1) * count)
        out_refs[0][here, :freq] = weighted
        for c, out_ref in enumerate(out_refs[1:]):
            out_ref[here, :chunk] = weighted[:, c * chunk : (c + 1) * chunk]
    for out_ref in out_refs[:2]:
        out_ref[:, out_ref.shape[1] - LANES :] = ids.astype(bf16)


def weigh(particles, ctf, noise_weight, group_ids):
    rows, _, freq = particles.shape
    operands = (group_ids, particles, ctf, noise_weight)
    return call(
        weigh_kernel,
        "weigh",
        [ANY] * 4,
        [
            jax.ShapeDtypeStruct((2 * rows, width), bf16)
            for width in [freq + LANES, freq // CHUNKS + LANES] + [freq // CHUNKS] * (CHUNKS - 1)
        ],
        [pltpu.with_memory_space_constraint(x, pltpu.HBM) for x in operands],
        [
            pltpu.SMEM((rows,), jnp.int32),
            pltpu.VMEM(particles.shape, bf16),
            pltpu.VMEM(ctf.shape, f32),
            pltpu.VMEM((freq,), f32),
            pltpu.VMEM((rows, freq), f32),
            pltpu.SemaphoreType.DMA((4,)),
        ],
        flops=4 * rows * freq,
        moved=16 * rows * freq,
    )


def prepare_kernel(
    shifts_ref, cls_ref, ctf_hbm, nw_hbm, cos_ref, sin_ref, pow_ref, cw_ref, *scratch
):
    ctf_ref, nw_ref, angle_ref, sem = scratch
    freq = cls_ref.shape[2]
    poses = cos_ref.shape[0]
    copies = [
        pltpu.make_async_copy(source, target, sem.at[i])
        for i, (source, target) in enumerate(
            [(ctf_hbm, ctf_ref), (nw_hbm, nw_ref)]
        )
    ]
    for copy in copies:
        copy.start()
    lane = lax.broadcasted_iota(jnp.int32, (1, BOX), 1).astype(f32)
    step = 2.0 * jnp.pi / BOX
    for r in range(poses):
        angle_ref[0, r : r + 1, :] = step * (shifts_ref[0, r].astype(f32) * (lane - BOX // 2))
        angle_ref[1, r : r + 1, :] = step * (shifts_ref[1, r].astype(f32) * lane)
    x_cos, x_sin = jnp.cos(angle_ref[0]), jnp.sin(angle_ref[0])
    y_cos, y_sin = jnp.cos(angle_ref[1]), jnp.sin(angle_ref[1])
    for t in range(freq // BOX):
        c = jnp.broadcast_to(y_cos[:, t : t + 1], x_cos.shape)
        s = jnp.broadcast_to(y_sin[:, t : t + 1], x_cos.shape)
        cos_ref[:, t * BOX : (t + 1) * BOX] = x_cos * c - x_sin * s
        sin_ref[:, t * BOX : (t + 1) * BOX] = x_sin * c + x_cos * s
    for copy in copies:
        copy.wait()
    noise = nw_ref[...].reshape(1, freq)
    cut = freq // 4
    power = jnp.zeros(pow_ref.shape, f32)
    for q in range(4):
        at = slice(q * cut, (q + 1) * cut)
        re = cls_ref[0, :, at].astype(f32)
        im = cls_ref[1, :, at].astype(f32)
        ctf = ctf_ref[:, at]
        weight = ctf * ctf * noise[:, at]
        cw_ref[:, at] = weight
        power += lax.dot_general(
            re * re + im * im, weight, NT, precision=HIGHEST, preferred_element_type=f32
        )
    pow_ref[...] = power


def prepare(shifts, split, ctf, noise_weight):
    _, rows, freq = split.shape
    poses, groups = shifts.shape[0], ctf.shape[0]
    return call(
        prepare_kernel,
        "prepare",
        [SMEM, VMEM, ANY, ANY],
        [
            jax.ShapeDtypeStruct((poses, freq), f32),
            jax.ShapeDtypeStruct((poses, freq), f32),
            jax.ShapeDtypeStruct((rows, groups), f32),
            jax.ShapeDtypeStruct((groups, freq), f32),
        ],
        (
            shifts.T,
            split,
            *[pltpu.with_memory_space_constraint(x, pltpu.HBM) for x in (ctf, noise_weight)],
        ),
        [
            pltpu.VMEM(ctf.shape, f32),
            pltpu.VMEM((freq,), f32),
            pltpu.VMEM((2, poses, BOX), f32),
            pltpu.SemaphoreType.DMA((2,)),
        ],
        flops=24 * rows * groups * freq,
    )


def write_templates(cls_ref, cos_ref, sin_ref, temp_ref, start, tile):
    rows = cls_ref.shape[1]
    for a in range(0, tile, LANES):
        at = pl.ds(pl.multiple_of(start + a, LANES), LANES)
        re = cls_ref[0, :, at].astype(f32)
        im = cls_ref[1, :, at].astype(f32)
        for r in range(cos_ref.shape[0]):
            cos_r = cos_ref[r : r + 1, at]
            sin_r = sin_ref[r : r + 1, at]
            here = slice(r * rows, (r + 1) * rows)
            temp_ref[here, a : a + LANES] = (re * cos_r - im * sin_r).astype(bf16)
            temp_ref[here, tile + a : tile + a + LANES] = (re * sin_r + im * cos_r).astype(bf16)


def template_tile(freq):
    return max(t for t in range(LANES, 385, LANES) if freq // CHUNKS % t == 0)


def early_kernel(cls_ref, cos_ref, sin_ref, temp_ref):
    write_templates(cls_ref, cos_ref, sin_ref, temp_ref, 0, cls_ref.shape[2])


def early_templates(split, cos_t, sin_t, skip, count, tile):
    _, rows, _ = split.shape
    poses = cos_t.shape[0]
    return pl.pallas_call(
        early_kernel,
        grid=(count,),
        in_specs=[
            pl.BlockSpec((2, rows, tile), lambda j: (0, 0, skip + j)),
            pl.BlockSpec((poses, tile), lambda j: (0, skip + j)),
            pl.BlockSpec((poses, tile), lambda j: (0, skip + j)),
        ],
        out_specs=pl.BlockSpec((None, poses * rows, 2 * tile), lambda j: (j, 0, 0)),
        out_shape=jax.ShapeDtypeStruct((count, poses * rows, 2 * tile), bf16),
        compiler_params=pltpu.CompilerParams(vmem_limit_bytes=VMEM_LIMIT),
        cost_estimate=pl.CostEstimate(
            flops=40 * poses * rows * count * tile,
            bytes_accessed=4 * poses * rows * count * tile,
            transcendentals=0,
        ),
        name=f"early_templates{skip}",
    )(split, cos_t, sin_t)


def template_kernel(cls_ref, cos_ref, sin_ref, temp_ref):
    count, _, width = temp_ref.shape
    tile = width // 2

    @pl.loop(0, count)
    def _(t):
        write_templates(cls_ref, cos_ref, sin_ref, temp_ref.at[t], t * tile, tile)


def regroup(refs, counts):
    refs = list(refs)
    return [[refs.pop(0) for _ in range(count)] for count in counts]


def tile_of_particles(shards, chunk, span, t, tile, half):
    cuts = []
    for ref, chunked in shards:
        at = t * tile if chunked else chunk * span + t * tile
        cuts.append(ref[:, at : at + tile])
    wide = jnp.concatenate(cuts, axis=0).astype(f32)
    real = real_index(wide.shape, 0, half)
    return jnp.concatenate(
        [jnp.where(real, wide, 0.0).astype(bf16), jnp.where(real, 0.0, wide).astype(bf16)], axis=1
    )


def first_score_kernel(chunked, half, built_ref, early_ref, *refs):
    refs, acc_ref = refs[:-1], refs[-1]
    tile = built_ref.shape[2] // 2
    temps = [ref.at[t] for ref in (built_ref, early_ref) for t in range(ref.shape[0])]
    count = len(temps)
    shards = list(zip(refs, chunked))
    acc_ref[...] = jnp.zeros_like(acc_ref)
    for t in range(count):
        acc_ref[...] += lax.dot_general(
            temps[t][...],
            tile_of_particles(shards, 0, count * tile, t, tile, half),
            NT,
            preferred_element_type=f32,
        )


def last_score_kernel(chunked, half, temp_ref, pow_ref, acc_ref, *refs):
    refs, (s_ref, marks_ref, stat_ref) = refs[:-3], refs[-3:]
    tail_refs, shards = refs[: len(chunked)], list(zip(refs[len(chunked) :], chunked))
    count, _, width = temp_ref.shape
    tile = width // 2
    rows, groups = pow_ref.shape
    lanes = s_ref.shape[1]
    poses = s_ref.shape[0] // rows
    tails = [ref[:, ref.shape[1] - LANES :] for ref in tail_refs]
    ids = jnp.concatenate(tails, axis=0).astype(f32)
    group = lax.broadcasted_iota(jnp.int32, (lanes, groups), 1).astype(f32)
    marks = (ids[:, :groups] == group).astype(f32)
    marks_ref[...] = marks
    penalty = lax.dot_general(
        pow_ref[...], marks, NT, precision=HIGHEST, preferred_element_type=f32
    )
    s_ref[...] = acc_ref[...]
    for t in range(count):
        s_ref[...] += lax.dot_general(
            temp_ref[t],
            tile_of_particles(shards, 1, count * tile, t, tile, half),
            NT,
            preferred_element_type=f32,
        )
    acc = s_ref[...]
    acc = acc + jnp.where(
        real_index(acc.shape, 1, half), pltpu.roll(acc, lanes - half, 1), pltpu.roll(acc, half, 1)
    )
    scores = acc.reshape(poses, rows, lanes) - 0.5 * penalty[None]
    peak = jnp.max(jnp.max(scores, axis=0), axis=0, keepdims=True)
    total = jnp.sum(jnp.sum(jnp.exp(scores - peak[None]), axis=0), axis=0, keepdims=True)
    s_ref[...] = scores.reshape(poses * rows, lanes)
    stat_ref[0:1, :] = peak
    stat_ref[1:2, :] = total
    stat_ref[2:8, :] = jnp.zeros((6, lanes), f32)


def score(early, split, cos_t, sin_t, power, shards, half):
    first, late = early
    count, columns, width = late.shape
    freq = split.shape[2]
    lanes = sum(refs[0].shape[0] for refs in shards)
    chunked = [len(refs) > 1 for refs in shards]
    flops = 2 * columns * 256 * count * width
    acc_shape = jax.ShapeDtypeStruct((columns, lanes), f32)
    built = count - first.shape[0]
    temps = call(
        template_kernel,
        "templates",
        [VMEM] * 3,
        [pltpu.VMEM((built, columns, width), bf16)],
        (split, cos_t, sin_t),
        flops=40 * columns * built * width // 2,
    )[0]
    operands = [temps, first, *[refs[0] for refs in shards]]
    acc = call(
        functools.partial(first_score_kernel, chunked, half),
        "score0",
        [VMEM] * len(operands),
        [acc_shape],
        operands,
        flops=flops,
    )[0]
    operands = [late, power, acc]
    operands += [refs[0] for refs in shards] + [refs[-1] for refs in shards]
    return call(
        functools.partial(last_score_kernel, chunked, half),
        "score1",
        [VMEM] * len(operands),
        [
            acc_shape,
            jax.ShapeDtypeStruct((lanes, power.shape[1]), f32),
            jax.ShapeDtypeStruct((8, lanes), f32),
        ],
        operands,
        flops=flops,
    )


def slices_kernel(counts, targets, me_ref, *refs):
    whole_ref, refs = refs[-1], refs[:-1]
    shards, out_refs = regroup(refs[: -len(targets)], counts), refs[-len(targets) :]
    span = out_refs[0].shape[1]
    filled = [0] * len(targets)
    for k, refs in enumerate(shards):
        source = refs[0]
        height = source.shape[0]
        if len(refs) > 1:
            width = refs[-1].shape[1]
            for c, ref in enumerate(refs):
                whole_ref[:, c * width : (c + 1) * width] = ref[:, :width]
            source = whole_ref
        for i, (distance, skip) in enumerate(targets):
            if k >= skip:
                base = pl.multiple_of((me_ref[0] ^ distance) * span, LANES)
                out_refs[i][filled[i] : filled[i] + height, :] = source[:, pl.ds(base, span)]
                filled[i] += height


def cut_slices(me, shards, targets, span, freq):
    heights = [refs[0].shape[0] for refs in shards]
    operands = [me, *[ref for refs in shards for ref in refs]]
    out_heights = [sum(heights[skip:]) for _, skip in targets]
    return call(
        functools.partial(slices_kernel, [len(refs) for refs in shards], targets),
        "cut_slices",
        [SMEM] + [VMEM] * (len(operands) - 1),
        [jax.ShapeDtypeStruct((height, span), bf16) for height in out_heights],
        operands,
        [pltpu.VMEM((heights[-1], freq), bf16)],
        moved=4 * span * sum(out_heights),
        limit=VMEM_LIMIT if sum(heights) <= 128 else 2 * VMEM_LIMIT,
    )


def bundle_kernel(*refs):
    sources, out_ref = refs[:-1], refs[-1]
    rows = out_ref.shape[0] // len(sources)
    for i, ref in enumerate(sources):
        out_ref[i * rows : (i + 1) * rows, :] = ref[ref.shape[0] - rows :, :]


def bundle(slices, rows):
    span = slices[0].shape[1]
    return call(
        bundle_kernel,
        "bundle",
        [VMEM] * len(slices),
        [jax.ShapeDtypeStruct((len(slices) * rows, span), bf16)],
        slices,
        moved=4 * len(slices) * rows * span,
    )[0]


def xor_blocks(values, block, distance):
    lanes = values.shape[1]
    lane = lax.broadcasted_iota(jnp.int32, values.shape, 1)
    width = block
    while distance:
        if distance % 2:
            low = lax.rem(lane // width, 2) == 0
            values = jnp.where(
                low, pltpu.roll(values, lanes - width, 1), pltpu.roll(values, width, 1)
            )
        distance //= 2
        width *= 2
    return values


def rho_kernel(poses, half, paired, s_ref, marks_ref, *refs):
    stat_refs, (norm_ref, out_ref) = refs[: len(paired)], refs[len(paired) :]
    lanes = s_ref.shape[1]
    rows = s_ref.shape[0] // poses
    groups = marks_ref.shape[1]
    block = 2 * half
    peaks, totals = [], []
    for ref, distance in zip(stat_refs, paired):
        for at in range(0, ref.shape[0], 8):
            stats = xor_blocks(ref[at : at + 8, :], block, distance)
            peaks.append(stats[0:1])
            totals.append(stats[1:2])
    peak = functools.reduce(jnp.maximum, peaks)
    total = sum(t * jnp.exp(p - peak) for t, p in zip(totals, peaks))
    log_norm = peak + jnp.log(total)
    norm_ref[...] = log_norm
    rho = jnp.exp(s_ref[...].reshape(poses, rows, lanes) - log_norm[None])
    mass = lax.dot_general(
        jnp.where(real_index((rows, lanes), 1, half), jnp.sum(rho, axis=0), 0.0),
        marks_ref[...],
        NN,
        precision=HIGHEST,
        preferred_element_type=f32,
    )
    high = mass.astype(bf16)
    low = (mass - high.astype(f32)).astype(bf16)
    rho_low = rho.reshape(poses * rows, lanes).astype(bf16)
    cut = poses // 2 * rows
    lane = lax.broadcasted_iota(jnp.int32, (lanes, lanes), 0)
    column = lax.broadcasted_iota(jnp.int32, (lanes, lanes), 1)
    particle = lane // block * half + lax.rem(lane, block)
    real = lax.rem(lane, block) < half
    first = (real & (column == particle)).astype(f32).astype(bf16)
    second = (real & (column == particle + lanes // 2)).astype(f32).astype(bf16)
    packed = jnp.dot(rho_low[:cut], first, preferred_element_type=f32)
    packed += jnp.dot(rho_low[cut:], second, preferred_element_type=f32)
    out_ref[:cut, :] = packed.astype(bf16)
    if lanes > 2 * groups:
        out_ref[cut:, :] = jnp.zeros((rows, lanes), bf16)
    out_ref[cut:, :groups] = high
    out_ref[cut:, groups : 2 * groups] = low


def responsibilities(scores, marks, stats, paired, poses, half):
    columns, lanes = scores.shape
    return call(
        functools.partial(rho_kernel, poses, half, paired),
        "responsibilities",
        [VMEM] * (2 + len(stats)),
        [
            jax.ShapeDtypeStruct((1, lanes), f32),
            jax.ShapeDtypeStruct((columns // 2 + columns // poses, lanes), bf16),
        ],
        (scores, marks, *stats),
        flops=40 * columns * lanes,
    )


def gather_kernel(poses, half, counts, me_ref, s_ref, norm_ref, weight_ref, *refs):
    w_refs, (resp_ref, cw_ref, rows_ref) = refs[:-3], refs[-3:]
    span = rows_ref.shape[2]
    block = 2 * half
    here = pl.ds(pl.multiple_of(me_ref[0] * span, LANES), span)
    at = 0
    for refs in regroup(w_refs, counts):
        for ref in refs:
            for start in range(0, ref.shape[0], block):
                rows_ref[0, at : at + half, :] = ref[start : start + half, :]
                rows_ref[1, at : at + half, :] = ref[start + half : start + block, :]
                at += half
    weight = weight_ref[:, here]
    high = weight.astype(bf16)
    cw_ref[:, :span] = high
    cw_ref[:, span:] = (weight - high.astype(f32)).astype(bf16)
    rows = resp_ref.shape[0]
    lanes = s_ref.shape[1]
    scores = s_ref[...].reshape(poses, rows, lanes)
    pose_peak = jnp.max(scores, axis=0)
    total = jnp.sum(jnp.exp(scores - pose_peak[None]), axis=0)
    log_resp = pose_peak + jnp.log(total) - norm_ref[...]
    shape = (resp_ref.shape[1], lanes)
    lane = lax.broadcasted_iota(jnp.int32, shape, 1)
    row = ((lane // block) ^ me_ref[1]) * half + lax.rem(lane, block)
    take = (lax.broadcasted_iota(jnp.int32, shape, 0) == row) & (lax.rem(lane, block) < half)
    resp_ref[...] = lax.dot_general(
        log_resp, take.astype(f32), NT, precision=HIGHEST, preferred_element_type=f32
    )


def gather_rows(me, scores, norm, weight, slices, poses, half, span):
    columns, lanes = scores.shape
    counts = [len(refs) for refs in slices]
    slices = [w for refs in slices for w in refs]
    particles = sum(w.shape[0] for w in slices) // 2
    return call(
        functools.partial(gather_kernel, poses, half, counts),
        "gather_rows",
        [SMEM] + [VMEM] * (3 + len(slices)),
        [
            jax.ShapeDtypeStruct((columns // poses, lanes // 2), f32),
            jax.ShapeDtypeStruct((weight.shape[0], 2 * span), bf16),
            jax.ShapeDtypeStruct((2, particles, span), bf16),
        ],
        (me, scores, norm, weight, *slices),
        flops=GATHER_FLOPS,
        moved=8 * particles * span,
        limit=VMEM_LIMIT if particles <= 512 else 2 * VMEM_LIMIT,
    )


def finish_kernel(poses, groups, sources, half, me_ref, cw_ref, cos_ref, sin_ref, rows_ref, *refs):
    payloads, refs = refs[:sources], refs[sources:]
    last, (out_ref, rho_ref, inverse_ref, *buffers) = refs[:-5], refs[-5:]
    rows, _, span = out_ref.shape
    cut = poses // 2 * rows
    count = payloads[0].shape[1] // 2
    mass = jnp.zeros((rows, groups), f32)
    for i, ref in enumerate(payloads):
        rho_ref[:cut, i * count : (i + 1) * count] = ref[:cut, :count]
        rho_ref[cut:, i * count : (i + 1) * count] = ref[:cut, count:]
        mass += ref[cut:, :groups].astype(f32) + ref[cut:, groups : 2 * groups].astype(f32)
    high = mass.astype(bf16)
    mass = jnp.concatenate([high, (mass - high.astype(f32)).astype(bf16)], axis=0)
    terms = jnp.dot(mass, cw_ref[...], preferred_element_type=f32)
    denom = (terms[:rows, :span] + terms[rows:, :span]) + (terms[:rows, span:] + terms[rows:, span:])
    inverse_ref[...] = 1.0 / (denom + prior_precision)
    tiles = [(a, min(256, span - a)) for a in range(0, span, 256)]
    known = rows_ref.shape[1] // sources

    def rows_of(part, start, width):
        here = slice(start, start + width)
        if not last:
            return rows_ref[part, :, here]
        pieces = []
        for i in range(sources):
            pieces.append(rows_ref[part, i * known : (i + 1) * known, here])
            if i == 0:
                pieces.append(last[0][part * half : (part + 1) * half, here])
            else:
                at = (2 * (i - 1) + part) * half
                pieces.append(last[1][at : at + half, here])
        return jnp.concatenate(pieces, axis=0)

    def products(i):
        start, width = tiles[i]
        for part in range(2):
            buffers[i % 2][part, :, :width] = jnp.dot(
                rho_ref[...], rows_of(part, start, width), preferred_element_type=f32
            )

    def rotate(i):
        start, width = tiles[i]
        buffer = buffers[i % 2]
        for a in range(0, width, LANES):
            at = pl.ds(pl.multiple_of(me_ref[0] * span + start + a, LANES), LANES)
            numer_re = jnp.zeros((rows, LANES), f32)
            numer_im = jnp.zeros((rows, LANES), f32)
            for r in range(poses):
                cos_r = cos_ref[r : r + 1, at]
                sin_r = sin_ref[r : r + 1, at]
                s_re = buffer[0, r * rows : (r + 1) * rows, a : a + LANES]
                s_im = buffer[1, r * rows : (r + 1) * rows, a : a + LANES]
                numer_re = numer_re + s_re * cos_r + s_im * sin_r
                numer_im = numer_im + s_im * cos_r - s_re * sin_r
            here = slice(start + a, start + a + LANES)
            inverse = inverse_ref[:, here]
            out_ref[:, 0, here] = numer_re * inverse
            out_ref[:, 1, here] = numer_im * inverse

    products(0)
    for i in range(1, len(tiles)):
        products(i)
        rotate(i - 1)
    rotate(len(tiles) - 1)


def finish(me, weight, cos_t, sin_t, rows, payloads, last, cls_rows, half):
    poses = cos_t.shape[0]
    span = rows.shape[2]
    particles = len(payloads) * payloads[0].shape[1] // 2
    return call(
        functools.partial(finish_kernel, poses, weight.shape[0], len(payloads), half),
        "finish",
        [SMEM] + [VMEM] * (4 + len(payloads) + len(last)),
        [jax.ShapeDtypeStruct((cls_rows, 2, span), f32)],
        (me, weight, cos_t, sin_t, rows, *payloads, *last),
        [
            pltpu.VMEM((poses * cls_rows, particles), bf16),
            pltpu.VMEM((cls_rows, span), f32),
            pltpu.VMEM((2, poses * cls_rows, 256), f32),
            pltpu.VMEM((2, poses * cls_rows, 256), f32),
        ],
        flops=4 * poses * cls_rows * particles * span,
        limit=VMEM_LIMIT if particles <= 512 else 2 * VMEM_LIMIT,
    )[0]


def swap(values, axis, distance):
    size = lax.axis_size(axis)
    return lax.ppermute(values, axis, [(i, i ^ distance) for i in range(size)])


def local(particles, classes, ctf, noise_weight, group_ids, shifts):
    half, _, freq = particles.shape
    cls_rows = classes.shape[0]
    poses = shifts.shape[0]
    n_cls = lax.axis_size("cls")
    n_img = lax.axis_size("img")
    span = freq // n_img
    pairwise = n_cls == 4
    me_cls = lax.axis_index("cls") if pairwise else 0
    me = jnp.stack([lax.axis_index("img"), me_cls]).astype(jnp.int32)
    others = tuple(range(n_img - 1, 0, -1))

    own, *own_chunks = weigh(particles, ctf, noise_weight, group_ids)
    if pairwise:
        far = [swap(w, "cls", 2) for w in own_chunks]
        near = swap(own, "cls", 1)
        mine, *outgoing = cut_slices(me, [[own]], [(d, 0) for d in (0,) + others[:-1]], span, freq)
        slices = [mine] + [swap(w, "img", d) for w, d in zip(outgoing, others)]
    else:
        shards = [[lax.all_gather(own, "cls", axis=0, tiled=True)]]
        mine, *outgoing = cut_slices(me, shards, [(d, 0) for d in (0,) + others], span, freq)
        slices = [[w] for w in [mine] + [swap(w, "img", d) for w, d in zip(outgoing, others)]]

    split = jnp.transpose(classes, (1, 0, 2))
    cos_t, sin_t, power, weight = prepare(shifts, split, ctf, noise_weight)
    tile = template_tile(freq)
    count = freq // CHUNKS // tile
    built = count - count // 3
    early = [
        early_templates(split, cos_t, sin_t, count, count, tile),
        early_templates(split, cos_t, sin_t, built, count - built, tile),
    ][::-1]
    if pairwise:
        far, near, slices, split, early = lax.optimization_barrier(
            (far, near, slices, split, early)
        )
        third = [swap(w, "cls", 1) for w in far]
        targets = [(d, 1) for d in (0,) + others[:-1]] + [(others[-1], 0)]
        mine, *outgoing = cut_slices(me, [[own], [near], far], targets, span, freq)
        arrived = [mine] + [swap(w, "img", d) for w, d in zip(outgoing, others)]
        shards = [[own], [near], far, third]
    scores, marks, stat = score(early, split, cos_t, sin_t, power, shards, half)
    if pairwise:
        stat, arrived[-1] = lax.optimization_barrier((stat, arrived[-1]))
        stats = [stat] + [swap(stat, "cls", k) for k in range(n_cls - 1, 0, -1)]
        paired = (0,) + tuple(range(n_cls - 1, 0, -1))
        last = [*cut_slices(me, [third], [(0, 0)], span, freq)]
        last.append(swap(bundle(arrived[1:], 2 * half), "cls", 1))
        slices = [[a, b] for a, b in zip(slices, arrived)] + [arrived[-1:]]
    else:
        stats = [lax.all_gather(stat, "cls", axis=0, tiled=True)]
        paired = (0,)
        last = []
    norm, payload = responsibilities(scores, marks, stats, paired, poses, half)
    payloads = [payload] + [swap(payload, "img", d) for d in others]
    log_resp, weight_here, rows = gather_rows(
        me, scores, norm, weight, slices, poses, half, span
    )
    averages = finish(me, weight_here, cos_t, sin_t, rows, payloads, last, cls_rows, half)
    return (log_resp.T, averages)


def solution(mesh):
    placed = (
        P(("groups", "img", "cls"), None, None),
        P(("groups", "cls"), None, None),
        P("groups", None),
        P("groups"),
        P(("groups", "img", "cls")),
        P("groups", None),
    )
    return jax.shard_map(
        local,
        mesh=mesh,
        in_specs=placed,
        out_specs=(P(("groups", "img"), "cls"), P(("groups", "cls"), None, "img")),
        check_vma=False,
    )
```

```python
import functools

import jax
import jax.numpy as jnp
from jax import lax
from jax.experimental import pallas as pl
from jax.experimental.pallas import tpu as pltpu
from jax.sharding import PartitionSpec as P

BOX = 128
CHUNKS = 2
LANES = 128
VMEM_LIMIT = 24 * 1024 * 1024
GATHER_FLOPS = 20_000_000_000

prior_precision = 0.02

NT = (((1,), (1,)), ((), ()))
NN = (((1,), (0,)), ((), ()))
HIGHEST = lax.Precision.HIGHEST
f32 = jnp.float32
bf16 = jnp.bfloat16

SMEM = pl.BlockSpec(memory_space=pltpu.SMEM)
VMEM = pl.BlockSpec(memory_space=pltpu.VMEM)
ANY = pl.BlockSpec(memory_space=pl.ANY)


def call(kernel, name, in_specs, out_shape, operands, scratch=(), flops=0, moved=0, limit=VMEM_LIMIT):
    return pl.pallas_call(
        kernel,
        in_specs=in_specs,
        out_specs=[VMEM] * len(out_shape),
        out_shape=out_shape,
        scratch_shapes=list(scratch),
        compiler_params=pltpu.CompilerParams(vmem_limit_bytes=limit),
        cost_estimate=pl.CostEstimate(flops=flops, bytes_accessed=moved, transcendentals=0),
        name=name,
    )(*operands)


def real_index(shape, axis, half):
    return lax.rem(lax.broadcasted_iota(jnp.int32, shape, axis) // half, 2) == 0


def weigh_kernel(ids_hbm, p_hbm, ctf_hbm, nw_hbm, *refs):
    out_refs, (ids_ref, p_ref, ctf_ref, nw_ref, scale_ref, sem) = refs[:-6], refs[-6:]
    count, _, freq = p_ref.shape
    copies = [
        pltpu.make_async_copy(source, target, sem.at[i])
        for i, (source, target) in enumerate(
            [(ids_hbm, ids_ref), (ctf_hbm, ctf_ref), (nw_hbm, nw_ref), (p_hbm, p_ref)]
        )
    ]
    for copy in copies:
        copy.start()
    copies[0].wait()
    row = lax.rem(lax.broadcasted_iota(jnp.int32, (2 * count, LANES), 0), count)
    ids = jnp.zeros((2 * count, LANES), f32)
    for n in range(count):
        ids = jnp.where(row == n, ids_ref[n].astype(f32), ids)
    for copy in copies[1:]:
        copy.wait()
    noise = nw_ref[...].reshape(1, freq)
    for n in range(count):
        scale_ref[n : n + 1, :] = ctf_ref[pl.ds(ids_ref[n], 1), :] * noise
    scale = scale_ref[...]
    values = p_ref[...].astype(f32)
    chunk = freq // CHUNKS
    for part in range(2):
        weighted = (values[:, part, :] * scale).astype(bf16)
        here = slice(part * count, (part + 1) * count)
        out_refs[0][here, :freq] = weighted
        for c, out_ref in enumerate(out_refs[1:]):
            out_ref[here, :chunk] = weighted[:, c * chunk : (c + 1) * chunk]
    for out_ref in out_refs[:2]:
        out_ref[:, out_ref.shape[1] - LANES :] = ids.astype(bf16)


def weigh(particles, ctf, noise_weight, group_ids):
    rows, _, freq = particles.shape
    operands = (group_ids, particles, ctf, noise_weight)
    return call(
        weigh_kernel,
        "weigh",
        [ANY] * 4,
        [
            jax.ShapeDtypeStruct((2 * rows, width), bf16)
            for width in [freq + LANES, freq // CHUNKS + LANES] + [freq // CHUNKS] * (CHUNKS - 1)
        ],
        [pltpu.with_memory_space_constraint(x, pltpu.HBM) for x in operands],
        [
            pltpu.SMEM((rows,), jnp.int32),
            pltpu.VMEM(particles.shape, bf16),
            pltpu.VMEM(ctf.shape, f32),
            pltpu.VMEM((freq,), f32),
            pltpu.VMEM((rows, freq), f32),
            pltpu.SemaphoreType.DMA((4,)),
        ],
        flops=4 * rows * freq,
        moved=16 * rows * freq,
    )


def prepare_kernel(
    shifts_ref, cls_ref, ctf_hbm, nw_hbm, cos_ref, sin_ref, pow_ref, cw_ref, *scratch
):
    ctf_ref, nw_ref, angle_ref, sem = scratch
    freq = cls_ref.shape[2]
    poses = cos_ref.shape[0]
    copies = [
        pltpu.make_async_copy(source, target, sem.at[i])
        for i, (source, target) in enumerate(
            [(ctf_hbm, ctf_ref), (nw_hbm, nw_ref)]
        )
    ]
    for copy in copies:
        copy.start()
    lane = lax.broadcasted_iota(jnp.int32, (1, BOX), 1).astype(f32)
    step = 2.0 * jnp.pi / BOX
    for r in range(poses):
        angle_ref[0, r : r + 1, :] = step * (shifts_ref[0, r].astype(f32) * (lane - BOX // 2))
        angle_ref[1, r : r + 1, :] = step * (shifts_ref[1, r].astype(f32) * lane)
    x_cos, x_sin = jnp.cos(angle_ref[0]), jnp.sin(angle_ref[0])
    y_cos, y_sin = jnp.cos(angle_ref[1]), jnp.sin(angle_ref[1])
    for t in range(freq // BOX):
        c = jnp.broadcast_to(y_cos[:, t : t + 1], x_cos.shape)
        s = jnp.broadcast_to(y_sin[:, t : t + 1], x_cos.shape)
        cos_ref[:, t * BOX : (t + 1) * BOX] = x_cos * c - x_sin * s
        sin_ref[:, t * BOX : (t + 1) * BOX] = x_sin * c + x_cos * s
    for copy in copies:
        copy.wait()
    noise = nw_ref[...].reshape(1, freq)
    cut = freq // 4
    power = jnp.zeros(pow_ref.shape, f32)
    for q in range(4):
        at = slice(q * cut, (q + 1) * cut)
        re = cls_ref[0, :, at].astype(f32)
        im = cls_ref[1, :, at].astype(f32)
        ctf = ctf_ref[:, at]
        weight = ctf * ctf * noise[:, at]
        cw_ref[:, at] = weight
        power += lax.dot_general(
            re * re + im * im, weight, NT, precision=HIGHEST, preferred_element_type=f32
        )
    pow_ref[...] = power


def prepare(shifts, split, ctf, noise_weight):
    _, rows, freq = split.shape
    poses, groups = shifts.shape[0], ctf.shape[0]
    return call(
        prepare_kernel,
        "prepare",
        [SMEM, VMEM, ANY, ANY],
        [
            jax.ShapeDtypeStruct((poses, freq), f32),
            jax.ShapeDtypeStruct((poses, freq), f32),
            jax.ShapeDtypeStruct((rows, groups), f32),
            jax.ShapeDtypeStruct((groups, freq), f32),
        ],
        (
            shifts.T,
            split,
            *[pltpu.with_memory_space_constraint(x, pltpu.HBM) for x in (ctf, noise_weight)],
        ),
        [
            pltpu.VMEM(ctf.shape, f32),
            pltpu.VMEM((freq,), f32),
            pltpu.VMEM((2, poses, BOX), f32),
            pltpu.SemaphoreType.DMA((2,)),
        ],
        flops=24 * rows * groups * freq,
    )


def write_templates(cls_ref, cos_ref, sin_ref, temp_ref, start, tile):
    rows = cls_ref.shape[1]
    for a in range(0, tile, LANES):
        at = pl.ds(pl.multiple_of(start + a, LANES), LANES)
        re = cls_ref[0, :, at].astype(f32)
        im = cls_ref[1, :, at].astype(f32)
        for r in range(cos_ref.shape[0]):
            cos_r = cos_ref[r : r + 1, at]
            sin_r = sin_ref[r : r + 1, at]
            here = slice(r * rows, (r + 1) * rows)
            temp_ref[here, a : a + LANES] = (re * cos_r - im * sin_r).astype(bf16)
            temp_ref[here, tile + a : tile + a + LANES] = (re * sin_r + im * cos_r).astype(bf16)


def template_tile(freq):
    return max(t for t in range(LANES, 385, LANES) if freq // CHUNKS % t == 0)


def template_kernel(cls_ref, cos_ref, sin_ref, temp_ref):
    write_templates(cls_ref, cos_ref, sin_ref, temp_ref, 0, cls_ref.shape[2])


def build_templates(split, cos_t, sin_t, skip, count, tile):
    _, rows, _ = split.shape
    poses = cos_t.shape[0]
    return pl.pallas_call(
        template_kernel,
        grid=(count,),
        in_specs=[
            pl.BlockSpec((2, rows, tile), lambda j: (0, 0, skip + j)),
            pl.BlockSpec((poses, tile), lambda j: (0, skip + j)),
            pl.BlockSpec((poses, tile), lambda j: (0, skip + j)),
        ],
        out_specs=pl.BlockSpec((None, poses * rows, 2 * tile), lambda j: (j, 0, 0)),
        out_shape=jax.ShapeDtypeStruct((count, poses * rows, 2 * tile), bf16),
        compiler_params=pltpu.CompilerParams(vmem_limit_bytes=VMEM_LIMIT),
        cost_estimate=pl.CostEstimate(
            flops=40 * poses * rows * count * tile,
            bytes_accessed=4 * poses * rows * count * tile,
            transcendentals=0,
        ),
        name=f"templates{skip}",
    )(split, cos_t, sin_t)


def regroup(refs, counts):
    refs = list(refs)
    return [[refs.pop(0) for _ in range(count)] for count in counts]


def tile_of_particles(shards, chunk, span, t, tile, half):
    cuts = []
    for ref, chunked in shards:
        at = t * tile if chunked else chunk * span + t * tile
        cuts.append(ref[:, at : at + tile])
    wide = jnp.concatenate(cuts, axis=0).astype(f32)
    real = real_index(wide.shape, 0, half)
    return jnp.concatenate(
        [jnp.where(real, wide, 0.0).astype(bf16), jnp.where(real, 0.0, wide).astype(bf16)], axis=1
    )


def first_score_kernel(chunked, half, temp_ref, *refs):
    refs, acc_ref = refs[:-1], refs[-1]
    count, _, width = temp_ref.shape
    tile = width // 2
    shards = list(zip(refs, chunked))
    acc_ref[...] = jnp.zeros_like(acc_ref)
    for t in range(count):
        acc_ref[...] += lax.dot_general(
            temp_ref[t],
            tile_of_particles(shards, 0, count * tile, t, tile, half),
            NT,
            preferred_element_type=f32,
        )


def last_score_kernel(chunked, half, temp_ref, pow_ref, acc_ref, *refs):
    refs, (s_ref, marks_ref, stat_ref) = refs[:-3], refs[-3:]
    tail_refs, shards = refs[: len(chunked)], list(zip(refs[len(chunked) :], chunked))
    count, _, width = temp_ref.shape
    tile = width // 2
    rows, groups = pow_ref.shape
    lanes = s_ref.shape[1]
    poses = s_ref.shape[0] // rows
    tails = [ref[:, ref.shape[1] - LANES :] for ref in tail_refs]
    ids = jnp.concatenate(tails, axis=0).astype(f32)
    group = lax.broadcasted_iota(jnp.int32, (lanes, groups), 1).astype(f32)
    marks = (ids[:, :groups] == group).astype(f32)
    marks_ref[...] = marks
    penalty = lax.dot_general(
        pow_ref[...], marks, NT, precision=HIGHEST, preferred_element_type=f32
    )
    s_ref[...] = acc_ref[...]
    for t in range(count):
        s_ref[...] += lax.dot_general(
            temp_ref[t],
            tile_of_particles(shards, 1, count * tile, t, tile, half),
            NT,
            preferred_element_type=f32,
        )
    acc = s_ref[...]
    acc = acc + jnp.where(
        real_index(acc.shape, 1, half), pltpu.roll(acc, lanes - half, 1), pltpu.roll(acc, half, 1)
    )
    scores = acc.reshape(poses, rows, lanes) - 0.5 * penalty[None]
    peak = jnp.max(jnp.max(scores, axis=0), axis=0, keepdims=True)
    total = jnp.sum(jnp.sum(jnp.exp(scores - peak[None]), axis=0), axis=0, keepdims=True)
    s_ref[...] = scores.reshape(poses * rows, lanes)
    stat_ref[0:1, :] = peak
    stat_ref[1:2, :] = total
    stat_ref[2:8, :] = jnp.zeros((6, lanes), f32)


def score(temps, power, shards, half):
    first, late = temps
    count, columns, width = late.shape
    lanes = sum(refs[0].shape[0] for refs in shards)
    chunked = [len(refs) > 1 for refs in shards]
    flops = 2 * columns * 256 * count * width
    acc_shape = jax.ShapeDtypeStruct((columns, lanes), f32)
    operands = [first, *[refs[0] for refs in shards]]
    acc = call(
        functools.partial(first_score_kernel, chunked, half),
        "score0",
        [VMEM] * len(operands),
        [acc_shape],
        operands,
        flops=flops,
    )[0]
    operands = [late, power, acc]
    operands += [refs[0] for refs in shards] + [refs[-1] for refs in shards]
    return call(
        functools.partial(last_score_kernel, chunked, half),
        "score1",
        [VMEM] * len(operands),
        [
            acc_shape,
            jax.ShapeDtypeStruct((lanes, power.shape[1]), f32),
            jax.ShapeDtypeStruct((8, lanes), f32),
        ],
        operands,
        flops=flops,
    )


def slices_kernel(counts, targets, me_ref, *refs):
    whole_ref, refs = refs[-1], refs[:-1]
    shards, out_refs = regroup(refs[: -len(targets)], counts), refs[-len(targets) :]
    span = out_refs[0].shape[1]
    filled = [0] * len(targets)
    for k, refs in enumerate(shards):
        source = refs[0]
        height = source.shape[0]
        if len(refs) > 1:
            width = refs[-1].shape[1]
            for c, ref in enumerate(refs):
                whole_ref[:, c * width : (c + 1) * width] = ref[:, :width]
            source = whole_ref
        for i, (distance, skip) in enumerate(targets):
            if k >= skip:
                base = pl.multiple_of((me_ref[0] ^ distance) * span, LANES)
                out_refs[i][filled[i] : filled[i] + height, :] = source[:, pl.ds(base, span)]
                filled[i] += height


def cut_slices(me, shards, targets, span, freq):
    heights = [refs[0].shape[0] for refs in shards]
    operands = [me, *[ref for refs in shards for ref in refs]]
    out_heights = [sum(heights[skip:]) for _, skip in targets]
    return call(
        functools.partial(slices_kernel, [len(refs) for refs in shards], targets),
        "cut_slices",
        [SMEM] + [VMEM] * (len(operands) - 1),
        [jax.ShapeDtypeStruct((height, span), bf16) for height in out_heights],
        operands,
        [pltpu.VMEM((heights[-1], freq), bf16)],
        moved=4 * span * sum(out_heights),
        limit=VMEM_LIMIT if sum(heights) <= 128 else 2 * VMEM_LIMIT,
    )


def bundle_kernel(*refs):
    sources, out_ref = refs[:-1], refs[-1]
    rows = out_ref.shape[0] // len(sources)
    for i, ref in enumerate(sources):
        out_ref[i * rows : (i + 1) * rows, :] = ref[ref.shape[0] - rows :, :]


def bundle(slices, rows):
    span = slices[0].shape[1]
    return call(
        bundle_kernel,
        "bundle",
        [VMEM] * len(slices),
        [jax.ShapeDtypeStruct((len(slices) * rows, span), bf16)],
        slices,
        moved=4 * len(slices) * rows * span,
    )[0]


def xor_blocks(values, block, distance):
    lanes = values.shape[1]
    lane = lax.broadcasted_iota(jnp.int32, values.shape, 1)
    width = block
    while distance:
        if distance % 2:
            low = lax.rem(lane // width, 2) == 0
            values = jnp.where(
                low, pltpu.roll(values, lanes - width, 1), pltpu.roll(values, width, 1)
            )
        distance //= 2
        width *= 2
    return values


def rho_kernel(poses, half, paired, s_ref, marks_ref, *refs):
    stat_refs, (norm_ref, out_ref) = refs[: len(paired)], refs[len(paired) :]
    lanes = s_ref.shape[1]
    rows = s_ref.shape[0] // poses
    groups = marks_ref.shape[1]
    block = 2 * half
    peaks, totals = [], []
    for ref, distance in zip(stat_refs, paired):
        for at in range(0, ref.shape[0], 8):
            stats = xor_blocks(ref[at : at + 8, :], block, distance)
            peaks.append(stats[0:1])
            totals.append(stats[1:2])
    peak = functools.reduce(jnp.maximum, peaks)
    total = sum(t * jnp.exp(p - peak) for t, p in zip(totals, peaks))
    log_norm = peak + jnp.log(total)
    norm_ref[...] = log_norm
    rho = jnp.exp(s_ref[...].reshape(poses, rows, lanes) - log_norm[None])
    mass = lax.dot_general(
        jnp.where(real_index((rows, lanes), 1, half), jnp.sum(rho, axis=0), 0.0),
        marks_ref[...],
        NN,
        precision=HIGHEST,
        preferred_element_type=f32,
    )
    high = mass.astype(bf16)
    low = (mass - high.astype(f32)).astype(bf16)
    rho_low = rho.reshape(poses * rows, lanes).astype(bf16)
    cut = poses // 2 * rows
    lane = lax.broadcasted_iota(jnp.int32, (lanes, lanes), 0)
    column = lax.broadcasted_iota(jnp.int32, (lanes, lanes), 1)
    particle = lane // block * half + lax.rem(lane, block)
    real = lax.rem(lane, block) < half
    first = (real & (column == particle)).astype(f32).astype(bf16)
    second = (real & (column == particle + lanes // 2)).astype(f32).astype(bf16)
    packed = jnp.dot(rho_low[:cut], first, preferred_element_type=f32)
    packed += jnp.dot(rho_low[cut:], second, preferred_element_type=f32)
    out_ref[:cut, :] = packed.astype(bf16)
    if lanes > 2 * groups:
        out_ref[cut:, :] = jnp.zeros((rows, lanes), bf16)
    out_ref[cut:, :groups] = high
    out_ref[cut:, groups : 2 * groups] = low


def responsibilities(scores, marks, stats, paired, poses, half):
    columns, lanes = scores.shape
    return call(
        functools.partial(rho_kernel, poses, half, paired),
        "responsibilities",
        [VMEM] * (2 + len(stats)),
        [
            jax.ShapeDtypeStruct((1, lanes), f32),
            jax.ShapeDtypeStruct((columns // 2 + columns // poses, lanes), bf16),
        ],
        (scores, marks, *stats),
        flops=40 * columns * lanes,
    )


def gather_kernel(poses, half, counts, me_ref, s_ref, norm_ref, weight_ref, *refs):
    w_refs, (resp_ref, cw_ref, rows_ref) = refs[:-3], refs[-3:]
    span = rows_ref.shape[2]
    block = 2 * half
    here = pl.ds(pl.multiple_of(me_ref[0] * span, LANES), span)
    at = 0
    for refs in regroup(w_refs, counts):
        for ref in refs:
            for start in range(0, ref.shape[0], block):
                rows_ref[0, at : at + half, :] = ref[start : start + half, :]
                rows_ref[1, at : at + half, :] = ref[start + half : start + block, :]
                at += half
    weight = weight_ref[:, here]
    high = weight.astype(bf16)
    cw_ref[:, :span] = high
    cw_ref[:, span:] = (weight - high.astype(f32)).astype(bf16)
    rows = resp_ref.shape[0]
    lanes = s_ref.shape[1]
    scores = s_ref[...].reshape(poses, rows, lanes)
    pose_peak = jnp.max(scores, axis=0)
    total = jnp.sum(jnp.exp(scores - pose_peak[None]), axis=0)
    log_resp = pose_peak + jnp.log(total) - norm_ref[...]
    shape = (resp_ref.shape[1], lanes)
    lane = lax.broadcasted_iota(jnp.int32, shape, 1)
    row = ((lane // block) ^ me_ref[1]) * half + lax.rem(lane, block)
    take = (lax.broadcasted_iota(jnp.int32, shape, 0) == row) & (lax.rem(lane, block) < half)
    resp_ref[...] = lax.dot_general(
        log_resp, take.astype(f32), NT, precision=HIGHEST, preferred_element_type=f32
    )


def gather_rows(me, scores, norm, weight, slices, poses, half, span):
    columns, lanes = scores.shape
    counts = [len(refs) for refs in slices]
    slices = [w for refs in slices for w in refs]
    particles = sum(w.shape[0] for w in slices) // 2
    return call(
        functools.partial(gather_kernel, poses, half, counts),
        "gather_rows",
        [SMEM] + [VMEM] * (3 + len(slices)),
        [
            jax.ShapeDtypeStruct((columns // poses, lanes // 2), f32),
            jax.ShapeDtypeStruct((weight.shape[0], 2 * span), bf16),
            jax.ShapeDtypeStruct((2, particles, span), bf16),
        ],
        (me, scores, norm, weight, *slices),
        flops=GATHER_FLOPS,
        moved=8 * particles * span,
        limit=VMEM_LIMIT if particles <= 512 else 2 * VMEM_LIMIT,
    )


def finish_kernel(poses, groups, sources, half, me_ref, cw_ref, cos_ref, sin_ref, rows_ref, *refs):
    payloads, refs = refs[:sources], refs[sources:]
    last, (out_ref, rho_ref, inverse_ref, *buffers) = refs[:-5], refs[-5:]
    rows, _, span = out_ref.shape
    cut = poses // 2 * rows
    count = payloads[0].shape[1] // 2
    mass = jnp.zeros((rows, groups), f32)
    for i, ref in enumerate(payloads):
        rho_ref[:cut, i * count : (i + 1) * count] = ref[:cut, :count]
        rho_ref[cut:, i * count : (i + 1) * count] = ref[:cut, count:]
        mass += ref[cut:, :groups].astype(f32) + ref[cut:, groups : 2 * groups].astype(f32)
    high = mass.astype(bf16)
    mass = jnp.concatenate([high, (mass - high.astype(f32)).astype(bf16)], axis=0)
    terms = jnp.dot(mass, cw_ref[...], preferred_element_type=f32)
    denom = (terms[:rows, :span] + terms[rows:, :span]) + (terms[:rows, span:] + terms[rows:, span:])
    inverse_ref[...] = 1.0 / (denom + prior_precision)
    tiles = [(a, min(256, span - a)) for a in range(0, span, 256)]
    known = rows_ref.shape[1] // sources

    def rows_of(part, start, width):
        here = slice(start, start + width)
        if not last:
            return rows_ref[part, :, here]
        pieces = []
        for i in range(sources):
            pieces.append(rows_ref[part, i * known : (i + 1) * known, here])
            if i == 0:
                pieces.append(last[0][part * half : (part + 1) * half, here])
            else:
                at = (2 * (i - 1) + part) * half
                pieces.append(last[1][at : at + half, here])
        return jnp.concatenate(pieces, axis=0)

    def products(i):
        start, width = tiles[i]
        for part in range(2):
            buffers[i % 2][part, :, :width] = jnp.dot(
                rho_ref[...], rows_of(part, start, width), preferred_element_type=f32
            )

    def rotate(i):
        start, width = tiles[i]
        buffer = buffers[i % 2]
        for a in range(0, width, LANES):
            at = pl.ds(pl.multiple_of(me_ref[0] * span + start + a, LANES), LANES)
            numer_re = jnp.zeros((rows, LANES), f32)
            numer_im = jnp.zeros((rows, LANES), f32)
            for r in range(poses):
                cos_r = cos_ref[r : r + 1, at]
                sin_r = sin_ref[r : r + 1, at]
                s_re = buffer[0, r * rows : (r + 1) * rows, a : a + LANES]
                s_im = buffer[1, r * rows : (r + 1) * rows, a : a + LANES]
                numer_re = numer_re + s_re * cos_r + s_im * sin_r
                numer_im = numer_im + s_im * cos_r - s_re * sin_r
            here = slice(start + a, start + a + LANES)
            inverse = inverse_ref[:, here]
            out_ref[:, 0, here] = numer_re * inverse
            out_ref[:, 1, here] = numer_im * inverse

    products(0)
    for i in range(1, len(tiles)):
        products(i)
        rotate(i - 1)
    rotate(len(tiles) - 1)


def finish(me, weight, cos_t, sin_t, rows, payloads, last, cls_rows, half):
    poses = cos_t.shape[0]
    span = rows.shape[2]
    particles = len(payloads) * payloads[0].shape[1] // 2
    return call(
        functools.partial(finish_kernel, poses, weight.shape[0], len(payloads), half),
        "finish",
        [SMEM] + [VMEM] * (4 + len(payloads) + len(last)),
        [jax.ShapeDtypeStruct((cls_rows, 2, span), f32)],
        (me, weight, cos_t, sin_t, rows, *payloads, *last),
        [
            pltpu.VMEM((poses * cls_rows, particles), bf16),
            pltpu.VMEM((cls_rows, span), f32),
            pltpu.VMEM((2, poses * cls_rows, 256), f32),
            pltpu.VMEM((2, poses * cls_rows, 256), f32),
        ],
        flops=4 * poses * cls_rows * particles * span,
        limit=VMEM_LIMIT if particles <= 512 else 2 * VMEM_LIMIT,
    )[0]


def swap(values, axis, distance):
    size = lax.axis_size(axis)
    return lax.ppermute(values, axis, [(i, i ^ distance) for i in range(size)])


def local(particles, classes, ctf, noise_weight, group_ids, shifts):
    half, _, freq = particles.shape
    cls_rows = classes.shape[0]
    poses = shifts.shape[0]
    n_cls = lax.axis_size("cls")
    n_img = lax.axis_size("img")
    span = freq // n_img
    pairwise = n_cls == 4
    me_cls = lax.axis_index("cls") if pairwise else 0
    me = jnp.stack([lax.axis_index("img"), me_cls]).astype(jnp.int32)
    others = tuple(range(n_img - 1, 0, -1))

    own, *own_chunks = weigh(particles, ctf, noise_weight, group_ids)
    if pairwise:
        far = [swap(w, "cls", 2) for w in own_chunks]
        near = swap(own, "cls", 1)
        mine, *outgoing = cut_slices(me, [[own]], [(d, 0) for d in (0,) + others[:-1]], span, freq)
        slices = [mine] + [swap(w, "img", d) for w, d in zip(outgoing, others)]
    else:
        shards = [[lax.all_gather(own, "cls", axis=0, tiled=True)]]
        mine, *outgoing = cut_slices(me, shards, [(d, 0) for d in (0,) + others], span, freq)
        slices = [[w] for w in [mine] + [swap(w, "img", d) for w, d in zip(outgoing, others)]]

    split = jnp.transpose(classes, (1, 0, 2))
    cos_t, sin_t, power, weight = prepare(shifts, split, ctf, noise_weight)
    tile = template_tile(freq)
    count = freq // CHUNKS // tile
    temps = [
        build_templates(split, cos_t, sin_t, c * count, count, tile) for c in range(CHUNKS)
    ]
    if pairwise:
        far, near, slices, power, temps = lax.optimization_barrier(
            (far, near, slices, power, temps)
        )
        third = [swap(w, "cls", 1) for w in far]
        targets = [(d, 1) for d in (0,) + others[:-1]] + [(others[-1], 0)]
        mine, *outgoing = cut_slices(me, [[own], [near], far], targets, span, freq)
        arrived = [mine] + [swap(w, "img", d) for w, d in zip(outgoing, others)]
        shards = [[own], [near], far, third]
    scores, marks, stat = score(temps, power, shards, half)
    if pairwise:
        stat, arrived[-1] = lax.optimization_barrier((stat, arrived[-1]))
        stats = [stat] + [swap(stat, "cls", k) for k in range(n_cls - 1, 0, -1)]
        paired = (0,) + tuple(range(n_cls - 1, 0, -1))
        last = [*cut_slices(me, [third], [(0, 0)], span, freq)]
        last.append(swap(bundle(arrived[1:], 2 * half), "cls", 1))
        slices = [[a, b] for a, b in zip(slices, arrived)] + [arrived[-1:]]
    else:
        stats = [lax.all_gather(stat, "cls", axis=0, tiled=True)]
        paired = (0,)
        last = []
    norm, payload = responsibilities(scores, marks, stats, paired, poses, half)
    payloads = [payload] + [swap(payload, "img", d) for d in others]
    log_resp, weight_here, rows = gather_rows(
        me, scores, norm, weight, slices, poses, half, span
    )
    averages = finish(me, weight_here, cos_t, sin_t, rows, payloads, last, cls_rows, half)
    return (log_resp.T, averages)


def solution(mesh):
    placed = (
        P(("groups", "img", "cls"), None, None),
        P(("groups", "cls"), None, None),
        P("groups", None),
        P("groups"),
        P(("groups", "img", "cls")),
        P("groups", None),
    )
    return jax.shard_map(
        local,
        mesh=mesh,
        in_specs=placed,
        out_specs=(P(("groups", "img"), "cls"), P(("groups", "cls"), None, "img")),
        check_vma=False,
    )
```

```python
import functools

import jax
import jax.numpy as jnp
from jax import lax
from jax.experimental import pallas as pl
from jax.experimental.pallas import tpu as pltpu
from jax.sharding import PartitionSpec as P

BOX = 128
LANES = 128
VMEM_LIMIT = 24 * 1024 * 1024
GATHER_FLOPS = 20_000_000_000

prior_precision = 0.02

NT = (((1,), (1,)), ((), ()))
NN = (((1,), (0,)), ((), ()))
HIGHEST = lax.Precision.HIGHEST
f32 = jnp.float32
bf16 = jnp.bfloat16

SMEM = pl.BlockSpec(memory_space=pltpu.SMEM)
VMEM = pl.BlockSpec(memory_space=pltpu.VMEM)
ANY = pl.BlockSpec(memory_space=pl.ANY)


def call(kernel, name, in_specs, out_shape, operands, scratch=(), flops=0, moved=0, limit=VMEM_LIMIT):
    return pl.pallas_call(
        kernel,
        in_specs=in_specs,
        out_specs=[VMEM] * len(out_shape),
        out_shape=out_shape,
        scratch_shapes=list(scratch),
        compiler_params=pltpu.CompilerParams(vmem_limit_bytes=limit),
        cost_estimate=pl.CostEstimate(flops=flops, bytes_accessed=moved, transcendentals=0),
        name=name,
    )(*operands)


def real_index(shape, axis, half):
    return lax.rem(lax.broadcasted_iota(jnp.int32, shape, axis) // half, 2) == 0


def weigh_kernel(
    ids_hbm, p_hbm, ctf_hbm, nw_hbm, out_ref, ids_ref, p_ref, ctf_ref, nw_ref, scale_ref, sem
):
    count, _, freq = p_ref.shape
    copies = [
        pltpu.make_async_copy(source, target, sem.at[i])
        for i, (source, target) in enumerate(
            [(ids_hbm, ids_ref), (ctf_hbm, ctf_ref), (nw_hbm, nw_ref), (p_hbm, p_ref)]
        )
    ]
    for copy in copies:
        copy.start()
    copies[0].wait()
    row = lax.rem(lax.broadcasted_iota(jnp.int32, (2 * count, LANES), 0), count)
    ids = jnp.zeros((2 * count, LANES), f32)
    for n in range(count):
        ids = jnp.where(row == n, ids_ref[n].astype(f32), ids)
    for copy in copies[1:]:
        copy.wait()
    noise = nw_ref[...].reshape(1, freq)
    for n in range(count):
        scale_ref[n : n + 1, :] = ctf_ref[pl.ds(ids_ref[n], 1), :] * noise
    scale = scale_ref[...]
    values = p_ref[...].astype(f32)
    for part in range(2):
        here = slice(part * count, (part + 1) * count)
        out_ref[here, :freq] = (values[:, part, :] * scale).astype(bf16)
    out_ref[:, freq:] = ids.astype(bf16)


def weigh(particles, ctf, noise_weight, group_ids):
    rows, _, freq = particles.shape
    operands = (group_ids, particles, ctf, noise_weight)
    return call(
        weigh_kernel,
        "weigh",
        [ANY] * 4,
        [jax.ShapeDtypeStruct((2 * rows, freq + LANES), bf16)],
        [pltpu.with_memory_space_constraint(x, pltpu.HBM) for x in operands],
        [
            pltpu.SMEM((rows,), jnp.int32),
            pltpu.VMEM(particles.shape, bf16),
            pltpu.VMEM(ctf.shape, f32),
            pltpu.VMEM((freq,), f32),
            pltpu.VMEM((rows, freq), f32),
            pltpu.SemaphoreType.DMA((4,)),
        ],
        flops=4 * rows * freq,
        moved=16 * rows * freq,
    )[0]


def prepare_kernel(
    shifts_ref, cls_ref, ctf_hbm, nw_hbm, cos_ref, sin_ref, pow_ref, cw_ref, *scratch
):
    ctf_ref, nw_ref, angle_ref, sem = scratch
    freq = cls_ref.shape[2]
    poses = cos_ref.shape[0]
    copies = [
        pltpu.make_async_copy(source, target, sem.at[i])
        for i, (source, target) in enumerate(
            [(ctf_hbm, ctf_ref), (nw_hbm, nw_ref)]
        )
    ]
    for copy in copies:
        copy.start()
    lane = lax.broadcasted_iota(jnp.int32, (1, BOX), 1).astype(f32)
    step = 2.0 * jnp.pi / BOX
    for r in range(poses):
        angle_ref[0, r : r + 1, :] = step * (shifts_ref[0, r].astype(f32) * (lane - BOX // 2))
        angle_ref[1, r : r + 1, :] = step * (shifts_ref[1, r].astype(f32) * lane)
    x_cos, x_sin = jnp.cos(angle_ref[0]), jnp.sin(angle_ref[0])
    y_cos, y_sin = jnp.cos(angle_ref[1]), jnp.sin(angle_ref[1])
    for t in range(freq // BOX):
        c = jnp.broadcast_to(y_cos[:, t : t + 1], x_cos.shape)
        s = jnp.broadcast_to(y_sin[:, t : t + 1], x_cos.shape)
        cos_ref[:, t * BOX : (t + 1) * BOX] = x_cos * c - x_sin * s
        sin_ref[:, t * BOX : (t + 1) * BOX] = x_sin * c + x_cos * s
    for copy in copies:
        copy.wait()
    noise = nw_ref[...].reshape(1, freq)
    cut = freq // 4
    power = jnp.zeros(pow_ref.shape, f32)
    for q in range(4):
        at = slice(q * cut, (q + 1) * cut)
        re = cls_ref[0, :, at].astype(f32)
        im = cls_ref[1, :, at].astype(f32)
        ctf = ctf_ref[:, at]
        weight = ctf * ctf * noise[:, at]
        cw_ref[:, at] = weight
        power += lax.dot_general(
            re * re + im * im, weight, NT, precision=HIGHEST, preferred_element_type=f32
        )
    pow_ref[...] = power


def prepare(shifts, split, ctf, noise_weight):
    _, rows, freq = split.shape
    poses, groups = shifts.shape[0], ctf.shape[0]
    return call(
        prepare_kernel,
        "prepare",
        [SMEM, VMEM, ANY, ANY],
        [
            jax.ShapeDtypeStruct((poses, freq), f32),
            jax.ShapeDtypeStruct((poses, freq), f32),
            jax.ShapeDtypeStruct((rows, groups), f32),
            jax.ShapeDtypeStruct((groups, freq), f32),
        ],
        (
            shifts.T,
            split,
            *[pltpu.with_memory_space_constraint(x, pltpu.HBM) for x in (ctf, noise_weight)],
        ),
        [
            pltpu.VMEM(ctf.shape, f32),
            pltpu.VMEM((freq,), f32),
            pltpu.VMEM((2, poses, BOX), f32),
            pltpu.SemaphoreType.DMA((2,)),
        ],
        flops=24 * rows * groups * freq,
    )


def write_templates(cls_ref, cos_ref, sin_ref, temp_ref, start, tile):
    rows = cls_ref.shape[1]
    for a in range(0, tile, LANES):
        at = pl.ds(pl.multiple_of(start + a, LANES), LANES)
        re = cls_ref[0, :, at].astype(f32)
        im = cls_ref[1, :, at].astype(f32)
        for r in range(cos_ref.shape[0]):
            cos_r = cos_ref[r : r + 1, at]
            sin_r = sin_ref[r : r + 1, at]
            here = slice(r * rows, (r + 1) * rows)
            temp_ref[here, a : a + LANES] = (re * cos_r - im * sin_r).astype(bf16)
            temp_ref[here, tile + a : tile + a + LANES] = (re * sin_r + im * cos_r).astype(bf16)


def template_tile(freq):
    return max(t for t in range(LANES, 385, LANES) if freq // 2 % t == 0)


def template_kernel(cls_ref, cos_ref, sin_ref, temp_ref):
    write_templates(cls_ref, cos_ref, sin_ref, temp_ref, 0, cls_ref.shape[2])


def build_templates(split, cos_t, sin_t, skip, count, tile):
    _, rows, _ = split.shape
    poses = cos_t.shape[0]
    return pl.pallas_call(
        template_kernel,
        grid=(count,),
        in_specs=[
            pl.BlockSpec((2, rows, tile), lambda j: (0, 0, skip + j)),
            pl.BlockSpec((poses, tile), lambda j: (0, skip + j)),
            pl.BlockSpec((poses, tile), lambda j: (0, skip + j)),
        ],
        out_specs=pl.BlockSpec((None, poses * rows, 2 * tile), lambda j: (j, 0, 0)),
        out_shape=jax.ShapeDtypeStruct((count, poses * rows, 2 * tile), bf16),
        compiler_params=pltpu.CompilerParams(vmem_limit_bytes=VMEM_LIMIT),
        cost_estimate=pl.CostEstimate(
            flops=40 * poses * rows * count * tile,
            bytes_accessed=4 * poses * rows * count * tile,
            transcendentals=0,
        ),
        name=f"templates{skip}",
    )(split, cos_t, sin_t)


def regroup(refs, counts):
    refs = list(refs)
    return [[refs.pop(0) for _ in range(count)] for count in counts]


def score_kernel(half, parts, pow_ref, *refs):
    temp_refs, refs = refs[:parts], refs[parts:]
    shards, (s_ref, marks_ref, stat_ref) = refs[:-3], refs[-3:]
    rows, groups = pow_ref.shape
    lanes = s_ref.shape[1]
    poses = s_ref.shape[0] // rows
    tails = [ref[:, ref.shape[1] - LANES :] for ref in shards]
    ids = jnp.concatenate(tails, axis=0).astype(f32)
    group = lax.broadcasted_iota(jnp.int32, (lanes, groups), 1).astype(f32)
    marks = (ids[:, :groups] == group).astype(f32)
    marks_ref[...] = marks
    penalty = lax.dot_general(
        pow_ref[...], marks, NT, precision=HIGHEST, preferred_element_type=f32
    )
    temps = [ref.at[t] for ref in temp_refs for t in range(ref.shape[0])]
    tile = temp_refs[0].shape[2] // 2
    real = real_index((lanes, tile), 0, half)
    s_ref[...] = jnp.zeros_like(s_ref)
    for t, temp in enumerate(temps):
        at = slice(t * tile, (t + 1) * tile)
        wide = jnp.concatenate([ref[:, at] for ref in shards], axis=0).astype(f32)
        split = jnp.concatenate(
            [jnp.where(real, wide, 0.0).astype(bf16), jnp.where(real, 0.0, wide).astype(bf16)],
            axis=1,
        )
        s_ref[...] += lax.dot_general(temp[...], split, NT, preferred_element_type=f32)
    acc = s_ref[...]
    acc = acc + jnp.where(
        real_index(acc.shape, 1, half), pltpu.roll(acc, lanes - half, 1), pltpu.roll(acc, half, 1)
    )
    scores = acc.reshape(poses, rows, lanes) - 0.5 * penalty[None]
    peak = jnp.max(jnp.max(scores, axis=0), axis=0, keepdims=True)
    total = jnp.sum(jnp.sum(jnp.exp(scores - peak[None]), axis=0), axis=0, keepdims=True)
    s_ref[...] = scores.reshape(poses * rows, lanes)
    stat_ref[0:1, :] = peak
    stat_ref[1:2, :] = total
    stat_ref[2:8, :] = jnp.zeros((6, lanes), f32)


def score(temps, power, shards, half):
    count, columns, width = temps[0].shape
    lanes = sum(ref.shape[0] for ref in shards)
    operands = [power, *temps, *shards]
    return call(
        functools.partial(score_kernel, half, len(temps)),
        "score",
        [VMEM] * len(operands),
        [
            jax.ShapeDtypeStruct((columns, lanes), f32),
            jax.ShapeDtypeStruct((lanes, power.shape[1]), f32),
            jax.ShapeDtypeStruct((8, lanes), f32),
        ],
        operands,
        flops=2 * columns * 256 * count * len(temps) * width,
    )


def regroup(refs, counts):
    refs = list(refs)
    return [[refs.pop(0) for _ in range(count)] for count in counts]


def slices_kernel(targets, me_ref, *refs):
    shards, out_refs = refs[: -len(targets)], refs[-len(targets) :]
    span = out_refs[0].shape[1]
    filled = [0] * len(targets)
    for k, ref in enumerate(shards):
        height = ref.shape[0]
        for i, (distance, skip) in enumerate(targets):
            if k >= skip:
                base = pl.multiple_of((me_ref[0] ^ distance) * span, LANES)
                out_refs[i][filled[i] : filled[i] + height, :] = ref[:, pl.ds(base, span)]
                filled[i] += height


def cut_slices(me, shards, targets, span):
    heights = [ref.shape[0] for ref in shards]
    out_heights = [sum(heights[skip:]) for _, skip in targets]
    return call(
        functools.partial(slices_kernel, targets),
        "cut_slices",
        [SMEM] + [VMEM] * len(shards),
        [jax.ShapeDtypeStruct((height, span), bf16) for height in out_heights],
        (me, *shards),
        moved=4 * span * sum(out_heights),
        limit=VMEM_LIMIT if sum(heights) <= 128 else 2 * VMEM_LIMIT,
    )


def bundle_kernel(*refs):
    sources, out_ref = refs[:-1], refs[-1]
    rows = out_ref.shape[0] // len(sources)
    for i, ref in enumerate(sources):
        out_ref[i * rows : (i + 1) * rows, :] = ref[ref.shape[0] - rows :, :]


def bundle(slices, rows):
    span = slices[0].shape[1]
    return call(
        bundle_kernel,
        "bundle",
        [VMEM] * len(slices),
        [jax.ShapeDtypeStruct((len(slices) * rows, span), bf16)],
        slices,
        moved=4 * len(slices) * rows * span,
    )[0]


def xor_blocks(values, block, distance):
    lanes = values.shape[1]
    lane = lax.broadcasted_iota(jnp.int32, values.shape, 1)
    width = block
    while distance:
        if distance % 2:
            low = lax.rem(lane // width, 2) == 0
            values = jnp.where(
                low, pltpu.roll(values, lanes - width, 1), pltpu.roll(values, width, 1)
            )
        distance //= 2
        width *= 2
    return values


def rho_kernel(poses, half, paired, s_ref, marks_ref, *refs):
    stat_refs, (norm_ref, out_ref) = refs[: len(paired)], refs[len(paired) :]
    lanes = s_ref.shape[1]
    rows = s_ref.shape[0] // poses
    groups = marks_ref.shape[1]
    block = 2 * half
    peaks, totals = [], []
    for ref, distance in zip(stat_refs, paired):
        for at in range(0, ref.shape[0], 8):
            stats = xor_blocks(ref[at : at + 8, :], block, distance)
            peaks.append(stats[0:1])
            totals.append(stats[1:2])
    peak = functools.reduce(jnp.maximum, peaks)
    total = sum(t * jnp.exp(p - peak) for t, p in zip(totals, peaks))
    log_norm = peak + jnp.log(total)
    norm_ref[...] = log_norm
    rho = jnp.exp(s_ref[...].reshape(poses, rows, lanes) - log_norm[None])
    mass = lax.dot_general(
        jnp.where(real_index((rows, lanes), 1, half), jnp.sum(rho, axis=0), 0.0),
        marks_ref[...],
        NN,
        precision=HIGHEST,
        preferred_element_type=f32,
    )
    high = mass.astype(bf16)
    low = (mass - high.astype(f32)).astype(bf16)
    rho_low = rho.reshape(poses * rows, lanes).astype(bf16)
    cut = poses // 2 * rows
    lane = lax.broadcasted_iota(jnp.int32, (lanes, lanes), 0)
    column = lax.broadcasted_iota(jnp.int32, (lanes, lanes), 1)
    particle = lane // block * half + lax.rem(lane, block)
    real = lax.rem(lane, block) < half
    first = (real & (column == particle)).astype(f32).astype(bf16)
    second = (real & (column == particle + lanes // 2)).astype(f32).astype(bf16)
    packed = jnp.dot(rho_low[:cut], first, preferred_element_type=f32)
    packed += jnp.dot(rho_low[cut:], second, preferred_element_type=f32)
    out_ref[:cut, :] = packed.astype(bf16)
    if lanes > 2 * groups:
        out_ref[cut:, :] = jnp.zeros((rows, lanes), bf16)
    out_ref[cut:, :groups] = high
    out_ref[cut:, groups : 2 * groups] = low


def responsibilities(scores, marks, stats, paired, poses, half):
    columns, lanes = scores.shape
    return call(
        functools.partial(rho_kernel, poses, half, paired),
        "responsibilities",
        [VMEM] * (2 + len(stats)),
        [
            jax.ShapeDtypeStruct((1, lanes), f32),
            jax.ShapeDtypeStruct((columns // 2 + columns // poses, lanes), bf16),
        ],
        (scores, marks, *stats),
        flops=40 * columns * lanes,
    )


def gather_kernel(poses, half, counts, me_ref, s_ref, norm_ref, weight_ref, *refs):
    w_refs, (resp_ref, cw_ref, rows_ref) = refs[:-3], refs[-3:]
    span = rows_ref.shape[2]
    block = 2 * half
    here = pl.ds(pl.multiple_of(me_ref[0] * span, LANES), span)
    at = 0
    for refs in regroup(w_refs, counts):
        for ref in refs:
            for start in range(0, ref.shape[0], block):
                rows_ref[0, at : at + half, :] = ref[start : start + half, :]
                rows_ref[1, at : at + half, :] = ref[start + half : start + block, :]
                at += half
    weight = weight_ref[:, here]
    high = weight.astype(bf16)
    cw_ref[:, :span] = high
    cw_ref[:, span:] = (weight - high.astype(f32)).astype(bf16)
    rows = resp_ref.shape[0]
    lanes = s_ref.shape[1]
    scores = s_ref[...].reshape(poses, rows, lanes)
    pose_peak = jnp.max(scores, axis=0)
    total = jnp.sum(jnp.exp(scores - pose_peak[None]), axis=0)
    log_resp = pose_peak + jnp.log(total) - norm_ref[...]
    shape = (resp_ref.shape[1], lanes)
    lane = lax.broadcasted_iota(jnp.int32, shape, 1)
    row = ((lane // block) ^ me_ref[1]) * half + lax.rem(lane, block)
    take = (lax.broadcasted_iota(jnp.int32, shape, 0) == row) & (lax.rem(lane, block) < half)
    resp_ref[...] = lax.dot_general(
        log_resp, take.astype(f32), NT, precision=HIGHEST, preferred_element_type=f32
    )


def gather_rows(me, scores, norm, weight, slices, poses, half, span):
    columns, lanes = scores.shape
    counts = [len(refs) for refs in slices]
    slices = [w for refs in slices for w in refs]
    particles = sum(w.shape[0] for w in slices) // 2
    return call(
        functools.partial(gather_kernel, poses, half, counts),
        "gather_rows",
        [SMEM] + [VMEM] * (3 + len(slices)),
        [
            jax.ShapeDtypeStruct((columns // poses, lanes // 2), f32),
            jax.ShapeDtypeStruct((weight.shape[0], 2 * span), bf16),
            jax.ShapeDtypeStruct((2, particles, span), bf16),
        ],
        (me, scores, norm, weight, *slices),
        flops=GATHER_FLOPS,
        moved=8 * particles * span,
        limit=VMEM_LIMIT if particles <= 512 else 2 * VMEM_LIMIT,
    )


def finish_kernel(poses, groups, sources, half, me_ref, cw_ref, cos_ref, sin_ref, rows_ref, *refs):
    payloads, refs = refs[:sources], refs[sources:]
    last, (out_ref, rho_ref, inverse_ref, *buffers) = refs[:-5], refs[-5:]
    rows, _, span = out_ref.shape
    cut = poses // 2 * rows
    count = payloads[0].shape[1] // 2
    mass = jnp.zeros((rows, groups), f32)
    for i, ref in enumerate(payloads):
        rho_ref[:cut, i * count : (i + 1) * count] = ref[:cut, :count]
        rho_ref[cut:, i * count : (i + 1) * count] = ref[:cut, count:]
        mass += ref[cut:, :groups].astype(f32) + ref[cut:, groups : 2 * groups].astype(f32)
    high = mass.astype(bf16)
    mass = jnp.concatenate([high, (mass - high.astype(f32)).astype(bf16)], axis=0)
    terms = jnp.dot(mass, cw_ref[...], preferred_element_type=f32)
    denom = (terms[:rows, :span] + terms[rows:, :span]) + (terms[:rows, span:] + terms[rows:, span:])
    inverse_ref[...] = 1.0 / (denom + prior_precision)
    tiles = [(a, min(256, span - a)) for a in range(0, span, 256)]
    known = rows_ref.shape[1] // sources

    def rows_of(part, start, width):
        here = slice(start, start + width)
        if not last:
            return rows_ref[part, :, here]
        pieces = []
        for i in range(sources):
            pieces.append(rows_ref[part, i * known : (i + 1) * known, here])
            if i == 0:
                pieces.append(last[0][part * half : (part + 1) * half, here])
            else:
                at = (2 * (i - 1) + part) * half
                pieces.append(last[1][at : at + half, here])
        return jnp.concatenate(pieces, axis=0)

    def products(i):
        start, width = tiles[i]
        for part in range(2):
            buffers[i % 2][part, :, :width] = jnp.dot(
                rho_ref[...], rows_of(part, start, width), preferred_element_type=f32
            )

    def rotate(i):
        start, width = tiles[i]
        buffer = buffers[i % 2]
        for a in range(0, width, LANES):
            at = pl.ds(pl.multiple_of(me_ref[0] * span + start + a, LANES), LANES)
            numer_re = jnp.zeros((rows, LANES), f32)
            numer_im = jnp.zeros((rows, LANES), f32)
            for r in range(poses):
                cos_r = cos_ref[r : r + 1, at]
                sin_r = sin_ref[r : r + 1, at]
                s_re = buffer[0, r * rows : (r + 1) * rows, a : a + LANES]
                s_im = buffer[1, r * rows : (r + 1) * rows, a : a + LANES]
                numer_re = numer_re + s_re * cos_r + s_im * sin_r
                numer_im = numer_im + s_im * cos_r - s_re * sin_r
            here = slice(start + a, start + a + LANES)
            inverse = inverse_ref[:, here]
            out_ref[:, 0, here] = numer_re * inverse
            out_ref[:, 1, here] = numer_im * inverse

    products(0)
    for i in range(1, len(tiles)):
        products(i)
        rotate(i - 1)
    rotate(len(tiles) - 1)


def finish(me, weight, cos_t, sin_t, rows, payloads, last, cls_rows, half):
    poses = cos_t.shape[0]
    span = rows.shape[2]
    particles = len(payloads) * payloads[0].shape[1] // 2
    return call(
        functools.partial(finish_kernel, poses, weight.shape[0], len(payloads), half),
        "finish",
        [SMEM] + [VMEM] * (4 + len(payloads) + len(last)),
        [jax.ShapeDtypeStruct((cls_rows, 2, span), f32)],
        (me, weight, cos_t, sin_t, rows, *payloads, *last),
        [
            pltpu.VMEM((poses * cls_rows, particles), bf16),
            pltpu.VMEM((cls_rows, span), f32),
            pltpu.VMEM((2, poses * cls_rows, 256), f32),
            pltpu.VMEM((2, poses * cls_rows, 256), f32),
        ],
        flops=4 * poses * cls_rows * particles * span,
        limit=VMEM_LIMIT if particles <= 512 else 2 * VMEM_LIMIT,
    )[0]


def swap(values, axis, distance):
    size = lax.axis_size(axis)
    return lax.ppermute(values, axis, [(i, i ^ distance) for i in range(size)])


def local(particles, classes, ctf, noise_weight, group_ids, shifts):
    half, _, freq = particles.shape
    cls_rows = classes.shape[0]
    poses = shifts.shape[0]
    n_cls = lax.axis_size("cls")
    n_img = lax.axis_size("img")
    span = freq // n_img
    pairwise = n_cls == 4
    me_cls = lax.axis_index("cls") if pairwise else 0
    me = jnp.stack([lax.axis_index("img"), me_cls]).astype(jnp.int32)
    others = tuple(range(n_img - 1, 0, -1))

    own = weigh(particles, ctf, noise_weight, group_ids)
    if pairwise:
        far, near = swap(own, "cls", 2), swap(own, "cls", 1)
        mine, *outgoing = cut_slices(me, [own], [(d, 0) for d in (0,) + others[:-1]], span)
        slices = [mine] + [swap(w, "img", d) for w, d in zip(outgoing, others)]
    else:
        shards = [lax.all_gather(own, "cls", axis=0, tiled=True)]
        mine, *outgoing = cut_slices(me, shards, [(d, 0) for d in (0,) + others], span)
        slices = [[w] for w in [mine] + [swap(w, "img", d) for w, d in zip(outgoing, others)]]

    split = jnp.transpose(classes, (1, 0, 2))
    cos_t, sin_t, power, weight = prepare(shifts, split, ctf, noise_weight)
    tile = template_tile(freq)
    count = freq // tile // 2
    temps = [
        build_templates(split, cos_t, sin_t, part * count, count, tile) for part in range(2)
    ]
    if pairwise:
        far, near, slices, power, temps = lax.optimization_barrier(
            (far, near, slices, power, temps)
        )
        third = swap(far, "cls", 1)
        targets = [(d, 1) for d in (0,) + others[:-1]] + [(others[-1], 0)]
        mine, *outgoing = cut_slices(me, [own, near, far], targets, span)
        arrived = [mine] + [swap(w, "img", d) for w, d in zip(outgoing, others)]
        shards = [own, near, far, third]
    scores, marks, stat = score(temps, power, shards, half)
    if pairwise:
        stat, arrived[-1] = lax.optimization_barrier((stat, arrived[-1]))
        stats = [stat] + [swap(stat, "cls", k) for k in range(n_cls - 1, 0, -1)]
        paired = (0,) + tuple(range(n_cls - 1, 0, -1))
        last = [*cut_slices(me, [third], [(0, 0)], span)]
        last.append(swap(bundle(arrived[1:], 2 * half), "cls", 1))
        slices = [[a, b] for a, b in zip(slices, arrived)] + [arrived[-1:]]
    else:
        stats = [lax.all_gather(stat, "cls", axis=0, tiled=True)]
        paired = (0,)
        last = []
    norm, payload = responsibilities(scores, marks, stats, paired, poses, half)
    payloads = [payload] + [swap(payload, "img", d) for d in others]
    log_resp, weight_here, rows = gather_rows(
        me, scores, norm, weight, slices, poses, half, span
    )
    averages = finish(me, weight_here, cos_t, sin_t, rows, payloads, last, cls_rows, half)
    return (log_resp.T, averages)


def solution(mesh):
    placed = (
        P(("groups", "img", "cls"), None, None),
        P(("groups", "cls"), None, None),
        P("groups", None),
        P("groups"),
        P(("groups", "img", "cls")),
        P("groups", None),
    )
    return jax.shard_map(
        local,
        mesh=mesh,
        in_specs=placed,
        out_specs=(P(("groups", "img"), "cls"), P(("groups", "cls"), None, "img")),
        check_vma=False,
    )
```

```python
import functools

import jax
import jax.numpy as jnp
from jax import lax
from jax.experimental import pallas as pl
from jax.experimental.pallas import tpu as pltpu
from jax.sharding import PartitionSpec as P

BOX = 128
LANES = 128
VMEM_LIMIT = 24 * 1024 * 1024
GATHER_FLOPS = 20_000_000_000

prior_precision = 0.02

NT = (((1,), (1,)), ((), ()))
NN = (((1,), (0,)), ((), ()))
HIGHEST = lax.Precision.HIGHEST
f32 = jnp.float32
bf16 = jnp.bfloat16

SMEM = pl.BlockSpec(memory_space=pltpu.SMEM)
VMEM = pl.BlockSpec(memory_space=pltpu.VMEM)
ANY = pl.BlockSpec(memory_space=pl.ANY)


def call(kernel, name, in_specs, out_shape, operands, scratch=(), flops=0, moved=0, limit=VMEM_LIMIT):
    return pl.pallas_call(
        kernel,
        in_specs=in_specs,
        out_specs=[VMEM] * len(out_shape),
        out_shape=out_shape,
        scratch_shapes=list(scratch),
        compiler_params=pltpu.CompilerParams(vmem_limit_bytes=limit),
        cost_estimate=pl.CostEstimate(flops=flops, bytes_accessed=moved, transcendentals=0),
        name=name,
    )(*operands)


def real_index(shape, axis, half):
    return lax.rem(lax.broadcasted_iota(jnp.int32, shape, axis) // half, 2) == 0


def weigh_kernel(
    ids_hbm, p_hbm, ctf_hbm, nw_hbm, out_ref, ids_ref, p_ref, ctf_ref, nw_ref, scale_ref, sem
):
    count, _, freq = p_ref.shape
    copies = [
        pltpu.make_async_copy(source, target, sem.at[i])
        for i, (source, target) in enumerate(
            [(ids_hbm, ids_ref), (ctf_hbm, ctf_ref), (nw_hbm, nw_ref), (p_hbm, p_ref)]
        )
    ]
    for copy in copies:
        copy.start()
    copies[0].wait()
    row = lax.rem(lax.broadcasted_iota(jnp.int32, (2 * count, LANES), 0), count)
    ids = jnp.zeros((2 * count, LANES), f32)
    for n in range(count):
        ids = jnp.where(row == n, ids_ref[n].astype(f32), ids)
    for copy in copies[1:]:
        copy.wait()
    noise = nw_ref[...].reshape(1, freq)
    for n in range(count):
        scale_ref[n : n + 1, :] = ctf_ref[pl.ds(ids_ref[n], 1), :] * noise
    scale = scale_ref[...]
    values = p_ref[...].astype(f32)
    for part in range(2):
        here = slice(part * count, (part + 1) * count)
        out_ref[here, :freq] = (values[:, part, :] * scale).astype(bf16)
    out_ref[:, freq:] = ids.astype(bf16)


def weigh(particles, ctf, noise_weight, group_ids):
    rows, _, freq = particles.shape
    operands = (group_ids, particles, ctf, noise_weight)
    return call(
        weigh_kernel,
        "weigh",
        [ANY] * 4,
        [jax.ShapeDtypeStruct((2 * rows, freq + LANES), bf16)],
        [pltpu.with_memory_space_constraint(x, pltpu.HBM) for x in operands],
        [
            pltpu.SMEM((rows,), jnp.int32),
            pltpu.VMEM(particles.shape, bf16),
            pltpu.VMEM(ctf.shape, f32),
            pltpu.VMEM((freq,), f32),
            pltpu.VMEM((rows, freq), f32),
            pltpu.SemaphoreType.DMA((4,)),
        ],
        flops=4 * rows * freq,
        moved=16 * rows * freq,
    )[0]


def prepare_kernel(
    shifts_ref, cls_ref, ctf_hbm, nw_hbm, cos_ref, sin_ref, pow_ref, cw_ref, *scratch
):
    ctf_ref, nw_ref, angle_ref, sem = scratch
    freq = cls_ref.shape[2]
    poses = cos_ref.shape[0]
    copies = [
        pltpu.make_async_copy(source, target, sem.at[i])
        for i, (source, target) in enumerate(
            [(ctf_hbm, ctf_ref), (nw_hbm, nw_ref)]
        )
    ]
    for copy in copies:
        copy.start()
    lane = lax.broadcasted_iota(jnp.int32, (1, BOX), 1).astype(f32)
    step = 2.0 * jnp.pi / BOX
    for r in range(poses):
        angle_ref[0, r : r + 1, :] = step * (shifts_ref[0, r].astype(f32) * (lane - BOX // 2))
        angle_ref[1, r : r + 1, :] = step * (shifts_ref[1, r].astype(f32) * lane)
    x_cos, x_sin = jnp.cos(angle_ref[0]), jnp.sin(angle_ref[0])
    y_cos, y_sin = jnp.cos(angle_ref[1]), jnp.sin(angle_ref[1])
    for t in range(freq // BOX):
        c = jnp.broadcast_to(y_cos[:, t : t + 1], x_cos.shape)
        s = jnp.broadcast_to(y_sin[:, t : t + 1], x_cos.shape)
        cos_ref[:, t * BOX : (t + 1) * BOX] = x_cos * c - x_sin * s
        sin_ref[:, t * BOX : (t + 1) * BOX] = x_sin * c + x_cos * s
    for copy in copies:
        copy.wait()
    noise = nw_ref[...].reshape(1, freq)
    cut = freq // 4
    power = jnp.zeros(pow_ref.shape, f32)
    for q in range(4):
        at = slice(q * cut, (q + 1) * cut)
        re = cls_ref[0, :, at].astype(f32)
        im = cls_ref[1, :, at].astype(f32)
        ctf = ctf_ref[:, at]
        weight = ctf * ctf * noise[:, at]
        cw_ref[:, at] = weight
        power += lax.dot_general(
            re * re + im * im, weight, NT, precision=HIGHEST, preferred_element_type=f32
        )
    pow_ref[...] = power


def prepare(shifts, split, ctf, noise_weight):
    _, rows, freq = split.shape
    poses, groups = shifts.shape[0], ctf.shape[0]
    return call(
        prepare_kernel,
        "prepare",
        [SMEM, VMEM, ANY, ANY],
        [
            jax.ShapeDtypeStruct((poses, freq), f32),
            jax.ShapeDtypeStruct((poses, freq), f32),
            jax.ShapeDtypeStruct((rows, groups), f32),
            jax.ShapeDtypeStruct((groups, freq), f32),
        ],
        (
            shifts.T,
            split,
            *[pltpu.with_memory_space_constraint(x, pltpu.HBM) for x in (ctf, noise_weight)],
        ),
        [
            pltpu.VMEM(ctf.shape, f32),
            pltpu.VMEM((freq,), f32),
            pltpu.VMEM((2, poses, BOX), f32),
            pltpu.SemaphoreType.DMA((2,)),
        ],
        flops=24 * rows * groups * freq,
    )


def write_templates(cls_ref, cos_ref, sin_ref, temp_ref, start, tile):
    rows = cls_ref.shape[1]
    for a in range(0, tile, LANES):
        at = pl.ds(pl.multiple_of(start + a, LANES), LANES)
        re = cls_ref[0, :, at].astype(f32)
        im = cls_ref[1, :, at].astype(f32)
        for r in range(cos_ref.shape[0]):
            cos_r = cos_ref[r : r + 1, at]
            sin_r = sin_ref[r : r + 1, at]
            here = slice(r * rows, (r + 1) * rows)
            temp_ref[here, a : a + LANES] = (re * cos_r - im * sin_r).astype(bf16)
            temp_ref[here, tile + a : tile + a + LANES] = (re * sin_r + im * cos_r).astype(bf16)


def template_tile(freq):
    return max(t for t in range(LANES, 385, LANES) if freq // 2 % t == 0)


def template_kernel(cls_ref, cos_ref, sin_ref, temp_ref):
    write_templates(cls_ref, cos_ref, sin_ref, temp_ref, 0, cls_ref.shape[2])


def build_templates(split, cos_t, sin_t, skip, count, tile):
    _, rows, _ = split.shape
    poses = cos_t.shape[0]
    return pl.pallas_call(
        template_kernel,
        grid=(count,),
        in_specs=[
            pl.BlockSpec((2, rows, tile), lambda j: (0, 0, skip + j)),
            pl.BlockSpec((poses, tile), lambda j: (0, skip + j)),
            pl.BlockSpec((poses, tile), lambda j: (0, skip + j)),
        ],
        out_specs=pl.BlockSpec((None, poses * rows, 2 * tile), lambda j: (j, 0, 0)),
        out_shape=jax.ShapeDtypeStruct((count, poses * rows, 2 * tile), bf16),
        compiler_params=pltpu.CompilerParams(vmem_limit_bytes=VMEM_LIMIT),
        cost_estimate=pl.CostEstimate(
            flops=40 * poses * rows * count * tile,
            bytes_accessed=4 * poses * rows * count * tile,
            transcendentals=0,
        ),
        name=f"templates{skip}",
    )(split, cos_t, sin_t)


def regroup(refs, counts):
    refs = list(refs)
    return [[refs.pop(0) for _ in range(count)] for count in counts]


def score_kernel(half, parts, pow_ref, *refs):
    temp_refs, refs = refs[:parts], refs[parts:]
    shards, (s_ref, marks_ref, stat_ref) = refs[:-3], refs[-3:]
    rows, groups = pow_ref.shape
    lanes = s_ref.shape[1]
    poses = s_ref.shape[0] // rows
    tails = [ref[:, ref.shape[1] - LANES :] for ref in shards]
    ids = jnp.concatenate(tails, axis=0).astype(f32)
    group = lax.broadcasted_iota(jnp.int32, (lanes, groups), 1).astype(f32)
    marks = (ids[:, :groups] == group).astype(f32)
    marks_ref[...] = marks
    penalty = lax.dot_general(
        pow_ref[...], marks, NT, precision=HIGHEST, preferred_element_type=f32
    )
    temps = [ref.at[t] for ref in temp_refs for t in range(ref.shape[0])]
    tile = temp_refs[0].shape[2] // 2
    real = real_index((lanes, tile), 0, half)
    s_ref[...] = jnp.zeros_like(s_ref)
    for t, temp in enumerate(temps):
        at = slice(t * tile, (t + 1) * tile)
        wide = jnp.concatenate([ref[:, at] for ref in shards], axis=0).astype(f32)
        split = jnp.concatenate(
            [jnp.where(real, wide, 0.0).astype(bf16), jnp.where(real, 0.0, wide).astype(bf16)],
            axis=1,
        )
        s_ref[...] += lax.dot_general(temp[...], split, NT, preferred_element_type=f32)
    acc = s_ref[...]
    acc = acc + jnp.where(
        real_index(acc.shape, 1, half), pltpu.roll(acc, lanes - half, 1), pltpu.roll(acc, half, 1)
    )
    scores = acc.reshape(poses, rows, lanes) - 0.5 * penalty[None]
    peak = jnp.max(jnp.max(scores, axis=0), axis=0, keepdims=True)
    total = jnp.sum(jnp.sum(jnp.exp(scores - peak[None]), axis=0), axis=0, keepdims=True)
    s_ref[...] = scores.reshape(poses * rows, lanes)
    stat_ref[0:1, :] = peak
    stat_ref[1:2, :] = total
    stat_ref[2:8, :] = jnp.zeros((6, lanes), f32)


def score(temps, power, shards, half):
    count, columns, width = temps[0].shape
    lanes = sum(ref.shape[0] for ref in shards)
    operands = [power, *temps, *shards]
    return call(
        functools.partial(score_kernel, half, len(temps)),
        "score",
        [VMEM] * len(operands),
        [
            jax.ShapeDtypeStruct((columns, lanes), f32),
            jax.ShapeDtypeStruct((lanes, power.shape[1]), f32),
            jax.ShapeDtypeStruct((8, lanes), f32),
        ],
        operands,
        flops=2 * columns * 256 * count * len(temps) * width,
    )


def regroup(refs, counts):
    refs = list(refs)
    return [[refs.pop(0) for _ in range(count)] for count in counts]


def slices_kernel(targets, me_ref, *refs):
    shards, out_refs = refs[: -len(targets)], refs[-len(targets) :]
    span = out_refs[0].shape[1]
    filled = [0] * len(targets)
    for k, ref in enumerate(shards):
        height = ref.shape[0]
        for i, (distance, skip) in enumerate(targets):
            if k >= skip:
                base = pl.multiple_of((me_ref[0] ^ distance) * span, LANES)
                out_refs[i][filled[i] : filled[i] + height, :] = ref[:, pl.ds(base, span)]
                filled[i] += height


def cut_slices(me, shards, targets, span):
    heights = [ref.shape[0] for ref in shards]
    out_heights = [sum(heights[skip:]) for _, skip in targets]
    return call(
        functools.partial(slices_kernel, targets),
        "cut_slices",
        [SMEM] + [VMEM] * len(shards),
        [jax.ShapeDtypeStruct((height, span), bf16) for height in out_heights],
        (me, *shards),
        moved=4 * span * sum(out_heights),
        limit=VMEM_LIMIT if sum(heights) <= 128 else 2 * VMEM_LIMIT,
    )


def bundle_kernel(*refs):
    sources, out_ref = refs[:-1], refs[-1]
    rows = out_ref.shape[0] // len(sources)
    for i, ref in enumerate(sources):
        out_ref[i * rows : (i + 1) * rows, :] = ref[ref.shape[0] - rows :, :]


def bundle(slices, rows):
    span = slices[0].shape[1]
    return call(
        bundle_kernel,
        "bundle",
        [VMEM] * len(slices),
        [jax.ShapeDtypeStruct((len(slices) * rows, span), bf16)],
        slices,
        moved=4 * len(slices) * rows * span,
    )[0]


def xor_blocks(values, block, distance):
    lanes = values.shape[1]
    lane = lax.broadcasted_iota(jnp.int32, values.shape, 1)
    width = block
    while distance:
        if distance % 2:
            low = lax.rem(lane // width, 2) == 0
            values = jnp.where(
                low, pltpu.roll(values, lanes - width, 1), pltpu.roll(values, width, 1)
            )
        distance //= 2
        width *= 2
    return values


def rho_kernel(poses, half, paired, s_ref, marks_ref, *refs):
    stat_refs, (norm_ref, out_ref) = refs[: len(paired)], refs[len(paired) :]
    lanes = s_ref.shape[1]
    rows = s_ref.shape[0] // poses
    groups = marks_ref.shape[1]
    block = 2 * half
    peaks, totals = [], []
    for ref, distance in zip(stat_refs, paired):
        for at in range(0, ref.shape[0], 8):
            stats = xor_blocks(ref[at : at + 8, :], block, distance)
            peaks.append(stats[0:1])
            totals.append(stats[1:2])
    peak = functools.reduce(jnp.maximum, peaks)
    total = sum(t * jnp.exp(p - peak) for t, p in zip(totals, peaks))
    log_norm = peak + jnp.log(total)
    norm_ref[...] = log_norm
    rho = jnp.exp(s_ref[...].reshape(poses, rows, lanes) - log_norm[None])
    mass = lax.dot_general(
        jnp.where(real_index((rows, lanes), 1, half), jnp.sum(rho, axis=0), 0.0),
        marks_ref[...],
        NN,
        precision=HIGHEST,
        preferred_element_type=f32,
    )
    high = mass.astype(bf16)
    low = (mass - high.astype(f32)).astype(bf16)
    rho_low = rho.reshape(poses * rows, lanes).astype(bf16)
    cut = poses // 2 * rows
    lane = lax.broadcasted_iota(jnp.int32, (lanes, lanes), 0)
    column = lax.broadcasted_iota(jnp.int32, (lanes, lanes), 1)
    particle = lane // block * half + lax.rem(lane, block)
    real = lax.rem(lane, block) < half
    first = (real & (column == particle)).astype(f32).astype(bf16)
    second = (real & (column == particle + lanes // 2)).astype(f32).astype(bf16)
    packed = jnp.dot(rho_low[:cut], first, preferred_element_type=f32)
    packed += jnp.dot(rho_low[cut:], second, preferred_element_type=f32)
    out_ref[:cut, :] = packed.astype(bf16)
    if lanes > 2 * groups:
        out_ref[cut:, :] = jnp.zeros((rows, lanes), bf16)
    out_ref[cut:, :groups] = high
    out_ref[cut:, groups : 2 * groups] = low


def responsibilities(scores, marks, stats, paired, poses, half):
    columns, lanes = scores.shape
    return call(
        functools.partial(rho_kernel, poses, half, paired),
        "responsibilities",
        [VMEM] * (2 + len(stats)),
        [
            jax.ShapeDtypeStruct((1, lanes), f32),
            jax.ShapeDtypeStruct((columns // 2 + columns // poses, lanes), bf16),
        ],
        (scores, marks, *stats),
        flops=40 * columns * lanes,
    )


def gather_kernel(poses, half, counts, me_ref, s_ref, norm_ref, weight_ref, *refs):
    w_refs, (resp_ref, cw_ref, rows_ref) = refs[:-3], refs[-3:]
    span = rows_ref.shape[2]
    block = 2 * half
    here = pl.ds(pl.multiple_of(me_ref[0] * span, LANES), span)
    at = 0
    for refs in regroup(w_refs, counts):
        for ref in refs:
            for start in range(0, ref.shape[0], block):
                rows_ref[0, at : at + half, :] = ref[start : start + half, :]
                rows_ref[1, at : at + half, :] = ref[start + half : start + block, :]
                at += half
    weight = weight_ref[:, here]
    high = weight.astype(bf16)
    cw_ref[:, :span] = high
    cw_ref[:, span:] = (weight - high.astype(f32)).astype(bf16)
    rows = resp_ref.shape[0]
    lanes = s_ref.shape[1]
    scores = s_ref[...].reshape(poses, rows, lanes)
    pose_peak = jnp.max(scores, axis=0)
    total = jnp.sum(jnp.exp(scores - pose_peak[None]), axis=0)
    log_resp = pose_peak + jnp.log(total) - norm_ref[...]
    shape = (resp_ref.shape[1], lanes)
    lane = lax.broadcasted_iota(jnp.int32, shape, 1)
    row = ((lane // block) ^ me_ref[1]) * half + lax.rem(lane, block)
    take = (lax.broadcasted_iota(jnp.int32, shape, 0) == row) & (lax.rem(lane, block) < half)
    resp_ref[...] = lax.dot_general(
        log_resp, take.astype(f32), NT, precision=HIGHEST, preferred_element_type=f32
    )


def gather_rows(me, scores, norm, weight, slices, poses, half, span):
    columns, lanes = scores.shape
    counts = [len(refs) for refs in slices]
    slices = [w for refs in slices for w in refs]
    particles = sum(w.shape[0] for w in slices) // 2
    return call(
        functools.partial(gather_kernel, poses, half, counts),
        "gather_rows",
        [SMEM] + [VMEM] * (3 + len(slices)),
        [
            jax.ShapeDtypeStruct((columns // poses, lanes // 2), f32),
            jax.ShapeDtypeStruct((weight.shape[0], 2 * span), bf16),
            jax.ShapeDtypeStruct((2, particles, span), bf16),
        ],
        (me, scores, norm, weight, *slices),
        flops=GATHER_FLOPS,
        moved=8 * particles * span,
        limit=VMEM_LIMIT if particles <= 512 else 2 * VMEM_LIMIT,
    )


def finish_kernel(poses, groups, sources, half, me_ref, cw_ref, cos_ref, sin_ref, rows_ref, *refs):
    payloads, refs = refs[:1] + refs[sources - 1 : 0 : -1], refs[sources:]
    last, (out_ref, rho_ref, inverse_ref, *buffers) = refs[:-5], refs[-5:]
    rows, _, span = out_ref.shape
    cut = poses // 2 * rows
    count = payloads[0].shape[1] // 2
    mass = jnp.zeros((rows, groups), f32)
    for i, ref in enumerate(payloads):
        rho_ref[:cut, i * count : (i + 1) * count] = ref[:cut, :count]
        rho_ref[cut:, i * count : (i + 1) * count] = ref[:cut, count:]
        mass += ref[cut:, :groups].astype(f32) + ref[cut:, groups : 2 * groups].astype(f32)
    high = mass.astype(bf16)
    mass = jnp.concatenate([high, (mass - high.astype(f32)).astype(bf16)], axis=0)
    terms = jnp.dot(mass, cw_ref[...], preferred_element_type=f32)
    denom = (terms[:rows, :span] + terms[rows:, :span]) + (terms[:rows, span:] + terms[rows:, span:])
    inverse_ref[...] = 1.0 / (denom + prior_precision)
    tiles = [(a, min(256, span - a)) for a in range(0, span, 256)]
    known = rows_ref.shape[1] // sources

    def rows_of(part, start, width):
        here = slice(start, start + width)
        if not last:
            return rows_ref[part, :, here]
        pieces = []
        for i in range(sources):
            pieces.append(rows_ref[part, i * known : (i + 1) * known, here])
            if i == 0:
                pieces.append(last[0][part * half : (part + 1) * half, here])
            else:
                at = (2 * (i - 1) + part) * half
                pieces.append(last[1][at : at + half, here])
        return jnp.concatenate(pieces, axis=0)

    def products(i):
        start, width = tiles[i]
        for part in range(2):
            buffers[i % 2][part, :, :width] = jnp.dot(
                rho_ref[...], rows_of(part, start, width), preferred_element_type=f32
            )

    def rotate(i):
        start, width = tiles[i]
        buffer = buffers[i % 2]
        for a in range(0, width, LANES):
            at = pl.ds(pl.multiple_of(me_ref[0] * span + start + a, LANES), LANES)
            numer_re = jnp.zeros((rows, LANES), f32)
            numer_im = jnp.zeros((rows, LANES), f32)
            for r in range(poses):
                cos_r = cos_ref[r : r + 1, at]
                sin_r = sin_ref[r : r + 1, at]
                s_re = buffer[0, r * rows : (r + 1) * rows, a : a + LANES]
                s_im = buffer[1, r * rows : (r + 1) * rows, a : a + LANES]
                numer_re = numer_re + s_re * cos_r + s_im * sin_r
                numer_im = numer_im + s_im * cos_r - s_re * sin_r
            here = slice(start + a, start + a + LANES)
            inverse = inverse_ref[:, here]
            out_ref[:, 0, here] = numer_re * inverse
            out_ref[:, 1, here] = numer_im * inverse

    products(0)
    for i in range(1, len(tiles)):
        products(i)
        rotate(i - 1)
    rotate(len(tiles) - 1)


def finish(me, weight, cos_t, sin_t, rows, payloads, last, cls_rows, half):
    poses = cos_t.shape[0]
    span = rows.shape[2]
    particles = len(payloads) * payloads[0].shape[1] // 2
    return call(
        functools.partial(finish_kernel, poses, weight.shape[0], len(payloads), half),
        "finish",
        [SMEM] + [VMEM] * (4 + len(payloads) + len(last)),
        [jax.ShapeDtypeStruct((cls_rows, 2, span), f32)],
        (me, weight, cos_t, sin_t, rows, *payloads, *last),
        [
            pltpu.VMEM((poses * cls_rows, particles), bf16),
            pltpu.VMEM((cls_rows, span), f32),
            pltpu.VMEM((2, poses * cls_rows, 256), f32),
            pltpu.VMEM((2, poses * cls_rows, 256), f32),
        ],
        flops=4 * poses * cls_rows * particles * span,
        limit=VMEM_LIMIT if particles <= 512 else 2 * VMEM_LIMIT,
    )[0]


def swap(values, axis, distance):
    size = lax.axis_size(axis)
    return lax.ppermute(values, axis, [(i, i ^ distance) for i in range(size)])


def local(particles, classes, ctf, noise_weight, group_ids, shifts):
    half, _, freq = particles.shape
    cls_rows = classes.shape[0]
    poses = shifts.shape[0]
    n_cls = lax.axis_size("cls")
    n_img = lax.axis_size("img")
    span = freq // n_img
    pairwise = n_cls == 4
    me_cls = lax.axis_index("cls") if pairwise else 0
    me = jnp.stack([lax.axis_index("img"), me_cls]).astype(jnp.int32)
    others = tuple(range(n_img - 1, 0, -1))

    own = weigh(particles, ctf, noise_weight, group_ids)
    if pairwise:
        far, near = swap(own, "cls", 2), swap(own, "cls", 1)
        mine, *outgoing = cut_slices(me, [own], [(d, 0) for d in (0,) + others[:-1]], span)
        slices = [mine] + [swap(w, "img", d) for w, d in zip(outgoing, others)]
    else:
        shards = [lax.all_gather(own, "cls", axis=0, tiled=True)]
        mine, *outgoing = cut_slices(me, shards, [(d, 0) for d in (0,) + others], span)
        slices = [[w] for w in [mine] + [swap(w, "img", d) for w, d in zip(outgoing, others)]]

    split = jnp.transpose(classes, (1, 0, 2))
    cos_t, sin_t, power, weight = prepare(shifts, split, ctf, noise_weight)
    tile = template_tile(freq)
    count = freq // tile // 2
    temps = [
        build_templates(split, cos_t, sin_t, part * count, count, tile) for part in range(2)
    ]
    if pairwise:
        far, near, slices, power, temps = lax.optimization_barrier(
            (far, near, slices, power, temps)
        )
        third = swap(far, "cls", 1)
        targets = [(d, 1) for d in (0,) + others[:-1]] + [(others[-1], 0)]
        mine, *outgoing = cut_slices(me, [own, near, far], targets, span)
        arrived = [mine] + [swap(w, "img", d) for w, d in zip(outgoing, others)]
        shards = [own, near, far, third]
    scores, marks, stat = score(temps, power, shards, half)
    if pairwise:
        stat, arrived[-1] = lax.optimization_barrier((stat, arrived[-1]))
        stats = [stat] + [swap(stat, "cls", k) for k in range(1, n_cls)]
        paired = tuple(range(n_cls))
        last = [*cut_slices(me, [third], [(0, 0)], span)]
        last.append(swap(bundle(arrived[1:], 2 * half), "cls", 1))
        slices = [[a, b] for a, b in zip(slices, arrived)] + [arrived[-1:]]
    else:
        stats = [lax.all_gather(stat, "cls", axis=0, tiled=True)]
        paired = (0,)
        last = []
    norm, payload = responsibilities(scores, marks, stats, paired, poses, half)
    payloads = [payload] + [swap(payload, "img", d) for d in others[::-1]]
    log_resp, weight_here, rows = gather_rows(
        me, scores, norm, weight, slices, poses, half, span
    )
    averages = finish(me, weight_here, cos_t, sin_t, rows, payloads, last, cls_rows, half)
    return (log_resp.T, averages)


def solution(mesh):
    placed = (
        P(("groups", "img", "cls"), None, None),
        P(("groups", "cls"), None, None),
        P("groups", None),
        P("groups"),
        P(("groups", "img", "cls")),
        P("groups", None),
    )
    return jax.shard_map(
        local,
        mesh=mesh,
        in_specs=placed,
        out_specs=(P(("groups", "img"), "cls"), P(("groups", "cls"), None, "img")),
        check_vma=False,
    )
```

```python
import functools

import jax
import jax.numpy as jnp
from jax import lax
from jax.experimental import pallas as pl
from jax.experimental.pallas import tpu as pltpu
from jax.sharding import PartitionSpec as P

BOX = 128
CHUNKS = 2
LANES = 128
VMEM_LIMIT = 24 * 1024 * 1024
GATHER_FLOPS = 20_000_000_000

prior_precision = 0.02

NT = (((1,), (1,)), ((), ()))
NN = (((1,), (0,)), ((), ()))
HIGHEST = lax.Precision.HIGHEST
f32 = jnp.float32
bf16 = jnp.bfloat16

SMEM = pl.BlockSpec(memory_space=pltpu.SMEM)
VMEM = pl.BlockSpec(memory_space=pltpu.VMEM)
ANY = pl.BlockSpec(memory_space=pl.ANY)


def call(kernel, name, in_specs, out_shape, operands, scratch=(), flops=0, moved=0, limit=VMEM_LIMIT):
    return pl.pallas_call(
        kernel,
        in_specs=in_specs,
        out_specs=[VMEM] * len(out_shape),
        out_shape=out_shape,
        scratch_shapes=list(scratch),
        compiler_params=pltpu.CompilerParams(vmem_limit_bytes=limit),
        cost_estimate=pl.CostEstimate(flops=flops, bytes_accessed=moved, transcendentals=0),
        name=name,
    )(*operands)


def real_index(shape, axis, half):
    return lax.rem(lax.broadcasted_iota(jnp.int32, shape, axis) // half, 2) == 0


def weigh_kernel(ids_hbm, p_hbm, ctf_hbm, nw_hbm, *refs):
    out_refs, (ids_ref, p_ref, ctf_ref, nw_ref, raw_ref, scale_ref, sem) = refs[:-7], refs[-7:]
    count, _, freq = p_ref.shape
    copies = [
        pltpu.make_async_copy(source, target, sem.at[i])
        for i, (source, target) in enumerate(
            [(p_hbm, p_ref), (ids_hbm, ids_ref), (nw_hbm, nw_ref), (ctf_hbm, ctf_ref)]
        )
    ]
    for copy in copies:
        copy.start()
    copies[0].wait()
    values = p_ref[...].astype(f32)
    for part in range(2):
        raw_ref[part] = values[:, part, :]
    copies[1].wait()
    row = lax.rem(lax.broadcasted_iota(jnp.int32, (2 * count, LANES), 0), count)
    ids = jnp.zeros((2 * count, LANES), f32)
    for n in range(count):
        ids = jnp.where(row == n, ids_ref[n].astype(f32), ids)
    for out_ref in out_refs[:2]:
        out_ref[:, out_ref.shape[1] - LANES :] = ids.astype(bf16)
    copies[2].wait()
    noise = nw_ref[...].reshape(1, freq)
    copies[3].wait()
    for n in range(count):
        scale_ref[n : n + 1, :] = ctf_ref[pl.ds(ids_ref[n], 1), :] * noise
    scale = scale_ref[...]
    chunk = freq // CHUNKS
    for part in range(2):
        weighted = (raw_ref[part] * scale).astype(bf16)
        here = slice(part * count, (part + 1) * count)
        out_refs[0][here, :freq] = weighted
        for c, out_ref in enumerate(out_refs[1:]):
            out_ref[here, :chunk] = weighted[:, c * chunk : (c + 1) * chunk]


def weigh(particles, ctf, noise_weight, group_ids):
    rows, _, freq = particles.shape
    operands = (group_ids, particles, ctf, noise_weight)
    return call(
        weigh_kernel,
        "weigh",
        [ANY] * 4,
        [
            jax.ShapeDtypeStruct((2 * rows, width), bf16)
            for width in [freq + LANES, freq // CHUNKS + LANES] + [freq // CHUNKS] * (CHUNKS - 1)
        ],
        [pltpu.with_memory_space_constraint(x, pltpu.HBM) for x in operands],
        [
            pltpu.SMEM((rows,), jnp.int32),
            pltpu.VMEM(particles.shape, bf16),
            pltpu.VMEM(ctf.shape, f32),
            pltpu.VMEM((freq,), f32),
            pltpu.VMEM((2, rows, freq), f32),
            pltpu.VMEM((rows, freq), f32),
            pltpu.SemaphoreType.DMA((4,)),
        ],
        flops=4 * rows * freq,
        moved=16 * rows * freq,
    )


def prepare_kernel(
    shifts_ref, cls_ref, ctf_hbm, nw_hbm, cos_ref, sin_ref, pow_ref, cw_ref, *scratch
):
    ctf_ref, nw_ref, angle_ref, sem = scratch
    freq = cls_ref.shape[2]
    poses = cos_ref.shape[0]
    copies = [
        pltpu.make_async_copy(source, target, sem.at[i])
        for i, (source, target) in enumerate(
            [(ctf_hbm, ctf_ref), (nw_hbm, nw_ref)]
        )
    ]
    for copy in copies:
        copy.start()
    lane = lax.broadcasted_iota(jnp.int32, (1, BOX), 1).astype(f32)
    step = 2.0 * jnp.pi / BOX
    for r in range(poses):
        angle_ref[0, r : r + 1, :] = step * (shifts_ref[0, r].astype(f32) * (lane - BOX // 2))
        angle_ref[1, r : r + 1, :] = step * (shifts_ref[1, r].astype(f32) * lane)
    x_cos, x_sin = jnp.cos(angle_ref[0]), jnp.sin(angle_ref[0])
    y_cos, y_sin = jnp.cos(angle_ref[1]), jnp.sin(angle_ref[1])
    for t in range(freq // BOX):
        c = jnp.broadcast_to(y_cos[:, t : t + 1], x_cos.shape)
        s = jnp.broadcast_to(y_sin[:, t : t + 1], x_cos.shape)
        cos_ref[:, t * BOX : (t + 1) * BOX] = x_cos * c - x_sin * s
        sin_ref[:, t * BOX : (t + 1) * BOX] = x_sin * c + x_cos * s
    for copy in copies:
        copy.wait()
    noise = nw_ref[...].reshape(1, freq)
    cut = freq // 4
    power = jnp.zeros(pow_ref.shape, f32)
    for q in range(4):
        at = slice(q * cut, (q + 1) * cut)
        re = cls_ref[0, :, at].astype(f32)
        im = cls_ref[1, :, at].astype(f32)
        ctf = ctf_ref[:, at]
        weight = ctf * ctf * noise[:, at]
        cw_ref[:, at] = weight
        power += lax.dot_general(
            re * re + im * im, weight, NT, precision=HIGHEST, preferred_element_type=f32
        )
    pow_ref[...] = power


def prepare(shifts, split, ctf, noise_weight):
    _, rows, freq = split.shape
    poses, groups = shifts.shape[0], ctf.shape[0]
    return call(
        prepare_kernel,
        "prepare",
        [SMEM, VMEM, ANY, ANY],
        [
            jax.ShapeDtypeStruct((poses, freq), f32),
            jax.ShapeDtypeStruct((poses, freq), f32),
            jax.ShapeDtypeStruct((rows, groups), f32),
            jax.ShapeDtypeStruct((groups, freq), f32),
        ],
        (
            shifts.T,
            split,
            *[pltpu.with_memory_space_constraint(x, pltpu.HBM) for x in (ctf, noise_weight)],
        ),
        [
            pltpu.VMEM(ctf.shape, f32),
            pltpu.VMEM((freq,), f32),
            pltpu.VMEM((2, poses, BOX), f32),
            pltpu.SemaphoreType.DMA((2,)),
        ],
        flops=24 * rows * groups * freq,
    )


def write_templates(cls_ref, cos_ref, sin_ref, temp_ref, start, tile):
    rows = cls_ref.shape[1]
    for a in range(0, tile, LANES):
        at = pl.ds(pl.multiple_of(start + a, LANES), LANES)
        re = cls_ref[0, :, at].astype(f32)
        im = cls_ref[1, :, at].astype(f32)
        for r in range(cos_ref.shape[0]):
            cos_r = cos_ref[r : r + 1, at]
            sin_r = sin_ref[r : r + 1, at]
            here = slice(r * rows, (r + 1) * rows)
            temp_ref[here, a : a + LANES] = (re * cos_r - im * sin_r).astype(bf16)
            temp_ref[here, tile + a : tile + a + LANES] = (re * sin_r + im * cos_r).astype(bf16)


def template_tile(freq):
    return max(t for t in range(LANES, 385, LANES) if freq // CHUNKS % t == 0)


def early_kernel(cls_ref, cos_ref, sin_ref, temp_ref):
    write_templates(cls_ref, cos_ref, sin_ref, temp_ref, 0, cls_ref.shape[2])


def early_templates(split, cos_t, sin_t, skip, count, tile):
    _, rows, _ = split.shape
    poses = cos_t.shape[0]
    return pl.pallas_call(
        early_kernel,
        grid=(count,),
        in_specs=[
            pl.BlockSpec((2, rows, tile), lambda j: (0, 0, skip + j)),
            pl.BlockSpec((poses, tile), lambda j: (0, skip + j)),
            pl.BlockSpec((poses, tile), lambda j: (0, skip + j)),
        ],
        out_specs=pl.BlockSpec((None, poses * rows, 2 * tile), lambda j: (j, 0, 0)),
        out_shape=jax.ShapeDtypeStruct((count, poses * rows, 2 * tile), bf16),
        compiler_params=pltpu.CompilerParams(vmem_limit_bytes=VMEM_LIMIT),
        cost_estimate=pl.CostEstimate(
            flops=40 * poses * rows * count * tile,
            bytes_accessed=4 * poses * rows * count * tile,
            transcendentals=0,
        ),
        name=f"early_templates{skip}",
    )(split, cos_t, sin_t)


def template_kernel(cls_ref, cos_ref, sin_ref, temp_ref):
    count, _, width = temp_ref.shape
    tile = width // 2

    @pl.loop(0, count)
    def _(t):
        write_templates(cls_ref, cos_ref, sin_ref, temp_ref.at[t], t * tile, tile)


def regroup(refs, counts):
    refs = list(refs)
    return [[refs.pop(0) for _ in range(count)] for count in counts]


def tile_of_particles(shards, chunk, span, t, tile, half):
    cuts = []
    for ref, chunked in shards:
        at = t * tile if chunked else chunk * span + t * tile
        cuts.append(ref[:, at : at + tile])
    wide = jnp.concatenate(cuts, axis=0).astype(f32)
    real = real_index(wide.shape, 0, half)
    return jnp.concatenate(
        [jnp.where(real, wide, 0.0).astype(bf16), jnp.where(real, 0.0, wide).astype(bf16)], axis=1
    )


def first_score_kernel(chunked, half, built_ref, early_ref, *refs):
    refs, acc_ref = refs[:-1], refs[-1]
    tile = built_ref.shape[2] // 2
    temps = [ref.at[t] for ref in (built_ref, early_ref) for t in range(ref.shape[0])]
    count = len(temps)
    shards = list(zip(refs, chunked))
    acc_ref[...] = jnp.zeros_like(acc_ref)
    for t in range(count):
        acc_ref[...] += lax.dot_general(
            temps[t][...],
            tile_of_particles(shards, 0, count * tile, t, tile, half),
            NT,
            preferred_element_type=f32,
        )


def last_score_kernel(chunked, half, temp_ref, pow_ref, acc_ref, *refs):
    refs, (s_ref, marks_ref, stat_ref) = refs[:-3], refs[-3:]
    tail_refs, shards = refs[: len(chunked)], list(zip(refs[len(chunked) :], chunked))
    count, _, width = temp_ref.shape
    tile = width // 2
    rows, groups = pow_ref.shape
    lanes = s_ref.shape[1]
    poses = s_ref.shape[0] // rows
    tails = [ref[:, ref.shape[1] - LANES :] for ref in tail_refs]
    ids = jnp.concatenate(tails, axis=0).astype(f32)
    group = lax.broadcasted_iota(jnp.int32, (lanes, groups), 1).astype(f32)
    marks = (ids[:, :groups] == group).astype(f32)
    marks_ref[...] = marks
    penalty = lax.dot_general(
        pow_ref[...], marks, NT, precision=HIGHEST, preferred_element_type=f32
    )
    s_ref[...] = acc_ref[...]
    for t in range(count):
        s_ref[...] += lax.dot_general(
            temp_ref[t],
            tile_of_particles(shards, 1, count * tile, t, tile, half),
            NT,
            preferred_element_type=f32,
        )
    acc = s_ref[...]
    acc = acc + jnp.where(
        real_index(acc.shape, 1, half), pltpu.roll(acc, lanes - half, 1), pltpu.roll(acc, half, 1)
    )
    scores = acc.reshape(poses, rows, lanes) - 0.5 * penalty[None]
    peak = jnp.max(jnp.max(scores, axis=0), axis=0, keepdims=True)
    total = jnp.sum(jnp.sum(jnp.exp(scores - peak[None]), axis=0), axis=0, keepdims=True)
    s_ref[...] = scores.reshape(poses * rows, lanes)
    stat_ref[0:1, :] = peak
    stat_ref[1:2, :] = total
    stat_ref[2:8, :] = jnp.zeros((6, lanes), f32)


def score(early, split, cos_t, sin_t, power, shards, half):
    first, late = early
    count, columns, width = late.shape
    freq = split.shape[2]
    lanes = sum(refs[0].shape[0] for refs in shards)
    chunked = [len(refs) > 1 for refs in shards]
    flops = 2 * columns * 256 * count * width
    acc_shape = jax.ShapeDtypeStruct((columns, lanes), f32)
    built = count - first.shape[0]
    temps = call(
        template_kernel,
        "templates",
        [VMEM] * 3,
        [pltpu.VMEM((built, columns, width), bf16)],
        (split, cos_t, sin_t),
        flops=40 * columns * built * width // 2,
    )[0]
    operands = [temps, first, *[refs[0] for refs in shards]]
    acc = call(
        functools.partial(first_score_kernel, chunked, half),
        "score0",
        [VMEM] * len(operands),
        [acc_shape],
        operands,
        flops=flops,
    )[0]
    operands = [late, power, acc]
    operands += [refs[0] for refs in shards] + [refs[-1] for refs in shards]
    return call(
        functools.partial(last_score_kernel, chunked, half),
        "score1",
        [VMEM] * len(operands),
        [
            acc_shape,
            jax.ShapeDtypeStruct((lanes, power.shape[1]), f32),
            jax.ShapeDtypeStruct((8, lanes), f32),
        ],
        operands,
        flops=flops,
    )


def slices_kernel(counts, targets, me_ref, *refs):
    whole_ref, refs = refs[-1], refs[:-1]
    shards, out_refs = regroup(refs[: -len(targets)], counts), refs[-len(targets) :]
    span = out_refs[0].shape[1]
    filled = [0] * len(targets)
    for k, refs in enumerate(shards):
        source = refs[0]
        height = source.shape[0]
        if len(refs) > 1:
            width = refs[-1].shape[1]
            for c, ref in enumerate(refs):
                whole_ref[:, c * width : (c + 1) * width] = ref[:, :width]
            source = whole_ref
        for i, (distance, skip) in enumerate(targets):
            if k >= skip:
                base = pl.multiple_of((me_ref[0] ^ distance) * span, LANES)
                out_refs[i][filled[i] : filled[i] + height, :] = source[:, pl.ds(base, span)]
                filled[i] += height


def cut_slices(me, shards, targets, span, freq):
    heights = [refs[0].shape[0] for refs in shards]
    operands = [me, *[ref for refs in shards for ref in refs]]
    out_heights = [sum(heights[skip:]) for _, skip in targets]
    return call(
        functools.partial(slices_kernel, [len(refs) for refs in shards], targets),
        "cut_slices",
        [SMEM] + [VMEM] * (len(operands) - 1),
        [jax.ShapeDtypeStruct((height, span), bf16) for height in out_heights],
        operands,
        [pltpu.VMEM((heights[-1], freq), bf16)],
        moved=4 * span * sum(out_heights),
        limit=VMEM_LIMIT if sum(heights) <= 128 else 2 * VMEM_LIMIT,
    )


def bundle_kernel(*refs):
    sources, out_ref = refs[:-1], refs[-1]
    rows = out_ref.shape[0] // len(sources)
    for i, ref in enumerate(sources):
        out_ref[i * rows : (i + 1) * rows, :] = ref[ref.shape[0] - rows :, :]


def bundle(slices, rows):
    span = slices[0].shape[1]
    return call(
        bundle_kernel,
        "bundle",
        [VMEM] * len(slices),
        [jax.ShapeDtypeStruct((len(slices) * rows, span), bf16)],
        slices,
        moved=4 * len(slices) * rows * span,
    )[0]


def xor_blocks(values, block, distance):
    lanes = values.shape[1]
    lane = lax.broadcasted_iota(jnp.int32, values.shape, 1)
    width = block
    while distance:
        if distance % 2:
            low = lax.rem(lane // width, 2) == 0
            values = jnp.where(
                low, pltpu.roll(values, lanes - width, 1), pltpu.roll(values, width, 1)
            )
        distance //= 2
        width *= 2
    return values


def rho_kernel(poses, half, paired, s_ref, marks_ref, *refs):
    stat_refs, (norm_ref, out_ref) = refs[: len(paired)], refs[len(paired) :]
    lanes = s_ref.shape[1]
    rows = s_ref.shape[0] // poses
    groups = marks_ref.shape[1]
    block = 2 * half
    peaks, totals = [], []
    for ref, distance in zip(stat_refs, paired):
        for at in range(0, ref.shape[0], 8):
            stats = xor_blocks(ref[at : at + 8, :], block, distance)
            peaks.append(stats[0:1])
            totals.append(stats[1:2])
    peak = functools.reduce(jnp.maximum, peaks)
    total = sum(t * jnp.exp(p - peak) for t, p in zip(totals, peaks))
    log_norm = peak + jnp.log(total)
    norm_ref[...] = log_norm
    rho = jnp.exp(s_ref[...].reshape(poses, rows, lanes) - log_norm[None])
    mass = lax.dot_general(
        jnp.where(real_index((rows, lanes), 1, half), jnp.sum(rho, axis=0), 0.0),
        marks_ref[...],
        NN,
        precision=HIGHEST,
        preferred_element_type=f32,
    )
    high = mass.astype(bf16)
    low = (mass - high.astype(f32)).astype(bf16)
    rho_low = rho.reshape(poses * rows, lanes).astype(bf16)
    cut = poses // 2 * rows
    lane = lax.broadcasted_iota(jnp.int32, (lanes, lanes), 0)
    column = lax.broadcasted_iota(jnp.int32, (lanes, lanes), 1)
    particle = lane // block * half + lax.rem(lane, block)
    real = lax.rem(lane, block) < half
    first = (real & (column == particle)).astype(f32).astype(bf16)
    second = (real & (column == particle + lanes // 2)).astype(f32).astype(bf16)
    packed = jnp.dot(rho_low[:cut], first, preferred_element_type=f32)
    packed += jnp.dot(rho_low[cut:], second, preferred_element_type=f32)
    out_ref[:cut, :] = packed.astype(bf16)
    if lanes > 2 * groups:
        out_ref[cut:, :] = jnp.zeros((rows, lanes), bf16)
    out_ref[cut:, :groups] = high
    out_ref[cut:, groups : 2 * groups] = low


def responsibilities(scores, marks, stats, paired, poses, half):
    columns, lanes = scores.shape
    return call(
        functools.partial(rho_kernel, poses, half, paired),
        "responsibilities",
        [VMEM] * (2 + len(stats)),
        [
            jax.ShapeDtypeStruct((1, lanes), f32),
            jax.ShapeDtypeStruct((columns // 2 + columns // poses, lanes), bf16),
        ],
        (scores, marks, *stats),
        flops=40 * columns * lanes,
    )


def gather_kernel(poses, half, counts, me_ref, s_ref, norm_ref, weight_ref, *refs):
    w_refs, (resp_ref, cw_ref, rows_ref) = refs[:-3], refs[-3:]
    span = rows_ref.shape[2]
    block = 2 * half
    here = pl.ds(pl.multiple_of(me_ref[0] * span, LANES), span)
    at = 0
    for refs in regroup(w_refs, counts):
        for ref in refs:
            for start in range(0, ref.shape[0], block):
                rows_ref[0, at : at + half, :] = ref[start : start + half, :]
                rows_ref[1, at : at + half, :] = ref[start + half : start + block, :]
                at += half
    weight = weight_ref[:, here]
    high = weight.astype(bf16)
    cw_ref[:, :span] = high
    cw_ref[:, span:] = (weight - high.astype(f32)).astype(bf16)
    rows = resp_ref.shape[0]
    lanes = s_ref.shape[1]
    scores = s_ref[...].reshape(poses, rows, lanes)
    pose_peak = jnp.max(scores, axis=0)
    total = jnp.sum(jnp.exp(scores - pose_peak[None]), axis=0)
    log_resp = pose_peak + jnp.log(total) - norm_ref[...]
    shape = (resp_ref.shape[1], lanes)
    lane = lax.broadcasted_iota(jnp.int32, shape, 1)
    row = ((lane // block) ^ me_ref[1]) * half + lax.rem(lane, block)
    take = (lax.broadcasted_iota(jnp.int32, shape, 0) == row) & (lax.rem(lane, block) < half)
    resp_ref[...] = lax.dot_general(
        log_resp, take.astype(f32), NT, precision=HIGHEST, preferred_element_type=f32
    )


def gather_rows(me, scores, norm, weight, slices, poses, half, span):
    columns, lanes = scores.shape
    counts = [len(refs) for refs in slices]
    slices = [w for refs in slices for w in refs]
    particles = sum(w.shape[0] for w in slices) // 2
    return call(
        functools.partial(gather_kernel, poses, half, counts),
        "gather_rows",
        [SMEM] + [VMEM] * (3 + len(slices)),
        [
            jax.ShapeDtypeStruct((columns // poses, lanes // 2), f32),
            jax.ShapeDtypeStruct((weight.shape[0], 2 * span), bf16),
            jax.ShapeDtypeStruct((2, particles, span), bf16),
        ],
        (me, scores, norm, weight, *slices),
        flops=GATHER_FLOPS,
        moved=8 * particles * span,
        limit=VMEM_LIMIT if particles <= 512 else 2 * VMEM_LIMIT,
    )


def finish_kernel(poses, groups, sources, half, me_ref, cw_ref, cos_ref, sin_ref, rows_ref, *refs):
    payloads, refs = refs[:sources], refs[sources:]
    last, (out_ref, rho_ref, inverse_ref, *buffers) = refs[:-5], refs[-5:]
    rows, _, span = out_ref.shape
    cut = poses // 2 * rows
    count = payloads[0].shape[1] // 2
    mass = jnp.zeros((rows, groups), f32)
    for i, ref in enumerate(payloads):
        rho_ref[:cut, i * count : (i + 1) * count] = ref[:cut, :count]
        rho_ref[cut:, i * count : (i + 1) * count] = ref[:cut, count:]
        mass += ref[cut:, :groups].astype(f32) + ref[cut:, groups : 2 * groups].astype(f32)
    high = mass.astype(bf16)
    mass = jnp.concatenate([high, (mass - high.astype(f32)).astype(bf16)], axis=0)
    terms = jnp.dot(mass, cw_ref[...], preferred_element_type=f32)
    denom = (terms[:rows, :span] + terms[rows:, :span]) + (terms[:rows, span:] + terms[rows:, span:])
    inverse_ref[...] = 1.0 / (denom + prior_precision)
    tiles = [(a, min(256, span - a)) for a in range(0, span, 256)]
    known = rows_ref.shape[1] // sources

    def rows_of(part, start, width):
        here = slice(start, start + width)
        if not last:
            return rows_ref[part, :, here]
        pieces = []
        for i in range(sources):
            pieces.append(rows_ref[part, i * known : (i + 1) * known, here])
            if i == 0:
                pieces.append(last[0][part * half : (part + 1) * half, here])
            else:
                at = (2 * (i - 1) + part) * half
                pieces.append(last[1][at : at + half, here])
        return jnp.concatenate(pieces, axis=0)

    def products(i):
        start, width = tiles[i]
        for part in range(2):
            buffers[i % 2][part, :, :width] = jnp.dot(
                rho_ref[...], rows_of(part, start, width), preferred_element_type=f32
            )

    def rotate(i):
        start, width = tiles[i]
        buffer = buffers[i % 2]
        for a in range(0, width, LANES):
            at = pl.ds(pl.multiple_of(me_ref[0] * span + start + a, LANES), LANES)
            numer_re = jnp.zeros((rows, LANES), f32)
            numer_im = jnp.zeros((rows, LANES), f32)
            for r in range(poses):
                cos_r = cos_ref[r : r + 1, at]
                sin_r = sin_ref[r : r + 1, at]
                s_re = buffer[0, r * rows : (r + 1) * rows, a : a + LANES]
                s_im = buffer[1, r * rows : (r + 1) * rows, a : a + LANES]
                numer_re = numer_re + s_re * cos_r + s_im * sin_r
                numer_im = numer_im + s_im * cos_r - s_re * sin_r
            here = slice(start + a, start + a + LANES)
            inverse = inverse_ref[:, here]
            out_ref[:, 0, here] = numer_re * inverse
            out_ref[:, 1, here] = numer_im * inverse

    products(0)
    for i in range(1, len(tiles)):
        products(i)
        rotate(i - 1)
    rotate(len(tiles) - 1)


def finish(me, weight, cos_t, sin_t, rows, payloads, last, cls_rows, half):
    poses = cos_t.shape[0]
    span = rows.shape[2]
    particles = len(payloads) * payloads[0].shape[1] // 2
    return call(
        functools.partial(finish_kernel, poses, weight.shape[0], len(payloads), half),
        "finish",
        [SMEM] + [VMEM] * (4 + len(payloads) + len(last)),
        [jax.ShapeDtypeStruct((cls_rows, 2, span), f32)],
        (me, weight, cos_t, sin_t, rows, *payloads, *last),
        [
            pltpu.VMEM((poses * cls_rows, particles), bf16),
            pltpu.VMEM((cls_rows, span), f32),
            pltpu.VMEM((2, poses * cls_rows, 256), f32),
            pltpu.VMEM((2, poses * cls_rows, 256), f32),
        ],
        flops=4 * poses * cls_rows * particles * span,
        limit=VMEM_LIMIT if particles <= 512 else 2 * VMEM_LIMIT,
    )[0]


def swap(values, axis, distance):
    size = lax.axis_size(axis)
    return lax.ppermute(values, axis, [(i, i ^ distance) for i in range(size)])


def local(particles, classes, ctf, noise_weight, group_ids, shifts):
    half, _, freq = particles.shape
    cls_rows = classes.shape[0]
    poses = shifts.shape[0]
    n_cls = lax.axis_size("cls")
    n_img = lax.axis_size("img")
    span = freq // n_img
    pairwise = n_cls == 4
    me_cls = lax.axis_index("cls") if pairwise else 0
    me = jnp.stack([lax.axis_index("img"), me_cls]).astype(jnp.int32)
    others = tuple(range(n_img - 1, 0, -1))

    own, *own_chunks = weigh(particles, ctf, noise_weight, group_ids)
    if pairwise:
        far = [swap(w, "cls", 2) for w in own_chunks]
        near = swap(own, "cls", 1)
        mine, *outgoing = cut_slices(me, [[own]], [(d, 0) for d in (0,) + others[:-1]], span, freq)
        slices = [mine] + [swap(w, "img", d) for w, d in zip(outgoing, others)]
    else:
        shards = [[lax.all_gather(own, "cls", axis=0, tiled=True)]]
        mine, *outgoing = cut_slices(me, shards, [(d, 0) for d in (0,) + others], span, freq)
        slices = [[w] for w in [mine] + [swap(w, "img", d) for w, d in zip(outgoing, others)]]

    split = jnp.transpose(classes, (1, 0, 2))
    cos_t, sin_t, power, weight = prepare(shifts, split, ctf, noise_weight)
    tile = template_tile(freq)
    count = freq // CHUNKS // tile
    built = count - count // 3
    early = [
        early_templates(split, cos_t, sin_t, count, count, tile),
        early_templates(split, cos_t, sin_t, built, count - built, tile),
    ][::-1]
    if pairwise:
        far, near, slices, split, early = lax.optimization_barrier(
            (far, near, slices, split, early)
        )
        third = [swap(w, "cls", 1) for w in far]
        targets = [(d, 1) for d in (0,) + others[:-1]] + [(others[-1], 0)]
        mine, *outgoing = cut_slices(me, [[own], [near], far], targets, span, freq)
        arrived = [mine] + [swap(w, "img", d) for w, d in zip(outgoing, others)]
        shards = [[own], [near], far, third]
    scores, marks, stat = score(early, split, cos_t, sin_t, power, shards, half)
    if pairwise:
        stat, arrived[-1] = lax.optimization_barrier((stat, arrived[-1]))
        stats = [stat] + [swap(stat, "cls", k) for k in range(n_cls - 1, 0, -1)]
        paired = (0,) + tuple(range(n_cls - 1, 0, -1))
        last = [*cut_slices(me, [third], [(0, 0)], span, freq)]
        last.append(swap(bundle(arrived[1:], 2 * half), "cls", 1))
        slices = [[a, b] for a, b in zip(slices, arrived)] + [arrived[-1:]]
    else:
        stats = [lax.all_gather(stat, "cls", axis=0, tiled=True)]
        paired = (0,)
        last = []
    norm, payload = responsibilities(scores, marks, stats, paired, poses, half)
    payloads = [payload] + [swap(payload, "img", d) for d in others]
    log_resp, weight_here, rows = gather_rows(
        me, scores, norm, weight, slices, poses, half, span
    )
    averages = finish(me, weight_here, cos_t, sin_t, rows, payloads, last, cls_rows, half)
    return (log_resp.T, averages)


def solution(mesh):
    placed = (
        P(("groups", "img", "cls"), None, None),
        P(("groups", "cls"), None, None),
        P("groups", None),
        P("groups"),
        P(("groups", "img", "cls")),
        P("groups", None),
    )
    return jax.shard_map(
        local,
        mesh=mesh,
        in_specs=placed,
        out_specs=(P(("groups", "img"), "cls"), P(("groups", "cls"), None, "img")),
        check_vma=False,
    )
```

```python
import functools

import jax
import jax.numpy as jnp
from jax import lax
from jax.experimental import pallas as pl
from jax.experimental.pallas import tpu as pltpu
from jax.sharding import PartitionSpec as P

BOX = 128
CHUNKS = 2
LANES = 128
VMEM_LIMIT = 24 * 1024 * 1024
GATHER_FLOPS = 20_000_000_000

prior_precision = 0.02

NT = (((1,), (1,)), ((), ()))
NN = (((1,), (0,)), ((), ()))
HIGHEST = lax.Precision.HIGHEST
f32 = jnp.float32
bf16 = jnp.bfloat16

SMEM = pl.BlockSpec(memory_space=pltpu.SMEM)
VMEM = pl.BlockSpec(memory_space=pltpu.VMEM)
ANY = pl.BlockSpec(memory_space=pl.ANY)


def call(kernel, name, in_specs, out_shape, operands, scratch=(), flops=0, moved=0, limit=VMEM_LIMIT):
    return pl.pallas_call(
        kernel,
        in_specs=in_specs,
        out_specs=[VMEM] * len(out_shape),
        out_shape=out_shape,
        scratch_shapes=list(scratch),
        compiler_params=pltpu.CompilerParams(vmem_limit_bytes=limit),
        cost_estimate=pl.CostEstimate(flops=flops, bytes_accessed=moved, transcendentals=0),
        name=name,
    )(*operands)


def real_index(shape, axis, half):
    return lax.rem(lax.broadcasted_iota(jnp.int32, shape, axis) // half, 2) == 0


def weigh_kernel(ids_hbm, p_hbm, ctf_hbm, nw_hbm, *refs):
    out_refs, (ids_ref, p_ref, ctf_ref, nw_ref, raw_ref, scale_ref, sem) = refs[:-7], refs[-7:]
    count, _, freq = p_ref.shape
    copies = [
        pltpu.make_async_copy(source, target, sem.at[i])
        for i, (source, target) in enumerate(
            [(p_hbm, p_ref), (ids_hbm, ids_ref), (nw_hbm, nw_ref), (ctf_hbm, ctf_ref)]
        )
    ]
    for copy in copies:
        copy.start()
    copies[0].wait()
    values = p_ref[...].astype(f32)
    for part in range(2):
        raw_ref[part] = values[:, part, :]
    copies[1].wait()
    row = lax.rem(lax.broadcasted_iota(jnp.int32, (2 * count, LANES), 0), count)
    ids = jnp.zeros((2 * count, LANES), f32)
    for n in range(count):
        ids = jnp.where(row == n, ids_ref[n].astype(f32), ids)
    for out_ref in out_refs[:2]:
        out_ref[:, out_ref.shape[1] - LANES :] = ids.astype(bf16)
    copies[2].wait()
    noise = nw_ref[...].reshape(1, freq)
    copies[3].wait()
    for n in range(count):
        scale_ref[n : n + 1, :] = ctf_ref[pl.ds(ids_ref[n], 1), :] * noise
    scale = scale_ref[...]
    chunk = freq // CHUNKS
    for part in range(2):
        weighted = (raw_ref[part] * scale).astype(bf16)
        here = slice(part * count, (part + 1) * count)
        out_refs[0][here, :freq] = weighted
        for c, out_ref in enumerate(out_refs[1:]):
            out_ref[here, :chunk] = weighted[:, c * chunk : (c + 1) * chunk]


def weigh(particles, ctf, noise_weight, group_ids):
    rows, _, freq = particles.shape
    operands = (group_ids, particles, ctf, noise_weight)
    return call(
        weigh_kernel,
        "weigh",
        [ANY] * 4,
        [
            jax.ShapeDtypeStruct((2 * rows, width), bf16)
            for width in [freq + LANES, freq // CHUNKS + LANES] + [freq // CHUNKS] * (CHUNKS - 1)
        ],
        [pltpu.with_memory_space_constraint(x, pltpu.HBM) for x in operands],
        [
            pltpu.SMEM((rows,), jnp.int32),
            pltpu.VMEM(particles.shape, bf16),
            pltpu.VMEM(ctf.shape, f32),
            pltpu.VMEM((freq,), f32),
            pltpu.VMEM((2, rows, freq), f32),
            pltpu.VMEM((rows, freq), f32),
            pltpu.SemaphoreType.DMA((4,)),
        ],
        flops=4 * rows * freq,
        moved=16 * rows * freq,
    )


def prepare_kernel(
    shifts_ref, cls_ref, ctf_hbm, nw_hbm, cos_ref, sin_ref, pow_ref, cw_ref, *scratch
):
    ctf_ref, nw_ref, angle_ref, sem = scratch
    freq = cls_ref.shape[2]
    poses = cos_ref.shape[0]
    copies = [
        pltpu.make_async_copy(source, target, sem.at[i])
        for i, (source, target) in enumerate(
            [(ctf_hbm, ctf_ref), (nw_hbm, nw_ref)]
        )
    ]
    for copy in copies:
        copy.start()
    lane = lax.broadcasted_iota(jnp.int32, (1, BOX), 1).astype(f32)
    step = 2.0 * jnp.pi / BOX
    for r in range(poses):
        angle_ref[0, r : r + 1, :] = step * (shifts_ref[0, r].astype(f32) * (lane - BOX // 2))
        angle_ref[1, r : r + 1, :] = step * (shifts_ref[1, r].astype(f32) * lane)
    x_cos, x_sin = jnp.cos(angle_ref[0]), jnp.sin(angle_ref[0])
    y_cos, y_sin = jnp.cos(angle_ref[1]), jnp.sin(angle_ref[1])
    for t in range(freq // BOX):
        c = jnp.broadcast_to(y_cos[:, t : t + 1], x_cos.shape)
        s = jnp.broadcast_to(y_sin[:, t : t + 1], x_cos.shape)
        cos_ref[:, t * BOX : (t + 1) * BOX] = x_cos * c - x_sin * s
        sin_ref[:, t * BOX : (t + 1) * BOX] = x_sin * c + x_cos * s
    for copy in copies:
        copy.wait()
    noise = nw_ref[...].reshape(1, freq)
    cut = freq // 4
    power = jnp.zeros(pow_ref.shape, f32)
    for q in range(4):
        at = slice(q * cut, (q + 1) * cut)
        re = cls_ref[0, :, at].astype(f32)
        im = cls_ref[1, :, at].astype(f32)
        ctf = ctf_ref[:, at]
        weight = ctf * ctf * noise[:, at]
        cw_ref[:, at] = weight
        power += lax.dot_general(
            re * re + im * im, weight, NT, precision=HIGHEST, preferred_element_type=f32
        )
    pow_ref[...] = power


def prepare(shifts, split, ctf, noise_weight):
    _, rows, freq = split.shape
    poses, groups = shifts.shape[0], ctf.shape[0]
    return call(
        prepare_kernel,
        "prepare",
        [SMEM, VMEM, ANY, ANY],
        [
            jax.ShapeDtypeStruct((poses, freq), f32),
            jax.ShapeDtypeStruct((poses, freq), f32),
            jax.ShapeDtypeStruct((rows, groups), f32),
            jax.ShapeDtypeStruct((groups, freq), f32),
        ],
        (
            shifts.T,
            split,
            *[pltpu.with_memory_space_constraint(x, pltpu.HBM) for x in (ctf, noise_weight)],
        ),
        [
            pltpu.VMEM(ctf.shape, f32),
            pltpu.VMEM((freq,), f32),
            pltpu.VMEM((2, poses, BOX), f32),
            pltpu.SemaphoreType.DMA((2,)),
        ],
        flops=24 * rows * groups * freq,
    )


def write_templates(cls_ref, cos_ref, sin_ref, temp_ref, start, tile):
    rows = cls_ref.shape[1]
    for a in range(0, tile, LANES):
        at = pl.ds(pl.multiple_of(start + a, LANES), LANES)
        re = cls_ref[0, :, at].astype(f32)
        im = cls_ref[1, :, at].astype(f32)
        for r in range(cos_ref.shape[0]):
            cos_r = cos_ref[r : r + 1, at]
            sin_r = sin_ref[r : r + 1, at]
            here = slice(r * rows, (r + 1) * rows)
            temp_ref[here, a : a + LANES] = (re * cos_r - im * sin_r).astype(bf16)
            temp_ref[here, tile + a : tile + a + LANES] = (re * sin_r + im * cos_r).astype(bf16)


def template_tile(freq):
    return max(t for t in range(LANES, 385, LANES) if freq // CHUNKS % t == 0)


def early_kernel(cls_ref, cos_ref, sin_ref, temp_ref):
    write_templates(cls_ref, cos_ref, sin_ref, temp_ref, 0, cls_ref.shape[2])


def early_templates(split, cos_t, sin_t, skip, count, tile):
    _, rows, _ = split.shape
    poses = cos_t.shape[0]
    return pl.pallas_call(
        early_kernel,
        grid=(count,),
        in_specs=[
            pl.BlockSpec((2, rows, tile), lambda j: (0, 0, skip + j)),
            pl.BlockSpec((poses, tile), lambda j: (0, skip + j)),
            pl.BlockSpec((poses, tile), lambda j: (0, skip + j)),
        ],
        out_specs=pl.BlockSpec((None, poses * rows, 2 * tile), lambda j: (j, 0, 0)),
        out_shape=jax.ShapeDtypeStruct((count, poses * rows, 2 * tile), bf16),
        compiler_params=pltpu.CompilerParams(vmem_limit_bytes=VMEM_LIMIT),
        cost_estimate=pl.CostEstimate(
            flops=40 * poses * rows * count * tile,
            bytes_accessed=4 * poses * rows * count * tile,
            transcendentals=0,
        ),
        name=f"early_templates{skip}",
    )(split, cos_t, sin_t)


def template_kernel(cls_ref, cos_ref, sin_ref, temp_ref):
    count, _, width = temp_ref.shape
    tile = width // 2

    @pl.loop(0, count)
    def _(t):
        write_templates(cls_ref, cos_ref, sin_ref, temp_ref.at[t], t * tile, tile)


def regroup(refs, counts):
    refs = list(refs)
    return [[refs.pop(0) for _ in range(count)] for count in counts]


def tile_of_particles(shards, chunk, span, t, tile, half):
    cuts = []
    for ref, chunked in shards:
        at = t * tile if chunked else chunk * span + t * tile
        cuts.append(ref[:, at : at + tile])
    wide = jnp.concatenate(cuts, axis=0).astype(f32)
    real = real_index(wide.shape, 0, half)
    return jnp.concatenate(
        [jnp.where(real, wide, 0.0).astype(bf16), jnp.where(real, 0.0, wide).astype(bf16)], axis=1
    )


def first_score_kernel(chunked, half, built_ref, early_ref, *refs):
    refs, acc_ref = refs[:-1], refs[-1]
    tile = built_ref.shape[2] // 2
    temps = [ref.at[t] for ref in (built_ref, early_ref) for t in range(ref.shape[0])]
    count = len(temps)
    shards = list(zip(refs, chunked))
    acc_ref[...] = jnp.zeros_like(acc_ref)
    for t in range(count):
        acc_ref[...] += lax.dot_general(
            temps[t][...],
            tile_of_particles(shards, 0, count * tile, t, tile, half),
            NT,
            preferred_element_type=f32,
        )


def last_score_kernel(chunked, half, temp_ref, pow_ref, acc_ref, *refs):
    refs, (s_ref, marks_ref, stat_ref) = refs[:-3], refs[-3:]
    tail_refs, shards = refs[: len(chunked)], list(zip(refs[len(chunked) :], chunked))
    count, _, width = temp_ref.shape
    tile = width // 2
    rows, groups = pow_ref.shape
    lanes = s_ref.shape[1]
    poses = s_ref.shape[0] // rows
    tails = [ref[:, ref.shape[1] - LANES :] for ref in tail_refs]
    ids = jnp.concatenate(tails, axis=0).astype(f32)
    group = lax.broadcasted_iota(jnp.int32, (lanes, groups), 1).astype(f32)
    marks = (ids[:, :groups] == group).astype(f32)
    marks_ref[...] = marks
    penalty = lax.dot_general(
        pow_ref[...], marks, NT, precision=HIGHEST, preferred_element_type=f32
    )
    s_ref[...] = acc_ref[...]
    for t in range(count):
        s_ref[...] += lax.dot_general(
            temp_ref[t],
            tile_of_particles(shards, 1, count * tile, t, tile, half),
            NT,
            preferred_element_type=f32,
        )
    acc = s_ref[...]
    acc = acc + jnp.where(
        real_index(acc.shape, 1, half), pltpu.roll(acc, lanes - half, 1), pltpu.roll(acc, half, 1)
    )
    scores = acc.reshape(poses, rows, lanes) - 0.5 * penalty[None]
    peak = jnp.max(jnp.max(scores, axis=0), axis=0, keepdims=True)
    total = jnp.sum(jnp.sum(jnp.exp(scores - peak[None]), axis=0), axis=0, keepdims=True)
    s_ref[...] = scores.reshape(poses * rows, lanes)
    stat_ref[0:1, :] = peak
    stat_ref[1:2, :] = total
    stat_ref[2:8, :] = jnp.zeros((6, lanes), f32)


def score(early, split, cos_t, sin_t, power, shards, half):
    first, late = early
    count, columns, width = late.shape
    freq = split.shape[2]
    lanes = sum(refs[0].shape[0] for refs in shards)
    chunked = [len(refs) > 1 for refs in shards]
    flops = 2 * columns * 256 * count * width
    acc_shape = jax.ShapeDtypeStruct((columns, lanes), f32)
    built = count - first.shape[0]
    temps = call(
        template_kernel,
        "templates",
        [VMEM] * 3,
        [pltpu.VMEM((built, columns, width), bf16)],
        (split, cos_t, sin_t),
        flops=40 * columns * built * width // 2,
    )[0]
    operands = [temps, first, *[refs[0] for refs in shards]]
    acc = call(
        functools.partial(first_score_kernel, chunked, half),
        "score0",
        [VMEM] * len(operands),
        [acc_shape],
        operands,
        flops=flops,
    )[0]
    operands = [late, power, acc]
    operands += [refs[0] for refs in shards] + [refs[-1] for refs in shards]
    return call(
        functools.partial(last_score_kernel, chunked, half),
        "score1",
        [VMEM] * len(operands),
        [
            acc_shape,
            jax.ShapeDtypeStruct((lanes, power.shape[1]), f32),
            jax.ShapeDtypeStruct((8, lanes), f32),
        ],
        operands,
        flops=flops,
    )


def slices_kernel(counts, targets, me_ref, *refs):
    whole_ref, refs = refs[-1], refs[:-1]
    shards, out_refs = regroup(refs[: -len(targets)], counts), refs[-len(targets) :]
    span = out_refs[0].shape[1]
    filled = [0] * len(targets)
    for k, refs in enumerate(shards):
        source = refs[0]
        height = source.shape[0]
        if len(refs) > 1:
            width = refs[-1].shape[1]
            for c, ref in enumerate(refs):
                whole_ref[:, c * width : (c + 1) * width] = ref[:, :width]
            source = whole_ref
        for i, (distance, skip) in enumerate(targets):
            if k >= skip:
                base = pl.multiple_of((me_ref[0] ^ distance) * span, LANES)
                out_refs[i][filled[i] : filled[i] + height, :] = source[:, pl.ds(base, span)]
                filled[i] += height


def cut_slices(me, shards, targets, span, freq):
    heights = [refs[0].shape[0] for refs in shards]
    operands = [me, *[ref for refs in shards for ref in refs]]
    out_heights = [sum(heights[skip:]) for _, skip in targets]
    return call(
        functools.partial(slices_kernel, [len(refs) for refs in shards], targets),
        "cut_slices",
        [SMEM] + [VMEM] * (len(operands) - 1),
        [jax.ShapeDtypeStruct((height, span), bf16) for height in out_heights],
        operands,
        [pltpu.VMEM((heights[-1], freq), bf16)],
        moved=4 * span * sum(out_heights),
        limit=VMEM_LIMIT if sum(heights) <= 128 else 2 * VMEM_LIMIT,
    )


def bundle_kernel(*refs):
    sources, out_ref = refs[:-1], refs[-1]
    rows = out_ref.shape[0] // len(sources)
    for i, ref in enumerate(sources):
        out_ref[i * rows : (i + 1) * rows, :] = ref[ref.shape[0] - rows :, :]


def bundle(slices, rows):
    span = slices[0].shape[1]
    return call(
        bundle_kernel,
        "bundle",
        [VMEM] * len(slices),
        [jax.ShapeDtypeStruct((len(slices) * rows, span), bf16)],
        slices,
        moved=4 * len(slices) * rows * span,
    )[0]


def xor_blocks(values, block, distance):
    lanes = values.shape[1]
    lane = lax.broadcasted_iota(jnp.int32, values.shape, 1)
    width = block
    while distance:
        if distance % 2:
            low = lax.rem(lane // width, 2) == 0
            values = jnp.where(
                low, pltpu.roll(values, lanes - width, 1), pltpu.roll(values, width, 1)
            )
        distance //= 2
        width *= 2
    return values


def rho_kernel(poses, half, paired, s_ref, marks_ref, *refs):
    stat_refs, (norm_ref, out_ref) = refs[: len(paired)], refs[len(paired) :]
    lanes = s_ref.shape[1]
    rows = s_ref.shape[0] // poses
    groups = marks_ref.shape[1]
    block = 2 * half
    peaks, totals = [], []
    for ref, distance in zip(stat_refs, paired):
        for at in range(0, ref.shape[0], 8):
            stats = xor_blocks(ref[at : at + 8, :], block, distance)
            peaks.append(stats[0:1])
            totals.append(stats[1:2])
    peak = functools.reduce(jnp.maximum, peaks)
    total = sum(t * jnp.exp(p - peak) for t, p in zip(totals, peaks))
    log_norm = peak + jnp.log(total)
    norm_ref[...] = log_norm
    rho = jnp.exp(s_ref[...].reshape(poses, rows, lanes) - log_norm[None])
    mass = lax.dot_general(
        jnp.where(real_index((rows, lanes), 1, half), jnp.sum(rho, axis=0), 0.0),
        marks_ref[...],
        NN,
        precision=HIGHEST,
        preferred_element_type=f32,
    )
    high = mass.astype(bf16)
    low = (mass - high.astype(f32)).astype(bf16)
    rho_low = rho.reshape(poses * rows, lanes).astype(bf16)
    cut = poses // 2 * rows
    lane = lax.broadcasted_iota(jnp.int32, (lanes, lanes), 0)
    column = lax.broadcasted_iota(jnp.int32, (lanes, lanes), 1)
    particle = lane // block * half + lax.rem(lane, block)
    real = lax.rem(lane, block) < half
    first = (real & (column == particle)).astype(f32).astype(bf16)
    second = (real & (column == particle + lanes // 2)).astype(f32).astype(bf16)
    packed = jnp.dot(rho_low[:cut], first, preferred_element_type=f32)
    packed += jnp.dot(rho_low[cut:], second, preferred_element_type=f32)
    out_ref[:cut, :] = packed.astype(bf16)
    if lanes > 2 * groups:
        out_ref[cut:, :] = jnp.zeros((rows, lanes), bf16)
    out_ref[cut:, :groups] = high
    out_ref[cut:, groups : 2 * groups] = low


def responsibilities(scores, marks, stats, paired, poses, half):
    columns, lanes = scores.shape
    return call(
        functools.partial(rho_kernel, poses, half, paired),
        "responsibilities",
        [VMEM] * (2 + len(stats)),
        [
            jax.ShapeDtypeStruct((1, lanes), f32),
            jax.ShapeDtypeStruct((columns // 2 + columns // poses, lanes), bf16),
        ],
        (scores, marks, *stats),
        flops=40 * columns * lanes,
    )


def gather_kernel(poses, half, counts, me_ref, s_ref, norm_ref, weight_ref, *refs):
    w_refs, (resp_ref, cw_ref, rows_ref) = refs[:-3], refs[-3:]
    span = rows_ref.shape[2]
    block = 2 * half
    here = pl.ds(pl.multiple_of(me_ref[0] * span, LANES), span)
    at = 0
    for refs in regroup(w_refs, counts):
        for ref in refs:
            for start in range(0, ref.shape[0], block):
                rows_ref[0, at : at + half, :] = ref[start : start + half, :]
                rows_ref[1, at : at + half, :] = ref[start + half : start + block, :]
                at += half
    weight = weight_ref[:, here]
    high = weight.astype(bf16)
    cw_ref[:, :span] = high
    cw_ref[:, span:] = (weight - high.astype(f32)).astype(bf16)
    rows = resp_ref.shape[0]
    lanes = s_ref.shape[1]
    scores = s_ref[...].reshape(poses, rows, lanes)
    pose_peak = jnp.max(scores, axis=0)
    total = jnp.sum(jnp.exp(scores - pose_peak[None]), axis=0)
    log_resp = pose_peak + jnp.log(total) - norm_ref[...]
    shape = (resp_ref.shape[1], lanes)
    lane = lax.broadcasted_iota(jnp.int32, shape, 1)
    row = ((lane // block) ^ me_ref[1]) * half + lax.rem(lane, block)
    take = (lax.broadcasted_iota(jnp.int32, shape, 0) == row) & (lax.rem(lane, block) < half)
    resp_ref[...] = lax.dot_general(
        log_resp, take.astype(f32), NT, precision=HIGHEST, preferred_element_type=f32
    )


def gather_rows(me, scores, norm, weight, slices, poses, half, span):
    columns, lanes = scores.shape
    counts = [len(refs) for refs in slices]
    slices = [w for refs in slices for w in refs]
    particles = sum(w.shape[0] for w in slices) // 2
    return call(
        functools.partial(gather_kernel, poses, half, counts),
        "gather_rows",
        [SMEM] + [VMEM] * (3 + len(slices)),
        [
            jax.ShapeDtypeStruct((columns // poses, lanes // 2), f32),
            jax.ShapeDtypeStruct((weight.shape[0], 2 * span), bf16),
            jax.ShapeDtypeStruct((2, particles, span), bf16),
        ],
        (me, scores, norm, weight, *slices),
        flops=GATHER_FLOPS,
        moved=8 * particles * span,
        limit=VMEM_LIMIT if particles <= 512 else 2 * VMEM_LIMIT,
    )


def finish_kernel(poses, groups, sources, half, me_ref, cw_ref, cos_ref, sin_ref, rows_ref, *refs):
    payloads, refs = refs[:sources], refs[sources:]
    last, (out_ref, rho_ref, inverse_ref, *buffers) = refs[:-5], refs[-5:]
    rows, _, span = out_ref.shape
    cut = poses // 2 * rows
    count = payloads[0].shape[1] // 2
    mass = jnp.zeros((rows, groups), f32)
    for i, ref in enumerate(payloads):
        rho_ref[:cut, i * count : (i + 1) * count] = ref[:cut, :count]
        rho_ref[cut:, i * count : (i + 1) * count] = ref[:cut, count:]
        mass += ref[cut:, :groups].astype(f32) + ref[cut:, groups : 2 * groups].astype(f32)
    high = mass.astype(bf16)
    mass = jnp.concatenate([high, (mass - high.astype(f32)).astype(bf16)], axis=0)
    terms = jnp.dot(mass, cw_ref[...], preferred_element_type=f32)
    denom = (terms[:rows, :span] + terms[rows:, :span]) + (terms[:rows, span:] + terms[rows:, span:])
    inverse_ref[...] = 1.0 / (denom + prior_precision)
    tiles = [(a, min(256, span - a)) for a in range(0, span, 256)]
    known = rows_ref.shape[1] // sources

    def rows_of(part, start, width):
        here = slice(start, start + width)
        if not last:
            return rows_ref[part, :, here]
        pieces = []
        for i in range(sources):
            pieces.append(rows_ref[part, i * known : (i + 1) * known, here])
            if i == 0:
                pieces.append(last[0][part * half : (part + 1) * half, here])
            else:
                at = (2 * (i - 1) + part) * half
                pieces.append(last[1][at : at + half, here])
        return jnp.concatenate(pieces, axis=0)

    def products(i):
        start, width = tiles[i]
        for part in range(2):
            buffers[i % 2][part, :, :width] = jnp.dot(
                rho_ref[...], rows_of(part, start, width), preferred_element_type=f32
            )

    def rotate(i):
        start, width = tiles[i]
        buffer = buffers[i % 2]
        for a in range(0, width, LANES):
            at = pl.ds(pl.multiple_of(me_ref[0] * span + start + a, LANES), LANES)
            numer_re = jnp.zeros((rows, LANES), f32)
            numer_im = jnp.zeros((rows, LANES), f32)
            for r in range(poses):
                cos_r = cos_ref[r : r + 1, at]
                sin_r = sin_ref[r : r + 1, at]
                s_re = buffer[0, r * rows : (r + 1) * rows, a : a + LANES]
                s_im = buffer[1, r * rows : (r + 1) * rows, a : a + LANES]
                numer_re = numer_re + s_re * cos_r + s_im * sin_r
                numer_im = numer_im + s_im * cos_r - s_re * sin_r
            here = slice(start + a, start + a + LANES)
            inverse = inverse_ref[:, here]
            out_ref[:, 0, here] = numer_re * inverse
            out_ref[:, 1, here] = numer_im * inverse

    products(0)
    for i in range(1, len(tiles)):
        products(i)
        rotate(i - 1)
    rotate(len(tiles) - 1)


def finish(me, weight, cos_t, sin_t, rows, payloads, last, cls_rows, half):
    poses = cos_t.shape[0]
    span = rows.shape[2]
    particles = len(payloads) * payloads[0].shape[1] // 2
    return call(
        functools.partial(finish_kernel, poses, weight.shape[0], len(payloads), half),
        "finish",
        [SMEM] + [VMEM] * (4 + len(payloads) + len(last)),
        [jax.ShapeDtypeStruct((cls_rows, 2, span), f32)],
        (me, weight, cos_t, sin_t, rows, *payloads, *last),
        [
            pltpu.VMEM((poses * cls_rows, particles), bf16),
            pltpu.VMEM((cls_rows, span), f32),
            pltpu.VMEM((2, poses * cls_rows, 256), f32),
            pltpu.VMEM((2, poses * cls_rows, 256), f32),
        ],
        flops=4 * poses * cls_rows * particles * span,
        limit=VMEM_LIMIT if particles <= 512 else 2 * VMEM_LIMIT,
    )[0]


def swap(values, axis, distance):
    size = lax.axis_size(axis)
    return lax.ppermute(values, axis, [(i, i ^ distance) for i in range(size)])


def local(particles, classes, ctf, noise_weight, group_ids, shifts):
    half, _, freq = particles.shape
    cls_rows = classes.shape[0]
    poses = shifts.shape[0]
    n_cls = lax.axis_size("cls")
    n_img = lax.axis_size("img")
    span = freq // n_img
    pairwise = n_cls == 4
    me_cls = lax.axis_index("cls") if pairwise else 0
    me = jnp.stack([lax.axis_index("img"), me_cls]).astype(jnp.int32)
    others = tuple(range(n_img - 1, 0, -1))

    own, *own_chunks = weigh(particles, ctf, noise_weight, group_ids)
    if pairwise:
        far = [swap(w, "cls", 2) for w in own_chunks]
        near = swap(own, "cls", 1)
        mine, *outgoing = cut_slices(me, [[own]], [(d, 0) for d in (0,) + others[:-1]], span, freq)
        slices = [mine] + [swap(w, "img", d) for w, d in zip(outgoing, others)]
    else:
        shards = [[lax.all_gather(own, "cls", axis=0, tiled=True)]]
        mine, *outgoing = cut_slices(me, shards, [(d, 0) for d in (0,) + others], span, freq)
        slices = [[w] for w in [mine] + [swap(w, "img", d) for w, d in zip(outgoing, others)]]

    split = jnp.transpose(classes, (1, 0, 2))
    cos_t, sin_t, power, weight = prepare(shifts, split, ctf, noise_weight)
    tile = template_tile(freq)
    count = freq // CHUNKS // tile
    built = count - count // 3
    early = [
        early_templates(split, cos_t, sin_t, count, count, tile),
        early_templates(split, cos_t, sin_t, built, count - built, tile),
    ][::-1]
    if pairwise:
        far, near, slices, split, early = lax.optimization_barrier(
            (far, near, slices, split, early)
        )
        third = [swap(far[0], "cls", 1)]
        targets = [(d, 1) for d in (0,) + others[:-1]] + [(others[-1], 0)]
        mine, *outgoing = cut_slices(me, [[own], [near], far], targets, span, freq)
        rest, mine = lax.optimization_barrier((far[1], mine))
        third.append(swap(rest, "cls", 1))
        arrived = [mine] + [swap(w, "img", d) for w, d in zip(outgoing, others)]
        shards = [[own], [near], far, third]
    scores, marks, stat = score(early, split, cos_t, sin_t, power, shards, half)
    if pairwise:
        stat, arrived[-1] = lax.optimization_barrier((stat, arrived[-1]))
        stats = [stat] + [swap(stat, "cls", k) for k in range(n_cls - 1, 0, -1)]
        paired = (0,) + tuple(range(n_cls - 1, 0, -1))
        last = [*cut_slices(me, [third], [(0, 0)], span, freq)]
        last.append(swap(bundle(arrived[1:], 2 * half), "cls", 1))
        slices = [[a, b] for a, b in zip(slices, arrived)] + [arrived[-1:]]
    else:
        stats = [lax.all_gather(stat, "cls", axis=0, tiled=True)]
        paired = (0,)
        last = []
    norm, payload = responsibilities(scores, marks, stats, paired, poses, half)
    payloads = [payload] + [swap(payload, "img", d) for d in others]
    log_resp, weight_here, rows = gather_rows(
        me, scores, norm, weight, slices, poses, half, span
    )
    averages = finish(me, weight_here, cos_t, sin_t, rows, payloads, last, cls_rows, half)
    return (log_resp.T, averages)


def solution(mesh):
    placed = (
        P(("groups", "img", "cls"), None, None),
        P(("groups", "cls"), None, None),
        P("groups", None),
        P("groups"),
        P(("groups", "img", "cls")),
        P("groups", None),
    )
    return jax.shard_map(
        local,
        mesh=mesh,
        in_specs=placed,
        out_specs=(P(("groups", "img"), "cls"), P(("groups", "cls"), None, "img")),
        check_vma=False,
    )
```

```python
import functools

import jax
import jax.numpy as jnp
from jax import lax
from jax.experimental import pallas as pl
from jax.experimental.pallas import tpu as pltpu
from jax.sharding import PartitionSpec as P

BOX = 128
CHUNKS = 2
LANES = 128
VMEM_LIMIT = 24 * 1024 * 1024
GATHER_FLOPS = 20_000_000_000

prior_precision = 0.02

NT = (((1,), (1,)), ((), ()))
NN = (((1,), (0,)), ((), ()))
HIGHEST = lax.Precision.HIGHEST
f32 = jnp.float32
bf16 = jnp.bfloat16

SMEM = pl.BlockSpec(memory_space=pltpu.SMEM)
VMEM = pl.BlockSpec(memory_space=pltpu.VMEM)
ANY = pl.BlockSpec(memory_space=pl.ANY)


def call(kernel, name, in_specs, out_shape, operands, scratch=(), flops=0, moved=0, limit=VMEM_LIMIT):
    return pl.pallas_call(
        kernel,
        in_specs=in_specs,
        out_specs=[VMEM] * len(out_shape),
        out_shape=out_shape,
        scratch_shapes=list(scratch),
        compiler_params=pltpu.CompilerParams(vmem_limit_bytes=limit),
        cost_estimate=pl.CostEstimate(flops=flops, bytes_accessed=moved, transcendentals=0),
        name=name,
    )(*operands)


def real_index(shape, axis, half):
    return lax.rem(lax.broadcasted_iota(jnp.int32, shape, axis) // half, 2) == 0


def weigh_kernel(ids_hbm, p_hbm, ctf_hbm, nw_hbm, *refs):
    out_refs, (ids_ref, p_ref, ctf_ref, nw_ref, raw_ref, scale_ref, sem) = refs[:-7], refs[-7:]
    count, _, freq = p_ref.shape
    copies = [
        pltpu.make_async_copy(source, target, sem.at[i])
        for i, (source, target) in enumerate(
            [(p_hbm, p_ref), (ids_hbm, ids_ref), (nw_hbm, nw_ref), (ctf_hbm, ctf_ref)]
        )
    ]
    for copy in copies:
        copy.start()
    copies[0].wait()
    values = p_ref[...].astype(f32)
    for part in range(2):
        raw_ref[part] = values[:, part, :]
    copies[1].wait()
    row = lax.rem(lax.broadcasted_iota(jnp.int32, (2 * count, LANES), 0), count)
    ids = jnp.zeros((2 * count, LANES), f32)
    for n in range(count):
        ids = jnp.where(row == n, ids_ref[n].astype(f32), ids)
    for out_ref in out_refs[:2]:
        out_ref[:, out_ref.shape[1] - LANES :] = ids.astype(bf16)
    copies[2].wait()
    noise = nw_ref[...].reshape(1, freq)
    copies[3].wait()
    for n in range(count):
        scale_ref[n : n + 1, :] = ctf_ref[pl.ds(ids_ref[n], 1), :] * noise
    scale = scale_ref[...]
    chunk = freq // CHUNKS
    for part in range(2):
        weighted = (raw_ref[part] * scale).astype(bf16)
        here = slice(part * count, (part + 1) * count)
        out_refs[0][here, :freq] = weighted
        for c, out_ref in enumerate(out_refs[1:]):
            out_ref[here, :chunk] = weighted[:, c * chunk : (c + 1) * chunk]


def weigh(particles, ctf, noise_weight, group_ids):
    rows, _, freq = particles.shape
    operands = (group_ids, particles, ctf, noise_weight)
    return call(
        weigh_kernel,
        "weigh",
        [ANY] * 4,
        [
            jax.ShapeDtypeStruct((2 * rows, width), bf16)
            for width in [freq + LANES, freq // CHUNKS + LANES] + [freq // CHUNKS] * (CHUNKS - 1)
        ],
        [pltpu.with_memory_space_constraint(x, pltpu.HBM) for x in operands],
        [
            pltpu.SMEM((rows,), jnp.int32),
            pltpu.VMEM(particles.shape, bf16),
            pltpu.VMEM(ctf.shape, f32),
            pltpu.VMEM((freq,), f32),
            pltpu.VMEM((2, rows, freq), f32),
            pltpu.VMEM((rows, freq), f32),
            pltpu.SemaphoreType.DMA((4,)),
        ],
        flops=4 * rows * freq,
        moved=16 * rows * freq,
    )


def prepare_kernel(
    shifts_ref, cls_ref, ctf_hbm, nw_hbm, cos_ref, sin_ref, pow_ref, cw_ref, *scratch
):
    ctf_ref, nw_ref, angle_ref, sem = scratch
    freq = cls_ref.shape[2]
    poses = cos_ref.shape[0]
    copies = [
        pltpu.make_async_copy(source, target, sem.at[i])
        for i, (source, target) in enumerate(
            [(ctf_hbm, ctf_ref), (nw_hbm, nw_ref)]
        )
    ]
    for copy in copies:
        copy.start()
    lane = lax.broadcasted_iota(jnp.int32, (1, BOX), 1).astype(f32)
    step = 2.0 * jnp.pi / BOX
    for r in range(poses):
        angle_ref[0, r : r + 1, :] = step * (shifts_ref[0, r].astype(f32) * (lane - BOX // 2))
        angle_ref[1, r : r + 1, :] = step * (shifts_ref[1, r].astype(f32) * lane)
    x_cos, x_sin = jnp.cos(angle_ref[0]), jnp.sin(angle_ref[0])
    y_cos, y_sin = jnp.cos(angle_ref[1]), jnp.sin(angle_ref[1])
    for t in range(freq // BOX):
        c = jnp.broadcast_to(y_cos[:, t : t + 1], x_cos.shape)
        s = jnp.broadcast_to(y_sin[:, t : t + 1], x_cos.shape)
        cos_ref[:, t * BOX : (t + 1) * BOX] = x_cos * c - x_sin * s
        sin_ref[:, t * BOX : (t + 1) * BOX] = x_sin * c + x_cos * s
    for copy in copies:
        copy.wait()
    noise = nw_ref[...].reshape(1, freq)
    cut = freq // 4
    power = jnp.zeros(pow_ref.shape, f32)
    for q in range(4):
        at = slice(q * cut, (q + 1) * cut)
        re = cls_ref[0, :, at].astype(f32)
        im = cls_ref[1, :, at].astype(f32)
        ctf = ctf_ref[:, at]
        weight = ctf * ctf * noise[:, at]
        cw_ref[:, at] = weight
        power += lax.dot_general(
            re * re + im * im, weight, NT, precision=HIGHEST, preferred_element_type=f32
        )
    pow_ref[...] = power


def prepare(shifts, split, ctf, noise_weight):
    _, rows, freq = split.shape
    poses, groups = shifts.shape[0], ctf.shape[0]
    return call(
        prepare_kernel,
        "prepare",
        [SMEM, VMEM, ANY, ANY],
        [
            jax.ShapeDtypeStruct((poses, freq), f32),
            jax.ShapeDtypeStruct((poses, freq), f32),
            jax.ShapeDtypeStruct((rows, groups), f32),
            jax.ShapeDtypeStruct((groups, freq), f32),
        ],
        (
            shifts.T,
            split,
            *[pltpu.with_memory_space_constraint(x, pltpu.HBM) for x in (ctf, noise_weight)],
        ),
        [
            pltpu.VMEM(ctf.shape, f32),
            pltpu.VMEM((freq,), f32),
            pltpu.VMEM((2, poses, BOX), f32),
            pltpu.SemaphoreType.DMA((2,)),
        ],
        flops=24 * rows * groups * freq,
    )


def write_templates(cls_ref, cos_ref, sin_ref, temp_ref, start, tile):
    rows = cls_ref.shape[1]
    for a in range(0, tile, LANES):
        at = pl.ds(pl.multiple_of(start + a, LANES), LANES)
        re = cls_ref[0, :, at].astype(f32)
        im = cls_ref[1, :, at].astype(f32)
        for r in range(cos_ref.shape[0]):
            cos_r = cos_ref[r : r + 1, at]
            sin_r = sin_ref[r : r + 1, at]
            here = slice(r * rows, (r + 1) * rows)
            temp_ref[here, a : a + LANES] = (re * cos_r - im * sin_r).astype(bf16)
            temp_ref[here, tile + a : tile + a + LANES] = (re * sin_r + im * cos_r).astype(bf16)


def template_tile(freq):
    return max(t for t in range(LANES, 385, LANES) if freq // CHUNKS % t == 0)


def early_kernel(cls_ref, cos_ref, sin_ref, temp_ref):
    write_templates(cls_ref, cos_ref, sin_ref, temp_ref, 0, cls_ref.shape[2])


def early_templates(split, cos_t, sin_t, skip, count, tile):
    _, rows, _ = split.shape
    poses = cos_t.shape[0]
    return pl.pallas_call(
        early_kernel,
        grid=(count,),
        in_specs=[
            pl.BlockSpec((2, rows, tile), lambda j: (0, 0, skip + j)),
            pl.BlockSpec((poses, tile), lambda j: (0, skip + j)),
            pl.BlockSpec((poses, tile), lambda j: (0, skip + j)),
        ],
        out_specs=pl.BlockSpec((None, poses * rows, 2 * tile), lambda j: (j, 0, 0)),
        out_shape=jax.ShapeDtypeStruct((count, poses * rows, 2 * tile), bf16),
        compiler_params=pltpu.CompilerParams(vmem_limit_bytes=VMEM_LIMIT),
        cost_estimate=pl.CostEstimate(
            flops=40 * poses * rows * count * tile,
            bytes_accessed=4 * poses * rows * count * tile,
            transcendentals=0,
        ),
        name=f"early_templates{skip}",
    )(split, cos_t, sin_t)


def template_kernel(cls_ref, cos_ref, sin_ref, temp_ref):
    count, _, width = temp_ref.shape
    tile = width // 2

    @pl.loop(0, count)
    def _(t):
        write_templates(cls_ref, cos_ref, sin_ref, temp_ref.at[t], t * tile, tile)


def regroup(refs, counts):
    refs = list(refs)
    return [[refs.pop(0) for _ in range(count)] for count in counts]


def tile_of_particles(shards, chunk, span, t, tile, half):
    cuts = []
    for ref, chunked in shards:
        at = t * tile if chunked else chunk * span + t * tile
        cuts.append(ref[:, at : at + tile])
    wide = jnp.concatenate(cuts, axis=0).astype(f32)
    real = real_index(wide.shape, 0, half)
    return jnp.concatenate(
        [jnp.where(real, wide, 0.0).astype(bf16), jnp.where(real, 0.0, wide).astype(bf16)], axis=1
    )


def first_score_kernel(chunked, half, built_ref, early_ref, *refs):
    refs, acc_ref = refs[:-1], refs[-1]
    tile = built_ref.shape[2] // 2
    temps = [ref.at[t] for ref in (built_ref, early_ref) for t in range(ref.shape[0])]
    count = len(temps)
    shards = list(zip(refs, chunked))
    acc_ref[...] = jnp.zeros_like(acc_ref)
    for t in range(count):
        acc_ref[...] += lax.dot_general(
            temps[t][...],
            tile_of_particles(shards, 0, count * tile, t, tile, half),
            NT,
            preferred_element_type=f32,
        )


def last_score_kernel(chunked, half, temp_ref, pow_ref, acc_ref, *refs):
    refs, (s_ref, marks_ref, stat_ref) = refs[:-3], refs[-3:]
    tail_refs, shards = refs[: len(chunked)], list(zip(refs[len(chunked) :], chunked))
    count, _, width = temp_ref.shape
    tile = width // 2
    rows, groups = pow_ref.shape
    lanes = s_ref.shape[1]
    poses = s_ref.shape[0] // rows
    tails = [ref[:, ref.shape[1] - LANES :] for ref in tail_refs]
    ids = jnp.concatenate(tails, axis=0).astype(f32)
    group = lax.broadcasted_iota(jnp.int32, (lanes, groups), 1).astype(f32)
    marks = (ids[:, :groups] == group).astype(f32)
    marks_ref[...] = marks
    penalty = lax.dot_general(
        pow_ref[...], marks, NT, precision=HIGHEST, preferred_element_type=f32
    )
    s_ref[...] = acc_ref[...]
    for t in range(count):
        s_ref[...] += lax.dot_general(
            temp_ref[t],
            tile_of_particles(shards, 1, count * tile, t, tile, half),
            NT,
            preferred_element_type=f32,
        )
    acc = s_ref[...]
    acc = acc + jnp.where(
        real_index(acc.shape, 1, half), pltpu.roll(acc, lanes - half, 1), pltpu.roll(acc, half, 1)
    )
    scores = acc.reshape(poses, rows, lanes) - 0.5 * penalty[None]
    peak = jnp.max(jnp.max(scores, axis=0), axis=0, keepdims=True)
    total = jnp.sum(jnp.sum(jnp.exp(scores - peak[None]), axis=0), axis=0, keepdims=True)
    s_ref[...] = scores.reshape(poses * rows, lanes)
    stat_ref[0:1, :] = peak
    stat_ref[1:2, :] = total
    stat_ref[2:8, :] = jnp.zeros((6, lanes), f32)


def score(early, split, cos_t, sin_t, power, shards, half):
    first, late = early
    count, columns, width = late.shape
    freq = split.shape[2]
    lanes = sum(refs[0].shape[0] for refs in shards)
    chunked = [len(refs) > 1 for refs in shards]
    flops = 2 * columns * 256 * count * width
    acc_shape = jax.ShapeDtypeStruct((columns, lanes), f32)
    built = count - first.shape[0]
    temps = call(
        template_kernel,
        "templates",
        [VMEM] * 3,
        [pltpu.VMEM((built, columns, width), bf16)],
        (split, cos_t, sin_t),
        flops=40 * columns * built * width // 2,
    )[0]
    operands = [temps, first, *[refs[0] for refs in shards]]
    acc = call(
        functools.partial(first_score_kernel, chunked, half),
        "score0",
        [VMEM] * len(operands),
        [acc_shape],
        operands,
        flops=flops,
    )[0]
    operands = [late, power, acc]
    operands += [refs[0] for refs in shards] + [refs[-1] for refs in shards]
    return call(
        functools.partial(last_score_kernel, chunked, half),
        "score1",
        [VMEM] * len(operands),
        [
            acc_shape,
            jax.ShapeDtypeStruct((lanes, power.shape[1]), f32),
            jax.ShapeDtypeStruct((8, lanes), f32),
        ],
        operands,
        flops=flops,
    )


def slices_kernel(counts, targets, me_ref, *refs):
    whole_ref, refs = refs[-1], refs[:-1]
    shards, out_refs = regroup(refs[: -len(targets)], counts), refs[-len(targets) :]
    span = out_refs[0].shape[1]
    filled = [0] * len(targets)
    for k, refs in enumerate(shards):
        source = refs[0]
        height = source.shape[0]
        if len(refs) > 1:
            width = refs[-1].shape[1]
            for c, ref in enumerate(refs):
                whole_ref[:, c * width : (c + 1) * width] = ref[:, :width]
            source = whole_ref
        for i, (distance, skip) in enumerate(targets):
            if k >= skip:
                base = pl.multiple_of((me_ref[0] ^ distance) * span, LANES)
                out_refs[i][filled[i] : filled[i] + height, :] = source[:, pl.ds(base, span)]
                filled[i] += height


def cut_slices(me, shards, targets, span, freq):
    heights = [refs[0].shape[0] for refs in shards]
    operands = [me, *[ref for refs in shards for ref in refs]]
    out_heights = [sum(heights[skip:]) for _, skip in targets]
    return call(
        functools.partial(slices_kernel, [len(refs) for refs in shards], targets),
        "cut_slices",
        [SMEM] + [VMEM] * (len(operands) - 1),
        [jax.ShapeDtypeStruct((height, span), bf16) for height in out_heights],
        operands,
        [pltpu.VMEM((heights[-1], freq), bf16)],
        moved=4 * span * sum(out_heights),
        limit=VMEM_LIMIT if sum(heights) <= 128 else 2 * VMEM_LIMIT,
    )


def bundle_kernel(*refs):
    sources, out_ref = refs[:-1], refs[-1]
    rows = out_ref.shape[0] // len(sources)
    for i, ref in enumerate(sources):
        out_ref[i * rows : (i + 1) * rows, :] = ref[ref.shape[0] - rows :, :]


def bundle(slices, rows):
    span = slices[0].shape[1]
    return call(
        bundle_kernel,
        "bundle",
        [VMEM] * len(slices),
        [jax.ShapeDtypeStruct((len(slices) * rows, span), bf16)],
        slices,
        moved=4 * len(slices) * rows * span,
    )[0]


def xor_blocks(values, block, distance):
    lanes = values.shape[1]
    lane = lax.broadcasted_iota(jnp.int32, values.shape, 1)
    width = block
    while distance:
        if distance % 2:
            low = lax.rem(lane // width, 2) == 0
            values = jnp.where(
                low, pltpu.roll(values, lanes - width, 1), pltpu.roll(values, width, 1)
            )
        distance //= 2
        width *= 2
    return values


def rho_kernel(poses, half, paired, s_ref, marks_ref, *refs):
    stat_refs, (norm_ref, out_ref) = refs[: len(paired)], refs[len(paired) :]
    lanes = s_ref.shape[1]
    rows = s_ref.shape[0] // poses
    groups = marks_ref.shape[1]
    block = 2 * half
    peaks, totals = [], []
    for ref, distance in zip(stat_refs, paired):
        for at in range(0, ref.shape[0], 8):
            stats = xor_blocks(ref[at : at + 8, :], block, distance)
            peaks.append(stats[0:1])
            totals.append(stats[1:2])
    peak = functools.reduce(jnp.maximum, peaks)
    total = sum(t * jnp.exp(p - peak) for t, p in zip(totals, peaks))
    log_norm = peak + jnp.log(total)
    norm_ref[...] = log_norm
    rho = jnp.exp(s_ref[...].reshape(poses, rows, lanes) - log_norm[None])
    mass = lax.dot_general(
        jnp.where(real_index((rows, lanes), 1, half), jnp.sum(rho, axis=0), 0.0),
        marks_ref[...],
        NN,
        precision=HIGHEST,
        preferred_element_type=f32,
    )
    high = mass.astype(bf16)
    low = (mass - high.astype(f32)).astype(bf16)
    rho_low = rho.reshape(poses * rows, lanes).astype(bf16)
    cut = poses // 2 * rows
    lane = lax.broadcasted_iota(jnp.int32, (lanes, lanes), 0)
    column = lax.broadcasted_iota(jnp.int32, (lanes, lanes), 1)
    particle = lane // block * half + lax.rem(lane, block)
    real = lax.rem(lane, block) < half
    first = (real & (column == particle)).astype(f32).astype(bf16)
    second = (real & (column == particle + lanes // 2)).astype(f32).astype(bf16)
    packed = jnp.dot(rho_low[:cut], first, preferred_element_type=f32)
    packed += jnp.dot(rho_low[cut:], second, preferred_element_type=f32)
    out_ref[:cut, :] = packed.astype(bf16)
    if lanes > 2 * groups:
        out_ref[cut:, :] = jnp.zeros((rows, lanes), bf16)
    out_ref[cut:, :groups] = high
    out_ref[cut:, groups : 2 * groups] = low


def responsibilities(scores, marks, stats, paired, poses, half):
    columns, lanes = scores.shape
    return call(
        functools.partial(rho_kernel, poses, half, paired),
        "responsibilities",
        [VMEM] * (2 + len(stats)),
        [
            jax.ShapeDtypeStruct((1, lanes), f32),
            jax.ShapeDtypeStruct((columns // 2 + columns // poses, lanes), bf16),
        ],
        (scores, marks, *stats),
        flops=40 * columns * lanes,
    )


def gather_kernel(poses, half, counts, me_ref, s_ref, norm_ref, weight_ref, *refs):
    w_refs, (resp_ref, cw_ref, rows_ref) = refs[:-3], refs[-3:]
    span = rows_ref.shape[2]
    block = 2 * half
    here = pl.ds(pl.multiple_of(me_ref[0] * span, LANES), span)
    at = 0
    for refs in regroup(w_refs, counts):
        for ref in refs:
            for start in range(0, ref.shape[0], block):
                rows_ref[0, at : at + half, :] = ref[start : start + half, :]
                rows_ref[1, at : at + half, :] = ref[start + half : start + block, :]
                at += half
    weight = weight_ref[:, here]
    high = weight.astype(bf16)
    cw_ref[:, :span] = high
    cw_ref[:, span:] = (weight - high.astype(f32)).astype(bf16)
    rows = resp_ref.shape[0]
    lanes = s_ref.shape[1]
    scores = s_ref[...].reshape(poses, rows, lanes)
    pose_peak = jnp.max(scores, axis=0)
    total = jnp.sum(jnp.exp(scores - pose_peak[None]), axis=0)
    log_resp = pose_peak + jnp.log(total) - norm_ref[...]
    shape = (resp_ref.shape[1], lanes)
    lane = lax.broadcasted_iota(jnp.int32, shape, 1)
    row = ((lane // block) ^ me_ref[1]) * half + lax.rem(lane, block)
    take = (lax.broadcasted_iota(jnp.int32, shape, 0) == row) & (lax.rem(lane, block) < half)
    resp_ref[...] = lax.dot_general(
        log_resp, take.astype(f32), NT, precision=HIGHEST, preferred_element_type=f32
    )


def gather_rows(me, scores, norm, weight, slices, poses, half, span):
    columns, lanes = scores.shape
    counts = [len(refs) for refs in slices]
    slices = [w for refs in slices for w in refs]
    particles = sum(w.shape[0] for w in slices) // 2
    return call(
        functools.partial(gather_kernel, poses, half, counts),
        "gather_rows",
        [SMEM] + [VMEM] * (3 + len(slices)),
        [
            jax.ShapeDtypeStruct((columns // poses, lanes // 2), f32),
            jax.ShapeDtypeStruct((weight.shape[0], 2 * span), bf16),
            jax.ShapeDtypeStruct((2, particles, span), bf16),
        ],
        (me, scores, norm, weight, *slices),
        flops=GATHER_FLOPS,
        moved=8 * particles * span,
        limit=VMEM_LIMIT if particles <= 512 else 2 * VMEM_LIMIT,
    )


def finish_kernel(poses, groups, sources, half, me_ref, cw_ref, cos_ref, sin_ref, rows_ref, *refs):
    payloads, refs = refs[:sources], refs[sources:]
    last, (out_ref, rho_ref, inverse_ref, *buffers) = refs[:-5], refs[-5:]
    rows, _, span = out_ref.shape
    cut = poses // 2 * rows
    count = payloads[0].shape[1] // 2
    mass = jnp.zeros((rows, groups), f32)
    for i, ref in enumerate(payloads):
        rho_ref[:cut, i * count : (i + 1) * count] = ref[:cut, :count]
        rho_ref[cut:, i * count : (i + 1) * count] = ref[:cut, count:]
        mass += ref[cut:, :groups].astype(f32) + ref[cut:, groups : 2 * groups].astype(f32)
    high = mass.astype(bf16)
    mass = jnp.concatenate([high, (mass - high.astype(f32)).astype(bf16)], axis=0)
    terms = jnp.dot(mass, cw_ref[...], preferred_element_type=f32)
    denom = (terms[:rows, :span] + terms[rows:, :span]) + (terms[:rows, span:] + terms[rows:, span:])
    inverse_ref[...] = 1.0 / (denom + prior_precision)
    tiles = [(a, min(256, span - a)) for a in range(0, span, 256)]
    known = rows_ref.shape[1] // sources

    def rows_of(part, start, width):
        here = slice(start, start + width)
        if not last:
            return rows_ref[part, :, here]
        pieces = []
        for i in range(sources):
            pieces.append(rows_ref[part, i * known : (i + 1) * known, here])
            if i == 0:
                pieces.append(last[0][part * half : (part + 1) * half, here])
            else:
                at = (2 * (i - 1) + part) * half
                pieces.append(last[1][at : at + half, here])
        return jnp.concatenate(pieces, axis=0)

    def products(i):
        start, width = tiles[i]
        if 2 * width <= 256:
            both = jnp.concatenate([rows_of(0, start, width), rows_of(1, start, width)], axis=1)
            buffers[i % 2][0, :, : 2 * width] = jnp.dot(
                rho_ref[...], both, preferred_element_type=f32
            )
            return
        for part in range(2):
            buffers[i % 2][part, :, :width] = jnp.dot(
                rho_ref[...], rows_of(part, start, width), preferred_element_type=f32
            )

    def rotate(i):
        start, width = tiles[i]
        buffer = buffers[i % 2]
        for a in range(0, width, LANES):
            at = pl.ds(pl.multiple_of(me_ref[0] * span + start + a, LANES), LANES)
            numer_re = jnp.zeros((rows, LANES), f32)
            numer_im = jnp.zeros((rows, LANES), f32)
            for r in range(poses):
                cos_r = cos_ref[r : r + 1, at]
                sin_r = sin_ref[r : r + 1, at]
                s_re = buffer[0, r * rows : (r + 1) * rows, a : a + LANES]
                row = slice(r * rows, (r + 1) * rows)
                if 2 * width <= 256:
                    s_im = buffer[0, row, width + a : width + a + LANES]
                else:
                    s_im = buffer[1, row, a : a + LANES]
                numer_re = numer_re + s_re * cos_r + s_im * sin_r
                numer_im = numer_im + s_im * cos_r - s_re * sin_r
            here = slice(start + a, start + a + LANES)
            inverse = inverse_ref[:, here]
            out_ref[:, 0, here] = numer_re * inverse
            out_ref[:, 1, here] = numer_im * inverse

    products(0)
    for i in range(1, len(tiles)):
        products(i)
        rotate(i - 1)
    rotate(len(tiles) - 1)


def finish(me, weight, cos_t, sin_t, rows, payloads, last, cls_rows, half):
    poses = cos_t.shape[0]
    span = rows.shape[2]
    particles = len(payloads) * payloads[0].shape[1] // 2
    return call(
        functools.partial(finish_kernel, poses, weight.shape[0], len(payloads), half),
        "finish",
        [SMEM] + [VMEM] * (4 + len(payloads) + len(last)),
        [jax.ShapeDtypeStruct((cls_rows, 2, span), f32)],
        (me, weight, cos_t, sin_t, rows, *payloads, *last),
        [
            pltpu.VMEM((poses * cls_rows, particles), bf16),
            pltpu.VMEM((cls_rows, span), f32),
            pltpu.VMEM((2, poses * cls_rows, 256), f32),
            pltpu.VMEM((2, poses * cls_rows, 256), f32),
        ],
        flops=4 * poses * cls_rows * particles * span,
        limit=VMEM_LIMIT if particles <= 512 else 2 * VMEM_LIMIT,
    )[0]


def swap(values, axis, distance):
    size = lax.axis_size(axis)
    return lax.ppermute(values, axis, [(i, i ^ distance) for i in range(size)])


def local(particles, classes, ctf, noise_weight, group_ids, shifts):
    half, _, freq = particles.shape
    cls_rows = classes.shape[0]
    poses = shifts.shape[0]
    n_cls = lax.axis_size("cls")
    n_img = lax.axis_size("img")
    span = freq // n_img
    pairwise = n_cls == 4
    me_cls = lax.axis_index("cls") if pairwise else 0
    me = jnp.stack([lax.axis_index("img"), me_cls]).astype(jnp.int32)
    others = tuple(range(n_img - 1, 0, -1))

    own, *own_chunks = weigh(particles, ctf, noise_weight, group_ids)
    if pairwise:
        far = [swap(w, "cls", 2) for w in own_chunks]
        near = swap(own, "cls", 1)
        mine, *outgoing = cut_slices(me, [[own]], [(d, 0) for d in (0,) + others[:-1]], span, freq)
        slices = [mine] + [swap(w, "img", d) for w, d in zip(outgoing, others)]
    else:
        shards = [[lax.all_gather(own, "cls", axis=0, tiled=True)]]
        mine, *outgoing = cut_slices(me, shards, [(d, 0) for d in (0,) + others], span, freq)
        slices = [[w] for w in [mine] + [swap(w, "img", d) for w, d in zip(outgoing, others)]]

    split = jnp.transpose(classes, (1, 0, 2))
    cos_t, sin_t, power, weight = prepare(shifts, split, ctf, noise_weight)
    tile = template_tile(freq)
    count = freq // CHUNKS // tile
    built = count - count // 3
    early = [
        early_templates(split, cos_t, sin_t, count, count, tile),
        early_templates(split, cos_t, sin_t, built, count - built, tile),
    ][::-1]
    if pairwise:
        far, near, slices, split, early = lax.optimization_barrier(
            (far, near, slices, split, early)
        )
        third = [swap(w, "cls", 1) for w in far]
        targets = [(d, 1) for d in (0,) + others[:-1]] + [(others[-1], 0)]
        mine, *outgoing = cut_slices(me, [[own], [near], far], targets, span, freq)
        arrived = [mine] + [swap(w, "img", d) for w, d in zip(outgoing, others)]
        shards = [[own], [near], far, third]
    scores, marks, stat = score(early, split, cos_t, sin_t, power, shards, half)
    if pairwise:
        stat, arrived[-1] = lax.optimization_barrier((stat, arrived[-1]))
        stats = [stat] + [swap(stat, "cls", k) for k in range(n_cls - 1, 0, -1)]
        paired = (0,) + tuple(range(n_cls - 1, 0, -1))
        last = [*cut_slices(me, [third], [(0, 0)], span, freq)]
        last.append(swap(bundle(arrived[1:], 2 * half), "cls", 1))
        slices = [[a, b] for a, b in zip(slices, arrived)] + [arrived[-1:]]
    else:
        stats = [lax.all_gather(stat, "cls", axis=0, tiled=True)]
        paired = (0,)
        last = []
    norm, payload = responsibilities(scores, marks, stats, paired, poses, half)
    payloads = [payload] + [swap(payload, "img", d) for d in others]
    log_resp, weight_here, rows = gather_rows(
        me, scores, norm, weight, slices, poses, half, span
    )
    averages = finish(me, weight_here, cos_t, sin_t, rows, payloads, last, cls_rows, half)
    return (log_resp.T, averages)


def solution(mesh):
    placed = (
        P(("groups", "img", "cls"), None, None),
        P(("groups", "cls"), None, None),
        P("groups", None),
        P("groups"),
        P(("groups", "img", "cls")),
        P("groups", None),
    )
    return jax.shard_map(
        local,
        mesh=mesh,
        in_specs=placed,
        out_specs=(P(("groups", "img"), "cls"), P(("groups", "cls"), None, "img")),
        check_vma=False,
    )
```
